128 devices in a mesh: section: 2 (over core), dp: 32 (over y, z_lo, x), tensor: 2 (over z_hi).
Axes of the slice: x: 4, y: 4, z: 4 (z_hi: 2, z_lo: 2; z = z_hi * 2 + z_lo), core: 2. Of those that a mesh axis runs over, the one named last changes fastest.
Arguments:
- inputs: bfloat16 [3, 32, 128, 1536], P(None, 'dp', 'tensor'), may hold values from -24 to 24
- cotangent: bfloat16 [3, 32, 128, 1536], P(None, 'dp', 'tensor'), may hold values from -6 to 6
- plan: int32 [3], replicated, may hold values from 0 to 2, each once
- attn_gain: bfloat16 [2, 1536], P('section', 'dp'), may hold values from 0.099609375 to 1.8984375
- mlp_gain: bfloat16 [2, 1536], P('section', 'dp'), may hold values from 0.099609375 to 1.8984375
- w_query: bfloat16 [2, 1536, 1536], P('section', 'dp', 'tensor'), may hold values from -0.21875 to 0.21875
- key_weight: bfloat16 [2, 1536, 768], P('section', 'dp', 'tensor'), may hold values from -0.15625 to 0.15625
- value_weight: bfloat16 [2, 1536, 768], P('section', 'dp', 'tensor'), may hold values from -0.15625 to 0.15625
- w_out: bfloat16 [2, 1536, 1536], P('section', 'tensor', 'dp'), may hold values from -0.625 to 0.625
- w_gate: bfloat16 [2, 1536, 4096], P('section', 'dp', 'tensor'), may hold values from -0.15625 to 0.15625
- w_up: bfloat16 [2, 1536, 4096], P('section', 'dp', 'tensor'), may hold values from -0.15625 to 0.15625
- w_down: bfloat16 [2, 4096, 1536], P('section', 'tensor', 'dp'), may hold values from -0.125 to 0.125
Outputs:
- layer_outputs: bfloat16 [2, 3, 32, 128, 1536], P('section', None, 'dp', 'tensor')
- input_grads: bfloat16 [2, 3, 32, 128, 1536], P('section', None, 'dp', 'tensor')
- attn_gain_grad: float32 [2, 1536], P('section', 'dp')
- mlp_gain_grad: float32 [2, 1536], P('section', 'dp')
- w_query_grad: float32 [2, 1536, 1536], P('section', 'dp', 'tensor')
- w_key_grad: float32 [2, 1536, 768], P('section', 'dp', 'tensor')
- w_value_grad: float32 [2, 1536, 768], P('section', 'dp', 'tensor')
- w_out_grad: float32 [2, 1536, 1536], P('section', 'tensor', 'dp')
- w_gate_grad: float32 [2, 1536, 4096], P('section', 'dp', 'tensor')
- w_up_grad: float32 [2, 1536, 4096], P('section', 'dp', 'tensor')
- w_down_grad: float32 [2, 4096, 1536], P('section', 'tensor', 'dp')
The draws below stay inside these ranges and needn't reach their ends.
Inputs may be any that keep to these rules, and one draw needn't show every extreme that they name: `plan`: a permutation of the 3 micro-batches.
All inputs are finite; a program needn't handle non-finite values.
Results may differ from the reference program's by a relative error of at most 0.04.
Values may be sent and summed in bfloat16 or wider, within the bound.
No kernel may reach another device: no remote copies, remote signals or barrier semaphores. Data moves between devices by JAX's collectives and lax.ppermute only.
A program may use at most 192 MiB of HBM per device.

```python
import math
import jax
import jax.numpy as jnp
from jax import lax

MODEL_WIDTH = 1536
QUERY_HEADS = 16
SHARED_KV_HEADS = 8
HEAD_WIDTH = 96
FF = 4096
SEQUENCE_LENGTH = 128
MB = 3
BATCH = 32
N_SECTION = 2


def draw_inputs(key, part):
    key = jax.random.fold_in(key, 11)
    base_key, row_key, column_key = jax.random.split(key, 3)
    base = jnp.clip(jax.random.normal(base_key, (MB, BATCH, SEQUENCE_LENGTH, MODEL_WIDTH), jnp.float32), -4.0, 4.0)
    row_scale = jnp.exp(jax.random.uniform(row_key, (MB, BATCH, SEQUENCE_LENGTH, 1), jnp.float32, math.log(0.3), math.log(3.0)))
    column_scale = jnp.exp(jax.random.uniform(column_key, (MODEL_WIDTH,), jnp.float32, math.log(0.5), math.log(2.0)))
    return (base * row_scale * column_scale).astype(jnp.bfloat16)


def levels(own_key, dims, cuts, low, high):
    def one(axis_at, parts):
        steps = jax.random.uniform(jax.random.fold_in(jax.random.fold_in(own_key, 6), axis_at), (parts,), jnp.float32, low / len(cuts), high / len(cuts))
        return jnp.repeat(jnp.exp(steps), dims[axis_at] // parts).reshape((-1,) + (1,) * (len(dims) - axis_at - 1))

    level = one(*cuts[0])
    for cut in cuts[1:]:
        level = level * one(*cut)
    return level


def normal_values(own_key, extent, deviation, reach, shards=(), dtype=jnp.bfloat16):
    gain = levels(own_key, extent, shards, -0.22, 0.18) if shards else 1.0
    drawn = jax.random.normal(own_key, extent, jnp.float32) * deviation * gain
    return jnp.minimum(jnp.maximum(drawn, -reach), reach).astype(dtype)


def setup_inputs(seed: int = 0) -> dict:
    key_list = jax.random.split(jax.random.key(seed), 13)
    inputs = draw_inputs(jax.random.fold_in(key_list[12], 71), 0)
    cotangent = normal_values(key_list[1], (MB, BATCH, SEQUENCE_LENGTH, MODEL_WIDTH), 1.0, 6.0, ((1, 32), (2, 2)))
    plan = jax.random.permutation(key_list[2], MB).astype(jnp.int32)
    attn_gain = jnp.clip(1.0 + 0.18 * jax.random.normal(key_list[3], (N_SECTION, MODEL_WIDTH), jnp.float32), 0.099609375, 1.8984375).astype(jnp.bfloat16)
    mlp_gain = jnp.clip(1.0 + 0.18 * jax.random.normal(key_list[4], (N_SECTION, MODEL_WIDTH), jnp.float32), 0.099609375, 1.8984375).astype(jnp.bfloat16)
    w_query = normal_values(key_list[5], (N_SECTION, MODEL_WIDTH, QUERY_HEADS * HEAD_WIDTH), (MODEL_WIDTH // 2) ** -0.5, 0.21875, ((0, 2), (1, 32), (2, 2)))
    key_weight = normal_values(key_list[6], (N_SECTION, MODEL_WIDTH, SHARED_KV_HEADS * HEAD_WIDTH), MODEL_WIDTH ** -0.5, 0.15625, ((0, 2), (1, 32), (2, 2)))
    value_weight = normal_values(key_list[7], (N_SECTION, MODEL_WIDTH, SHARED_KV_HEADS * HEAD_WIDTH), MODEL_WIDTH ** -0.5, 0.15625, ((0, 2), (1, 32), (2, 2)))
    w_out = normal_values(key_list[8], (N_SECTION, QUERY_HEADS * HEAD_WIDTH, MODEL_WIDTH), (QUERY_HEADS * HEAD_WIDTH // 16) ** -0.5, 0.625, ((0, 2), (1, 2), (2, 32)))
    w_gate = normal_values(key_list[9], (N_SECTION, MODEL_WIDTH, FF), MODEL_WIDTH ** -0.5, 0.15625, ((0, 2), (1, 32), (2, 2)))
    w_up = normal_values(key_list[10], (N_SECTION, MODEL_WIDTH, FF), MODEL_WIDTH ** -0.5, 0.15625, ((0, 2), (1, 32), (2, 2)))
    w_down = normal_values(key_list[11], (N_SECTION, FF, MODEL_WIDTH), (FF // 2) ** -0.5, 0.125, ((0, 2), (1, 2), (2, 32)))
    return {"inputs": inputs, "cotangent": cotangent, "plan": plan, "attn_gain": attn_gain, "mlp_gain": mlp_gain, "w_query": w_query, "key_weight": key_weight, "value_weight": value_weight, "w_out": w_out, "w_gate": w_gate, "w_up": w_up, "w_down": w_down}


EPSILON = 1e-05
PRECISE = lax.Precision.HIGHEST
BLOCKED = -1e+30

@jax.custom_vjp
def low(v):
    return lax.optimization_barrier(v.astype(jnp.bfloat16)).astype(jnp.float32)

@jax.custom_vjp
def low_back(v):
    return v

def low_keep(v):
    return (low(v), None)

def low_pass(kept, grad):
    return (grad,)

def back_keep(v):
    return (v, None)

def back_low(kept, grad):
    return (low(grad),)
low.defvjp(low_keep, low_pass)
low_back.defvjp(back_keep, back_low)

def product(left_side, right_side):
    return jnp.dot(left_side, right_side, precision=PRECISE)

def norm_rows(residual, gain_row):
    inverse = lax.rsqrt(lax.optimization_barrier(jnp.mean(residual * residual, axis=-1, keepdims=True)) + EPSILON)
    return residual * inverse * gain_row

def attend(blocks):
    query_rows, projected_key_rows, projected_value_rows = blocks
    sequence_count = query_rows.shape[0]
    query_group_width = QUERY_HEADS // SHARED_KV_HEADS
    head_queries = query_rows.reshape(sequence_count, SEQUENCE_LENGTH, SHARED_KV_HEADS, query_group_width, HEAD_WIDTH)
    head_keys = projected_key_rows.reshape(sequence_count, SEQUENCE_LENGTH, SHARED_KV_HEADS, HEAD_WIDTH)
    head_values = projected_value_rows.reshape(sequence_count, SEQUENCE_LENGTH, SHARED_KV_HEADS, HEAD_WIDTH)
    scores = jnp.einsum('bqhgd,bkhd->bhgqk', head_queries, head_keys, precision=PRECISE) * HEAD_WIDTH ** (-0.5)
    scores = low_back(scores)
    causal = lax.broadcasted_iota(jnp.int32, (SEQUENCE_LENGTH, SEQUENCE_LENGTH), 0) >= lax.broadcasted_iota(jnp.int32, (SEQUENCE_LENGTH, SEQUENCE_LENGTH), 1)
    scores = jnp.where(causal, scores, BLOCKED)
    probability = low(jax.nn.softmax(scores, axis=-1))
    mixture = jnp.einsum('bhgqk,bkhd->bqhgd', probability, head_values, precision=PRECISE)
    return mixture.reshape(sequence_count, SEQUENCE_LENGTH, QUERY_HEADS * HEAD_WIDTH)

def layer_block(residual, attn_scale, mlp_scale, w_query, key_weight, value_weight, w_out, w_gate, w_up, w_down):
    sequence_count = residual.shape[0]
    group_count = math.gcd(sequence_count, max(1, 4096 // SEQUENCE_LENGTH))
    normed = low(norm_rows(residual, attn_scale))
    query_rows = low_back(low(product(normed, w_query)))
    projected_key_rows = low_back(low(product(normed, key_weight)))
    projected_value_rows = low_back(low(product(normed, value_weight)))

    def regroup(matrix):
        return matrix.reshape(sequence_count // group_count, group_count, SEQUENCE_LENGTH, matrix.shape[-1])
    mixture = lax.map(jax.checkpoint(attend), (regroup(query_rows), regroup(projected_key_rows), regroup(projected_value_rows)))
    mixture = low_back(low(mixture.reshape(sequence_count, SEQUENCE_LENGTH, QUERY_HEADS * HEAD_WIDTH)))
    middle = residual + low_back(product(mixture, w_out))
    normed_mid = low(norm_rows(middle, mlp_scale))
    gate_out = low_back(product(normed_mid, w_gate))
    up_out = low_back(product(normed_mid, w_up))
    hidden = low(jax.nn.silu(gate_out) * up_out)
    return middle + low_back(product(hidden, w_down))

def rounded(values):
    return lax.optimization_barrier(values.astype(jnp.bfloat16)).astype(jnp.float32)

def reference(inputs, cotangent, plan, attn_gain, mlp_gain, w_query, key_weight, value_weight, w_out, w_gate, w_up, w_down):
    seq_total = MB * BATCH
    residual = inputs.astype(jnp.float32).reshape(seq_total, SEQUENCE_LENGTH, MODEL_WIDTH)
    weights_all = (attn_gain, mlp_gain, w_query, key_weight, value_weight, w_out, w_gate, w_up, w_down)
    pullbacks = []
    outputs = []
    for section_index in range(N_SECTION):
        params = tuple((weight[section_index].astype(jnp.float32) for weight in weights_all))
        result, pullback = jax.vjp(layer_block, residual, *params)
        pullbacks.append(pullback)
        residual = rounded(result)
        outputs.append(residual)
    gradient = cotangent.astype(jnp.float32).reshape(seq_total, SEQUENCE_LENGTH, MODEL_WIDTH)
    input_list = [None] * N_SECTION
    weight_list = [None] * N_SECTION
    for section_index in reversed(range(N_SECTION)):
        pieces = pullbacks[section_index](gradient)
        gradient = rounded(pieces[0])
        input_list[section_index] = gradient
        weight_list[section_index] = pieces[1:]
    layer_outputs = jnp.stack(outputs).reshape(N_SECTION, MB, BATCH, SEQUENCE_LENGTH, MODEL_WIDTH)[:, plan].astype(jnp.bfloat16)
    input_grads = jnp.stack(input_list).reshape(N_SECTION, MB, BATCH, SEQUENCE_LENGTH, MODEL_WIDTH)[:, plan].astype(jnp.bfloat16)
    stacked = [jnp.stack([weight_list[section_index][number] for section_index in range(N_SECTION)]) for number in range(9)]
    return (layer_outputs, input_grads, stacked[0], stacked[1], stacked[2], stacked[3], stacked[4], stacked[5], stacked[6], stacked[7], stacked[8])
```

```python
import jax
import jax.numpy as jnp
from jax import lax
from jax.sharding import Mesh, PartitionSpec as P

HEAD_WIDTH = 96
EPSILON = 1e-05
BLOCKED = -1e30
SCORE_SCALE = HEAD_WIDTH ** (-0.5)
BF16 = jnp.bfloat16
F32 = jnp.float32

QUERY_COLS, KV_COLS = 384, 192
QKV_COLS = QUERY_COLS + 2 * KV_COLS
OUT_COLS = 384
HIDDEN_COLS = 1024


def swap(value, axis):
    return lax.ppermute(value, axis, [(0, 1), (1, 0)])


def pick(index, first, second):
    return jnp.where(index == 0, first, second)


def product(left_side, right_side):
    return jnp.dot(left_side, right_side, preferred_element_type=F32)


def times_transposed(left_side, right_side):
    return lax.dot_general(
        left_side, right_side, (((1,), (1,)), ((), ())), preferred_element_type=F32
    )


def contract_rows(left_side, right_side):
    return lax.dot_general(
        left_side, right_side, (((0,), (0,)), ((), ())), preferred_element_type=F32
    )


def norm_rows(residual):
    inverse = lax.rsqrt(jnp.mean(residual * residual, axis=-1, keepdims=True) + EPSILON)
    return inverse, (residual * inverse).astype(BF16)


def norm_back(weighted, residual, inverse):
    scaled = residual * inverse
    return inverse * (weighted - scaled * jnp.mean(weighted * scaled, axis=-1, keepdims=True))


def sum_four(core, partial):
    half = partial.shape[1] // 2
    keep = pick(core, partial[:, :half], partial[:, half:])
    give = pick(core, partial[:, half:], partial[:, :half])
    chip = (keep.astype(F32) + swap(give, "section").astype(F32)).astype(BF16)
    total = (chip.astype(F32) + swap(chip, "tensor").astype(F32)).astype(BF16)
    other = swap(total, "section")
    return jnp.concatenate([pick(core, total, other), pick(core, other, total)], axis=1)


def split_heads(rows):
    return rows.reshape(3, 128, -1, HEAD_WIDTH)


def attend(qkv):
    queries = qkv[:, :QUERY_COLS].reshape(3, 128, 2, 2, HEAD_WIDTH)
    keys = split_heads(qkv[:, QUERY_COLS : QUERY_COLS + KV_COLS])
    values = split_heads(qkv[:, QUERY_COLS + KV_COLS :])
    scores = (
        jnp.einsum("sqhgd,skhd->shgqk", queries, keys, preferred_element_type=F32) * SCORE_SCALE
    )
    causal = lax.broadcasted_iota(jnp.int32, (128, 128), 0) >= lax.broadcasted_iota(
        jnp.int32, (128, 128), 1
    )
    scores = jnp.where(causal, scores, BLOCKED)
    expanded = jnp.exp(scores - jnp.max(scores, axis=-1, keepdims=True))
    probability = expanded / jnp.sum(expanded, axis=-1, keepdims=True)
    mixture = jnp.einsum(
        "shgqk,skhd->sqhgd", probability.astype(BF16), values, preferred_element_type=F32
    )
    return mixture.astype(BF16).reshape(384, OUT_COLS), probability


def attend_back(qkv, probability, mixture_grad):
    queries = qkv[:, :QUERY_COLS].reshape(3, 128, 2, 2, HEAD_WIDTH)
    keys = split_heads(qkv[:, QUERY_COLS : QUERY_COLS + KV_COLS])
    values = split_heads(qkv[:, QUERY_COLS + KV_COLS :])
    grads = mixture_grad.reshape(3, 128, 2, 2, HEAD_WIDTH)
    values_grad = jnp.einsum(
        "shgqk,sqhgd->skhd", probability.astype(BF16), grads, preferred_element_type=F32
    )
    prob_grad = jnp.einsum("sqhgd,skhd->shgqk", grads, values, preferred_element_type=F32)
    centred = jnp.sum(probability * prob_grad, axis=-1, keepdims=True)
    score_grad = (probability * (prob_grad - centred)).astype(BF16)
    queries_grad = (
        jnp.einsum("shgqk,skhd->sqhgd", score_grad, keys, preferred_element_type=F32) * SCORE_SCALE
    )
    keys_grad = (
        jnp.einsum("shgqk,sqhgd->skhd", score_grad, queries, preferred_element_type=F32)
        * SCORE_SCALE
    )
    return jnp.concatenate(
        [
            queries_grad.astype(BF16).reshape(384, QUERY_COLS),
            keys_grad.astype(BF16).reshape(384, KV_COLS),
            values_grad.astype(BF16).reshape(384, KV_COLS),
        ],
        axis=1,
    )


def forward_layer(core, layer_in, w_attn, w_mlp):
    first_inverse, first = norm_rows(layer_in)
    qkv = product(first, w_attn[:, :QKV_COLS]).astype(BF16)
    mixture, probability = attend(qkv)
    attn_part = times_transposed(mixture, w_attn[:, QKV_COLS:]).astype(BF16)
    middle = layer_in + sum_four(core, attn_part).astype(F32)
    second_inverse, second = norm_rows(middle)
    gate_out = product(second, w_mlp[:, :HIDDEN_COLS])
    up_out = product(second, w_mlp[:, HIDDEN_COLS : 2 * HIDDEN_COLS])
    hidden = (jax.nn.silu(gate_out) * up_out).astype(BF16)
    mlp_part = times_transposed(hidden, w_mlp[:, 2 * HIDDEN_COLS :]).astype(BF16)
    result = (middle + sum_four(core, mlp_part).astype(F32)).astype(BF16)
    saved = (
        layer_in, first_inverse, first, qkv, probability, mixture,
        middle, second_inverse, second, gate_out, up_out, hidden,
    )
    return result, saved


def backward_layer(core, out_grad, saved, w_attn, w_mlp):
    (
        layer_in, first_inverse, first, qkv, probability, mixture,
        middle, second_inverse, second, gate_out, up_out, hidden,
    ) = saved
    hidden_grad = product(out_grad, w_mlp[:, 2 * HIDDEN_COLS :])
    sigmoid_gate = jax.nn.sigmoid(gate_out)
    gate_grad = (
        hidden_grad * up_out * (sigmoid_gate * (1.0 + gate_out * (1.0 - sigmoid_gate)))
    ).astype(BF16)
    up_grad = (hidden_grad * (gate_out * sigmoid_gate)).astype(BF16)
    pair_grad = jnp.concatenate([gate_grad, up_grad], axis=1)
    mlp_part = times_transposed(pair_grad, w_mlp[:, : 2 * HIDDEN_COLS]).astype(BF16)
    mlp_sum = sum_four(core, mlp_part).astype(F32)
    mlp_grad = jnp.concatenate(
        [
            contract_rows(second, pair_grad).astype(BF16),
            contract_rows(out_grad, hidden).astype(BF16),
        ],
        axis=1,
    )
    middle_grad = out_grad.astype(F32) + norm_back(mlp_sum, middle, second_inverse)
    attn_in = middle_grad.astype(BF16)
    mixture_grad = product(attn_in, w_attn[:, QKV_COLS:]).astype(BF16)
    qkv_grad = attend_back(qkv, probability, mixture_grad)
    attn_part = times_transposed(qkv_grad, w_attn[:, :QKV_COLS]).astype(BF16)
    attn_sum = sum_four(core, attn_part).astype(F32)
    attn_grad = jnp.concatenate(
        [
            contract_rows(first, qkv_grad).astype(BF16),
            contract_rows(attn_in, mixture).astype(BF16),
        ],
        axis=1,
    )
    input_grad = middle_grad + norm_back(attn_sum, layer_in, first_inverse)
    return input_grad.astype(BF16), attn_grad, mlp_grad


def halves(value):
    middle = value.shape[1] // 2
    return value[:, :middle], value[:, middle:]


def to_layers(core, low, high):
    mine, give = pick(core, low, high), pick(core, high, low)
    got = swap(give, "section")
    return pick(core, mine, got), pick(core, got, mine)


def from_layers(core, layer_zero, layer_one):
    mine, give = pick(core, layer_zero, layer_one), pick(core, layer_one, layer_zero)
    got = swap(give, "section")
    return pick(core, mine, got), pick(core, got, mine)


def gather_rows(z_low, share):
    other = swap(share, "zl")
    pair = jnp.concatenate([pick(z_low, share, other), pick(z_low, other, share)], axis=0)
    return lax.all_gather(pair, ("y", "x"), axis=0, tiled=True)


def scatter_rows(z_low, grad):
    pair = lax.psum_scatter(grad, ("y", "x"), scatter_dimension=0, tiled=True)
    keep = pick(z_low, pair[:48], pair[48:])
    give = pick(z_low, pair[48:], pair[:48])
    return (keep.astype(F32) + swap(give, "zl").astype(F32)).astype(BF16)


def to_ring_order(rows):
    lead = rows.shape[:-1]
    return jnp.swapaxes(rows.reshape(lead + (4, 2, 4, 48)), -3, -2).reshape(rows.shape)


def from_ring_order(rows):
    lead = rows.shape[:-1]
    return jnp.swapaxes(rows.reshape(lead + (4, 4, 2, 48)), -3, -2).reshape(rows.shape)


def join_positions(tensor, own):
    other = swap(own, "tensor")
    return jnp.concatenate(
        [pick(tensor, own, other), pick(tensor, other, own)], axis=1
    ).reshape(384, 1536)


def own_positions(tensor, rows):
    rows = rows.reshape(3, 128, 1536)
    return pick(tensor, rows[:, :64], rows[:, 64:])


def per_device(
    inputs, cotangent, plan, attn_gain, mlp_gain, w_query, key_weight, value_weight,
    w_out, w_gate, w_up, w_down,
):
    core = lax.axis_index("section")
    z_low = lax.axis_index("zl")
    tensor = lax.axis_index("tensor")

    attn_scale = attn_gain[0].astype(F32)[:, None]
    mlp_scale = mlp_gain[0].astype(F32)[:, None]

    def scaled(weight, scale):
        return (weight.astype(F32) * scale).astype(BF16)

    attn_shards = (w_query[0], key_weight[0], value_weight[0])
    mlp_shards = (w_gate[0], w_up[0])
    attn_pairs = [halves(scaled(weight, attn_scale)) for weight in attn_shards]
    attn_pairs.append(halves(w_out[0].T))
    mlp_pairs = [halves(scaled(weight, mlp_scale)) for weight in mlp_shards]
    mlp_pairs.append(halves(w_down[0].T))
    attn_low, attn_high = (jnp.concatenate(side, axis=1) for side in zip(*attn_pairs))
    mlp_low, mlp_high = (jnp.concatenate(side, axis=1) for side in zip(*mlp_pairs))
    attn_layers = to_layers(core, attn_low, attn_high)
    mlp_layers = to_layers(core, mlp_low, mlp_high)
    attn_weights, mlp_weights = [], []
    for layer in range(2):
        attn_weights.append(gather_rows(z_low, attn_layers[layer]))
        mlp_weights.append(gather_rows(z_low, mlp_layers[layer]))

    stream = join_positions(tensor, to_ring_order(inputs[:, 0][plan]))
    out_grad = join_positions(tensor, to_ring_order(cotangent[:, 0][plan]))

    kept, outputs = [], []
    for layer in range(2):
        stream, saved = forward_layer(
            core, stream.astype(F32), attn_weights[layer], mlp_weights[layer]
        )
        outputs.append(own_positions(tensor, stream))
        kept.append(saved)
    grads, attn_grads, mlp_grads = [None] * 2, [None] * 2, [None] * 2
    for layer in (1, 0):
        out_grad, attn_term, mlp_term = backward_layer(
            core, out_grad, kept[layer], attn_weights[layer], mlp_weights[layer]
        )
        grads[layer] = own_positions(tensor, out_grad)
        mlp_grads[layer] = scatter_rows(z_low, mlp_term)
        attn_grads[layer] = scatter_rows(z_low, attn_term)

    layer_outputs = from_ring_order(pick(core, outputs[0], outputs[1]))
    input_grads = from_ring_order(pick(core, grads[0], grads[1]))
    attn_low, attn_high = from_layers(core, *attn_grads)
    mlp_low, mlp_high = from_layers(core, *mlp_grads)

    def joined(low, high, start, width):
        return jnp.concatenate(
            [low[:, start : start + width], high[:, start : start + width]], axis=1
        ).astype(F32)

    query_grad = joined(attn_low, attn_high, 0, QUERY_COLS)
    key_grad = joined(attn_low, attn_high, QUERY_COLS, KV_COLS)
    value_grad = joined(attn_low, attn_high, QUERY_COLS + KV_COLS, KV_COLS)
    out_weight_grad = joined(attn_low, attn_high, QKV_COLS, OUT_COLS).T
    gate_grad = joined(mlp_low, mlp_high, 0, HIDDEN_COLS)
    up_grad = joined(mlp_low, mlp_high, HIDDEN_COLS, HIDDEN_COLS)
    down_grad = joined(mlp_low, mlp_high, 2 * HIDDEN_COLS, HIDDEN_COLS).T

    def gain_term(weights, weight_grads):
        return sum(
            jnp.sum(weight.astype(F32) * grad, axis=1)
            for weight, grad in zip(weights, weight_grads)
        )

    gain_terms = jnp.stack(
        [
            gain_term(attn_shards, (query_grad, key_grad, value_grad)),
            gain_term(mlp_shards, (gate_grad, up_grad)),
        ]
    )
    gain_terms = gain_terms + swap(gain_terms, "tensor")
    return (
        layer_outputs[None, :, None],
        input_grads[None, :, None],
        gain_terms[0][None],
        gain_terms[1][None],
        (query_grad * attn_scale)[None],
        (key_grad * attn_scale)[None],
        (value_grad * attn_scale)[None],
        out_weight_grad[None],
        (gate_grad * mlp_scale)[None],
        (up_grad * mlp_scale)[None],
        down_grad[None],
    )


def solution(mesh):
    split = Mesh(mesh.devices.reshape(2, 4, 2, 4, 2), ("section", "y", "zl", "x", "tensor"))
    dp = ("y", "zl", "x")
    rows = P("section", dp, "tensor")
    columns = P("section", "tensor", dp)
    return jax.shard_map(
        per_device,
        mesh=split,
        in_specs=(
            P(None, dp, "tensor", None),
            P(None, dp, "tensor", None),
            P(),
            P("section", dp),
            P("section", dp),
            rows,
            rows,
            rows,
            columns,
            rows,
            rows,
            columns,
        ),
        out_specs=(
            P("section", None, dp, "tensor", None),
            P("section", None, dp, "tensor", None),
            P("section", dp),
            P("section", dp),
            rows,
            rows,
            rows,
            columns,
            rows,
            rows,
            columns,
        ),
        check_vma=False,
    )
```

```python
import functools

import jax
import jax.numpy as jnp
from jax import lax
from jax.experimental import pallas as pl
from jax.experimental.pallas import tpu as pltpu
from jax.sharding import Mesh, PartitionSpec as P

HEAD_WIDTH = 96
EPSILON = 1e-05
BLOCKED = -1e30
SCORE_SCALE = HEAD_WIDTH ** (-0.5)
BF16 = jnp.bfloat16
F32 = jnp.float32

QUERY_COLS, KV_COLS = 384, 192
QKV_COLS = QUERY_COLS + 2 * KV_COLS
OUT_COLS = 384
HIDDEN_COLS = 1024
ATTN_COLS = QKV_COLS + OUT_COLS
MLP_COLS = 3 * HIDDEN_COLS
HIDDEN_TILE = 256
WIDTH = 1536
HALF = WIDTH // 2
VMEM_LIMIT = 56 * 1024 * 1024


def swap(value, axis):
    return lax.ppermute(value, axis, [(0, 1), (1, 0)])


def pick(index, first, second):
    return jnp.where(index == 0, first, second)


def contract_rows(left_side, right_side):
    return lax.dot_general(
        left_side, right_side, (((0,), (0,)), ((), ())), preferred_element_type=F32
    )


def norm_back(weighted, residual, inverse):
    scaled = residual * inverse
    return inverse * (weighted - scaled * jnp.mean(weighted * scaled, axis=-1, keepdims=True))


def vmem_whole():
    return pl.BlockSpec(memory_space=pltpu.VMEM)


def smem_whole():
    return pl.BlockSpec(memory_space=pltpu.SMEM)


def shape(rows, columns, dtype):
    return jax.ShapeDtypeStruct((rows, columns), dtype)


def half_of(core_ref, which):
    position = core_ref[0] if which == 0 else 1 - core_ref[0]
    return pl.ds(pl.multiple_of(position * HALF, HALF), HALF)


def nt_dot(left_side, right_side):
    return lax.dot_general(
        left_side, right_side, (((1,), (1,)), ((), ())), preferred_element_type=F32
    )


def tn_dot(left_side, right_side):
    return lax.dot_general(
        left_side, right_side, (((0,), (0,)), ((), ())), preferred_element_type=F32
    )


def nn_dot(left_side, right_side):
    return jnp.dot(left_side, right_side, preferred_element_type=F32)


def inverse_norm(rows):
    return lax.rsqrt(jnp.mean(rows * rows, axis=-1, keepdims=True) + EPSILON)


def causal_mask():
    row = lax.broadcasted_iota(jnp.int32, (128, 128), 0)
    return row >= lax.broadcasted_iota(jnp.int32, (128, 128), 1)


def two_heads(ref, rows, start):
    return jnp.concatenate(
        [
            ref[rows, start : start + HEAD_WIDTH],
            ref[rows, start + HEAD_WIDTH : start + 2 * HEAD_WIDTH],
        ],
        axis=0,
    )


def attention_forward_body(sequences, core_ref, first_ref, w_ref, qkv_ref, prob_ref, mix_ref, keep_ref, give_ref):
    qkv_ref[...] = nn_dot(first_ref[...], w_ref[:, :QKV_COLS]).astype(BF16)
    mask = causal_mask()
    mask = jnp.concatenate([mask, mask], axis=0)
    for sequence in range(sequences):
        rows = slice(128 * sequence, 128 * (sequence + 1))
        for group in range(2):
            queries = two_heads(qkv_ref, rows, 2 * HEAD_WIDTH * group)
            key_at = QUERY_COLS + HEAD_WIDTH * group
            value_at = key_at + KV_COLS
            scores = nt_dot(queries, qkv_ref[rows, key_at : key_at + HEAD_WIDTH]) * SCORE_SCALE
            scores = jnp.where(mask, scores, BLOCKED)
            expanded = jnp.exp(scores - jnp.max(scores, axis=-1, keepdims=True))
            probability = expanded / jnp.sum(expanded, axis=-1, keepdims=True)
            prob_ref[2 * sequence + group] = probability
            mixed = nn_dot(
                probability.astype(BF16), qkv_ref[rows, value_at : value_at + HEAD_WIDTH]
            ).astype(BF16)
            at = 2 * HEAD_WIDTH * group
            mix_ref[rows, at : at + HEAD_WIDTH] = mixed[:128]
            mix_ref[rows, at + HEAD_WIDTH : at + 2 * HEAD_WIDTH] = mixed[128:]
    mixture = mix_ref[...]
    give_ref[...] = nt_dot(mixture, w_ref[half_of(core_ref, 1), QKV_COLS:]).astype(BF16)
    keep_ref[...] = nt_dot(mixture, w_ref[half_of(core_ref, 0), QKV_COLS:]).astype(BF16)


def attention_first_kernel(sequences, core_ref, x_ref, w_ref, first_ref, *rest):
    rows = x_ref[...].astype(F32)
    first_ref[...] = (rows * inverse_norm(rows)).astype(BF16)
    attention_forward_body(sequences, core_ref, first_ref, w_ref, *rest)


def attention_next_kernel(sequences, core_ref, middle_ref, own_ref, other_ref, w_ref, x_ref, first_ref, *rest):
    for which, part in ((0, own_ref), (1, other_ref)):
        at = half_of(core_ref, which)
        x_ref[:, at] = (middle_ref[:, at] + part[...].astype(F32)).astype(BF16)
    rows = x_ref[...].astype(F32)
    first_ref[...] = (rows * inverse_norm(rows)).astype(BF16)
    attention_forward_body(sequences, core_ref, first_ref, w_ref, *rest)


def attention_forward(core, x, middle, sums, w_attn):
    rows = (x if middle is None else middle).shape[0]
    sequences = rows // 128
    outs = [
        shape(rows, WIDTH, BF16),
        shape(rows, QKV_COLS, BF16),
        jax.ShapeDtypeStruct((2 * sequences, 256, 128), F32),
        shape(rows, OUT_COLS, BF16),
        shape(rows, HALF, BF16),
        shape(rows, HALF, BF16),
    ]
    if middle is None:
        operands, kernel = (core, x, w_attn), attention_first_kernel
    else:
        operands, kernel = (core, middle, *sums, w_attn), attention_next_kernel
        outs = [shape(rows, WIDTH, BF16)] + outs
    results = pl.pallas_call(
        functools.partial(kernel, sequences),
        in_specs=[smem_whole()] + [vmem_whole()] * (len(operands) - 1),
        out_specs=[vmem_whole()] * len(outs),
        out_shape=outs,
        compiler_params=pltpu.CompilerParams(vmem_limit_bytes=VMEM_LIMIT),
        cost_estimate=pl.CostEstimate(
            flops=2 * rows * WIDTH * ATTN_COLS, bytes_accessed=8_000_000, transcendentals=0
        ),
        name="attention_forward",
    )(*operands)
    return ([x] if middle is None else []) + list(results)


def mlp_forward_kernel(core_ref, x_ref, own_ref, other_ref, gate_w, up_w, down_w, middle_ref, second_ref, gate_ref, up_ref, hidden_ref, keep_ref, give_ref, total):
    step = pl.program_id(0)

    @pl.when(step == 0)
    def _():
        for which, part in ((0, own_ref), (1, other_ref)):
            at = half_of(core_ref, which)
            middle_ref[:, at] = x_ref[:, at].astype(F32) + part[...].astype(F32)
        rows = middle_ref[...]
        second_ref[...] = (rows * inverse_norm(rows)).astype(BF16)
        total[...] = jnp.zeros_like(total)

    gate_out = nn_dot(second_ref[...], gate_w[...])
    up_out = nn_dot(second_ref[...], up_w[...])
    gate_ref[...] = gate_out
    up_ref[...] = up_out
    hidden = (gate_out * (1.0 / (1.0 + jnp.exp(-gate_out))) * up_out).astype(BF16)
    hidden_ref[...] = hidden
    total[...] += nt_dot(hidden, down_w[...])

    @pl.when(step == pl.num_programs(0) - 1)
    def _():
        give_ref[...] = total[:, half_of(core_ref, 1)].astype(BF16)
        keep_ref[...] = total[:, half_of(core_ref, 0)].astype(BF16)


def fixed(rows, columns):
    return pl.BlockSpec((rows, columns), lambda j: (0, 0))


def tile(rows, first=0):
    return pl.BlockSpec((rows, HIDDEN_TILE), lambda j: (0, first + j))


HIDDEN_STEPS = HIDDEN_COLS // HIDDEN_TILE


def mlp_forward(core, x, sums, w_mlp):
    rows = x.shape[0]
    return pl.pallas_call(
        mlp_forward_kernel,
        grid=(HIDDEN_STEPS,),
        in_specs=[
            smem_whole(),
            fixed(rows, WIDTH),
            fixed(rows, HALF),
            fixed(rows, HALF),
            tile(WIDTH),
            tile(WIDTH, HIDDEN_STEPS),
            tile(WIDTH, 2 * HIDDEN_STEPS),
        ],
        out_specs=[
            fixed(rows, WIDTH),
            fixed(rows, WIDTH),
            tile(rows),
            tile(rows),
            tile(rows),
            fixed(rows, HALF),
            fixed(rows, HALF),
        ],
        out_shape=[
            shape(rows, WIDTH, F32),
            shape(rows, WIDTH, BF16),
            shape(rows, HIDDEN_COLS, F32),
            shape(rows, HIDDEN_COLS, F32),
            shape(rows, HIDDEN_COLS, BF16),
            shape(rows, HALF, BF16),
            shape(rows, HALF, BF16),
        ],
        scratch_shapes=[pltpu.VMEM((rows, WIDTH), F32)],
        compiler_params=pltpu.CompilerParams(vmem_limit_bytes=VMEM_LIMIT),
        cost_estimate=pl.CostEstimate(
            flops=2 * rows * WIDTH * MLP_COLS, bytes_accessed=15_000_000, transcendentals=0
        ),
        name="mlp_forward",
    )(core, x, *sums, w_mlp, w_mlp, w_mlp)


def mlp_backward_kernel(core_ref, g_ref, gate_ref, up_ref, gate_w, up_w, down_w, gate_grad_ref, up_grad_ref, keep_ref, give_ref, total):
    step = pl.program_id(0)

    @pl.when(step == 0)
    def _():
        total[...] = jnp.zeros_like(total)

    hidden_grad = nn_dot(g_ref[...], down_w[...])
    gate_out = gate_ref[...]
    sigmoid_gate = 1.0 / (1.0 + jnp.exp(-gate_out))
    gate_grad = (
        hidden_grad * up_ref[...] * (sigmoid_gate * (1.0 + gate_out * (1.0 - sigmoid_gate)))
    ).astype(BF16)
    up_grad = (hidden_grad * (gate_out * sigmoid_gate)).astype(BF16)
    gate_grad_ref[...] = gate_grad
    up_grad_ref[...] = up_grad
    total[...] += nt_dot(gate_grad, gate_w[...]) + nt_dot(up_grad, up_w[...])

    @pl.when(step == pl.num_programs(0) - 1)
    def _():
        give_ref[...] = total[:, half_of(core_ref, 1)].astype(BF16)
        keep_ref[...] = total[:, half_of(core_ref, 0)].astype(BF16)


def mlp_backward_next_kernel(core_ref, x_ref, middle_grad_ref, own_ref, other_ref, gate_ref, up_ref, gate_w, up_w, down_w, g_ref, gate_grad_ref, up_grad_ref, keep_ref, give_ref, total):
    @pl.when(pl.program_id(0) == 0)
    def _():
        for which, part in ((0, own_ref), (1, other_ref)):
            total[:, half_of(core_ref, which)] = part[...].astype(F32)
        rows = x_ref[...].astype(F32)
        inverse = inverse_norm(rows)
        g_ref[...] = (middle_grad_ref[...] + norm_back(total[...], rows, inverse)).astype(BF16)

    mlp_backward_kernel(core_ref, g_ref, gate_ref, up_ref, gate_w, up_w, down_w, gate_grad_ref, up_grad_ref, keep_ref, give_ref, total)


def mlp_backward(core, g, above, gate_out, up_out, w_mlp):
    rows = gate_out.shape[0]
    if above is None:
        lead, kernel, lead_specs = (g,), mlp_backward_kernel, [fixed(rows, WIDTH)]
    else:
        lead, kernel = above, mlp_backward_next_kernel
        lead_specs = [fixed(rows, WIDTH)] * 2 + [fixed(rows, HALF)] * 2
    out_specs = [tile(rows), tile(rows), fixed(rows, HALF), fixed(rows, HALF)]
    out_shape = [
        shape(rows, HIDDEN_COLS, BF16),
        shape(rows, HIDDEN_COLS, BF16),
        shape(rows, HALF, BF16),
        shape(rows, HALF, BF16),
    ]
    if above is not None:
        out_specs = [fixed(rows, WIDTH)] + out_specs
        out_shape = [shape(rows, WIDTH, BF16)] + out_shape
    results = pl.pallas_call(
        kernel,
        grid=(HIDDEN_STEPS,),
        in_specs=[smem_whole()]
        + lead_specs
        + [
            tile(rows),
            tile(rows),
            tile(WIDTH),
            tile(WIDTH, HIDDEN_STEPS),
            tile(WIDTH, 2 * HIDDEN_STEPS),
        ],
        out_specs=out_specs,
        out_shape=out_shape,
        scratch_shapes=[pltpu.VMEM((rows, WIDTH), F32)],
        compiler_params=pltpu.CompilerParams(vmem_limit_bytes=VMEM_LIMIT),
        cost_estimate=pl.CostEstimate(
            flops=2 * rows * WIDTH * MLP_COLS, bytes_accessed=15_000_000, transcendentals=0
        ),
        name="mlp_backward",
    )(core, *lead, gate_out, up_out, w_mlp, w_mlp, w_mlp)
    return ([g] if above is None else []) + list(results)


def attention_backward_kernel(sequences, core_ref, g_ref, middle_ref, own_ref, other_ref, qkv_ref, prob_ref, w_ref, middle_grad_ref, attn_in_ref, qkv_grad_ref, keep_ref, give_ref, mix_grad):
    for which, part in ((0, own_ref), (1, other_ref)):
        middle_grad_ref[:, half_of(core_ref, which)] = part[...].astype(F32)
    middle = middle_ref[...]
    middle_grad = g_ref[...].astype(F32) + norm_back(
        middle_grad_ref[...], middle, inverse_norm(middle)
    )
    middle_grad_ref[...] = middle_grad
    attn_in_ref[...] = middle_grad.astype(BF16)
    mix_grad[...] = nn_dot(attn_in_ref[...], w_ref[:, QKV_COLS:]).astype(BF16)
    for sequence in range(sequences):
        rows = slice(128 * sequence, 128 * (sequence + 1))
        for group in range(2):
            at = 2 * HEAD_WIDTH * group
            key_at = QUERY_COLS + HEAD_WIDTH * group
            value_at = key_at + KV_COLS
            grads = two_heads(mix_grad, rows, at)
            queries = two_heads(qkv_ref, rows, at)
            keys = qkv_ref[rows, key_at : key_at + HEAD_WIDTH]
            probability = prob_ref[2 * sequence + group]
            prob_grad = nt_dot(grads, qkv_ref[rows, value_at : value_at + HEAD_WIDTH])
            centred = jnp.sum(probability * prob_grad, axis=-1, keepdims=True)
            score_grad = (probability * (prob_grad - centred)).astype(BF16)
            query_grad = (nn_dot(score_grad, keys) * SCORE_SCALE).astype(BF16)
            qkv_grad_ref[rows, at : at + HEAD_WIDTH] = query_grad[:128]
            qkv_grad_ref[rows, at + HEAD_WIDTH : at + 2 * HEAD_WIDTH] = query_grad[128:]
            qkv_grad_ref[rows, key_at : key_at + HEAD_WIDTH] = (
                tn_dot(score_grad, queries) * SCORE_SCALE
            ).astype(BF16)
            qkv_grad_ref[rows, value_at : value_at + HEAD_WIDTH] = tn_dot(
                probability.astype(BF16), grads
            ).astype(BF16)
    qkv_grad = qkv_grad_ref[...]
    give_ref[...] = nt_dot(qkv_grad, w_ref[half_of(core_ref, 1), :QKV_COLS]).astype(BF16)
    keep_ref[...] = nt_dot(qkv_grad, w_ref[half_of(core_ref, 0), :QKV_COLS]).astype(BF16)


def attention_backward(core, g, middle, sums, qkv, probability, w_attn):
    rows = g.shape[0]
    return pl.pallas_call(
        functools.partial(attention_backward_kernel, rows // 128),
        in_specs=[smem_whole()] + [vmem_whole()] * 7,
        out_specs=[vmem_whole()] * 5,
        out_shape=[
            shape(rows, WIDTH, F32),
            shape(rows, WIDTH, BF16),
            shape(rows, QKV_COLS, BF16),
            shape(rows, HALF, BF16),
            shape(rows, HALF, BF16),
        ],
        scratch_shapes=[pltpu.VMEM((rows, OUT_COLS), BF16)],
        compiler_params=pltpu.CompilerParams(vmem_limit_bytes=VMEM_LIMIT),
        cost_estimate=pl.CostEstimate(
            flops=2 * rows * WIDTH * ATTN_COLS, bytes_accessed=12_000_000, transcendentals=0
        ),
        name="attention_backward",
    )(core, g, middle, *sums, qkv, probability, w_attn)


def sum_four(keep, give):
    chip = (keep.astype(F32) + swap(give, "section").astype(F32)).astype(BF16)
    total = (chip.astype(F32) + swap(chip, "tensor").astype(F32)).astype(BF16)
    return total, swap(total, "section")


def halves(value):
    middle = value.shape[1] // 2
    return value[:, :middle], value[:, middle:]


def to_layers(core, low, high):
    mine, give = pick(core, low, high), pick(core, high, low)
    got = swap(give, "section")
    return pick(core, mine, got), pick(core, got, mine)


def from_layers(core, layer_zero, layer_one):
    mine, give = pick(core, layer_zero, layer_one), pick(core, layer_one, layer_zero)
    got = swap(give, "section")
    return pick(core, mine, got), pick(core, got, mine)


def gather_rows(z_low, share):
    other = swap(share, "zl")
    pair = jnp.concatenate([pick(z_low, share, other), pick(z_low, other, share)], axis=0)
    return lax.all_gather(pair, ("y", "x"), axis=0, tiled=True)


def scatter_rows(z_low, grad):
    pair = lax.psum_scatter(grad, ("y", "x"), scatter_dimension=0, tiled=True)
    keep = pick(z_low, pair[:48], pair[48:])
    give = pick(z_low, pair[48:], pair[:48])
    return (keep.astype(F32) + swap(give, "zl").astype(F32)).astype(BF16)


def to_ring_order(rows):
    lead = rows.shape[:-1]
    return jnp.swapaxes(rows.reshape(lead + (4, 2, 4, 48)), -3, -2).reshape(rows.shape)


def from_ring_order(rows):
    lead = rows.shape[:-1]
    return jnp.swapaxes(rows.reshape(lead + (4, 4, 2, 48)), -3, -2).reshape(rows.shape)


def join_positions(tensor, own):
    other = swap(own, "tensor")
    return jnp.concatenate(
        [pick(tensor, own, other), pick(tensor, other, own)], axis=2
    ).reshape(2, 384, WIDTH)


def own_positions(tensor, rows):
    rows = rows.reshape(3, 128, 1536)
    return pick(tensor, rows[:, :64], rows[:, 64:])


def per_device(
    inputs, cotangent, plan, attn_gain, mlp_gain, w_query, key_weight, value_weight,
    w_out, w_gate, w_up, w_down,
):
    core = lax.axis_index("section")
    z_low = lax.axis_index("zl")
    tensor = lax.axis_index("tensor")

    attn_scale = attn_gain[0].astype(F32)[:, None]
    mlp_scale = mlp_gain[0].astype(F32)[:, None]

    def scaled(weight, scale):
        return (weight.astype(F32) * scale).astype(BF16)

    attn_shards = (w_query[0], key_weight[0], value_weight[0])
    mlp_shards = (w_gate[0], w_up[0])
    attn_pairs = [halves(scaled(weight, attn_scale)) for weight in attn_shards]
    attn_pairs.append(halves(w_out[0].T))
    mlp_pairs = [halves(scaled(weight, mlp_scale)) for weight in mlp_shards]
    mlp_pairs.append(halves(w_down[0].T))
    attn_low, attn_high = (jnp.concatenate(side, axis=1) for side in zip(*attn_pairs))
    mlp_low, mlp_high = (jnp.concatenate(side, axis=1) for side in zip(*mlp_pairs))
    attn_layers = to_layers(core, attn_low, attn_high)
    mlp_layers = to_layers(core, mlp_low, mlp_high)
    attn_weights, mlp_weights = [], []
    for layer in range(2):
        attn_weights.append(gather_rows(z_low, attn_layers[layer]))
        mlp_weights.append(gather_rows(z_low, mlp_layers[layer]))

    core_ref = core.astype(jnp.int32).reshape(1)
    both = to_ring_order(jnp.stack([inputs[:, 0][plan], cotangent[:, 0][plan]]))
    stream, out_grad = join_positions(tensor, both)

    kept, outputs = [], []
    x, middle, sums = stream, None, None
    for layer in range(2):
        x, first, qkv, probability, mixture, keep, give = attention_forward(
            core_ref, x, middle, sums, attn_weights[layer]
        )
        if layer == 1:
            outputs.append(own_positions(tensor, x))
        middle, second, gate_out, up_out, hidden, keep, give = mlp_forward(
            core_ref, x, sum_four(keep, give), mlp_weights[layer]
        )
        sums = sum_four(keep, give)
        kept.append((x, first, qkv, probability, mixture, middle, second, gate_out, up_out, hidden))
    last = middle + jnp.concatenate(
        [pick(core, sums[0], sums[1]), pick(core, sums[1], sums[0])], axis=1
    ).astype(F32)
    outputs.append(own_positions(tensor, last.astype(BF16)))

    grads, attn_grads, mlp_grads = [None] * 2, [None] * 2, [None] * 2
    above = None
    for layer in (1, 0):
        x, first, qkv, probability, mixture, middle, second, gate_out, up_out, hidden = kept[layer]
        out_grad, gate_grad, up_grad, keep, give = mlp_backward(
            core_ref, out_grad, above, gate_out, up_out, mlp_weights[layer]
        )
        if layer == 0:
            grads[1] = own_positions(tensor, out_grad)
        mlp_term = jnp.concatenate(
            [
                contract_rows(second, gate_grad).astype(BF16),
                contract_rows(second, up_grad).astype(BF16),
                contract_rows(out_grad, hidden).astype(BF16),
            ],
            axis=1,
        )
        sums = sum_four(keep, give)
        sums, mlp_term = lax.optimization_barrier((sums, mlp_term))
        mlp_grads[layer] = scatter_rows(z_low, mlp_term)
        middle_grad, attn_in, qkv_grad, keep, give = attention_backward(
            core_ref, out_grad, middle, sums, qkv, probability, attn_weights[layer]
        )
        attn_term = jnp.concatenate(
            [
                contract_rows(first, qkv_grad).astype(BF16),
                contract_rows(attn_in, mixture).astype(BF16),
            ],
            axis=1,
        )
        sums = sum_four(keep, give)
        sums, attn_term = lax.optimization_barrier((sums, attn_term))
        attn_grads[layer] = scatter_rows(z_low, attn_term)
        above = (x, middle_grad, *sums)
    x, middle_grad, own, other = above
    rows = x.astype(F32)
    weighted = jnp.concatenate(
        [pick(core, own, other), pick(core, other, own)], axis=1
    ).astype(F32)
    last = middle_grad + norm_back(weighted, rows, inverse_norm(rows))
    grads[0] = own_positions(tensor, last.astype(BF16))

    layer_outputs = from_ring_order(pick(core, outputs[0], outputs[1]))
    input_grads = from_ring_order(pick(core, grads[0], grads[1]))
    attn_low, attn_high = from_layers(core, *attn_grads)
    mlp_low, mlp_high = from_layers(core, *mlp_grads)

    def joined(low, high, start, width):
        return jnp.concatenate(
            [low[:, start : start + width], high[:, start : start + width]], axis=1
        ).astype(F32)

    query_grad = joined(attn_low, attn_high, 0, QUERY_COLS)
    key_grad = joined(attn_low, attn_high, QUERY_COLS, KV_COLS)
    value_grad = joined(attn_low, attn_high, QUERY_COLS + KV_COLS, KV_COLS)
    out_weight_grad = joined(attn_low, attn_high, QKV_COLS, OUT_COLS).T
    gate_grad = joined(mlp_low, mlp_high, 0, HIDDEN_COLS)
    up_grad = joined(mlp_low, mlp_high, HIDDEN_COLS, HIDDEN_COLS)
    down_grad = joined(mlp_low, mlp_high, 2 * HIDDEN_COLS, HIDDEN_COLS).T

    def gain_term(weights, weight_grads):
        return sum(
            jnp.sum(weight.astype(F32) * grad, axis=1)
            for weight, grad in zip(weights, weight_grads)
        )

    gain_terms = jnp.stack(
        [
            gain_term(attn_shards, (query_grad, key_grad, value_grad)),
            gain_term(mlp_shards, (gate_grad, up_grad)),
        ]
    )
    gain_terms = gain_terms + swap(gain_terms, "tensor")
    return (
        layer_outputs[None, :, None],
        input_grads[None, :, None],
        gain_terms[0][None],
        gain_terms[1][None],
        (query_grad * attn_scale)[None],
        (key_grad * attn_scale)[None],
        (value_grad * attn_scale)[None],
        out_weight_grad[None],
        (gate_grad * mlp_scale)[None],
        (up_grad * mlp_scale)[None],
        down_grad[None],
    )


def solution(mesh):
    split = Mesh(mesh.devices.reshape(2, 4, 2, 4, 2), ("section", "y", "zl", "x", "tensor"))
    dp = ("y", "zl", "x")
    rows = P("section", dp, "tensor")
    columns = P("section", "tensor", dp)
    return jax.shard_map(
        per_device,
        mesh=split,
        in_specs=(
            P(None, dp, "tensor", None),
            P(None, dp, "tensor", None),
            P(),
            P("section", dp),
            P("section", dp),
            rows,
            rows,
            rows,
            columns,
            rows,
            rows,
            columns,
        ),
        out_specs=(
            P("section", None, dp, "tensor", None),
            P("section", None, dp, "tensor", None),
            P("section", dp),
            P("section", dp),
            rows,
            rows,
            rows,
            columns,
            rows,
            rows,
            columns,
        ),
        check_vma=False,
    )
```

```python
import functools

import jax
import jax.numpy as jnp
from jax import lax
from jax.experimental import pallas as pl
from jax.experimental.pallas import tpu as pltpu
from jax.sharding import Mesh, PartitionSpec as P

HEAD_WIDTH = 96
EPSILON = 1e-05
BLOCKED = -1e30
SCORE_SCALE = HEAD_WIDTH ** (-0.5)
BF16 = jnp.bfloat16
F32 = jnp.float32

QUERY_COLS, KV_COLS = 384, 192
QKV_COLS = QUERY_COLS + 2 * KV_COLS
OUT_COLS = 384
HIDDEN_COLS = 1024
ATTN_COLS = QKV_COLS + OUT_COLS
MLP_COLS = 3 * HIDDEN_COLS
HIDDEN_TILE = 256
WIDTH = 1536
HALF = WIDTH // 2
GRANULE = 48
VMEM_LIMIT = 56 * 1024 * 1024


def swap(value, axis):
    return lax.ppermute(value, axis, [(0, 1), (1, 0)])


def pick(index, first, second):
    return jnp.where(index == 0, first, second)


def contract_rows(left_side, right_side):
    return lax.dot_general(
        left_side, right_side, (((0,), (0,)), ((), ())), preferred_element_type=F32
    )


def norm_back(weighted, residual, inverse):
    scaled = residual * inverse
    return inverse * (weighted - scaled * jnp.mean(weighted * scaled, axis=-1, keepdims=True))


def vmem_whole():
    return pl.BlockSpec(memory_space=pltpu.VMEM)


def smem_whole():
    return pl.BlockSpec(memory_space=pltpu.SMEM)


def shape(rows, columns, dtype):
    return jax.ShapeDtypeStruct((rows, columns), dtype)


def half_of(core_ref, which):
    position = core_ref[0] if which == 0 else 1 - core_ref[0]
    return pl.ds(pl.multiple_of(position * HALF, HALF), HALF)


def nt_dot(left_side, right_side):
    return lax.dot_general(
        left_side, right_side, (((1,), (1,)), ((), ())), preferred_element_type=F32
    )


def tn_dot(left_side, right_side):
    return lax.dot_general(
        left_side, right_side, (((0,), (0,)), ((), ())), preferred_element_type=F32
    )


def nn_dot(left_side, right_side):
    return jnp.dot(left_side, right_side, preferred_element_type=F32)


def inverse_norm(rows):
    return lax.rsqrt(jnp.mean(rows * rows, axis=-1, keepdims=True) + EPSILON)


def causal_mask():
    row = lax.broadcasted_iota(jnp.int32, (128, 128), 0)
    return row >= lax.broadcasted_iota(jnp.int32, (128, 128), 1)


def two_heads(ref, rows, start):
    return jnp.concatenate(
        [
            ref[rows, start : start + HEAD_WIDTH],
            ref[rows, start + HEAD_WIDTH : start + 2 * HEAD_WIDTH],
        ],
        axis=0,
    )


def granule_rows(place_ref, y_step, x_step, own_low):
    y_at = lax.rem(place_ref[1] + y_step, 4)
    x_at = lax.rem(place_ref[2] + x_step, 4)
    low = place_ref[3] if own_low else 1 - place_ref[3]
    return pl.ds(pl.multiple_of(((y_at * 4 + x_at) * 2 + low) * GRANULE, GRANULE), GRANULE)


def piece_copies(place_ref, pieces, whole, sems, outward):
    copies = []
    for number, piece in enumerate(pieces):
        for part in range(4):
            y_step, x_step = (number, part) if number < 4 else (part, number - 4)
            inner = piece.at[pl.ds(part * GRANULE, GRANULE), :]
            outer = whole.at[granule_rows(place_ref, y_step, x_step, number < 4), :]
            source, target = (outer, inner) if outward else (inner, outer)
            copies.append(pltpu.make_async_copy(source, target, sems.at[4 * number + part]))
    return copies


def attention_forward_body(sequences, core_ref, first_ref, w_ref, qkv_ref, prob_ref, mix_ref, keep_ref, give_ref):
    qkv_ref[...] = nn_dot(first_ref[...], w_ref[:, :QKV_COLS]).astype(BF16)
    mask = causal_mask()
    mask = jnp.concatenate([mask, mask], axis=0)
    for sequence in range(sequences):
        rows = slice(128 * sequence, 128 * (sequence + 1))
        for group in range(2):
            queries = two_heads(qkv_ref, rows, 2 * HEAD_WIDTH * group)
            key_at = QUERY_COLS + HEAD_WIDTH * group
            value_at = key_at + KV_COLS
            scores = nt_dot(queries, qkv_ref[rows, key_at : key_at + HEAD_WIDTH]) * SCORE_SCALE
            scores = jnp.where(mask, scores, BLOCKED)
            expanded = jnp.exp(scores - jnp.max(scores, axis=-1, keepdims=True))
            probability = expanded / jnp.sum(expanded, axis=-1, keepdims=True)
            prob_ref[2 * sequence + group] = probability
            mixed = nn_dot(
                probability.astype(BF16), qkv_ref[rows, value_at : value_at + HEAD_WIDTH]
            ).astype(BF16)
            at = 2 * HEAD_WIDTH * group
            mix_ref[rows, at : at + HEAD_WIDTH] = mixed[:128]
            mix_ref[rows, at + HEAD_WIDTH : at + 2 * HEAD_WIDTH] = mixed[128:]
    mixture = mix_ref[...]
    give_ref[...] = nt_dot(mixture, w_ref[half_of(core_ref, 1), QKV_COLS:]).astype(BF16)
    keep_ref[...] = nt_dot(mixture, w_ref[half_of(core_ref, 0), QKV_COLS:]).astype(BF16)


def attention_first_kernel(sequences, core_ref, x_ref, *rest):
    pieces, first_ref, outs, w_ref, sems = rest[:8], rest[8], rest[9:-2], rest[-2], rest[-1]
    copies = piece_copies(core_ref, pieces, w_ref, sems, False)
    for copy in copies:
        copy.start()
    rows = x_ref[...].astype(F32)
    first_ref[...] = (rows * inverse_norm(rows)).astype(BF16)
    for copy in copies:
        copy.wait()
    attention_forward_body(sequences, core_ref, first_ref, w_ref, *outs)


def attention_next_kernel(sequences, core_ref, middle_ref, own_ref, other_ref, *rest):
    pieces, x_ref, first_ref, outs, w_ref, sems = rest[:8], rest[8], rest[9], rest[10:-2], rest[-2], rest[-1]
    copies = piece_copies(core_ref, pieces, w_ref, sems, False)
    for copy in copies:
        copy.start()
    for which, part in ((0, own_ref), (1, other_ref)):
        at = half_of(core_ref, which)
        x_ref[:, at] = (middle_ref[:, at] + part[...].astype(F32)).astype(BF16)
    rows = x_ref[...].astype(F32)
    first_ref[...] = (rows * inverse_norm(rows)).astype(BF16)
    for copy in copies:
        copy.wait()
    attention_forward_body(sequences, core_ref, first_ref, w_ref, *outs)


def piece_specs():
    return [pl.BlockSpec(memory_space=pl.ANY)] * 8


def piece_scratch():
    return [pltpu.VMEM((WIDTH, ATTN_COLS), BF16), pltpu.SemaphoreType.DMA((32,))]


def attention_forward(core, x, middle, sums, w_attn):
    rows = (x if middle is None else middle).shape[0]
    sequences = rows // 128
    outs = [
        shape(rows, WIDTH, BF16),
        shape(rows, QKV_COLS, BF16),
        jax.ShapeDtypeStruct((2 * sequences, 256, 128), F32),
        shape(rows, OUT_COLS, BF16),
        shape(rows, HALF, BF16),
        shape(rows, HALF, BF16),
    ]
    if middle is None:
        operands, kernel = (core, x), attention_first_kernel
    else:
        operands, kernel = (core, middle, *sums), attention_next_kernel
        outs = [shape(rows, WIDTH, BF16)] + outs
    results = pl.pallas_call(
        functools.partial(kernel, sequences),
        in_specs=[smem_whole()] + [vmem_whole()] * (len(operands) - 1) + piece_specs(),
        out_specs=[vmem_whole()] * len(outs),
        out_shape=outs,
        scratch_shapes=piece_scratch(),
        compiler_params=pltpu.CompilerParams(vmem_limit_bytes=VMEM_LIMIT),
        cost_estimate=pl.CostEstimate(
            flops=2 * rows * WIDTH * ATTN_COLS, bytes_accessed=8_000_000, transcendentals=0
        ),
        name="attention_forward",
    )(*operands, *w_attn)
    return ([x] if middle is None else []) + list(results)


def mlp_forward_kernel(core_ref, x_ref, own_ref, other_ref, gate_w, up_w, down_w, middle_ref, second_ref, gate_ref, up_ref, hidden_ref, keep_ref, give_ref, total):
    step = pl.program_id(0)

    @pl.when(step == 0)
    def _():
        for which, part in ((0, own_ref), (1, other_ref)):
            at = half_of(core_ref, which)
            middle_ref[:, at] = x_ref[:, at].astype(F32) + part[...].astype(F32)
        rows = middle_ref[...]
        second_ref[...] = (rows * inverse_norm(rows)).astype(BF16)
        total[...] = jnp.zeros_like(total)

    gate_out = nn_dot(second_ref[...], gate_w[...])
    up_out = nn_dot(second_ref[...], up_w[...])
    gate_ref[...] = gate_out
    up_ref[...] = up_out
    hidden = (gate_out * (1.0 / (1.0 + jnp.exp(-gate_out))) * up_out).astype(BF16)
    hidden_ref[...] = hidden
    total[...] += nt_dot(hidden, down_w[...])

    @pl.when(step == pl.num_programs(0) - 1)
    def _():
        give_ref[...] = total[:, half_of(core_ref, 1)].astype(BF16)
        keep_ref[...] = total[:, half_of(core_ref, 0)].astype(BF16)


def fixed(rows, columns):
    return pl.BlockSpec((rows, columns), lambda j: (0, 0))


def tile(rows, first=0):
    return pl.BlockSpec((rows, HIDDEN_TILE), lambda j: (0, first + j))


HIDDEN_STEPS = HIDDEN_COLS // HIDDEN_TILE


def mlp_forward(core, x, sums, w_mlp):
    rows = x.shape[0]
    return pl.pallas_call(
        mlp_forward_kernel,
        grid=(HIDDEN_STEPS,),
        in_specs=[
            smem_whole(),
            fixed(rows, WIDTH),
            fixed(rows, HALF),
            fixed(rows, HALF),
            tile(WIDTH),
            tile(WIDTH, HIDDEN_STEPS),
            tile(WIDTH, 2 * HIDDEN_STEPS),
        ],
        out_specs=[
            fixed(rows, WIDTH),
            fixed(rows, WIDTH),
            tile(rows),
            tile(rows),
            tile(rows),
            fixed(rows, HALF),
            fixed(rows, HALF),
        ],
        out_shape=[
            shape(rows, WIDTH, F32),
            shape(rows, WIDTH, BF16),
            shape(rows, HIDDEN_COLS, F32),
            shape(rows, HIDDEN_COLS, F32),
            shape(rows, HIDDEN_COLS, BF16),
            shape(rows, HALF, BF16),
            shape(rows, HALF, BF16),
        ],
        scratch_shapes=[pltpu.VMEM((rows, WIDTH), F32)],
        compiler_params=pltpu.CompilerParams(vmem_limit_bytes=VMEM_LIMIT),
        cost_estimate=pl.CostEstimate(
            flops=2 * rows * WIDTH * MLP_COLS, bytes_accessed=15_000_000, transcendentals=0
        ),
        name="mlp_forward",
    )(core, x, *sums, w_mlp, w_mlp, w_mlp)


def mlp_backward_kernel(core_ref, g_ref, gate_ref, up_ref, gate_w, up_w, down_w, gate_grad_ref, up_grad_ref, keep_ref, give_ref, total):
    step = pl.program_id(0)

    @pl.when(step == 0)
    def _():
        total[...] = jnp.zeros_like(total)

    hidden_grad = nn_dot(g_ref[...], down_w[...])
    gate_out = gate_ref[...]
    sigmoid_gate = 1.0 / (1.0 + jnp.exp(-gate_out))
    gate_grad = (
        hidden_grad * up_ref[...] * (sigmoid_gate * (1.0 + gate_out * (1.0 - sigmoid_gate)))
    ).astype(BF16)
    up_grad = (hidden_grad * (gate_out * sigmoid_gate)).astype(BF16)
    gate_grad_ref[...] = gate_grad
    up_grad_ref[...] = up_grad
    total[...] += nt_dot(gate_grad, gate_w[...]) + nt_dot(up_grad, up_w[...])

    @pl.when(step == pl.num_programs(0) - 1)
    def _():
        give_ref[...] = total[:, half_of(core_ref, 1)].astype(BF16)
        keep_ref[...] = total[:, half_of(core_ref, 0)].astype(BF16)


def mlp_backward_next_kernel(core_ref, x_ref, middle_grad_ref, own_ref, other_ref, gate_ref, up_ref, gate_w, up_w, down_w, g_ref, gate_grad_ref, up_grad_ref, keep_ref, give_ref, total):
    @pl.when(pl.program_id(0) == 0)
    def _():
        for which, part in ((0, own_ref), (1, other_ref)):
            total[:, half_of(core_ref, which)] = part[...].astype(F32)
        rows = x_ref[...].astype(F32)
        inverse = inverse_norm(rows)
        g_ref[...] = (middle_grad_ref[...] + norm_back(total[...], rows, inverse)).astype(BF16)

    mlp_backward_kernel(core_ref, g_ref, gate_ref, up_ref, gate_w, up_w, down_w, gate_grad_ref, up_grad_ref, keep_ref, give_ref, total)


def mlp_backward(core, g, above, gate_out, up_out, w_mlp):
    rows = gate_out.shape[0]
    if above is None:
        lead, kernel, lead_specs = (g,), mlp_backward_kernel, [fixed(rows, WIDTH)]
    else:
        lead, kernel = above, mlp_backward_next_kernel
        lead_specs = [fixed(rows, WIDTH)] * 2 + [fixed(rows, HALF)] * 2
    out_specs = [tile(rows), tile(rows), fixed(rows, HALF), fixed(rows, HALF)]
    out_shape = [
        shape(rows, HIDDEN_COLS, BF16),
        shape(rows, HIDDEN_COLS, BF16),
        shape(rows, HALF, BF16),
        shape(rows, HALF, BF16),
    ]
    if above is not None:
        out_specs = [fixed(rows, WIDTH)] + out_specs
        out_shape = [shape(rows, WIDTH, BF16)] + out_shape
    results = pl.pallas_call(
        kernel,
        grid=(HIDDEN_STEPS,),
        in_specs=[smem_whole()]
        + lead_specs
        + [
            tile(rows),
            tile(rows),
            tile(WIDTH),
            tile(WIDTH, HIDDEN_STEPS),
            tile(WIDTH, 2 * HIDDEN_STEPS),
        ],
        out_specs=out_specs,
        out_shape=out_shape,
        scratch_shapes=[pltpu.VMEM((rows, WIDTH), F32)],
        compiler_params=pltpu.CompilerParams(vmem_limit_bytes=VMEM_LIMIT),
        cost_estimate=pl.CostEstimate(
            flops=2 * rows * WIDTH * MLP_COLS, bytes_accessed=15_000_000, transcendentals=0
        ),
        name="mlp_backward",
    )(core, *lead, gate_out, up_out, w_mlp, w_mlp, w_mlp)
    return ([g] if above is None else []) + list(results)


def attention_backward_kernel(sequences, core_ref, g_ref, middle_ref, own_ref, other_ref, qkv_ref, prob_ref, *rest):
    pieces, outs, (mix_grad, w_ref, sems) = rest[:8], rest[8:-3], rest[-3:]
    middle_grad_ref, attn_in_ref, qkv_grad_ref, keep_ref, give_ref = outs
    copies = piece_copies(core_ref, pieces, w_ref, sems, False)
    for copy in copies:
        copy.start()
    for which, part in ((0, own_ref), (1, other_ref)):
        middle_grad_ref[:, half_of(core_ref, which)] = part[...].astype(F32)
    middle = middle_ref[...]
    middle_grad = g_ref[...].astype(F32) + norm_back(
        middle_grad_ref[...], middle, inverse_norm(middle)
    )
    middle_grad_ref[...] = middle_grad
    attn_in_ref[...] = middle_grad.astype(BF16)
    for copy in copies:
        copy.wait()
    mix_grad[...] = nn_dot(attn_in_ref[...], w_ref[:, QKV_COLS:]).astype(BF16)
    for sequence in range(sequences):
        rows = slice(128 * sequence, 128 * (sequence + 1))
        for group in range(2):
            at = 2 * HEAD_WIDTH * group
            key_at = QUERY_COLS + HEAD_WIDTH * group
            value_at = key_at + KV_COLS
            grads = two_heads(mix_grad, rows, at)
            queries = two_heads(qkv_ref, rows, at)
            keys = qkv_ref[rows, key_at : key_at + HEAD_WIDTH]
            probability = prob_ref[2 * sequence + group]
            prob_grad = nt_dot(grads, qkv_ref[rows, value_at : value_at + HEAD_WIDTH])
            centred = jnp.sum(probability * prob_grad, axis=-1, keepdims=True)
            score_grad = (probability * (prob_grad - centred)).astype(BF16)
            query_grad = (nn_dot(score_grad, keys) * SCORE_SCALE).astype(BF16)
            qkv_grad_ref[rows, at : at + HEAD_WIDTH] = query_grad[:128]
            qkv_grad_ref[rows, at + HEAD_WIDTH : at + 2 * HEAD_WIDTH] = query_grad[128:]
            qkv_grad_ref[rows, key_at : key_at + HEAD_WIDTH] = (
                tn_dot(score_grad, queries) * SCORE_SCALE
            ).astype(BF16)
            qkv_grad_ref[rows, value_at : value_at + HEAD_WIDTH] = tn_dot(
                probability.astype(BF16), grads
            ).astype(BF16)
    qkv_grad = qkv_grad_ref[...]
    give_ref[...] = nt_dot(qkv_grad, w_ref[half_of(core_ref, 1), :QKV_COLS]).astype(BF16)
    keep_ref[...] = nt_dot(qkv_grad, w_ref[half_of(core_ref, 0), :QKV_COLS]).astype(BF16)


def attention_backward(core, g, middle, sums, qkv, probability, w_attn):
    rows = g.shape[0]
    return pl.pallas_call(
        functools.partial(attention_backward_kernel, rows // 128),
        in_specs=[smem_whole()] + [vmem_whole()] * 6 + piece_specs(),
        out_specs=[vmem_whole()] * 5,
        out_shape=[
            shape(rows, WIDTH, F32),
            shape(rows, WIDTH, BF16),
            shape(rows, QKV_COLS, BF16),
            shape(rows, HALF, BF16),
            shape(rows, HALF, BF16),
        ],
        scratch_shapes=[pltpu.VMEM((rows, OUT_COLS), BF16)] + piece_scratch(),
        compiler_params=pltpu.CompilerParams(vmem_limit_bytes=VMEM_LIMIT),
        cost_estimate=pl.CostEstimate(
            flops=2 * rows * WIDTH * ATTN_COLS, bytes_accessed=12_000_000, transcendentals=0
        ),
        name="attention_backward",
    )(core, g, middle, *sums, qkv, probability, *w_attn)


def attention_weights_kernel(place_ref, first_ref, qkv_grad_ref, attn_in_ref, mix_ref, *rest):
    pieces, grad, sems = rest[:8], rest[8], rest[9]
    for at in range(0, WIDTH, 256):
        features = slice(at, at + 256)
        grad[features, :QKV_COLS] = tn_dot(first_ref[:, features], qkv_grad_ref[...]).astype(BF16)
        grad[features, QKV_COLS:] = tn_dot(attn_in_ref[:, features], mix_ref[...]).astype(BF16)
    copies = piece_copies(place_ref, pieces, grad, sems, True)
    for copy in copies:
        copy.start()
    for copy in copies:
        copy.wait()


def attention_weights(place, first, qkv_grad, attn_in, mixture):
    rows = first.shape[0]
    return pl.pallas_call(
        attention_weights_kernel,
        in_specs=[smem_whole()] + [vmem_whole()] * 4,
        out_specs=piece_specs(),
        out_shape=[shape(4 * GRANULE, ATTN_COLS, BF16)] * 8,
        scratch_shapes=piece_scratch(),
        compiler_params=pltpu.CompilerParams(vmem_limit_bytes=VMEM_LIMIT),
        cost_estimate=pl.CostEstimate(
            flops=2 * rows * WIDTH * ATTN_COLS, bytes_accessed=7_000_000, transcendentals=0
        ),
        name="attention_weights",
    )(place, first, qkv_grad, attn_in, mixture)


def sum_four(keep, give):
    chip = (keep.astype(F32) + swap(give, "section").astype(F32)).astype(BF16)
    total = (chip.astype(F32) + swap(chip, "tensor").astype(F32)).astype(BF16)
    return total, swap(total, "section")


def halves(value):
    middle = value.shape[1] // 2
    return value[:, :middle], value[:, middle:]


def to_layers(core, low, high):
    mine, give = pick(core, low, high), pick(core, high, low)
    got = swap(give, "section")
    return pick(core, mine, got), pick(core, got, mine)


def from_layers(core, layer_zero, layer_one):
    mine, give = pick(core, layer_zero, layer_one), pick(core, layer_one, layer_zero)
    got = swap(give, "section")
    return pick(core, mine, got), pick(core, got, mine)


def gather_rows(z_low, share):
    other = swap(share, "zl")
    pair = jnp.concatenate([pick(z_low, share, other), pick(z_low, other, share)], axis=0)
    return lax.all_gather(pair, ("y", "x"), axis=0, tiled=True)


def from_step(value, axis, step):
    return lax.ppermute(value, axis, [((place + step) % 4, place) for place in range(4)])


def gather_pieces(share):
    other = swap(share, "zl")
    pieces = []
    for rows, near, far in ((share, "x", "y"), (other, "y", "x")):
        line = jnp.concatenate([rows] + [from_step(rows, near, step) for step in (1, 2, 3)], axis=0)
        pieces += [line] + [from_step(line, far, step) for step in (1, 2, 3)]
    return pieces


def add_parts(parts):
    return sum(part.astype(F32) for part in parts).astype(BF16)


def scatter_pieces(pieces):
    sums = []
    for own, near, far in ((pieces[:4], "x", "y"), (pieces[4:], "y", "x")):
        line = add_parts([own[0]] + [from_step(own[step], far, 4 - step) for step in (1, 2, 3)])
        parts = [line[GRANULE * step : GRANULE * (step + 1)] for step in range(4)]
        sums.append(
            add_parts([parts[0]] + [from_step(parts[step], near, 4 - step) for step in (1, 2, 3)])
        )
    return add_parts([sums[0], swap(sums[1], "zl")])


def scatter_rows(z_low, grad):
    pair = lax.psum_scatter(grad, ("y", "x"), scatter_dimension=0, tiled=True)
    keep = pick(z_low, pair[:48], pair[48:])
    give = pick(z_low, pair[48:], pair[:48])
    return (keep.astype(F32) + swap(give, "zl").astype(F32)).astype(BF16)


def to_ring_order(rows):
    lead = rows.shape[:-1]
    return jnp.swapaxes(rows.reshape(lead + (4, 2, 4, 48)), -3, -2).reshape(rows.shape)


def from_ring_order(rows):
    lead = rows.shape[:-1]
    return jnp.swapaxes(rows.reshape(lead + (4, 4, 2, 48)), -3, -2).reshape(rows.shape)


def join_positions(tensor, own):
    other = swap(own, "tensor")
    return jnp.concatenate(
        [pick(tensor, own, other), pick(tensor, other, own)], axis=1
    ).reshape(384, WIDTH)


def own_positions(tensor, rows):
    rows = rows.reshape(3, 128, 1536)
    return pick(tensor, rows[:, :64], rows[:, 64:])


def per_device(
    inputs, cotangent, plan, attn_gain, mlp_gain, w_query, key_weight, value_weight,
    w_out, w_gate, w_up, w_down,
):
    core = lax.axis_index("section")
    z_low = lax.axis_index("zl")
    tensor = lax.axis_index("tensor")

    attn_scale = attn_gain[0].astype(F32)[:, None]
    mlp_scale = mlp_gain[0].astype(F32)[:, None]

    def scaled(weight, scale):
        return (weight.astype(F32) * scale).astype(BF16)

    attn_shards = (w_query[0], key_weight[0], value_weight[0])
    mlp_shards = (w_gate[0], w_up[0])
    attn_pairs = [halves(scaled(weight, attn_scale)) for weight in attn_shards]
    attn_pairs.append(halves(w_out[0].T))
    mlp_pairs = [halves(scaled(weight, mlp_scale)) for weight in mlp_shards]
    mlp_pairs.append(halves(w_down[0].T))
    attn_low, attn_high = (jnp.concatenate(side, axis=1) for side in zip(*attn_pairs))
    mlp_low, mlp_high = (jnp.concatenate(side, axis=1) for side in zip(*mlp_pairs))
    attn_layers = to_layers(core, attn_low, attn_high)
    mlp_layers = to_layers(core, mlp_low, mlp_high)
    attn_weights, mlp_weights = [], []
    for layer in range(2):
        attn_weights.append(gather_pieces(attn_layers[layer]))
        mlp_weights.append(gather_rows(z_low, mlp_layers[layer]))

    core_ref = jnp.stack([core, lax.axis_index("y"), lax.axis_index("x"), z_low]).astype(jnp.int32)
    stream = join_positions(tensor, to_ring_order(inputs[:, 0][plan]))

    kept, outputs = [], []
    x, middle, sums = stream, None, None
    for layer in range(2):
        x, first, qkv, probability, mixture, keep, give = attention_forward(
            core_ref, x, middle, sums, attn_weights[layer]
        )
        if layer == 0:
            late, keep = lax.optimization_barrier((cotangent, keep))
            out_grad = join_positions(tensor, to_ring_order(late[:, 0][plan]))
        else:
            outputs.append(own_positions(tensor, x))
        middle, second, gate_out, up_out, hidden, keep, give = mlp_forward(
            core_ref, x, sum_four(keep, give), mlp_weights[layer]
        )
        sums = sum_four(keep, give)
        kept.append((x, first, qkv, probability, mixture, middle, second, gate_out, up_out, hidden))
    last = middle + jnp.concatenate(
        [pick(core, sums[0], sums[1]), pick(core, sums[1], sums[0])], axis=1
    ).astype(F32)
    outputs.append(own_positions(tensor, last.astype(BF16)))

    grads, attn_grads, mlp_grads = [None] * 2, [None] * 2, [None] * 2
    above = None
    for layer in (1, 0):
        x, first, qkv, probability, mixture, middle, second, gate_out, up_out, hidden = kept[layer]
        out_grad, gate_grad, up_grad, keep, give = mlp_backward(
            core_ref, out_grad, above, gate_out, up_out, mlp_weights[layer]
        )
        if layer == 0:
            grads[1] = own_positions(tensor, out_grad)
        mlp_term = jnp.concatenate(
            [
                contract_rows(second, gate_grad).astype(BF16),
                contract_rows(second, up_grad).astype(BF16),
                contract_rows(out_grad, hidden).astype(BF16),
            ],
            axis=1,
        )
        sums = sum_four(keep, give)
        if layer == 0:
            mlp_term, mlp_grads[1] = lax.optimization_barrier((mlp_term, mlp_grads[1]))
        sums, mlp_term = lax.optimization_barrier((sums, mlp_term))
        mlp_grads[layer] = scatter_rows(z_low, mlp_term)
        middle_grad, attn_in, qkv_grad, keep, give = attention_backward(
            core_ref, out_grad, middle, sums, qkv, probability, attn_weights[layer]
        )
        attn_term = attention_weights(core_ref, first, qkv_grad, attn_in, mixture)
        sums = sum_four(keep, give)
        sums, attn_term = lax.optimization_barrier((sums, attn_term))
        attn_grads[layer] = scatter_pieces(attn_term)
        above = (x, middle_grad, *sums)
    x, middle_grad, own, other = above
    rows = x.astype(F32)
    weighted = jnp.concatenate(
        [pick(core, own, other), pick(core, other, own)], axis=1
    ).astype(F32)
    last = middle_grad + norm_back(weighted, rows, inverse_norm(rows))
    grads[0] = own_positions(tensor, last.astype(BF16))

    layer_outputs = from_ring_order(pick(core, outputs[0], outputs[1]))
    input_grads = from_ring_order(pick(core, grads[0], grads[1]))
    attn_low, attn_high = from_layers(core, *attn_grads)
    mlp_low, mlp_high = from_layers(core, *mlp_grads)

    def joined(low, high, start, width):
        return jnp.concatenate(
            [low[:, start : start + width], high[:, start : start + width]], axis=1
        ).astype(F32)

    query_grad = joined(attn_low, attn_high, 0, QUERY_COLS)
    key_grad = joined(attn_low, attn_high, QUERY_COLS, KV_COLS)
    value_grad = joined(attn_low, attn_high, QUERY_COLS + KV_COLS, KV_COLS)
    out_weight_grad = joined(attn_low, attn_high, QKV_COLS, OUT_COLS).T
    gate_grad = joined(mlp_low, mlp_high, 0, HIDDEN_COLS)
    up_grad = joined(mlp_low, mlp_high, HIDDEN_COLS, HIDDEN_COLS)
    down_grad = joined(mlp_low, mlp_high, 2 * HIDDEN_COLS, HIDDEN_COLS).T

    def gain_term(weights, weight_grads):
        return sum(
            jnp.sum(weight.astype(F32) * grad, axis=1)
            for weight, grad in zip(weights, weight_grads)
        )

    gain_terms = jnp.stack(
        [
            gain_term(attn_shards, (query_grad, key_grad, value_grad)),
            gain_term(mlp_shards, (gate_grad, up_grad)),
        ]
    )
    gain_terms = gain_terms + swap(gain_terms, "tensor")
    return (
        layer_outputs[None, :, None],
        input_grads[None, :, None],
        gain_terms[0][None],
        gain_terms[1][None],
        (query_grad * attn_scale)[None],
        (key_grad * attn_scale)[None],
        (value_grad * attn_scale)[None],
        out_weight_grad[None],
        (gate_grad * mlp_scale)[None],
        (up_grad * mlp_scale)[None],
        down_grad[None],
    )


def solution(mesh):
    split = Mesh(mesh.devices.reshape(2, 4, 2, 4, 2), ("section", "y", "zl", "x", "tensor"))
    dp = ("y", "zl", "x")
    rows = P("section", dp, "tensor")
    columns = P("section", "tensor", dp)
    return jax.shard_map(
        per_device,
        mesh=split,
        in_specs=(
            P(None, dp, "tensor", None),
            P(None, dp, "tensor", None),
            P(),
            P("section", dp),
            P("section", dp),
            rows,
            rows,
            rows,
            columns,
            rows,
            rows,
            columns,
        ),
        out_specs=(
            P("section", None, dp, "tensor", None),
            P("section", None, dp, "tensor", None),
            P("section", dp),
            P("section", dp),
            rows,
            rows,
            rows,
            columns,
            rows,
            rows,
            columns,
        ),
        check_vma=False,
    )
```

```python
import functools

import jax
import jax.numpy as jnp
from jax import lax
from jax.experimental import pallas as pl
from jax.experimental.pallas import tpu as pltpu
from jax.sharding import Mesh, PartitionSpec as P

HEAD_WIDTH = 96
EPSILON = 1e-05
BLOCKED = -1e30
SCORE_SCALE = HEAD_WIDTH ** (-0.5)
BF16 = jnp.bfloat16
F32 = jnp.float32

QUERY_COLS, KV_COLS = 384, 192
QKV_COLS = QUERY_COLS + 2 * KV_COLS
OUT_COLS = 384
HIDDEN_COLS = 1024
ATTN_COLS = QKV_COLS + OUT_COLS
MLP_COLS = 3 * HIDDEN_COLS
LAYER_COLS = MLP_COLS + ATTN_COLS
HIDDEN_TILE = 256
WIDTH = 1536
HALF = WIDTH // 2
VMEM_LIMIT = 56 * 1024 * 1024


def swap(value, axis):
    return lax.ppermute(value, axis, [(0, 1), (1, 0)])


def pick(index, first, second):
    return jnp.where(index == 0, first, second)


def norm_back(weighted, residual, inverse):
    scaled = residual * inverse
    return inverse * (weighted - scaled * jnp.mean(weighted * scaled, axis=-1, keepdims=True))


def vmem_whole():
    return pl.BlockSpec(memory_space=pltpu.VMEM)


def smem_whole():
    return pl.BlockSpec(memory_space=pltpu.SMEM)


def shape(rows, columns, dtype):
    return jax.ShapeDtypeStruct((rows, columns), dtype)


def half_of(core_ref, which):
    position = core_ref[0] if which == 0 else 1 - core_ref[0]
    return pl.ds(pl.multiple_of(position * HALF, HALF), HALF)


def nt_dot(left_side, right_side):
    return lax.dot_general(
        left_side, right_side, (((1,), (1,)), ((), ())), preferred_element_type=F32
    )


def tn_dot(left_side, right_side):
    return lax.dot_general(
        left_side, right_side, (((0,), (0,)), ((), ())), preferred_element_type=F32
    )


def nn_dot(left_side, right_side):
    return jnp.dot(left_side, right_side, preferred_element_type=F32)


def inverse_norm(rows):
    return lax.rsqrt(jnp.mean(rows * rows, axis=-1, keepdims=True) + EPSILON)


def causal_mask():
    row = lax.broadcasted_iota(jnp.int32, (128, 128), 0)
    return row >= lax.broadcasted_iota(jnp.int32, (128, 128), 1)


def two_heads(ref, rows, start):
    return jnp.concatenate(
        [
            ref[rows, start : start + HEAD_WIDTH],
            ref[rows, start + HEAD_WIDTH : start + 2 * HEAD_WIDTH],
        ],
        axis=0,
    )


def attention_weights_copy(w_any, w_ref, sem, column):
    return pltpu.make_async_copy(w_any.at[:, pl.ds(column, ATTN_COLS)], w_ref, sem)


def attention_forward_body(sequences, core_ref, first_ref, w_ref, qkv_ref, prob_ref, mix_ref, keep_ref, give_ref):
    qkv_ref[...] = nn_dot(first_ref[...], w_ref[:, :QKV_COLS]).astype(BF16)
    mask = causal_mask()
    mask = jnp.concatenate([mask, mask], axis=0)
    for sequence in range(sequences):
        rows = slice(128 * sequence, 128 * (sequence + 1))
        for group in range(2):
            queries = two_heads(qkv_ref, rows, 2 * HEAD_WIDTH * group)
            key_at = QUERY_COLS + HEAD_WIDTH * group
            value_at = key_at + KV_COLS
            scores = nt_dot(queries, qkv_ref[rows, key_at : key_at + HEAD_WIDTH]) * SCORE_SCALE
            scores = jnp.where(mask, scores, BLOCKED)
            expanded = jnp.exp(scores - jnp.max(scores, axis=-1, keepdims=True))
            probability = expanded / jnp.sum(expanded, axis=-1, keepdims=True)
            prob_ref[2 * sequence + group] = probability
            mixed = nn_dot(
                probability.astype(BF16), qkv_ref[rows, value_at : value_at + HEAD_WIDTH]
            ).astype(BF16)
            at = 2 * HEAD_WIDTH * group
            mix_ref[rows, at : at + HEAD_WIDTH] = mixed[:128]
            mix_ref[rows, at + HEAD_WIDTH : at + 2 * HEAD_WIDTH] = mixed[128:]
    mixture = mix_ref[...]
    give_ref[...] = nt_dot(mixture, w_ref[half_of(core_ref, 1), QKV_COLS:]).astype(BF16)
    keep_ref[...] = nt_dot(mixture, w_ref[half_of(core_ref, 0), QKV_COLS:]).astype(BF16)


def attention_first_kernel(sequences, column, core_ref, x_ref, w_any, first_ref, *rest):
    outs, w_ref, sem = rest[:-2], rest[-2], rest[-1]
    copy = attention_weights_copy(w_any, w_ref, sem, column)
    copy.start()
    rows = x_ref[...].astype(F32)
    first_ref[...] = (rows * inverse_norm(rows)).astype(BF16)
    copy.wait()
    attention_forward_body(sequences, core_ref, first_ref, w_ref, *outs)


def attention_next_kernel(sequences, column, core_ref, middle_ref, own_ref, other_ref, w_any, x_ref, first_ref, *rest):
    outs, w_ref, sem = rest[:-2], rest[-2], rest[-1]
    copy = attention_weights_copy(w_any, w_ref, sem, column)
    copy.start()
    for which, part in ((0, own_ref), (1, other_ref)):
        at = half_of(core_ref, which)
        x_ref[:, at] = (middle_ref[:, at] + part[...].astype(F32)).astype(BF16)
    rows = x_ref[...].astype(F32)
    first_ref[...] = (rows * inverse_norm(rows)).astype(BF16)
    copy.wait()
    attention_forward_body(sequences, core_ref, first_ref, w_ref, *outs)


def any_whole():
    return pl.BlockSpec(memory_space=pl.ANY)


def attention_scratch():
    return [pltpu.VMEM((WIDTH, ATTN_COLS), BF16), pltpu.SemaphoreType.DMA(())]


def attention_forward(core, x, middle, sums, weights, column):
    rows = (x if middle is None else middle).shape[0]
    sequences = rows // 128
    outs = [
        shape(rows, WIDTH, BF16),
        shape(rows, QKV_COLS, BF16),
        jax.ShapeDtypeStruct((2 * sequences, 256, 128), F32),
        shape(rows, OUT_COLS, BF16),
        shape(rows, HALF, BF16),
        shape(rows, HALF, BF16),
    ]
    if middle is None:
        operands, kernel = (core, x), attention_first_kernel
    else:
        operands, kernel = (core, middle, *sums), attention_next_kernel
        outs = [shape(rows, WIDTH, BF16)] + outs
    results = pl.pallas_call(
        functools.partial(kernel, sequences, column),
        in_specs=[smem_whole()] + [vmem_whole()] * (len(operands) - 1) + [any_whole()],
        out_specs=[vmem_whole()] * len(outs),
        out_shape=outs,
        scratch_shapes=attention_scratch(),
        compiler_params=pltpu.CompilerParams(vmem_limit_bytes=VMEM_LIMIT),
        cost_estimate=pl.CostEstimate(
            flops=2 * rows * WIDTH * ATTN_COLS, bytes_accessed=8_000_000, transcendentals=0
        ),
        name="attention_forward",
    )(*operands, weights)
    return ([x] if middle is None else []) + list(results)


def mlp_forward_kernel(core_ref, x_ref, own_ref, other_ref, gate_w, up_w, down_w, middle_ref, second_ref, gate_ref, up_ref, hidden_ref, keep_ref, give_ref, total):
    step = pl.program_id(0)

    @pl.when(step == 0)
    def _():
        for which, part in ((0, own_ref), (1, other_ref)):
            at = half_of(core_ref, which)
            middle_ref[:, at] = x_ref[:, at].astype(F32) + part[...].astype(F32)
        rows = middle_ref[...]
        second_ref[...] = (rows * inverse_norm(rows)).astype(BF16)
        total[...] = jnp.zeros_like(total)

    gate_out = nn_dot(second_ref[...], gate_w[...])
    up_out = nn_dot(second_ref[...], up_w[...])
    gate_ref[...] = gate_out
    up_ref[...] = up_out
    hidden = (gate_out * (1.0 / (1.0 + jnp.exp(-gate_out))) * up_out).astype(BF16)
    hidden_ref[...] = hidden
    total[...] += nt_dot(hidden, down_w[...])

    @pl.when(step == pl.num_programs(0) - 1)
    def _():
        give_ref[...] = total[:, half_of(core_ref, 1)].astype(BF16)
        keep_ref[...] = total[:, half_of(core_ref, 0)].astype(BF16)


def fixed(rows, columns):
    return pl.BlockSpec((rows, columns), lambda j: (0, 0))


def tile(rows, first=0):
    return pl.BlockSpec((rows, HIDDEN_TILE), lambda j: (0, first + j))


HIDDEN_STEPS = HIDDEN_COLS // HIDDEN_TILE


def mlp_forward(core, x, sums, w_mlp):
    rows = x.shape[0]
    return pl.pallas_call(
        mlp_forward_kernel,
        grid=(HIDDEN_STEPS,),
        in_specs=[
            smem_whole(),
            fixed(rows, WIDTH),
            fixed(rows, HALF),
            fixed(rows, HALF),
            tile(WIDTH),
            tile(WIDTH, HIDDEN_STEPS),
            tile(WIDTH, 2 * HIDDEN_STEPS),
        ],
        out_specs=[
            fixed(rows, WIDTH),
            fixed(rows, WIDTH),
            tile(rows),
            tile(rows),
            tile(rows),
            fixed(rows, HALF),
            fixed(rows, HALF),
        ],
        out_shape=[
            shape(rows, WIDTH, F32),
            shape(rows, WIDTH, BF16),
            shape(rows, HIDDEN_COLS, F32),
            shape(rows, HIDDEN_COLS, F32),
            shape(rows, HIDDEN_COLS, BF16),
            shape(rows, HALF, BF16),
            shape(rows, HALF, BF16),
        ],
        scratch_shapes=[pltpu.VMEM((rows, WIDTH), F32)],
        compiler_params=pltpu.CompilerParams(vmem_limit_bytes=VMEM_LIMIT),
        cost_estimate=pl.CostEstimate(
            flops=2 * rows * WIDTH * MLP_COLS, bytes_accessed=15_000_000, transcendentals=0
        ),
        name="mlp_forward",
    )(core, x, *sums, w_mlp, w_mlp, w_mlp)


def mlp_backward_kernel(core_ref, g_ref, gate_ref, up_ref, gate_w, up_w, down_w, gate_grad_ref, up_grad_ref, keep_ref, give_ref, total):
    step = pl.program_id(0)

    @pl.when(step == 0)
    def _():
        total[...] = jnp.zeros_like(total)

    hidden_grad = nn_dot(g_ref[...], down_w[...])
    gate_out = gate_ref[...]
    sigmoid_gate = 1.0 / (1.0 + jnp.exp(-gate_out))
    gate_grad = (
        hidden_grad * up_ref[...] * (sigmoid_gate * (1.0 + gate_out * (1.0 - sigmoid_gate)))
    ).astype(BF16)
    up_grad = (hidden_grad * (gate_out * sigmoid_gate)).astype(BF16)
    gate_grad_ref[...] = gate_grad
    up_grad_ref[...] = up_grad
    total[...] += nt_dot(gate_grad, gate_w[...]) + nt_dot(up_grad, up_w[...])

    @pl.when(step == pl.num_programs(0) - 1)
    def _():
        give_ref[...] = total[:, half_of(core_ref, 1)].astype(BF16)
        keep_ref[...] = total[:, half_of(core_ref, 0)].astype(BF16)


def mlp_backward_next_kernel(core_ref, x_ref, middle_grad_ref, own_ref, other_ref, gate_ref, up_ref, gate_w, up_w, down_w, g_ref, gate_grad_ref, up_grad_ref, keep_ref, give_ref, total):
    @pl.when(pl.program_id(0) == 0)
    def _():
        for which, part in ((0, own_ref), (1, other_ref)):
            total[:, half_of(core_ref, which)] = part[...].astype(F32)
        rows = x_ref[...].astype(F32)
        inverse = inverse_norm(rows)
        g_ref[...] = (middle_grad_ref[...] + norm_back(total[...], rows, inverse)).astype(BF16)

    mlp_backward_kernel(core_ref, g_ref, gate_ref, up_ref, gate_w, up_w, down_w, gate_grad_ref, up_grad_ref, keep_ref, give_ref, total)


def mlp_backward(core, g, above, gate_out, up_out, w_mlp):
    rows = gate_out.shape[0]
    if above is None:
        lead, kernel, lead_specs = (g,), mlp_backward_kernel, [fixed(rows, WIDTH)]
    else:
        lead, kernel = above, mlp_backward_next_kernel
        lead_specs = [fixed(rows, WIDTH)] * 2 + [fixed(rows, HALF)] * 2
    out_specs = [tile(rows), tile(rows), fixed(rows, HALF), fixed(rows, HALF)]
    out_shape = [
        shape(rows, HIDDEN_COLS, BF16),
        shape(rows, HIDDEN_COLS, BF16),
        shape(rows, HALF, BF16),
        shape(rows, HALF, BF16),
    ]
    if above is not None:
        out_specs = [fixed(rows, WIDTH)] + out_specs
        out_shape = [shape(rows, WIDTH, BF16)] + out_shape
    results = pl.pallas_call(
        kernel,
        grid=(HIDDEN_STEPS,),
        in_specs=[smem_whole()]
        + lead_specs
        + [
            tile(rows),
            tile(rows),
            tile(WIDTH),
            tile(WIDTH, HIDDEN_STEPS),
            tile(WIDTH, 2 * HIDDEN_STEPS),
        ],
        out_specs=out_specs,
        out_shape=out_shape,
        scratch_shapes=[pltpu.VMEM((rows, WIDTH), F32)],
        compiler_params=pltpu.CompilerParams(vmem_limit_bytes=VMEM_LIMIT),
        cost_estimate=pl.CostEstimate(
            flops=2 * rows * WIDTH * MLP_COLS, bytes_accessed=15_000_000, transcendentals=0
        ),
        name="mlp_backward",
    )(core, *lead, gate_out, up_out, w_mlp, w_mlp, w_mlp)
    return ([g] if above is None else []) + list(results)


def attention_backward_kernel(sequences, column, core_ref, g_ref, middle_ref, own_ref, other_ref, qkv_ref, prob_ref, w_any, middle_grad_ref, attn_in_ref, qkv_grad_ref, keep_ref, give_ref, mix_grad, w_ref, sem):
    copy = attention_weights_copy(w_any, w_ref, sem, column)
    copy.start()
    for which, part in ((0, own_ref), (1, other_ref)):
        middle_grad_ref[:, half_of(core_ref, which)] = part[...].astype(F32)
    middle = middle_ref[...]
    middle_grad = g_ref[...].astype(F32) + norm_back(
        middle_grad_ref[...], middle, inverse_norm(middle)
    )
    middle_grad_ref[...] = middle_grad
    attn_in_ref[...] = middle_grad.astype(BF16)
    copy.wait()
    mix_grad[...] = nn_dot(attn_in_ref[...], w_ref[:, QKV_COLS:]).astype(BF16)
    for sequence in range(sequences):
        rows = slice(128 * sequence, 128 * (sequence + 1))
        for group in range(2):
            at = 2 * HEAD_WIDTH * group
            key_at = QUERY_COLS + HEAD_WIDTH * group
            value_at = key_at + KV_COLS
            grads = two_heads(mix_grad, rows, at)
            queries = two_heads(qkv_ref, rows, at)
            keys = qkv_ref[rows, key_at : key_at + HEAD_WIDTH]
            probability = prob_ref[2 * sequence + group]
            prob_grad = nt_dot(grads, qkv_ref[rows, value_at : value_at + HEAD_WIDTH])
            centred = jnp.sum(probability * prob_grad, axis=-1, keepdims=True)
            score_grad = (probability * (prob_grad - centred)).astype(BF16)
            query_grad = (nn_dot(score_grad, keys) * SCORE_SCALE).astype(BF16)
            qkv_grad_ref[rows, at : at + HEAD_WIDTH] = query_grad[:128]
            qkv_grad_ref[rows, at + HEAD_WIDTH : at + 2 * HEAD_WIDTH] = query_grad[128:]
            qkv_grad_ref[rows, key_at : key_at + HEAD_WIDTH] = (
                tn_dot(score_grad, queries) * SCORE_SCALE
            ).astype(BF16)
            qkv_grad_ref[rows, value_at : value_at + HEAD_WIDTH] = tn_dot(
                probability.astype(BF16), grads
            ).astype(BF16)
    qkv_grad = qkv_grad_ref[...]
    give_ref[...] = nt_dot(qkv_grad, w_ref[half_of(core_ref, 1), :QKV_COLS]).astype(BF16)
    keep_ref[...] = nt_dot(qkv_grad, w_ref[half_of(core_ref, 0), :QKV_COLS]).astype(BF16)


def attention_backward(core, g, middle, sums, qkv, probability, weights, column):
    rows = g.shape[0]
    return pl.pallas_call(
        functools.partial(attention_backward_kernel, rows // 128, column),
        in_specs=[smem_whole()] + [vmem_whole()] * 6 + [any_whole()],
        out_specs=[vmem_whole()] * 5,
        out_shape=[
            shape(rows, WIDTH, F32),
            shape(rows, WIDTH, BF16),
            shape(rows, QKV_COLS, BF16),
            shape(rows, HALF, BF16),
            shape(rows, HALF, BF16),
        ],
        scratch_shapes=[pltpu.VMEM((rows, OUT_COLS), BF16)] + attention_scratch(),
        compiler_params=pltpu.CompilerParams(vmem_limit_bytes=VMEM_LIMIT),
        cost_estimate=pl.CostEstimate(
            flops=2 * rows * WIDTH * ATTN_COLS, bytes_accessed=12_000_000, transcendentals=0
        ),
        name="attention_backward",
    )(core, g, middle, *sums, qkv, probability, weights)


def mlp_weights_kernel(second_ref, g_ref, gate_ref, up_ref, hidden_ref, out_ref, second_t, g_t):
    step = pl.program_id(0)

    @pl.when(step == 0)
    def _():
        second_t[...] = second_ref[...].T
        g_t[...] = g_ref[...].T

    @pl.when(step < HIDDEN_STEPS)
    def _():
        out_ref[...] = nn_dot(second_t[...], gate_ref[...]).astype(BF16)

    @pl.when((step >= HIDDEN_STEPS) & (step < 2 * HIDDEN_STEPS))
    def _():
        out_ref[...] = nn_dot(second_t[...], up_ref[...]).astype(BF16)

    @pl.when(step >= 2 * HIDDEN_STEPS)
    def _():
        out_ref[...] = nn_dot(g_t[...], hidden_ref[...]).astype(BF16)


def tile_from(rows, first, count):
    return pl.BlockSpec((rows, HIDDEN_TILE), lambda j: (0, jnp.clip(j - first, 0, count - 1)))


def mlp_weights(second, g, gate_grad, up_grad, hidden):
    rows = second.shape[0]
    return pl.pallas_call(
        mlp_weights_kernel,
        grid=(3 * HIDDEN_STEPS,),
        in_specs=[
            fixed(rows, WIDTH),
            fixed(rows, WIDTH),
            tile_from(rows, 0, HIDDEN_STEPS),
            tile_from(rows, HIDDEN_STEPS, HIDDEN_STEPS),
            tile_from(rows, 2 * HIDDEN_STEPS, HIDDEN_STEPS),
        ],
        out_specs=tile(WIDTH),
        out_shape=shape(WIDTH, LAYER_COLS, BF16),
        scratch_shapes=[pltpu.VMEM((WIDTH, rows), BF16)] * 2,
        compiler_params=pltpu.CompilerParams(vmem_limit_bytes=VMEM_LIMIT),
        cost_estimate=pl.CostEstimate(
            flops=2 * rows * WIDTH * MLP_COLS, bytes_accessed=15_000_000, transcendentals=0
        ),
        name="mlp_weights",
    )(second, g, gate_grad, up_grad, hidden)


QKV_STEPS = QKV_COLS // HIDDEN_TILE


def attention_weights_kernel(first_ref, attn_in_ref, qkv_grad_ref, mix_ref, buffer, out_ref, first_t, attn_in_t):
    del buffer
    step = pl.program_id(0)

    @pl.when(step == 0)
    def _():
        first_t[...] = first_ref[...].T
        attn_in_t[...] = attn_in_ref[...].T

    @pl.when(step < QKV_STEPS)
    def _():
        out_ref[...] = nn_dot(first_t[...], qkv_grad_ref[...]).astype(BF16)

    @pl.when(step >= QKV_STEPS)
    def _():
        out_ref[...] = nn_dot(attn_in_t[...], mix_ref[...]).astype(BF16)


def attention_weights(buffer, first, attn_in, qkv_grad, mixture):
    rows = first.shape[0]
    out_steps = -(-OUT_COLS // HIDDEN_TILE)
    return pl.pallas_call(
        attention_weights_kernel,
        grid=(QKV_STEPS + out_steps,),
        in_specs=[
            fixed(rows, WIDTH),
            fixed(rows, WIDTH),
            tile_from(rows, 0, QKV_STEPS),
            tile_from(rows, QKV_STEPS, out_steps),
            any_whole(),
        ],
        out_specs=tile(WIDTH, MLP_COLS // HIDDEN_TILE),
        out_shape=shape(WIDTH, LAYER_COLS, BF16),
        input_output_aliases={4: 0},
        scratch_shapes=[pltpu.VMEM((WIDTH, rows), BF16)] * 2,
        compiler_params=pltpu.CompilerParams(vmem_limit_bytes=VMEM_LIMIT),
        cost_estimate=pl.CostEstimate(
            flops=2 * rows * WIDTH * ATTN_COLS, bytes_accessed=8_000_000, transcendentals=0
        ),
        name="attention_weights",
    )(first, attn_in, qkv_grad, mixture, buffer)


def sum_four(keep, give, beside=None):
    chip = (keep.astype(F32) + swap(give, "section").astype(F32)).astype(BF16)
    arrived = swap(chip, "tensor")
    if beside is not None:
        arrived, beside = lax.optimization_barrier((arrived, beside))
    total = (chip.astype(F32) + arrived.astype(F32)).astype(BF16)
    sums = total, swap(total, "section")
    return sums if beside is None else (sums, beside)


def halves(value):
    middle = value.shape[1] // 2
    return value[:, :middle], value[:, middle:]


def to_layers(core, low, high):
    mine, give = pick(core, low, high), pick(core, high, low)
    got = swap(give, "section")
    return pick(core, mine, got), pick(core, got, mine)


def from_layers(core, layer_zero, layer_one):
    mine, give = pick(core, layer_zero, layer_one), pick(core, layer_one, layer_zero)
    got = swap(give, "section")
    return pick(core, mine, got), pick(core, got, mine)


def gather_rows(z_low, share):
    other = swap(share, "zl")
    pair = jnp.concatenate([pick(z_low, share, other), pick(z_low, other, share)], axis=0)
    return lax.all_gather(pair, ("y", "x"), axis=0, tiled=True)


def scatter_rows(z_low, grad):
    pair = lax.psum_scatter(grad, ("y", "x"), scatter_dimension=0, tiled=True)
    keep = pick(z_low, pair[:48], pair[48:])
    give = pick(z_low, pair[48:], pair[:48])
    return (keep.astype(F32) + swap(give, "zl").astype(F32)).astype(BF16)


def to_ring_order(rows):
    lead = rows.shape[:-1]
    return jnp.swapaxes(rows.reshape(lead + (4, 2, 4, 48)), -3, -2).reshape(rows.shape)


def from_ring_order(rows):
    lead = rows.shape[:-1]
    return jnp.swapaxes(rows.reshape(lead + (4, 4, 2, 48)), -3, -2).reshape(rows.shape)


def join_positions(tensor, own):
    other = swap(own, "tensor")
    return jnp.concatenate(
        [pick(tensor, own, other), pick(tensor, other, own)], axis=1
    ).reshape(384, WIDTH)


def own_positions(tensor, rows):
    rows = rows.reshape(3, 128, 1536)
    return pick(tensor, rows[:, :64], rows[:, 64:])


def per_device(
    inputs, cotangent, plan, attn_gain, mlp_gain, w_query, key_weight, value_weight,
    w_out, w_gate, w_up, w_down,
):
    core = lax.axis_index("section")
    z_low = lax.axis_index("zl")
    tensor = lax.axis_index("tensor")

    attn_scale = attn_gain[0].astype(F32)[:, None]
    mlp_scale = mlp_gain[0].astype(F32)[:, None]

    def scaled(weight, scale):
        return (weight.astype(F32) * scale).astype(BF16)

    attn_shards = (w_query[0], key_weight[0], value_weight[0])
    mlp_shards = (w_gate[0], w_up[0])
    attn_pairs = [halves(scaled(weight, attn_scale)) for weight in attn_shards]
    attn_pairs.append(halves(w_out[0].T))
    mlp_pairs = [halves(scaled(weight, mlp_scale)) for weight in mlp_shards]
    mlp_pairs.append(halves(w_down[0].T))
    low, high = (jnp.concatenate(side, axis=1) for side in zip(*mlp_pairs, *attn_pairs))
    layer_zero, layer_one = to_layers(core, low, high)
    first_weights = gather_rows(
        z_low, jnp.concatenate([layer_zero, layer_one[:, MLP_COLS:]], axis=1)
    )
    last_weights = gather_rows(z_low, layer_one[:, :MLP_COLS])
    attn_weights = ((first_weights, MLP_COLS), (first_weights, LAYER_COLS))
    mlp_weights_of = (first_weights, last_weights)

    core_ref = core.astype(jnp.int32).reshape(1)
    stream = join_positions(tensor, to_ring_order(inputs[:, 0][plan]))

    kept, outputs = [], []
    x, middle, sums = stream, None, None
    for layer in range(2):
        x, first, qkv, probability, mixture, keep, give = attention_forward(
            core_ref, x, middle, sums, *attn_weights[layer]
        )
        if layer == 0:
            late, keep = lax.optimization_barrier((cotangent, keep))
            out_grad = join_positions(tensor, to_ring_order(late[:, 0][plan]))
        else:
            outputs.append(own_positions(tensor, x))
        middle, second, gate_out, up_out, hidden, keep, give = mlp_forward(
            core_ref, x, sum_four(keep, give), mlp_weights_of[layer]
        )
        sums = sum_four(keep, give)
        kept.append((x, first, qkv, probability, mixture, middle, second, gate_out, up_out, hidden))
    last = middle + jnp.concatenate(
        [pick(core, sums[0], sums[1]), pick(core, sums[1], sums[0])], axis=1
    ).astype(F32)
    outputs.append(own_positions(tensor, last.astype(BF16)))

    grads, weight_grads = [None] * 2, [None] * 2
    above = None
    for layer in (1, 0):
        x, first, qkv, probability, mixture, middle, second, gate_out, up_out, hidden = kept[layer]
        out_grad, gate_grad, up_grad, keep, give = mlp_backward(
            core_ref, out_grad, above, gate_out, up_out, mlp_weights_of[layer]
        )
        if layer == 0:
            grads[1] = own_positions(tensor, out_grad)
        buffer = mlp_weights(second, out_grad, gate_grad, up_grad, hidden)
        sums, buffer = sum_four(keep, give, buffer)
        middle_grad, attn_in, qkv_grad, keep, give = attention_backward(
            core_ref, out_grad, middle, sums, qkv, probability, *attn_weights[layer]
        )
        buffer = attention_weights(buffer, first, attn_in, qkv_grad, mixture)
        sums, buffer = sum_four(keep, give, buffer)
        weight_grads[layer] = scatter_rows(z_low, buffer)
        above = (x, middle_grad, *sums)
    x, middle_grad, own, other = above
    rows = x.astype(F32)
    weighted = jnp.concatenate(
        [pick(core, own, other), pick(core, other, own)], axis=1
    ).astype(F32)
    last = middle_grad + norm_back(weighted, rows, inverse_norm(rows))
    grads[0] = own_positions(tensor, last.astype(BF16))

    layer_outputs = from_ring_order(pick(core, outputs[0], outputs[1]))
    input_grads = from_ring_order(pick(core, grads[0], grads[1]))
    low, high = from_layers(core, *weight_grads)

    def joined(start, width):
        return jnp.concatenate(
            [low[:, start : start + width], high[:, start : start + width]], axis=1
        ).astype(F32)

    gate_grad = joined(0, HIDDEN_COLS)
    up_grad = joined(HIDDEN_COLS, HIDDEN_COLS)
    down_grad = joined(2 * HIDDEN_COLS, HIDDEN_COLS).T
    query_grad = joined(MLP_COLS, QUERY_COLS)
    key_grad = joined(MLP_COLS + QUERY_COLS, KV_COLS)
    value_grad = joined(MLP_COLS + QUERY_COLS + KV_COLS, KV_COLS)
    out_weight_grad = joined(MLP_COLS + QKV_COLS, OUT_COLS).T

    def gain_term(weights, weight_grads):
        return sum(
            jnp.sum(weight.astype(F32) * grad, axis=1)
            for weight, grad in zip(weights, weight_grads)
        )

    gain_terms = jnp.stack(
        [
            gain_term(attn_shards, (query_grad, key_grad, value_grad)),
            gain_term(mlp_shards, (gate_grad, up_grad)),
        ]
    )
    gain_terms = gain_terms + swap(gain_terms, "tensor")
    return (
        layer_outputs[None, :, None],
        input_grads[None, :, None],
        gain_terms[0][None],
        gain_terms[1][None],
        (query_grad * attn_scale)[None],
        (key_grad * attn_scale)[None],
        (value_grad * attn_scale)[None],
        out_weight_grad[None],
        (gate_grad * mlp_scale)[None],
        (up_grad * mlp_scale)[None],
        down_grad[None],
    )


def solution(mesh):
    split = Mesh(mesh.devices.reshape(2, 4, 2, 4, 2), ("section", "y", "zl", "x", "tensor"))
    dp = ("y", "zl", "x")
    rows = P("section", dp, "tensor")
    columns = P("section", "tensor", dp)
    return jax.shard_map(
        per_device,
        mesh=split,
        in_specs=(
            P(None, dp, "tensor", None),
            P(None, dp, "tensor", None),
            P(),
            P("section", dp),
            P("section", dp),
            rows,
            rows,
            rows,
            columns,
            rows,
            rows,
            columns,
        ),
        out_specs=(
            P("section", None, dp, "tensor", None),
            P("section", None, dp, "tensor", None),
            P("section", dp),
            P("section", dp),
            rows,
            rows,
            rows,
            columns,
            rows,
            rows,
            columns,
        ),
        check_vma=False,
    )
```

```python
import functools

import jax
import jax.numpy as jnp
from jax import lax
from jax.experimental import pallas as pl
from jax.experimental.pallas import tpu as pltpu
from jax.sharding import Mesh, PartitionSpec as P

HEAD_WIDTH = 96
EPSILON = 1e-05
BLOCKED = -1e30
SCORE_SCALE = HEAD_WIDTH ** (-0.5)
BF16 = jnp.bfloat16
F32 = jnp.float32

QUERY_COLS, KV_COLS = 384, 192
QKV_COLS = QUERY_COLS + 2 * KV_COLS
OUT_COLS = 384
HIDDEN_COLS = 1024
ATTN_COLS = QKV_COLS + OUT_COLS
MLP_COLS = 3 * HIDDEN_COLS
LAYER_COLS = MLP_COLS + ATTN_COLS
REST_COLS = LAYER_COLS + ATTN_COLS
HIDDEN_TILE = 256
QKV_STEPS = QKV_COLS // OUT_COLS
WIDTH = 1536
HALF = WIDTH // 2
VMEM_LIMIT = 30 * 1024 * 1024


def swap(value, axis):
    return lax.ppermute(value, axis, [(0, 1), (1, 0)])


def pick(index, first, second):
    return jnp.where(index == 0, first, second)


def norm_back(weighted, residual, inverse):
    scaled = residual * inverse
    return inverse * (weighted - scaled * jnp.mean(weighted * scaled, axis=-1, keepdims=True))


def vmem_whole():
    return pl.BlockSpec(memory_space=pltpu.VMEM)


def smem_whole():
    return pl.BlockSpec(memory_space=pltpu.SMEM)


def shape(rows, columns, dtype):
    return jax.ShapeDtypeStruct((rows, columns), dtype)


def half_of(core_ref, which):
    position = core_ref[0] if which == 0 else 1 - core_ref[0]
    return pl.ds(pl.multiple_of(position * HALF, HALF), HALF)


def nt_dot(left_side, right_side):
    return lax.dot_general(
        left_side, right_side, (((1,), (1,)), ((), ())), preferred_element_type=F32
    )


def tn_dot(left_side, right_side):
    return lax.dot_general(
        left_side, right_side, (((0,), (0,)), ((), ())), preferred_element_type=F32
    )


def nn_dot(left_side, right_side):
    return jnp.dot(left_side, right_side, preferred_element_type=F32)


def inverse_norm(rows):
    return lax.rsqrt(jnp.mean(rows * rows, axis=-1, keepdims=True) + EPSILON)


def causal_mask():
    row = lax.broadcasted_iota(jnp.int32, (128, 128), 0)
    return row >= lax.broadcasted_iota(jnp.int32, (128, 128), 1)


def two_heads(ref, rows, start):
    return jnp.concatenate(
        [
            ref[rows, start : start + HEAD_WIDTH],
            ref[rows, start + HEAD_WIDTH : start + 2 * HEAD_WIDTH],
        ],
        axis=0,
    )


def attention_weights_copy(w_any, w_ref, sem, column):
    return pltpu.make_async_copy(w_any.at[:, pl.ds(column, ATTN_COLS)], w_ref, sem)


def attention_forward_body(sequences, core_ref, first_ref, w_ref, qkv_ref, prob_ref, mix_ref, keep_ref, give_ref):
    qkv_ref[...] = nn_dot(first_ref[...], w_ref[:, :QKV_COLS]).astype(BF16)
    mask = causal_mask()
    mask = jnp.concatenate([mask, mask], axis=0)
    for sequence in range(sequences):
        rows = slice(128 * sequence, 128 * (sequence + 1))
        for group in range(2):
            queries = two_heads(qkv_ref, rows, 2 * HEAD_WIDTH * group)
            key_at = QUERY_COLS + HEAD_WIDTH * group
            value_at = key_at + KV_COLS
            scores = nt_dot(queries, qkv_ref[rows, key_at : key_at + HEAD_WIDTH]) * SCORE_SCALE
            scores = jnp.where(mask, scores, BLOCKED)
            expanded = jnp.exp(scores - jnp.max(scores, axis=-1, keepdims=True))
            probability = expanded / jnp.sum(expanded, axis=-1, keepdims=True)
            prob_ref[2 * sequence + group] = probability
            mixed = nn_dot(
                probability.astype(BF16), qkv_ref[rows, value_at : value_at + HEAD_WIDTH]
            ).astype(BF16)
            at = 2 * HEAD_WIDTH * group
            mix_ref[rows, at : at + HEAD_WIDTH] = mixed[:128]
            mix_ref[rows, at + HEAD_WIDTH : at + 2 * HEAD_WIDTH] = mixed[128:]
    mixture = mix_ref[...]
    give_ref[...] = nt_dot(mixture, w_ref[half_of(core_ref, 1), QKV_COLS:]).astype(BF16)
    keep_ref[...] = nt_dot(mixture, w_ref[half_of(core_ref, 0), QKV_COLS:]).astype(BF16)


def attention_first_kernel(sequences, column, core_ref, x_ref, w_any, first_ref, *rest):
    outs, w_ref, sem = rest[:-2], rest[-2], rest[-1]
    copy = attention_weights_copy(w_any, w_ref, sem, column)
    copy.start()
    rows = x_ref[...].astype(F32)
    first_ref[...] = (rows * inverse_norm(rows)).astype(BF16)
    copy.wait()
    attention_forward_body(sequences, core_ref, first_ref, w_ref, *outs)


def attention_next_kernel(sequences, column, core_ref, middle_ref, own_ref, other_ref, w_any, x_ref, first_ref, *rest):
    outs, w_ref, sem = rest[:-2], rest[-2], rest[-1]
    copy = attention_weights_copy(w_any, w_ref, sem, column)
    copy.start()
    for which, part in ((0, own_ref), (1, other_ref)):
        at = half_of(core_ref, which)
        x_ref[:, at] = (middle_ref[:, at] + part[...].astype(F32)).astype(BF16)
    rows = x_ref[...].astype(F32)
    first_ref[...] = (rows * inverse_norm(rows)).astype(BF16)
    copy.wait()
    attention_forward_body(sequences, core_ref, first_ref, w_ref, *outs)


def any_whole():
    return pl.BlockSpec(memory_space=pl.ANY)


def attention_scratch():
    return [pltpu.VMEM((WIDTH, ATTN_COLS), BF16), pltpu.SemaphoreType.DMA(())]


def attention_forward(core, x, middle, sums, weights, column):
    rows = (x if middle is None else middle).shape[0]
    sequences = rows // 128
    outs = [
        shape(rows, WIDTH, BF16),
        shape(rows, QKV_COLS, BF16),
        jax.ShapeDtypeStruct((2 * sequences, 256, 128), F32),
        shape(rows, OUT_COLS, BF16),
        shape(rows, HALF, BF16),
        shape(rows, HALF, BF16),
    ]
    if middle is None:
        operands, kernel = (core, x), attention_first_kernel
    else:
        operands, kernel = (core, middle, *sums), attention_next_kernel
        outs = [shape(rows, WIDTH, BF16)] + outs
    results = pl.pallas_call(
        functools.partial(kernel, sequences, column),
        in_specs=[smem_whole()] + [vmem_whole()] * (len(operands) - 1) + [any_whole()],
        out_specs=[vmem_whole()] * len(outs),
        out_shape=outs,
        scratch_shapes=attention_scratch(),
        compiler_params=pltpu.CompilerParams(vmem_limit_bytes=VMEM_LIMIT),
        cost_estimate=pl.CostEstimate(
            flops=2 * rows * WIDTH * ATTN_COLS, bytes_accessed=8_000_000, transcendentals=0
        ),
        name="attention_forward",
    )(*operands, weights)
    return ([x] if middle is None else []) + list(results)


def mlp_forward_kernel(core_ref, x_ref, own_ref, other_ref, gate_w, up_w, down_w, middle_ref, second_ref, gate_ref, up_ref, hidden_ref, keep_ref, give_ref, total):
    step = pl.program_id(0)

    @pl.when(step == 0)
    def _():
        for which, part in ((0, own_ref), (1, other_ref)):
            at = half_of(core_ref, which)
            middle_ref[:, at] = x_ref[:, at].astype(F32) + part[...].astype(F32)
        rows = middle_ref[...]
        second_ref[...] = (rows * inverse_norm(rows)).astype(BF16)
        total[...] = jnp.zeros_like(total)

    gate_out = nn_dot(second_ref[...], gate_w[...])
    up_out = nn_dot(second_ref[...], up_w[...])
    gate_ref[...] = gate_out
    up_ref[...] = up_out
    hidden = (gate_out * (1.0 / (1.0 + jnp.exp(-gate_out))) * up_out).astype(BF16)
    hidden_ref[...] = hidden
    total[...] += nt_dot(hidden, down_w[...])

    @pl.when(step == pl.num_programs(0) - 1)
    def _():
        give_ref[...] = total[:, half_of(core_ref, 1)].astype(BF16)
        keep_ref[...] = total[:, half_of(core_ref, 0)].astype(BF16)


def fixed(rows, columns):
    return pl.BlockSpec((rows, columns), lambda j: (0, 0))


def tile(rows, first=0):
    return pl.BlockSpec((rows, HIDDEN_TILE), lambda j: (0, first + j))


HIDDEN_STEPS = HIDDEN_COLS // HIDDEN_TILE


def mlp_forward(core, x, sums, w_mlp):
    rows = x.shape[0]
    return pl.pallas_call(
        mlp_forward_kernel,
        grid=(HIDDEN_STEPS,),
        in_specs=[
            smem_whole(),
            fixed(rows, WIDTH),
            fixed(rows, HALF),
            fixed(rows, HALF),
            tile(WIDTH),
            tile(WIDTH, HIDDEN_STEPS),
            tile(WIDTH, 2 * HIDDEN_STEPS),
        ],
        out_specs=[
            fixed(rows, WIDTH),
            fixed(rows, WIDTH),
            tile(rows),
            tile(rows),
            tile(rows),
            fixed(rows, HALF),
            fixed(rows, HALF),
        ],
        out_shape=[
            shape(rows, WIDTH, F32),
            shape(rows, WIDTH, BF16),
            shape(rows, HIDDEN_COLS, F32),
            shape(rows, HIDDEN_COLS, F32),
            shape(rows, HIDDEN_COLS, BF16),
            shape(rows, HALF, BF16),
            shape(rows, HALF, BF16),
        ],
        scratch_shapes=[pltpu.VMEM((rows, WIDTH), F32)],
        compiler_params=pltpu.CompilerParams(vmem_limit_bytes=VMEM_LIMIT),
        cost_estimate=pl.CostEstimate(
            flops=2 * rows * WIDTH * MLP_COLS, bytes_accessed=15_000_000, transcendentals=0
        ),
        name="mlp_forward",
    )(core, x, *sums, w_mlp, w_mlp, w_mlp)


def mlp_backward_kernel(core_ref, g_ref, gate_ref, up_ref, gate_w, up_w, down_w, gate_grad_ref, up_grad_ref, keep_ref, give_ref, total):
    step = pl.program_id(0)

    @pl.when(step == 0)
    def _():
        total[...] = jnp.zeros_like(total)

    hidden_grad = nn_dot(g_ref[...], down_w[...])
    gate_out = gate_ref[...]
    sigmoid_gate = 1.0 / (1.0 + jnp.exp(-gate_out))
    gate_grad = (
        hidden_grad * up_ref[...] * (sigmoid_gate * (1.0 + gate_out * (1.0 - sigmoid_gate)))
    ).astype(BF16)
    up_grad = (hidden_grad * (gate_out * sigmoid_gate)).astype(BF16)
    gate_grad_ref[...] = gate_grad
    up_grad_ref[...] = up_grad
    total[...] += nt_dot(gate_grad, gate_w[...]) + nt_dot(up_grad, up_w[...])

    @pl.when(step == pl.num_programs(0) - 1)
    def _():
        give_ref[...] = total[:, half_of(core_ref, 1)].astype(BF16)
        keep_ref[...] = total[:, half_of(core_ref, 0)].astype(BF16)


def mlp_backward_next_kernel(core_ref, x_ref, middle_grad_ref, own_ref, other_ref, gate_ref, up_ref, gate_w, up_w, down_w, g_ref, gate_grad_ref, up_grad_ref, keep_ref, give_ref, total):
    @pl.when(pl.program_id(0) == 0)
    def _():
        for which, part in ((0, own_ref), (1, other_ref)):
            total[:, half_of(core_ref, which)] = part[...].astype(F32)
        rows = x_ref[...].astype(F32)
        inverse = inverse_norm(rows)
        g_ref[...] = (middle_grad_ref[...] + norm_back(total[...], rows, inverse)).astype(BF16)

    mlp_backward_kernel(core_ref, g_ref, gate_ref, up_ref, gate_w, up_w, down_w, gate_grad_ref, up_grad_ref, keep_ref, give_ref, total)


def mlp_backward(core, g, above, gate_out, up_out, w_mlp):
    rows = gate_out.shape[0]
    if above is None:
        lead, kernel, lead_specs = (g,), mlp_backward_kernel, [fixed(rows, WIDTH)]
    else:
        lead, kernel = above, mlp_backward_next_kernel
        lead_specs = [fixed(rows, WIDTH)] * 2 + [fixed(rows, HALF)] * 2
    out_specs = [tile(rows), tile(rows), fixed(rows, HALF), fixed(rows, HALF)]
    out_shape = [
        shape(rows, HIDDEN_COLS, BF16),
        shape(rows, HIDDEN_COLS, BF16),
        shape(rows, HALF, BF16),
        shape(rows, HALF, BF16),
    ]
    if above is not None:
        out_specs = [fixed(rows, WIDTH)] + out_specs
        out_shape = [shape(rows, WIDTH, BF16)] + out_shape
    results = pl.pallas_call(
        kernel,
        grid=(HIDDEN_STEPS,),
        in_specs=[smem_whole()]
        + lead_specs
        + [
            tile(rows),
            tile(rows),
            tile(WIDTH),
            tile(WIDTH, HIDDEN_STEPS),
            tile(WIDTH, 2 * HIDDEN_STEPS),
        ],
        out_specs=out_specs,
        out_shape=out_shape,
        scratch_shapes=[pltpu.VMEM((rows, WIDTH), F32)],
        compiler_params=pltpu.CompilerParams(vmem_limit_bytes=VMEM_LIMIT),
        cost_estimate=pl.CostEstimate(
            flops=2 * rows * WIDTH * MLP_COLS, bytes_accessed=15_000_000, transcendentals=0
        ),
        name="mlp_backward",
    )(core, *lead, gate_out, up_out, w_mlp, w_mlp, w_mlp)
    return ([g] if above is None else []) + list(results)


def attention_backward_kernel(sequences, column, core_ref, g_ref, middle_ref, own_ref, other_ref, qkv_ref, prob_ref, w_any, middle_grad_ref, attn_in_ref, qkv_grad_ref, keep_ref, give_ref, mix_grad, w_ref, sem):
    copy = attention_weights_copy(w_any, w_ref, sem, column)
    copy.start()
    for which, part in ((0, own_ref), (1, other_ref)):
        middle_grad_ref[:, half_of(core_ref, which)] = part[...].astype(F32)
    middle = middle_ref[...]
    middle_grad = g_ref[...].astype(F32) + norm_back(
        middle_grad_ref[...], middle, inverse_norm(middle)
    )
    middle_grad_ref[...] = middle_grad
    attn_in_ref[...] = middle_grad.astype(BF16)
    copy.wait()
    mix_grad[...] = nn_dot(attn_in_ref[...], w_ref[:, QKV_COLS:]).astype(BF16)
    for sequence in range(sequences):
        rows = slice(128 * sequence, 128 * (sequence + 1))
        for group in range(2):
            at = 2 * HEAD_WIDTH * group
            key_at = QUERY_COLS + HEAD_WIDTH * group
            value_at = key_at + KV_COLS
            grads = two_heads(mix_grad, rows, at)
            queries = two_heads(qkv_ref, rows, at)
            keys = qkv_ref[rows, key_at : key_at + HEAD_WIDTH]
            probability = prob_ref[2 * sequence + group]
            prob_grad = nt_dot(grads, qkv_ref[rows, value_at : value_at + HEAD_WIDTH])
            centred = jnp.sum(probability * prob_grad, axis=-1, keepdims=True)
            score_grad = (probability * (prob_grad - centred)).astype(BF16)
            query_grad = (nn_dot(score_grad, keys) * SCORE_SCALE).astype(BF16)
            qkv_grad_ref[rows, at : at + HEAD_WIDTH] = query_grad[:128]
            qkv_grad_ref[rows, at + HEAD_WIDTH : at + 2 * HEAD_WIDTH] = query_grad[128:]
            qkv_grad_ref[rows, key_at : key_at + HEAD_WIDTH] = (
                tn_dot(score_grad, queries) * SCORE_SCALE
            ).astype(BF16)
            qkv_grad_ref[rows, value_at : value_at + HEAD_WIDTH] = tn_dot(
                probability.astype(BF16), grads
            ).astype(BF16)
    qkv_grad = qkv_grad_ref[...]
    give_ref[...] = nt_dot(qkv_grad, w_ref[half_of(core_ref, 1), :QKV_COLS]).astype(BF16)
    keep_ref[...] = nt_dot(qkv_grad, w_ref[half_of(core_ref, 0), :QKV_COLS]).astype(BF16)


def attention_backward(core, g, middle, sums, qkv, probability, weights, column):
    rows = g.shape[0]
    return pl.pallas_call(
        functools.partial(attention_backward_kernel, rows // 128, column),
        in_specs=[smem_whole()] + [vmem_whole()] * 6 + [any_whole()],
        out_specs=[vmem_whole()] * 5,
        out_shape=[
            shape(rows, WIDTH, F32),
            shape(rows, WIDTH, BF16),
            shape(rows, QKV_COLS, BF16),
            shape(rows, HALF, BF16),
            shape(rows, HALF, BF16),
        ],
        scratch_shapes=[pltpu.VMEM((rows, OUT_COLS), BF16)] + attention_scratch(),
        compiler_params=pltpu.CompilerParams(vmem_limit_bytes=VMEM_LIMIT),
        cost_estimate=pl.CostEstimate(
            flops=2 * rows * WIDTH * ATTN_COLS, bytes_accessed=12_000_000, transcendentals=0
        ),
        name="attention_backward",
    )(core, g, middle, *sums, qkv, probability, weights)


def mlp_weights_kernel(second_ref, g_ref, gate_ref, up_ref, hidden_ref, *rest):
    out_ref = rest[-1]
    step = pl.program_id(0)

    @pl.when(step < HIDDEN_STEPS)
    def _():
        out_ref[...] = tn_dot(second_ref[...], gate_ref[...]).astype(BF16)

    @pl.when((step >= HIDDEN_STEPS) & (step < 2 * HIDDEN_STEPS))
    def _():
        out_ref[...] = tn_dot(second_ref[...], up_ref[...]).astype(BF16)

    @pl.when(step >= 2 * HIDDEN_STEPS)
    def _():
        out_ref[...] = tn_dot(g_ref[...], hidden_ref[...]).astype(BF16)


def tile_from(rows, first, count, width):
    return pl.BlockSpec((rows, width), lambda j: (0, jnp.clip(j - first, 0, count - 1)))


def into_buffer(kernel, buffer, columns, specs, operands, flops, **call):
    aliases = {}
    if buffer is not None:
        aliases = {len(operands): 0}
        specs, operands = specs + [any_whole()], operands + (buffer,)
    return pl.pallas_call(
        kernel,
        in_specs=specs,
        out_shape=shape(WIDTH, columns, BF16),
        input_output_aliases=aliases,
        compiler_params=pltpu.CompilerParams(vmem_limit_bytes=VMEM_LIMIT),
        cost_estimate=pl.CostEstimate(flops=flops, bytes_accessed=flops // 250, transcendentals=0),
        **call,
    )(*operands)


def mlp_weights(buffer, columns, second, g, gate_grad, up_grad, hidden):
    rows = second.shape[0]
    return into_buffer(
        mlp_weights_kernel,
        buffer,
        columns,
        [fixed(rows, WIDTH)] * 2
        + [tile_from(rows, HIDDEN_STEPS * part, HIDDEN_STEPS, HIDDEN_TILE) for part in range(3)],
        (second, g, gate_grad, up_grad, hidden),
        2 * rows * WIDTH * MLP_COLS,
        grid=(3 * HIDDEN_STEPS,),
        out_specs=tile(WIDTH),
        name="mlp_weights",
    )


def attention_weights_kernel(first_ref, attn_in_ref, qkv_grad_ref, mix_ref, *rest):
    out_ref = rest[-1]
    step = pl.program_id(0)

    @pl.when(step < QKV_STEPS)
    def _():
        out_ref[...] = tn_dot(first_ref[...], qkv_grad_ref[...]).astype(BF16)

    @pl.when(step >= QKV_STEPS)
    def _():
        out_ref[...] = tn_dot(attn_in_ref[...], mix_ref[...]).astype(BF16)


def attention_weights(buffer, columns, start, first, attn_in, qkv_grad, mixture):
    rows = first.shape[0]
    return into_buffer(
        attention_weights_kernel,
        buffer,
        columns,
        [fixed(rows, WIDTH)] * 2
        + [
            tile_from(rows, 0, QKV_STEPS, OUT_COLS),
            tile_from(rows, QKV_STEPS, 1, OUT_COLS),
        ],
        (first, attn_in, qkv_grad, mixture),
        2 * rows * WIDTH * ATTN_COLS,
        grid=(QKV_STEPS + 1,),
        out_specs=pl.BlockSpec((WIDTH, OUT_COLS), lambda j: (0, start // OUT_COLS + j)),
        name="attention_weights",
    )


def sum_four(keep, give, beside=None):
    chip = (keep.astype(F32) + swap(give, "section").astype(F32)).astype(BF16)
    arrived = swap(chip, "tensor")
    if beside is not None:
        arrived, beside = lax.optimization_barrier((arrived, beside))
    total = (chip.astype(F32) + arrived.astype(F32)).astype(BF16)
    sums = total, swap(total, "section")
    return sums if beside is None else (sums, beside)


def halves(value):
    middle = value.shape[1] // 2
    return value[:, :middle], value[:, middle:]


def to_layers(core, low, high):
    mine, give = pick(core, low, high), pick(core, high, low)
    got = swap(give, "section")
    return pick(core, mine, got), pick(core, got, mine)


def from_layers(core, layer_zero, layer_one):
    mine, give = pick(core, layer_zero, layer_one), pick(core, layer_one, layer_zero)
    got = swap(give, "section")
    return pick(core, mine, got), pick(core, got, mine)


def gather_rows(z_low, share):
    other = swap(share, "zl")
    pair = jnp.concatenate([pick(z_low, share, other), pick(z_low, other, share)], axis=0)
    return lax.all_gather(pair, ("y", "x"), axis=0, tiled=True)


def scatter_rows(z_low, grad):
    pair = lax.psum_scatter(grad, ("y", "x"), scatter_dimension=0, tiled=True)
    keep = pick(z_low, pair[:48], pair[48:])
    give = pick(z_low, pair[48:], pair[:48])
    return (keep.astype(F32) + swap(give, "zl").astype(F32)).astype(BF16)


def to_ring_order(rows):
    lead = rows.shape[:-1]
    return jnp.swapaxes(rows.reshape(lead + (4, 2, 4, 48)), -3, -2).reshape(rows.shape)


def from_ring_order(rows):
    lead = rows.shape[:-1]
    return jnp.swapaxes(rows.reshape(lead + (4, 4, 2, 48)), -3, -2).reshape(rows.shape)


def join_positions(tensor, own):
    other = swap(own, "tensor")
    return jnp.concatenate(
        [pick(tensor, own, other), pick(tensor, other, own)], axis=1
    ).reshape(384, WIDTH)


def own_positions(tensor, rows):
    rows = rows.reshape(3, 128, 1536)
    return pick(tensor, rows[:, :64], rows[:, 64:])


def per_device(
    inputs, cotangent, plan, attn_gain, mlp_gain, w_query, key_weight, value_weight,
    w_out, w_gate, w_up, w_down,
):
    core = lax.axis_index("section")
    z_low = lax.axis_index("zl")
    tensor = lax.axis_index("tensor")

    attn_scale = attn_gain[0].astype(F32)[:, None]
    mlp_scale = mlp_gain[0].astype(F32)[:, None]

    def scaled(weight, scale):
        return (weight.astype(F32) * scale).astype(BF16)

    attn_shards = (w_query[0], key_weight[0], value_weight[0])
    mlp_shards = (w_gate[0], w_up[0])
    attn_pairs = [halves(scaled(weight, attn_scale)) for weight in attn_shards]
    attn_pairs.append(halves(w_out[0].T))
    mlp_pairs = [halves(scaled(weight, mlp_scale)) for weight in mlp_shards]
    mlp_pairs.append(halves(w_down[0].T))
    low, high = (jnp.concatenate(side, axis=1) for side in zip(*mlp_pairs, *attn_pairs))
    layer_zero, layer_one = to_layers(core, low, high)
    first_weights = gather_rows(
        z_low, jnp.concatenate([layer_zero, layer_one[:, MLP_COLS:]], axis=1)
    )
    last_weights = gather_rows(z_low, layer_one[:, :MLP_COLS])
    attn_weights = ((first_weights, MLP_COLS), (first_weights, LAYER_COLS))
    mlp_weights_of = (first_weights, last_weights)

    core_ref = core.astype(jnp.int32).reshape(1)
    stream = join_positions(tensor, to_ring_order(inputs[:, 0][plan]))
    stream, late = lax.optimization_barrier((stream, cotangent))
    out_grad = join_positions(tensor, to_ring_order(late[:, 0][plan]))
    stream, out_grad = lax.optimization_barrier((stream, out_grad))

    kept, outputs = [], []
    x, middle, sums = stream, None, None
    for layer in range(2):
        x, first, qkv, probability, mixture, keep, give = attention_forward(
            core_ref, x, middle, sums, *attn_weights[layer]
        )
        if layer == 1:
            outputs.append(own_positions(tensor, x))
        middle, second, gate_out, up_out, hidden, keep, give = mlp_forward(
            core_ref, x, sum_four(keep, give), mlp_weights_of[layer]
        )
        sums = sum_four(keep, give)
        kept.append((x, first, qkv, probability, mixture, middle, second, gate_out, up_out, hidden))
    last = middle + jnp.concatenate(
        [pick(core, sums[0], sums[1]), pick(core, sums[1], sums[0])], axis=1
    ).astype(F32)
    outputs.append(own_positions(tensor, last.astype(BF16)))

    grads = [None] * 2
    buffer = None
    above = None
    for layer in (1, 0):
        x, first, qkv, probability, mixture, middle, second, gate_out, up_out, hidden = kept[layer]
        out_grad, gate_grad, up_grad, keep, give = mlp_backward(
            core_ref, out_grad, above, gate_out, up_out, mlp_weights_of[layer]
        )
        if layer == 0:
            grads[1] = own_positions(tensor, out_grad)
        beside = mlp_weights(
            buffer, MLP_COLS if layer == 1 else REST_COLS,
            second, out_grad, gate_grad, up_grad, hidden,
        )
        sums, beside = sum_four(keep, give, beside)
        if layer == 1:
            last_grad = scatter_rows(z_low, beside)
        else:
            buffer = beside
        middle_grad, attn_in, qkv_grad, keep, give = attention_backward(
            core_ref, out_grad, middle, sums, qkv, probability, *attn_weights[layer]
        )
        buffer = attention_weights(
            buffer, REST_COLS, MLP_COLS if layer == 1 else LAYER_COLS,
            first, attn_in, qkv_grad, mixture,
        )
        sums, buffer = sum_four(keep, give, buffer)
        above = (x, middle_grad, *sums)
    x, middle_grad, own, other = above
    rows = x.astype(F32)
    weighted = jnp.concatenate(
        [pick(core, own, other), pick(core, other, own)], axis=1
    ).astype(F32)
    last = middle_grad + norm_back(weighted, rows, inverse_norm(rows))
    grads[0] = own_positions(tensor, last.astype(BF16))

    layer_outputs = from_ring_order(pick(core, outputs[0], outputs[1]))
    input_grads = from_ring_order(pick(core, grads[0], grads[1]))
    rest_grad = scatter_rows(z_low, buffer)
    zero_grad = jnp.concatenate([rest_grad[:, :MLP_COLS], rest_grad[:, LAYER_COLS:]], axis=1)
    one_grad = jnp.concatenate([last_grad, rest_grad[:, MLP_COLS:LAYER_COLS]], axis=1)
    low, high = from_layers(core, zero_grad, one_grad)

    def joined(start, width):
        return jnp.concatenate(
            [low[:, start : start + width], high[:, start : start + width]], axis=1
        ).astype(F32)

    gate_grad = joined(0, HIDDEN_COLS)
    up_grad = joined(HIDDEN_COLS, HIDDEN_COLS)
    down_grad = joined(2 * HIDDEN_COLS, HIDDEN_COLS).T
    query_grad = joined(MLP_COLS, QUERY_COLS)
    key_grad = joined(MLP_COLS + QUERY_COLS, KV_COLS)
    value_grad = joined(MLP_COLS + QUERY_COLS + KV_COLS, KV_COLS)
    out_weight_grad = joined(MLP_COLS + QKV_COLS, OUT_COLS).T

    def gain_terms(weights, grad):
        terms = weights.astype(F32) * grad.astype(F32)
        return jnp.stack(
            [
                jnp.sum(terms[:, MLP_COLS : MLP_COLS + QKV_COLS], axis=1),
                jnp.sum(terms[:, : 2 * HIDDEN_COLS], axis=1),
            ]
        )

    terms = jnp.stack([gain_terms(layer_zero, zero_grad), gain_terms(layer_one, one_grad)])
    terms = terms + swap(terms, "tensor")
    terms = pick(core, terms[0], terms[1]) + swap(pick(core, terms[1], terms[0]), "section")
    return (
        layer_outputs[None, :, None],
        input_grads[None, :, None],
        (terms[0] / attn_scale[:, 0])[None],
        (terms[1] / mlp_scale[:, 0])[None],
        (query_grad * attn_scale)[None],
        (key_grad * attn_scale)[None],
        (value_grad * attn_scale)[None],
        out_weight_grad[None],
        (gate_grad * mlp_scale)[None],
        (up_grad * mlp_scale)[None],
        down_grad[None],
    )


def solution(mesh):
    split = Mesh(mesh.devices.reshape(2, 4, 2, 4, 2), ("section", "y", "zl", "x", "tensor"))
    dp = ("y", "zl", "x")
    rows = P("section", dp, "tensor")
    columns = P("section", "tensor", dp)
    return jax.shard_map(
        per_device,
        mesh=split,
        in_specs=(
            P(None, dp, "tensor", None),
            P(None, dp, "tensor", None),
            P(),
            P("section", dp),
            P("section", dp),
            rows,
            rows,
            rows,
            columns,
            rows,
            rows,
            columns,
        ),
        out_specs=(
            P("section", None, dp, "tensor", None),
            P("section", None, dp, "tensor", None),
            P("section", dp),
            P("section", dp),
            rows,
            rows,
            rows,
            columns,
            rows,
            rows,
            columns,
        ),
        check_vma=False,
    )
```

```python
import functools

import jax
import jax.numpy as jnp
from jax import lax
from jax.experimental import pallas as pl
from jax.experimental.pallas import tpu as pltpu
from jax.sharding import Mesh, PartitionSpec as P

HEAD_WIDTH = 96
EPSILON = 1e-05
BLOCKED = -1e30
SCORE_SCALE = HEAD_WIDTH ** (-0.5)
BF16 = jnp.bfloat16
F32 = jnp.float32

QUERY_COLS, KV_COLS = 384, 192
QKV_COLS = QUERY_COLS + 2 * KV_COLS
OUT_COLS = 384
HIDDEN_COLS = 1024
ATTN_COLS = QKV_COLS + OUT_COLS
MLP_COLS = 3 * HIDDEN_COLS
LAYER_COLS = MLP_COLS + ATTN_COLS
REST_COLS = LAYER_COLS + ATTN_COLS
HIDDEN_TILE = 512
MLP_STRIP = 512
AHEAD = 3
WIDTH = 1536
HALF = WIDTH // 2
VMEM_LIMIT = 30 * 1024 * 1024


def swap(value, axis):
    return lax.ppermute(value, axis, [(0, 1), (1, 0)])


def pick(index, first, second):
    return jnp.where(index == 0, first, second)


def norm_back(weighted, residual, inverse):
    scaled = residual * inverse
    return inverse * (weighted - scaled * jnp.mean(weighted * scaled, axis=-1, keepdims=True))


def vmem_whole():
    return pl.BlockSpec(memory_space=pltpu.VMEM)


def smem_whole():
    return pl.BlockSpec(memory_space=pltpu.SMEM)


def shape(rows, columns, dtype):
    return jax.ShapeDtypeStruct((rows, columns), dtype)


def half_of(core_ref, which):
    position = core_ref[0] if which == 0 else 1 - core_ref[0]
    return pl.ds(pl.multiple_of(position * HALF, HALF), HALF)


def nt_dot(left_side, right_side):
    return lax.dot_general(
        left_side, right_side, (((1,), (1,)), ((), ())), preferred_element_type=F32
    )


def tn_dot(left_side, right_side):
    return lax.dot_general(
        left_side, right_side, (((0,), (0,)), ((), ())), preferred_element_type=F32
    )


def nn_dot(left_side, right_side):
    return jnp.dot(left_side, right_side, preferred_element_type=F32)


def inverse_norm(rows):
    return lax.rsqrt(jnp.mean(rows * rows, axis=-1, keepdims=True) + EPSILON)


def causal_mask():
    row = lax.broadcasted_iota(jnp.int32, (128, 128), 0)
    return row >= lax.broadcasted_iota(jnp.int32, (128, 128), 1)


def two_heads(ref, rows, start):
    return jnp.concatenate(
        [
            ref[rows, start : start + HEAD_WIDTH],
            ref[rows, start + HEAD_WIDTH : start + 2 * HEAD_WIDTH],
        ],
        axis=0,
    )


def attention_weights_copy(w_any, w_ref, sem, column):
    return pltpu.make_async_copy(w_any.at[:, pl.ds(column, ATTN_COLS)], w_ref, sem)


def attention_forward_body(sequences, core_ref, first_ref, w_ref, qkv_ref, prob_ref, mix_ref, keep_ref, give_ref):
    qkv_ref[...] = nn_dot(first_ref[...], w_ref[:, :QKV_COLS]).astype(BF16)
    mask = causal_mask()
    mask = jnp.concatenate([mask, mask], axis=0)
    for sequence in range(sequences):
        rows = slice(128 * sequence, 128 * (sequence + 1))
        for group in range(2):
            queries = two_heads(qkv_ref, rows, 2 * HEAD_WIDTH * group)
            key_at = QUERY_COLS + HEAD_WIDTH * group
            value_at = key_at + KV_COLS
            scores = nt_dot(queries, qkv_ref[rows, key_at : key_at + HEAD_WIDTH]) * SCORE_SCALE
            scores = jnp.where(mask, scores, BLOCKED)
            expanded = jnp.exp(scores - jnp.max(scores, axis=-1, keepdims=True))
            probability = expanded / jnp.sum(expanded, axis=-1, keepdims=True)
            prob_ref[2 * sequence + group] = probability
            mixed = nn_dot(
                probability.astype(BF16), qkv_ref[rows, value_at : value_at + HEAD_WIDTH]
            ).astype(BF16)
            at = 2 * HEAD_WIDTH * group
            mix_ref[rows, at : at + HEAD_WIDTH] = mixed[:128]
            mix_ref[rows, at + HEAD_WIDTH : at + 2 * HEAD_WIDTH] = mixed[128:]
    mixture = mix_ref[...]
    give_ref[...] = nt_dot(mixture, w_ref[half_of(core_ref, 1), QKV_COLS:]).astype(BF16)
    keep_ref[...] = nt_dot(mixture, w_ref[half_of(core_ref, 0), QKV_COLS:]).astype(BF16)


def attention_first_kernel(sequences, column, core_ref, x_ref, w_any, first_ref, *rest):
    outs, w_ref, sem = rest[:-2], rest[-2], rest[-1]
    copy = attention_weights_copy(w_any, w_ref, sem, column)
    copy.start()
    rows = x_ref[...].astype(F32)
    first_ref[...] = (rows * inverse_norm(rows)).astype(BF16)
    copy.wait()
    attention_forward_body(sequences, core_ref, first_ref, w_ref, *outs)


def attention_next_kernel(sequences, column, core_ref, middle_ref, own_ref, other_ref, w_any, x_ref, first_ref, *rest):
    outs, w_ref, sem = rest[:-2], rest[-2], rest[-1]
    copy = attention_weights_copy(w_any, w_ref, sem, column)
    copy.start()
    for which, part in ((0, own_ref), (1, other_ref)):
        at = half_of(core_ref, which)
        x_ref[:, at] = (middle_ref[:, at] + part[...].astype(F32)).astype(BF16)
    rows = x_ref[...].astype(F32)
    first_ref[...] = (rows * inverse_norm(rows)).astype(BF16)
    copy.wait()
    attention_forward_body(sequences, core_ref, first_ref, w_ref, *outs)


def in_hbm(value):
    return pltpu.with_memory_space_constraint(value, pltpu.HBM)


def hbm_whole():
    return pl.BlockSpec(memory_space=pltpu.HBM)


def attention_scratch():
    return [pltpu.VMEM((WIDTH, ATTN_COLS), BF16), pltpu.SemaphoreType.DMA(())]


def attention_forward(core, x, middle, sums, weights, column):
    rows = (x if middle is None else middle).shape[0]
    sequences = rows // 128
    outs = [
        shape(rows, WIDTH, BF16),
        shape(rows, QKV_COLS, BF16),
        jax.ShapeDtypeStruct((2 * sequences, 256, 128), F32),
        shape(rows, OUT_COLS, BF16),
        shape(rows, HALF, BF16),
        shape(rows, HALF, BF16),
    ]
    if middle is None:
        operands, kernel = (core, x), attention_first_kernel
    else:
        operands, kernel = (core, middle, *sums), attention_next_kernel
        outs = [shape(rows, WIDTH, BF16)] + outs
    results = pl.pallas_call(
        functools.partial(kernel, sequences, column),
        in_specs=[smem_whole()] + [vmem_whole()] * (len(operands) - 1) + [hbm_whole()],
        out_specs=[vmem_whole()] * len(outs),
        out_shape=outs,
        scratch_shapes=attention_scratch(),
        compiler_params=pltpu.CompilerParams(vmem_limit_bytes=VMEM_LIMIT),
        cost_estimate=pl.CostEstimate(
            flops=2 * rows * WIDTH * ATTN_COLS, bytes_accessed=8_000_000, transcendentals=0
        ),
        name="attention_forward",
    )(*operands, in_hbm(weights))
    return ([x] if middle is None else []) + list(results)


def column_tiles(first):
    return [pl.ds(first + HIDDEN_TILE * step, HIDDEN_TILE) for step in range(HIDDEN_STEPS)]


def row_halves(core_ref):
    return [half_of(core_ref, 1), half_of(core_ref, 0)]


def weight_copies(w_any, w_ref, sems, regions):
    return [
        pltpu.make_async_copy(w_any.at[rows, columns], w_ref.at[rows, columns], sems.at[number])
        for number, (rows, columns) in enumerate(regions)
    ]


def sigmoid(values):
    return 0.5 * jnp.tanh(0.5 * values) + 0.5


def arrivals(copies):
    for copy in copies[:AHEAD]:
        copy.start()
    place = iter(range(len(copies)))

    def arrive():
        number = next(place)
        copies[number].wait()
        if number + AHEAD < len(copies):
            copies[number + AHEAD].start()

    return arrive


def mlp_forward_kernel(core_ref, x_ref, own_ref, other_ref, w_any, middle_any, second_any, gate_any, up_any, hidden_any, keep_ref, give_ref, w_ref, middle_ref, second_ref, gate_ref, up_ref, hidden_ref, sems, out_sems):
    whole = pl.ds(0, WIDTH)
    tiles = [(gate, up) for gate, up in zip(column_tiles(0), column_tiles(HIDDEN_COLS))]
    down = pl.ds(2 * HIDDEN_COLS, HIDDEN_COLS)
    regions = [(whole, columns) for pair in tiles for columns in pair]
    regions += [(rows, down) for rows in row_halves(core_ref)]
    arrive = arrivals(weight_copies(w_any, w_ref, sems, regions))
    for which, part in ((0, own_ref), (1, other_ref)):
        at = half_of(core_ref, which)
        middle_ref[:, at] = x_ref[:, at].astype(F32) + part[...].astype(F32)
    rows = middle_ref[...]
    second_ref[...] = (rows * inverse_norm(rows)).astype(BF16)
    outward = []

    def send(source, target):
        outward.append(pltpu.make_async_copy(source, target, out_sems.at[len(outward)]))
        outward[-1].start()

    send(middle_ref, middle_any)
    send(second_ref, second_any)
    for step, (gate, up) in enumerate(tiles):
        at = slice(HIDDEN_TILE * step, HIDDEN_TILE * (step + 1))
        arrive()
        gate_out = nn_dot(second_ref[...], w_ref[:, gate])
        arrive()
        up_out = nn_dot(second_ref[...], w_ref[:, up])
        gate_ref[:, at] = gate_out
        up_ref[:, at] = up_out
        hidden_ref[:, at] = (gate_out * sigmoid(gate_out) * up_out).astype(BF16)
    send(gate_ref, gate_any)
    send(up_ref, up_any)
    send(hidden_ref, hidden_any)
    for half, out_ref in zip(row_halves(core_ref), (give_ref, keep_ref)):
        arrive()
        out_ref[...] = nt_dot(hidden_ref[...], w_ref[half, down]).astype(BF16)
    for copy in outward:
        copy.wait()


HIDDEN_STEPS = HIDDEN_COLS // HIDDEN_TILE


def mlp_scratch():
    return [pltpu.VMEM((WIDTH, MLP_COLS), BF16), pltpu.SemaphoreType.DMA((2 * HIDDEN_STEPS + 2,))]


def mlp_forward(core, x, sums, weights):
    rows = x.shape[0]
    saved = [
        shape(rows, WIDTH, F32),
        shape(rows, WIDTH, BF16),
        shape(rows, HIDDEN_COLS, F32),
        shape(rows, HIDDEN_COLS, F32),
        shape(rows, HIDDEN_COLS, BF16),
    ]
    return pl.pallas_call(
        mlp_forward_kernel,
        in_specs=[smem_whole()] + [vmem_whole()] * 3 + [hbm_whole()],
        out_specs=[hbm_whole()] * 5 + [vmem_whole()] * 2,
        out_shape=saved + [shape(rows, HALF, BF16)] * 2,
        scratch_shapes=mlp_scratch()[:1]
        + [pltpu.VMEM(out.shape, out.dtype) for out in saved]
        + mlp_scratch()[1:]
        + [pltpu.SemaphoreType.DMA((5,))],
        compiler_params=pltpu.CompilerParams(vmem_limit_bytes=VMEM_LIMIT),
        cost_estimate=pl.CostEstimate(
            flops=2 * rows * WIDTH * MLP_COLS, bytes_accessed=15_000_000, transcendentals=0
        ),
        name="mlp_forward",
    )(core, x, *sums, in_hbm(weights))


def mlp_backward_body(core_ref, g_ref, gate_ref, up_ref, arrive, pair_grad_ref, keep_ref, give_ref, w_ref):
    for step, down in enumerate(column_tiles(2 * HIDDEN_COLS)):
        at = slice(HIDDEN_TILE * step, HIDDEN_TILE * (step + 1))
        up_at = slice(HIDDEN_COLS + at.start, HIDDEN_COLS + at.stop)
        arrive()
        hidden_grad = nn_dot(g_ref[...], w_ref[:, down])
        gate_out = gate_ref[:, at]
        sigmoid_gate = sigmoid(gate_out)
        pair_grad_ref[:, at] = (
            hidden_grad
            * up_ref[:, at]
            * (sigmoid_gate * (1.0 + gate_out * (1.0 - sigmoid_gate)))
        ).astype(BF16)
        pair_grad_ref[:, up_at] = (hidden_grad * (gate_out * sigmoid_gate)).astype(BF16)
    pair = pl.ds(0, 2 * HIDDEN_COLS)
    for half, out_ref in zip(row_halves(core_ref), (give_ref, keep_ref)):
        arrive()
        out_ref[...] = nt_dot(pair_grad_ref[...], w_ref[half, pair]).astype(BF16)


def mlp_backward_copies(core_ref, w_any, w_ref, sems):
    regions = [(pl.ds(0, WIDTH), columns) for columns in column_tiles(2 * HIDDEN_COLS)]
    regions += [(rows, pl.ds(0, 2 * HIDDEN_COLS)) for rows in row_halves(core_ref)]
    return arrivals(weight_copies(w_any, w_ref, sems, regions))


def mlp_backward_kernel(core_ref, g_ref, gate_ref, up_ref, w_any, pair_grad_ref, keep_ref, give_ref, w_ref, sems):
    arrive = mlp_backward_copies(core_ref, w_any, w_ref, sems)
    mlp_backward_body(
        core_ref, g_ref, gate_ref, up_ref, arrive, pair_grad_ref, keep_ref, give_ref, w_ref
    )


def mlp_backward_next_kernel(core_ref, x_ref, middle_grad_ref, own_ref, other_ref, gate_ref, up_ref, w_any, g_ref, pair_grad_ref, keep_ref, give_ref, w_ref, sems, weighted):
    arrive = mlp_backward_copies(core_ref, w_any, w_ref, sems)
    for which, part in ((0, own_ref), (1, other_ref)):
        weighted[:, half_of(core_ref, which)] = part[...].astype(F32)
    rows = x_ref[...].astype(F32)
    g_ref[...] = (
        middle_grad_ref[...] + norm_back(weighted[...], rows, inverse_norm(rows))
    ).astype(BF16)
    mlp_backward_body(
        core_ref, g_ref, gate_ref, up_ref, arrive, pair_grad_ref, keep_ref, give_ref, w_ref
    )


def mlp_backward(core, g, above, gate_out, up_out, weights):
    rows = gate_out.shape[0]
    out_shape = [
        shape(rows, 2 * HIDDEN_COLS, BF16),
        shape(rows, HALF, BF16),
        shape(rows, HALF, BF16),
    ]
    scratch = mlp_scratch()
    if above is None:
        lead, kernel = (g,), mlp_backward_kernel
    else:
        lead, kernel = above, mlp_backward_next_kernel
        out_shape = [shape(rows, WIDTH, BF16)] + out_shape
        scratch = scratch + [pltpu.VMEM((rows, WIDTH), F32)]
    results = pl.pallas_call(
        kernel,
        in_specs=[smem_whole()] + [vmem_whole()] * (len(lead) + 2) + [hbm_whole()],
        out_specs=[vmem_whole()] * len(out_shape),
        out_shape=out_shape,
        scratch_shapes=scratch,
        compiler_params=pltpu.CompilerParams(vmem_limit_bytes=VMEM_LIMIT),
        cost_estimate=pl.CostEstimate(
            flops=2 * rows * WIDTH * MLP_COLS, bytes_accessed=15_000_000, transcendentals=0
        ),
        name="mlp_backward",
    )(core, *lead, gate_out, up_out, in_hbm(weights))
    return ([g] if above is None else []) + list(results)


def attention_backward_kernel(sequences, column, core_ref, g_ref, middle_ref, own_ref, other_ref, qkv_ref, prob_ref, w_any, middle_grad_ref, attn_in_ref, qkv_grad_ref, keep_ref, give_ref, mix_grad, w_ref, sem):
    copy = attention_weights_copy(w_any, w_ref, sem, column)
    copy.start()
    for which, part in ((0, own_ref), (1, other_ref)):
        middle_grad_ref[:, half_of(core_ref, which)] = part[...].astype(F32)
    middle = middle_ref[...]
    middle_grad = g_ref[...].astype(F32) + norm_back(
        middle_grad_ref[...], middle, inverse_norm(middle)
    )
    middle_grad_ref[...] = middle_grad
    attn_in_ref[...] = middle_grad.astype(BF16)
    copy.wait()
    mix_grad[...] = nn_dot(attn_in_ref[...], w_ref[:, QKV_COLS:]).astype(BF16)
    for sequence in range(sequences):
        rows = slice(128 * sequence, 128 * (sequence + 1))
        for group in range(2):
            at = 2 * HEAD_WIDTH * group
            key_at = QUERY_COLS + HEAD_WIDTH * group
            value_at = key_at + KV_COLS
            grads = two_heads(mix_grad, rows, at)
            queries = two_heads(qkv_ref, rows, at)
            keys = qkv_ref[rows, key_at : key_at + HEAD_WIDTH]
            probability = prob_ref[2 * sequence + group]
            prob_grad = nt_dot(grads, qkv_ref[rows, value_at : value_at + HEAD_WIDTH])
            centred = jnp.sum(probability * prob_grad, axis=-1, keepdims=True)
            score_grad = (probability * (prob_grad - centred)).astype(BF16)
            query_grad = (nn_dot(score_grad, keys) * SCORE_SCALE).astype(BF16)
            qkv_grad_ref[rows, at : at + HEAD_WIDTH] = query_grad[:128]
            qkv_grad_ref[rows, at + HEAD_WIDTH : at + 2 * HEAD_WIDTH] = query_grad[128:]
            qkv_grad_ref[rows, key_at : key_at + HEAD_WIDTH] = (
                tn_dot(score_grad, queries) * SCORE_SCALE
            ).astype(BF16)
            qkv_grad_ref[rows, value_at : value_at + HEAD_WIDTH] = tn_dot(
                probability.astype(BF16), grads
            ).astype(BF16)
    qkv_grad = qkv_grad_ref[...]
    give_ref[...] = nt_dot(qkv_grad, w_ref[half_of(core_ref, 1), :QKV_COLS]).astype(BF16)
    keep_ref[...] = nt_dot(qkv_grad, w_ref[half_of(core_ref, 0), :QKV_COLS]).astype(BF16)


def attention_backward(core, g, middle, sums, qkv, probability, weights, column):
    rows = g.shape[0]
    return pl.pallas_call(
        functools.partial(attention_backward_kernel, rows // 128, column),
        in_specs=[smem_whole()] + [vmem_whole()] * 6 + [hbm_whole()],
        out_specs=[vmem_whole()] * 5,
        out_shape=[
            shape(rows, WIDTH, F32),
            shape(rows, WIDTH, BF16),
            shape(rows, QKV_COLS, BF16),
            shape(rows, HALF, BF16),
            shape(rows, HALF, BF16),
        ],
        scratch_shapes=[pltpu.VMEM((rows, OUT_COLS), BF16)] + attention_scratch(),
        compiler_params=pltpu.CompilerParams(vmem_limit_bytes=VMEM_LIMIT),
        cost_estimate=pl.CostEstimate(
            flops=2 * rows * WIDTH * ATTN_COLS, bytes_accessed=12_000_000, transcendentals=0
        ),
        name="attention_backward",
    )(core, g, middle, *sums, qkv, probability, in_hbm(weights))


def write_products(start, products, out_any, slots, sems):
    copies = []
    for number, (left, right, columns) in enumerate(products):
        width = columns.stop - columns.start
        if number >= 2:
            copies[number - 2].wait()
        slot = slots.at[number % 2]
        slot[...] = tn_dot(left[...], right[:, columns]).astype(BF16)
        target = out_any.at[:, pl.ds(start, width)]
        copies.append(pltpu.make_async_copy(slot, target, sems.at[number % 2]))
        copies[-1].start()
        start += width
    for copy in copies[-2:]:
        copy.wait()


def strips(columns, width):
    return [slice(at, at + width) for at in range(0, columns, width)]


def mlp_weights_kernel(second_ref, g_ref, pair_grad_ref, hidden_ref, *rest):
    out_any, slots, sems = rest[-3:]
    products = [(second_ref, pair_grad_ref, at) for at in strips(2 * HIDDEN_COLS, MLP_STRIP)]
    products += [(g_ref, hidden_ref, at) for at in strips(HIDDEN_COLS, MLP_STRIP)]
    write_products(0, products, out_any, slots, sems)


def into_buffer(kernel, buffer, columns, strip, operands, flops, name):
    aliases, specs = {}, [vmem_whole()] * len(operands)
    if buffer is not None:
        aliases = {len(operands): 0}
        specs, operands = specs + [hbm_whole()], operands + (in_hbm(buffer),)
    return pl.pallas_call(
        kernel,
        in_specs=specs,
        out_specs=hbm_whole(),
        out_shape=pltpu.HBM((WIDTH, columns), BF16),
        input_output_aliases=aliases,
        scratch_shapes=[pltpu.VMEM((2, WIDTH, strip), BF16), pltpu.SemaphoreType.DMA((2,))],
        compiler_params=pltpu.CompilerParams(vmem_limit_bytes=VMEM_LIMIT),
        cost_estimate=pl.CostEstimate(flops=flops, bytes_accessed=flops // 250, transcendentals=0),
        name=name,
    )(*operands)


def mlp_weights(buffer, columns, second, g, pair_grad, hidden):
    return into_buffer(
        mlp_weights_kernel,
        buffer,
        columns,
        MLP_STRIP,
        (second, g, pair_grad, hidden),
        2 * second.shape[0] * WIDTH * MLP_COLS,
        "mlp_weights",
    )


def attention_weights_kernel(start, first_ref, attn_in_ref, qkv_grad_ref, mix_ref, *rest):
    out_any, slots, sems = rest[-3:]
    products = [(first_ref, qkv_grad_ref, at) for at in strips(QKV_COLS, OUT_COLS)]
    products += [(attn_in_ref, mix_ref, slice(0, OUT_COLS))]
    write_products(start, products, out_any, slots, sems)


def attention_weights(buffer, columns, start, first, attn_in, qkv_grad, mixture):
    return into_buffer(
        functools.partial(attention_weights_kernel, start),
        buffer,
        columns,
        OUT_COLS,
        (first, attn_in, qkv_grad, mixture),
        2 * first.shape[0] * WIDTH * ATTN_COLS,
        "attention_weights",
    )


def sum_four(keep, give, beside=None):
    chip = (keep.astype(F32) + swap(give, "section").astype(F32)).astype(BF16)
    arrived = swap(chip, "tensor")
    if beside is not None:
        arrived, beside = lax.optimization_barrier((arrived, beside))
    total = (chip.astype(F32) + arrived.astype(F32)).astype(BF16)
    sums = total, swap(total, "section")
    return sums if beside is None else (sums, beside)


def halves(value):
    middle = value.shape[1] // 2
    return value[:, :middle], value[:, middle:]


def to_layers(core, low, high):
    mine, give = pick(core, low, high), pick(core, high, low)
    got = swap(give, "section")
    return pick(core, mine, got), pick(core, got, mine)


def from_layers(core, layer_zero, layer_one):
    mine, give = pick(core, layer_zero, layer_one), pick(core, layer_one, layer_zero)
    got = swap(give, "section")
    return pick(core, mine, got), pick(core, got, mine)


def gather_rows(z_low, share):
    other = swap(share, "zl")
    pair = jnp.concatenate([pick(z_low, share, other), pick(z_low, other, share)], axis=0)
    return lax.all_gather(pair, ("y", "x"), axis=0, tiled=True)


def scatter_rows(z_low, grad, beside=()):
    pair = lax.psum_scatter(grad, ("y", "x"), scatter_dimension=0, tiled=True)
    pair, _ = lax.optimization_barrier((pair, beside))
    keep = pick(z_low, pair[:48], pair[48:])
    give = pick(z_low, pair[48:], pair[:48])
    return (keep.astype(F32) + swap(give, "zl").astype(F32)).astype(BF16)


def to_ring_order(rows):
    lead = rows.shape[:-1]
    return jnp.swapaxes(rows.reshape(lead + (4, 2, 4, 48)), -3, -2).reshape(rows.shape)


def from_ring_order(rows):
    lead = rows.shape[:-1]
    return jnp.swapaxes(rows.reshape(lead + (4, 4, 2, 48)), -3, -2).reshape(rows.shape)


def join_positions(tensor, own):
    other = swap(own, "tensor")
    return jnp.concatenate(
        [pick(tensor, own, other), pick(tensor, other, own)], axis=1
    ).reshape(384, WIDTH)


def own_positions(tensor, rows):
    rows = rows.reshape(3, 128, 1536)
    return pick(tensor, rows[:, :64], rows[:, 64:])


def per_device(
    inputs, cotangent, plan, attn_gain, mlp_gain, w_query, key_weight, value_weight,
    w_out, w_gate, w_up, w_down,
):
    core = lax.axis_index("section")
    z_low = lax.axis_index("zl")
    tensor = lax.axis_index("tensor")

    attn_scale = attn_gain[0].astype(F32)[:, None]
    mlp_scale = mlp_gain[0].astype(F32)[:, None]

    def scaled(weight, scale):
        return (weight.astype(F32) * scale).astype(BF16)

    attn_shards = (w_query[0], key_weight[0], value_weight[0])
    mlp_shards = (w_gate[0], w_up[0])
    attn_pairs = [halves(scaled(weight, attn_scale)) for weight in attn_shards]
    attn_pairs.append(halves(w_out[0].T))
    mlp_pairs = [halves(scaled(weight, mlp_scale)) for weight in mlp_shards]
    mlp_pairs.append(halves(w_down[0].T))
    low, high = (jnp.concatenate(side, axis=1) for side in zip(*mlp_pairs, *attn_pairs))
    layer_zero, layer_one = to_layers(core, low, high)
    first_weights = gather_rows(
        z_low, jnp.concatenate([layer_zero, layer_one[:, MLP_COLS:]], axis=1)
    )
    last_weights = gather_rows(z_low, layer_one[:, :MLP_COLS])
    attn_weights = ((first_weights, MLP_COLS), (first_weights, LAYER_COLS))
    mlp_weights_of = (first_weights, last_weights)

    core_ref = core.astype(jnp.int32).reshape(1)
    stream = join_positions(tensor, to_ring_order(inputs[:, 0][plan]))
    stream, late = lax.optimization_barrier((stream, cotangent))
    out_grad = join_positions(tensor, to_ring_order(late[:, 0][plan]))
    stream, out_grad = lax.optimization_barrier((stream, out_grad))

    kept, outputs = [], []
    x, middle, sums = stream, None, None
    for layer in range(2):
        x, first, qkv, probability, mixture, keep, give = attention_forward(
            core_ref, x, middle, sums, *attn_weights[layer]
        )
        if layer == 1:
            outputs.append(own_positions(tensor, x))
        middle, second, gate_out, up_out, hidden, keep, give = mlp_forward(
            core_ref, x, sum_four(keep, give), mlp_weights_of[layer]
        )
        sums = sum_four(keep, give)
        kept.append((x, first, qkv, probability, mixture, middle, second, gate_out, up_out, hidden))
    last = middle + jnp.concatenate(
        [pick(core, sums[0], sums[1]), pick(core, sums[1], sums[0])], axis=1
    ).astype(F32)
    outputs.append(own_positions(tensor, last.astype(BF16)))

    grads = [None] * 2
    buffer = None
    above = None
    for layer in (1, 0):
        x, first, qkv, probability, mixture, middle, second, gate_out, up_out, hidden = kept[layer]
        out_grad, pair_grad, keep, give = mlp_backward(
            core_ref, out_grad, above, gate_out, up_out, mlp_weights_of[layer]
        )
        if layer == 0:
            grads[1] = own_positions(tensor, out_grad)
        beside = mlp_weights(
            buffer, MLP_COLS if layer == 1 else REST_COLS,
            second, out_grad, pair_grad, hidden,
        )
        sums, beside = sum_four(keep, give, beside)
        if layer == 1:
            last_grad = scatter_rows(z_low, beside)
        else:
            buffer = beside
        middle_grad, attn_in, qkv_grad, keep, give = attention_backward(
            core_ref, out_grad, middle, sums, qkv, probability, *attn_weights[layer]
        )
        buffer = attention_weights(
            buffer, REST_COLS, MLP_COLS if layer == 1 else LAYER_COLS,
            first, attn_in, qkv_grad, mixture,
        )
        sums, buffer = sum_four(keep, give, buffer)
        above = (x, middle_grad, *sums)
    x, middle_grad, own, other = above
    rows = x.astype(F32)
    weighted = jnp.concatenate(
        [pick(core, own, other), pick(core, other, own)], axis=1
    ).astype(F32)
    last = middle_grad + norm_back(weighted, rows, inverse_norm(rows))
    grads[0] = own_positions(tensor, last.astype(BF16))

    layer_outputs = from_ring_order(pick(core, outputs[0], outputs[1]))
    input_grads = from_ring_order(pick(core, grads[0], grads[1]))
    rest_grad = scatter_rows(z_low, buffer, (layer_outputs, input_grads))
    zero_grad = jnp.concatenate([rest_grad[:, :MLP_COLS], rest_grad[:, LAYER_COLS:]], axis=1)
    one_grad = jnp.concatenate([last_grad, rest_grad[:, MLP_COLS:LAYER_COLS]], axis=1)
    low, high = from_layers(core, zero_grad, one_grad)

    def joined(start, width):
        return jnp.concatenate(
            [low[:, start : start + width], high[:, start : start + width]], axis=1
        ).astype(F32)

    gate_grad = joined(0, HIDDEN_COLS)
    up_grad = joined(HIDDEN_COLS, HIDDEN_COLS)
    down_grad = joined(2 * HIDDEN_COLS, HIDDEN_COLS).T
    query_grad = joined(MLP_COLS, QUERY_COLS)
    key_grad = joined(MLP_COLS + QUERY_COLS, KV_COLS)
    value_grad = joined(MLP_COLS + QUERY_COLS + KV_COLS, KV_COLS)
    out_weight_grad = joined(MLP_COLS + QKV_COLS, OUT_COLS).T

    def gain_terms(weights, grad):
        terms = weights.astype(F32) * grad.astype(F32)
        return jnp.stack(
            [
                jnp.sum(terms[:, MLP_COLS : MLP_COLS + QKV_COLS], axis=1),
                jnp.sum(terms[:, : 2 * HIDDEN_COLS], axis=1),
            ]
        )

    terms = jnp.stack([gain_terms(layer_zero, zero_grad), gain_terms(layer_one, one_grad)])
    terms = terms + swap(terms, "tensor")
    terms = pick(core, terms[0], terms[1]) + swap(pick(core, terms[1], terms[0]), "section")
    return (
        layer_outputs[None, :, None],
        input_grads[None, :, None],
        (terms[0] / attn_scale[:, 0])[None],
        (terms[1] / mlp_scale[:, 0])[None],
        (query_grad * attn_scale)[None],
        (key_grad * attn_scale)[None],
        (value_grad * attn_scale)[None],
        out_weight_grad[None],
        (gate_grad * mlp_scale)[None],
        (up_grad * mlp_scale)[None],
        down_grad[None],
    )


def solution(mesh):
    split = Mesh(mesh.devices.reshape(2, 4, 2, 4, 2), ("section", "y", "zl", "x", "tensor"))
    dp = ("y", "zl", "x")
    rows = P("section", dp, "tensor")
    columns = P("section", "tensor", dp)
    return jax.shard_map(
        per_device,
        mesh=split,
        in_specs=(
            P(None, dp, "tensor", None),
            P(None, dp, "tensor", None),
            P(),
            P("section", dp),
            P("section", dp),
            rows,
            rows,
            rows,
            columns,
            rows,
            rows,
            columns,
        ),
        out_specs=(
            P("section", None, dp, "tensor", None),
            P("section", None, dp, "tensor", None),
            P("section", dp),
            P("section", dp),
            rows,
            rows,
            rows,
            columns,
            rows,
            rows,
            columns,
        ),
        check_vma=False,
    )
```

```python
import functools

import jax
import jax.numpy as jnp
from jax import lax
from jax.experimental import pallas as pl
from jax.experimental.pallas import tpu as pltpu
from jax.sharding import Mesh, PartitionSpec as P

HEAD_WIDTH = 96
EPSILON = 1e-05
BLOCKED = -1e30
SCORE_SCALE = HEAD_WIDTH ** (-0.5)
BF16 = jnp.bfloat16
F32 = jnp.float32

QUERY_COLS, KV_COLS = 384, 192
QKV_COLS = QUERY_COLS + 2 * KV_COLS
OUT_COLS = 384
HIDDEN_COLS = 1024
ATTN_COLS = QKV_COLS + OUT_COLS
MLP_COLS = 3 * HIDDEN_COLS
LAYER_COLS = MLP_COLS + ATTN_COLS
REST_COLS = LAYER_COLS + ATTN_COLS
HIDDEN_TILE = 512
MLP_STRIP = 512
AHEAD = 3
WIDTH = 1536
HALF = WIDTH // 2
VMEM_LIMIT = 30 * 1024 * 1024


def swap(value, axis):
    return lax.ppermute(value, axis, [(0, 1), (1, 0)])


def pick(index, first, second):
    return jnp.where(index == 0, first, second)


def norm_back(weighted, residual, inverse):
    scaled = residual * inverse
    return inverse * (weighted - scaled * jnp.mean(weighted * scaled, axis=-1, keepdims=True))


def vmem_whole():
    return pl.BlockSpec(memory_space=pltpu.VMEM)


def smem_whole():
    return pl.BlockSpec(memory_space=pltpu.SMEM)


def shape(rows, columns, dtype):
    return jax.ShapeDtypeStruct((rows, columns), dtype)


def half_of(core_ref, which):
    position = core_ref[0] if which == 0 else 1 - core_ref[0]
    return pl.ds(pl.multiple_of(position * HALF, HALF), HALF)


def nt_dot(left_side, right_side):
    return lax.dot_general(
        left_side, right_side, (((1,), (1,)), ((), ())), preferred_element_type=F32
    )


def tn_dot(left_side, right_side):
    return lax.dot_general(
        left_side, right_side, (((0,), (0,)), ((), ())), preferred_element_type=F32
    )


def nn_dot(left_side, right_side):
    return jnp.dot(left_side, right_side, preferred_element_type=F32)


def inverse_norm(rows):
    return lax.rsqrt(jnp.mean(rows * rows, axis=-1, keepdims=True) + EPSILON)


def causal_mask():
    row = lax.broadcasted_iota(jnp.int32, (128, 128), 0)
    return row >= lax.broadcasted_iota(jnp.int32, (128, 128), 1)


def two_heads(ref, rows, start):
    return jnp.concatenate(
        [
            ref[rows, start : start + HEAD_WIDTH],
            ref[rows, start + HEAD_WIDTH : start + 2 * HEAD_WIDTH],
        ],
        axis=0,
    )


def attention_weights_copy(w_any, w_ref, sem, column):
    return pltpu.make_async_copy(w_any.at[:, pl.ds(column, ATTN_COLS)], w_ref, sem)


def attention_forward_body(sequences, core_ref, first_ref, w_ref, qkv_ref, prob_ref, mix_ref, keep_ref, give_ref):
    qkv_ref[...] = nn_dot(first_ref[...], w_ref[:, :QKV_COLS]).astype(BF16)
    mask = causal_mask()
    mask = jnp.concatenate([mask, mask], axis=0)
    for sequence in range(sequences):
        rows = slice(128 * sequence, 128 * (sequence + 1))
        for group in range(2):
            queries = two_heads(qkv_ref, rows, 2 * HEAD_WIDTH * group)
            key_at = QUERY_COLS + HEAD_WIDTH * group
            value_at = key_at + KV_COLS
            scores = nt_dot(queries, qkv_ref[rows, key_at : key_at + HEAD_WIDTH]) * SCORE_SCALE
            scores = jnp.where(mask, scores, BLOCKED)
            expanded = jnp.exp(scores - jnp.max(scores, axis=-1, keepdims=True))
            probability = expanded / jnp.sum(expanded, axis=-1, keepdims=True)
            prob_ref[2 * sequence + group] = probability
            mixed = nn_dot(
                probability.astype(BF16), qkv_ref[rows, value_at : value_at + HEAD_WIDTH]
            ).astype(BF16)
            at = 2 * HEAD_WIDTH * group
            mix_ref[rows, at : at + HEAD_WIDTH] = mixed[:128]
            mix_ref[rows, at + HEAD_WIDTH : at + 2 * HEAD_WIDTH] = mixed[128:]
    mixture = mix_ref[...]
    give_ref[...] = nt_dot(mixture, w_ref[half_of(core_ref, 1), QKV_COLS:]).astype(BF16)
    keep_ref[...] = nt_dot(mixture, w_ref[half_of(core_ref, 0), QKV_COLS:]).astype(BF16)


def attention_first_kernel(sequences, column, core_ref, x_ref, w_any, first_ref, *rest):
    outs, w_ref, sem = rest[:-2], rest[-2], rest[-1]
    copy = attention_weights_copy(w_any, w_ref, sem, column)
    copy.start()
    rows = x_ref[...].astype(F32)
    first_ref[...] = (rows * inverse_norm(rows)).astype(BF16)
    copy.wait()
    attention_forward_body(sequences, core_ref, first_ref, w_ref, *outs)


def attention_next_kernel(sequences, column, core_ref, middle_ref, own_ref, other_ref, w_any, x_ref, first_ref, *rest):
    outs, w_ref, sem = rest[:-2], rest[-2], rest[-1]
    copy = attention_weights_copy(w_any, w_ref, sem, column)
    copy.start()
    for which, part in ((0, own_ref), (1, other_ref)):
        at = half_of(core_ref, which)
        x_ref[:, at] = (middle_ref[:, at] + part[...].astype(F32)).astype(BF16)
    rows = x_ref[...].astype(F32)
    first_ref[...] = (rows * inverse_norm(rows)).astype(BF16)
    copy.wait()
    attention_forward_body(sequences, core_ref, first_ref, w_ref, *outs)


def in_hbm(value):
    return pltpu.with_memory_space_constraint(value, pltpu.HBM)


def hbm_whole():
    return pl.BlockSpec(memory_space=pltpu.HBM)


def attention_scratch():
    return [pltpu.VMEM((WIDTH, ATTN_COLS), BF16), pltpu.SemaphoreType.DMA(())]


def attention_forward(core, x, middle, sums, weights, column):
    rows = (x if middle is None else middle).shape[0]
    sequences = rows // 128
    outs = [
        shape(rows, WIDTH, BF16),
        shape(rows, QKV_COLS, BF16),
        jax.ShapeDtypeStruct((2 * sequences, 256, 128), F32),
        shape(rows, OUT_COLS, BF16),
        shape(rows, HALF, BF16),
        shape(rows, HALF, BF16),
    ]
    if middle is None:
        operands, kernel = (core, x), attention_first_kernel
    else:
        operands, kernel = (core, middle, *sums), attention_next_kernel
        outs = [shape(rows, WIDTH, BF16)] + outs
    results = pl.pallas_call(
        functools.partial(kernel, sequences, column),
        in_specs=[smem_whole()] + [vmem_whole()] * (len(operands) - 1) + [hbm_whole()],
        out_specs=[vmem_whole()] * len(outs),
        out_shape=outs,
        scratch_shapes=attention_scratch(),
        compiler_params=pltpu.CompilerParams(vmem_limit_bytes=VMEM_LIMIT),
        cost_estimate=pl.CostEstimate(
            flops=2 * rows * WIDTH * ATTN_COLS, bytes_accessed=8_000_000, transcendentals=0
        ),
        name="attention_forward",
    )(*operands, in_hbm(weights))
    return ([x] if middle is None else []) + list(results)


def column_tiles(first):
    return [pl.ds(first + HIDDEN_TILE * step, HIDDEN_TILE) for step in range(HIDDEN_STEPS)]


def row_halves(core_ref):
    return [half_of(core_ref, 1), half_of(core_ref, 0)]


def weight_copies(w_any, w_ref, sems, regions):
    return [
        pltpu.make_async_copy(w_any.at[rows, columns], w_ref.at[rows, columns], sems.at[number])
        for number, (rows, columns) in enumerate(regions)
    ]


def sigmoid(values):
    return 0.5 * jnp.tanh(0.5 * values) + 0.5


def arrivals(copies):
    for copy in copies[:AHEAD]:
        copy.start()
    place = iter(range(len(copies)))

    def arrive():
        number = next(place)
        copies[number].wait()
        if number + AHEAD < len(copies):
            copies[number + AHEAD].start()

    return arrive


def mlp_forward_kernel(core_ref, x_ref, own_ref, other_ref, w_any, middle_any, second_any, gate_any, up_any, hidden_any, keep_ref, give_ref, w_ref, middle_ref, second_ref, gate_ref, up_ref, hidden_ref, sems, out_sems):
    whole = pl.ds(0, WIDTH)
    tiles = [(gate, up) for gate, up in zip(column_tiles(0), column_tiles(HIDDEN_COLS))]
    down = pl.ds(2 * HIDDEN_COLS, HIDDEN_COLS)
    regions = [(whole, columns) for pair in tiles for columns in pair]
    regions += [(rows, down) for rows in row_halves(core_ref)]
    arrive = arrivals(weight_copies(w_any, w_ref, sems, regions))
    for which, part in ((0, own_ref), (1, other_ref)):
        at = half_of(core_ref, which)
        middle_ref[:, at] = x_ref[:, at].astype(F32) + part[...].astype(F32)
    rows = middle_ref[...]
    second_ref[...] = (rows * inverse_norm(rows)).astype(BF16)
    outward = []

    def send(source, target):
        outward.append(pltpu.make_async_copy(source, target, out_sems.at[len(outward)]))
        outward[-1].start()

    send(middle_ref, middle_any)
    send(second_ref, second_any)
    for step, (gate, up) in enumerate(tiles):
        at = slice(HIDDEN_TILE * step, HIDDEN_TILE * (step + 1))
        arrive()
        gate_out = nn_dot(second_ref[...], w_ref[:, gate])
        arrive()
        up_out = nn_dot(second_ref[...], w_ref[:, up])
        gate_ref[:, at] = gate_out
        up_ref[:, at] = up_out
        hidden_ref[:, at] = (gate_out * sigmoid(gate_out) * up_out).astype(BF16)
    send(gate_ref, gate_any)
    send(up_ref, up_any)
    send(hidden_ref, hidden_any)
    for half, out_ref in zip(row_halves(core_ref), (give_ref, keep_ref)):
        arrive()
        out_ref[...] = nt_dot(hidden_ref[...], w_ref[half, down]).astype(BF16)
    for copy in outward:
        copy.wait()


HIDDEN_STEPS = HIDDEN_COLS // HIDDEN_TILE


def mlp_scratch():
    return [pltpu.VMEM((WIDTH, MLP_COLS), BF16), pltpu.SemaphoreType.DMA((2 * HIDDEN_STEPS + 2,))]


def mlp_forward(core, x, sums, weights):
    rows = x.shape[0]
    saved = [
        shape(rows, WIDTH, F32),
        shape(rows, WIDTH, BF16),
        shape(rows, HIDDEN_COLS, F32),
        shape(rows, HIDDEN_COLS, F32),
        shape(rows, HIDDEN_COLS, BF16),
    ]
    return pl.pallas_call(
        mlp_forward_kernel,
        in_specs=[smem_whole()] + [vmem_whole()] * 3 + [hbm_whole()],
        out_specs=[hbm_whole()] * 5 + [vmem_whole()] * 2,
        out_shape=saved + [shape(rows, HALF, BF16)] * 2,
        scratch_shapes=mlp_scratch()[:1]
        + [pltpu.VMEM(out.shape, out.dtype) for out in saved]
        + mlp_scratch()[1:]
        + [pltpu.SemaphoreType.DMA((5,))],
        compiler_params=pltpu.CompilerParams(vmem_limit_bytes=VMEM_LIMIT),
        cost_estimate=pl.CostEstimate(
            flops=2 * rows * WIDTH * MLP_COLS, bytes_accessed=15_000_000, transcendentals=0
        ),
        name="mlp_forward",
    )(core, x, *sums, in_hbm(weights))


def mlp_backward_tiles(g_ref, gate_ref, up_ref, arrive, pair_grad_ref, w_ref):
    for step, down in enumerate(column_tiles(2 * HIDDEN_COLS)):
        at = slice(HIDDEN_TILE * step, HIDDEN_TILE * (step + 1))
        up_at = slice(HIDDEN_COLS + at.start, HIDDEN_COLS + at.stop)
        arrive()
        hidden_grad = nn_dot(g_ref[...], w_ref[:, down])
        gate_out = gate_ref[:, at]
        sigmoid_gate = sigmoid(gate_out)
        pair_grad_ref[:, at] = (
            hidden_grad
            * up_ref[:, at]
            * (sigmoid_gate * (1.0 + gate_out * (1.0 - sigmoid_gate)))
        ).astype(BF16)
        pair_grad_ref[:, up_at] = (hidden_grad * (gate_out * sigmoid_gate)).astype(BF16)


def mlp_backward_body(core_ref, g_ref, gate_ref, up_ref, arrive, pair_grad_ref, keep_ref, give_ref, w_ref):
    mlp_backward_tiles(g_ref, gate_ref, up_ref, arrive, pair_grad_ref, w_ref)
    pair = pl.ds(0, 2 * HIDDEN_COLS)
    for half, out_ref in zip(row_halves(core_ref), (give_ref, keep_ref)):
        arrive()
        out_ref[...] = nt_dot(pair_grad_ref[...], w_ref[half, pair]).astype(BF16)


def mlp_backward_copies(core_ref, w_any, w_ref, sems):
    regions = [(pl.ds(0, WIDTH), columns) for columns in column_tiles(2 * HIDDEN_COLS)]
    regions += [(rows, pl.ds(0, 2 * HIDDEN_COLS)) for rows in row_halves(core_ref)]
    return arrivals(weight_copies(w_any, w_ref, sems, regions))


def mlp_backward_kernel(core_ref, x_ref, middle_grad_ref, own_ref, other_ref, gate_ref, up_ref, w_any, g_ref, pair_grad_ref, keep_ref, give_ref, w_ref, sems, weighted):
    arrive = mlp_backward_copies(core_ref, w_any, w_ref, sems)
    for which, part in ((0, own_ref), (1, other_ref)):
        weighted[:, half_of(core_ref, which)] = part[...].astype(F32)
    rows = x_ref[...].astype(F32)
    g_ref[...] = (
        middle_grad_ref[...] + norm_back(weighted[...], rows, inverse_norm(rows))
    ).astype(BF16)
    mlp_backward_body(
        core_ref, g_ref, gate_ref, up_ref, arrive, pair_grad_ref, keep_ref, give_ref, w_ref
    )


def mlp_backward(core, above, gate_out, up_out, weights):
    rows = gate_out.shape[0]
    return pl.pallas_call(
        mlp_backward_kernel,
        in_specs=[smem_whole()] + [vmem_whole()] * 6 + [hbm_whole()],
        out_specs=[vmem_whole()] * 4,
        out_shape=[
            shape(rows, WIDTH, BF16),
            shape(rows, 2 * HIDDEN_COLS, BF16),
            shape(rows, HALF, BF16),
            shape(rows, HALF, BF16),
        ],
        scratch_shapes=mlp_scratch() + [pltpu.VMEM((rows, WIDTH), F32)],
        compiler_params=pltpu.CompilerParams(vmem_limit_bytes=VMEM_LIMIT),
        cost_estimate=pl.CostEstimate(
            flops=2 * rows * WIDTH * MLP_COLS, bytes_accessed=15_000_000, transcendentals=0
        ),
        name="mlp_backward",
    )(core, *above, gate_out, up_out, in_hbm(weights))


def mlp_last_kernel(core_ref, x_ref, own_ref, other_ref, g_ref, w_any, middle_any, second_any, hidden_any, pair_grad_ref, keep_ref, give_ref, w_ref, middle_ref, second_ref, gate_ref, up_ref, hidden_ref, sems, out_sems):
    whole = pl.ds(0, WIDTH)
    tiles = [(gate, up) for gate, up in zip(column_tiles(0), column_tiles(HIDDEN_COLS))]
    regions = [(whole, columns) for pair in tiles for columns in pair]
    regions += [(whole, columns) for columns in column_tiles(2 * HIDDEN_COLS)]
    arrive = arrivals(weight_copies(w_any, w_ref, sems, regions))
    for which, part in ((0, own_ref), (1, other_ref)):
        at = half_of(core_ref, which)
        middle_ref[:, at] = x_ref[:, at].astype(F32) + part[...].astype(F32)
    rows = middle_ref[...]
    second_ref[...] = (rows * inverse_norm(rows)).astype(BF16)
    outward = []

    def send(source, target):
        outward.append(pltpu.make_async_copy(source, target, out_sems.at[len(outward)]))
        outward[-1].start()

    send(middle_ref, middle_any)
    send(second_ref, second_any)
    for step, (gate, up) in enumerate(tiles):
        at = slice(HIDDEN_TILE * step, HIDDEN_TILE * (step + 1))
        arrive()
        gate_out = nn_dot(second_ref[...], w_ref[:, gate])
        arrive()
        up_out = nn_dot(second_ref[...], w_ref[:, up])
        gate_ref[:, at] = gate_out
        up_ref[:, at] = up_out
        hidden_ref[:, at] = (gate_out * sigmoid(gate_out) * up_out).astype(BF16)
    send(hidden_ref, hidden_any)
    mlp_backward_tiles(g_ref, gate_ref, up_ref, arrive, pair_grad_ref, w_ref)
    pair = pl.ds(0, 2 * HIDDEN_COLS)
    for half, out_ref in zip(row_halves(core_ref), (give_ref, keep_ref)):
        out_ref[...] = nt_dot(pair_grad_ref[...], w_ref[half, pair]).astype(BF16)
    for copy in outward:
        copy.wait()


def mlp_last(core, x, sums, g, weights):
    rows = x.shape[0]
    saved = [
        shape(rows, WIDTH, F32),
        shape(rows, WIDTH, BF16),
        shape(rows, HIDDEN_COLS, BF16),
    ]
    inner = saved[:2] + [shape(rows, HIDDEN_COLS, F32)] * 2 + saved[2:]
    return pl.pallas_call(
        mlp_last_kernel,
        in_specs=[smem_whole()] + [vmem_whole()] * 4 + [hbm_whole()],
        out_specs=[hbm_whole()] * 3 + [vmem_whole()] * 3,
        out_shape=saved + [shape(rows, 2 * HIDDEN_COLS, BF16)] + [shape(rows, HALF, BF16)] * 2,
        scratch_shapes=mlp_scratch()[:1]
        + [pltpu.VMEM(array.shape, array.dtype) for array in inner]
        + [pltpu.SemaphoreType.DMA((3 * HIDDEN_STEPS,)), pltpu.SemaphoreType.DMA((3,))],
        compiler_params=pltpu.CompilerParams(vmem_limit_bytes=VMEM_LIMIT),
        cost_estimate=pl.CostEstimate(
            flops=4 * rows * WIDTH * MLP_COLS, bytes_accessed=15_000_000, transcendentals=0
        ),
        name="mlp_last",
    )(core, x, *sums, g, in_hbm(weights))


def mlp_down_kernel(core_ref, hidden_ref, w_any, keep_ref, give_ref, w_ref, sem):
    copy = pltpu.make_async_copy(w_any.at[:, pl.ds(2 * HIDDEN_COLS, HIDDEN_COLS)], w_ref, sem)
    copy.start()
    copy.wait()
    for half, out_ref in zip(row_halves(core_ref), (give_ref, keep_ref)):
        out_ref[...] = nt_dot(hidden_ref[...], w_ref[half, :]).astype(BF16)


def mlp_down(core, hidden, weights):
    rows = hidden.shape[0]
    return pl.pallas_call(
        mlp_down_kernel,
        in_specs=[smem_whole(), vmem_whole(), hbm_whole()],
        out_specs=[vmem_whole()] * 2,
        out_shape=[shape(rows, HALF, BF16)] * 2,
        scratch_shapes=[pltpu.VMEM((WIDTH, HIDDEN_COLS), BF16), pltpu.SemaphoreType.DMA(())],
        compiler_params=pltpu.CompilerParams(vmem_limit_bytes=VMEM_LIMIT),
        cost_estimate=pl.CostEstimate(
            flops=2 * rows * WIDTH * HIDDEN_COLS, bytes_accessed=5_000_000, transcendentals=0
        ),
        name="mlp_down",
    )(core, hidden, in_hbm(weights))


def attention_backward_kernel(sequences, column, core_ref, g_ref, middle_ref, own_ref, other_ref, qkv_ref, prob_ref, w_any, middle_grad_ref, attn_in_ref, qkv_grad_ref, keep_ref, give_ref, mix_grad, w_ref, sem):
    copy = attention_weights_copy(w_any, w_ref, sem, column)
    copy.start()
    for which, part in ((0, own_ref), (1, other_ref)):
        middle_grad_ref[:, half_of(core_ref, which)] = part[...].astype(F32)
    middle = middle_ref[...]
    middle_grad = g_ref[...].astype(F32) + norm_back(
        middle_grad_ref[...], middle, inverse_norm(middle)
    )
    middle_grad_ref[...] = middle_grad
    attn_in_ref[...] = middle_grad.astype(BF16)
    copy.wait()
    mix_grad[...] = nn_dot(attn_in_ref[...], w_ref[:, QKV_COLS:]).astype(BF16)
    for sequence in range(sequences):
        rows = slice(128 * sequence, 128 * (sequence + 1))
        for group in range(2):
            at = 2 * HEAD_WIDTH * group
            key_at = QUERY_COLS + HEAD_WIDTH * group
            value_at = key_at + KV_COLS
            grads = two_heads(mix_grad, rows, at)
            queries = two_heads(qkv_ref, rows, at)
            keys = qkv_ref[rows, key_at : key_at + HEAD_WIDTH]
            probability = prob_ref[2 * sequence + group]
            prob_grad = nt_dot(grads, qkv_ref[rows, value_at : value_at + HEAD_WIDTH])
            centred = jnp.sum(probability * prob_grad, axis=-1, keepdims=True)
            score_grad = (probability * (prob_grad - centred)).astype(BF16)
            query_grad = (nn_dot(score_grad, keys) * SCORE_SCALE).astype(BF16)
            qkv_grad_ref[rows, at : at + HEAD_WIDTH] = query_grad[:128]
            qkv_grad_ref[rows, at + HEAD_WIDTH : at + 2 * HEAD_WIDTH] = query_grad[128:]
            qkv_grad_ref[rows, key_at : key_at + HEAD_WIDTH] = (
                tn_dot(score_grad, queries) * SCORE_SCALE
            ).astype(BF16)
            qkv_grad_ref[rows, value_at : value_at + HEAD_WIDTH] = tn_dot(
                probability.astype(BF16), grads
            ).astype(BF16)
    qkv_grad = qkv_grad_ref[...]
    give_ref[...] = nt_dot(qkv_grad, w_ref[half_of(core_ref, 1), :QKV_COLS]).astype(BF16)
    keep_ref[...] = nt_dot(qkv_grad, w_ref[half_of(core_ref, 0), :QKV_COLS]).astype(BF16)


def attention_backward(core, g, middle, sums, qkv, probability, weights, column):
    rows = g.shape[0]
    return pl.pallas_call(
        functools.partial(attention_backward_kernel, rows // 128, column),
        in_specs=[smem_whole()] + [vmem_whole()] * 6 + [hbm_whole()],
        out_specs=[vmem_whole()] * 5,
        out_shape=[
            shape(rows, WIDTH, F32),
            shape(rows, WIDTH, BF16),
            shape(rows, QKV_COLS, BF16),
            shape(rows, HALF, BF16),
            shape(rows, HALF, BF16),
        ],
        scratch_shapes=[pltpu.VMEM((rows, OUT_COLS), BF16)] + attention_scratch(),
        compiler_params=pltpu.CompilerParams(vmem_limit_bytes=VMEM_LIMIT),
        cost_estimate=pl.CostEstimate(
            flops=2 * rows * WIDTH * ATTN_COLS, bytes_accessed=12_000_000, transcendentals=0
        ),
        name="attention_backward",
    )(core, g, middle, *sums, qkv, probability, in_hbm(weights))


def write_products(start, products, out_any, slots, sems):
    copies = []
    for number, (left, right, columns) in enumerate(products):
        width = columns.stop - columns.start
        if number >= 2:
            copies[number - 2].wait()
        slot = slots.at[number % 2]
        slot[...] = tn_dot(left[...], right[:, columns]).astype(BF16)
        target = out_any.at[:, pl.ds(start, width)]
        copies.append(pltpu.make_async_copy(slot, target, sems.at[number % 2]))
        copies[-1].start()
        start += width
    for copy in copies[-2:]:
        copy.wait()


def strips(columns, width):
    return [slice(at, at + width) for at in range(0, columns, width)]


def mlp_weights_kernel(second_ref, g_ref, pair_grad_ref, hidden_ref, *rest):
    out_any, slots, sems = rest[-3:]
    products = [(second_ref, pair_grad_ref, at) for at in strips(2 * HIDDEN_COLS, MLP_STRIP)]
    products += [(g_ref, hidden_ref, at) for at in strips(HIDDEN_COLS, MLP_STRIP)]
    write_products(0, products, out_any, slots, sems)


def into_buffer(kernel, buffer, columns, strip, operands, flops, name):
    aliases, specs = {}, [vmem_whole()] * len(operands)
    if buffer is not None:
        aliases = {len(operands): 0}
        specs, operands = specs + [hbm_whole()], operands + (in_hbm(buffer),)
    return pl.pallas_call(
        kernel,
        in_specs=specs,
        out_specs=hbm_whole(),
        out_shape=pltpu.HBM((WIDTH, columns), BF16),
        input_output_aliases=aliases,
        scratch_shapes=[pltpu.VMEM((2, WIDTH, strip), BF16), pltpu.SemaphoreType.DMA((2,))],
        compiler_params=pltpu.CompilerParams(vmem_limit_bytes=VMEM_LIMIT),
        cost_estimate=pl.CostEstimate(flops=flops, bytes_accessed=flops // 250, transcendentals=0),
        name=name,
    )(*operands)


def mlp_weights(buffer, columns, second, g, pair_grad, hidden):
    return into_buffer(
        mlp_weights_kernel,
        buffer,
        columns,
        MLP_STRIP,
        (second, g, pair_grad, hidden),
        2 * second.shape[0] * WIDTH * MLP_COLS,
        "mlp_weights",
    )


def attention_weights_kernel(start, first_ref, attn_in_ref, qkv_grad_ref, mix_ref, *rest):
    out_any, slots, sems = rest[-3:]
    products = [(first_ref, qkv_grad_ref, at) for at in strips(QKV_COLS, OUT_COLS)]
    products += [(attn_in_ref, mix_ref, slice(0, OUT_COLS))]
    write_products(start, products, out_any, slots, sems)


def attention_weights(buffer, columns, start, first, attn_in, qkv_grad, mixture):
    return into_buffer(
        functools.partial(attention_weights_kernel, start),
        buffer,
        columns,
        OUT_COLS,
        (first, attn_in, qkv_grad, mixture),
        2 * first.shape[0] * WIDTH * ATTN_COLS,
        "attention_weights",
    )


def sum_four(keep, give, before=None, beside=None):
    chip = (keep.astype(F32) + swap(give, "section").astype(F32)).astype(BF16)
    if before is not None:
        chip, before = lax.optimization_barrier((chip, before))
    arrived = swap(chip, "tensor")
    if beside is not None:
        arrived, beside = lax.optimization_barrier((arrived, beside))
    total = (chip.astype(F32) + arrived.astype(F32)).astype(BF16)
    return (total, swap(total, "section")), before, beside


def pack_kernel(core_ref, attn_scale_ref, mlp_scale_ref, gate_ref, up_ref, down_ref, query_ref, key_ref, value_ref, out_ref, mine_ref, give_ref):
    is_first = core_ref[0] == 0

    def place(start, weight):
        width = weight.shape[1] // 2
        low, high = weight[:, :width], weight[:, width:]
        mine_ref[:, start : start + width] = jnp.where(is_first, low, high)
        give_ref[:, start : start + width] = jnp.where(is_first, high, low)

    def scaled(ref, scale_ref):
        return (ref[...].astype(F32) * scale_ref[...]).astype(BF16)

    place(0, scaled(gate_ref, mlp_scale_ref))
    place(HIDDEN_COLS, scaled(up_ref, mlp_scale_ref))
    place(2 * HIDDEN_COLS, down_ref[...].T)
    place(MLP_COLS, scaled(query_ref, attn_scale_ref))
    place(MLP_COLS + QUERY_COLS, scaled(key_ref, attn_scale_ref))
    place(MLP_COLS + QUERY_COLS + KV_COLS, scaled(value_ref, attn_scale_ref))
    place(MLP_COLS + QKV_COLS, out_ref[...].T)


def pack_shards(core, *shards):
    return pl.pallas_call(
        pack_kernel,
        in_specs=[smem_whole()] + [vmem_whole()] * len(shards),
        out_specs=[vmem_whole()] * 2,
        out_shape=[shape(48, LAYER_COLS, BF16)] * 2,
        compiler_params=pltpu.CompilerParams(vmem_limit_bytes=VMEM_LIMIT),
        name="pack_shards",
    )(core, *shards)


def from_layers(core, layer_zero, layer_one):
    mine, give = pick(core, layer_zero, layer_one), pick(core, layer_one, layer_zero)
    got = swap(give, "section")
    return pick(core, mine, got), pick(core, got, mine)


def gather_rows(z_low, share):
    other = swap(share, "zl")
    pair = jnp.concatenate([pick(z_low, share, other), pick(z_low, other, share)], axis=0)
    return lax.all_gather(pair, ("y", "x"), axis=0, tiled=True)


def scatter_pair(grad):
    return lax.psum_scatter(grad, ("y", "x"), scatter_dimension=0, tiled=True)


def scatter_low(z_low, pair):
    keep = pick(z_low, pair[:48], pair[48:])
    give = pick(z_low, pair[48:], pair[:48])
    return (keep.astype(F32) + swap(give, "zl").astype(F32)).astype(BF16)


def to_ring_order(rows):
    lead = rows.shape[:-1]
    return jnp.swapaxes(rows.reshape(lead + (4, 2, 4, 48)), -3, -2).reshape(rows.shape)


def from_ring_order(rows):
    lead = rows.shape[:-1]
    return jnp.swapaxes(rows.reshape(lead + (4, 4, 2, 48)), -3, -2).reshape(rows.shape)


def join_positions(tensor, own):
    other = swap(own, "tensor")
    return jnp.concatenate(
        [pick(tensor, own, other), pick(tensor, other, own)], axis=1
    ).reshape(384, WIDTH)


def own_positions(tensor, rows):
    rows = rows.reshape(3, 128, 1536)
    return pick(tensor, rows[:, :64], rows[:, 64:])


def per_device(
    inputs, cotangent, plan, attn_gain, mlp_gain, w_query, key_weight, value_weight,
    w_out, w_gate, w_up, w_down,
):
    core = lax.axis_index("section")
    z_low = lax.axis_index("zl")
    tensor = lax.axis_index("tensor")

    attn_scale = attn_gain[0].astype(F32)[:, None]
    mlp_scale = mlp_gain[0].astype(F32)[:, None]

    core_ref = core.astype(jnp.int32).reshape(1)
    mine, give = pack_shards(
        core_ref, attn_scale, mlp_scale,
        w_gate[0], w_up[0], w_down[0], w_query[0], key_weight[0], value_weight[0], w_out[0],
    )
    got = swap(give, "section")
    layer_zero, layer_one = pick(core, mine, got), pick(core, got, mine)
    first_weights = gather_rows(
        z_low, jnp.concatenate([layer_zero, layer_one[:, MLP_COLS:]], axis=1)
    )
    last_weights = gather_rows(z_low, layer_one[:, :MLP_COLS])
    attn_weights = ((first_weights, MLP_COLS), (first_weights, LAYER_COLS))
    mlp_weights_of = (first_weights, last_weights)

    stream = join_positions(tensor, to_ring_order(inputs[:, 0][plan]))
    stream, late = lax.optimization_barrier((stream, cotangent))
    out_grad = join_positions(tensor, to_ring_order(late[:, 0][plan]))
    stream, out_grad = lax.optimization_barrier((stream, out_grad))

    def saved_rows(low, high):
        return jnp.concatenate([pick(core, low, high), pick(core, high, low)], axis=1).astype(F32)

    attn_zero, attn_one = attn_weights
    mlp_zero, mlp_one = mlp_weights_of

    x_zero = stream
    _, first_zero, qkv_zero, prob_zero, mix_zero, keep, give = attention_forward(
        core_ref, x_zero, None, None, *attn_zero
    )
    sums, _, _ = sum_four(keep, give)
    middle_zero, second_zero, gate_zero, up_zero, hidden_zero, keep, give = mlp_forward(
        core_ref, x_zero, sums, mlp_zero
    )
    sums, _, _ = sum_four(keep, give)
    x_one, first_one, qkv_one, prob_one, mix_one, keep, give = attention_forward(
        core_ref, None, middle_zero, sums, *attn_one
    )
    sums, _, _ = sum_four(keep, give)

    middle_one, second_one, hidden_one, pair_grad, keep, give = mlp_last(
        core_ref, x_one, sums, out_grad, mlp_one
    )
    one_mlp = mlp_weights(None, MLP_COLS, second_one, out_grad, pair_grad, hidden_one)
    sums, one_mlp, _ = sum_four(keep, give, before=one_mlp)
    last_pair = scatter_pair(one_mlp)
    middle_grad, attn_in, qkv_grad, keep, give = attention_backward(
        core_ref, out_grad, middle_one, sums, qkv_one, prob_one, *attn_one
    )
    buffer = attention_weights(None, REST_COLS, MLP_COLS, first_one, attn_in, qkv_grad, mix_one)
    down_keep, down_give = mlp_down(core_ref, hidden_one, mlp_one)
    sums, _, (buffer, down_keep, down_give) = sum_four(
        keep, give, beside=(buffer, down_keep, down_give)
    )

    grad_one, pair_grad, keep, give = mlp_backward(
        core_ref, (x_one, middle_grad, *sums), gate_zero, up_zero, mlp_zero
    )
    buffer = mlp_weights(buffer, REST_COLS, second_zero, grad_one, pair_grad, hidden_zero)
    sums, _, buffer = sum_four(keep, give, beside=buffer)
    middle_grad, attn_in, qkv_grad, keep, give = attention_backward(
        core_ref, grad_one, middle_zero, sums, qkv_zero, prob_zero, *attn_zero
    )
    buffer = attention_weights(
        buffer, REST_COLS, LAYER_COLS, first_zero, attn_in, qkv_grad, mix_zero
    )
    keep, give, buffer = lax.optimization_barrier((keep, give, buffer))
    rest_pair = scatter_pair(buffer)
    sums, _, _ = sum_four(keep, give)
    rows = x_zero.astype(F32)
    grad_zero = middle_grad + norm_back(saved_rows(*sums), rows, inverse_norm(rows))
    down_sums, _, _ = sum_four(down_keep, down_give)
    result_one = (middle_one + saved_rows(*down_sums)).astype(BF16)
    outputs = [own_positions(tensor, x_one), own_positions(tensor, result_one)]
    grads = [own_positions(tensor, grad_zero.astype(BF16)), own_positions(tensor, grad_one)]

    layer_outputs = from_ring_order(pick(core, outputs[0], outputs[1]))
    input_grads = from_ring_order(pick(core, grads[0], grads[1]))
    last_grad = scatter_low(z_low, last_pair)
    rest_pair, layer_outputs, input_grads, last_grad = lax.optimization_barrier(
        (rest_pair, layer_outputs, input_grads, last_grad)
    )
    rest_grad = scatter_low(z_low, rest_pair)
    zero_grad = jnp.concatenate([rest_grad[:, :MLP_COLS], rest_grad[:, LAYER_COLS:]], axis=1)
    one_grad = jnp.concatenate([last_grad, rest_grad[:, MLP_COLS:LAYER_COLS]], axis=1)
    low, high = from_layers(core, zero_grad, one_grad)

    def joined(start, width):
        return jnp.concatenate(
            [low[:, start : start + width], high[:, start : start + width]], axis=1
        ).astype(F32)

    gate_grad = joined(0, HIDDEN_COLS)
    up_grad = joined(HIDDEN_COLS, HIDDEN_COLS)
    down_grad = joined(2 * HIDDEN_COLS, HIDDEN_COLS).T
    query_grad = joined(MLP_COLS, QUERY_COLS)
    key_grad = joined(MLP_COLS + QUERY_COLS, KV_COLS)
    value_grad = joined(MLP_COLS + QUERY_COLS + KV_COLS, KV_COLS)
    out_weight_grad = joined(MLP_COLS + QKV_COLS, OUT_COLS).T

    def gain_terms(weights, grad):
        terms = weights.astype(F32) * grad.astype(F32)
        return jnp.stack(
            [
                jnp.sum(terms[:, MLP_COLS : MLP_COLS + QKV_COLS], axis=1),
                jnp.sum(terms[:, : 2 * HIDDEN_COLS], axis=1),
            ]
        )

    terms = jnp.stack([gain_terms(layer_zero, zero_grad), gain_terms(layer_one, one_grad)])
    terms = terms + swap(terms, "tensor")
    terms = pick(core, terms[0], terms[1]) + swap(pick(core, terms[1], terms[0]), "section")
    return (
        layer_outputs[None, :, None],
        input_grads[None, :, None],
        (terms[0] / attn_scale[:, 0])[None],
        (terms[1] / mlp_scale[:, 0])[None],
        (query_grad * attn_scale)[None],
        (key_grad * attn_scale)[None],
        (value_grad * attn_scale)[None],
        out_weight_grad[None],
        (gate_grad * mlp_scale)[None],
        (up_grad * mlp_scale)[None],
        down_grad[None],
    )


def solution(mesh):
    split = Mesh(mesh.devices.reshape(2, 4, 2, 4, 2), ("section", "y", "zl", "x", "tensor"))
    dp = ("y", "zl", "x")
    rows = P("section", dp, "tensor")
    columns = P("section", "tensor", dp)
    return jax.shard_map(
        per_device,
        mesh=split,
        in_specs=(
            P(None, dp, "tensor", None),
            P(None, dp, "tensor", None),
            P(),
            P("section", dp),
            P("section", dp),
            rows,
            rows,
            rows,
            columns,
            rows,
            rows,
            columns,
        ),
        out_specs=(
            P("section", None, dp, "tensor", None),
            P("section", None, dp, "tensor", None),
            P("section", dp),
            P("section", dp),
            rows,
            rows,
            rows,
            columns,
            rows,
            rows,
            columns,
        ),
        check_vma=False,
    )
```

```python
import functools

import jax
import jax.numpy as jnp
from jax import lax
from jax.experimental import pallas as pl
from jax.experimental.pallas import tpu as pltpu
from jax.sharding import Mesh, PartitionSpec as P

HEAD_WIDTH = 96
EPSILON = 1e-05
BLOCKED = -1e30
SCORE_SCALE = HEAD_WIDTH ** (-0.5)
BF16 = jnp.bfloat16
F32 = jnp.float32

QUERY_COLS, KV_COLS = 384, 192
QKV_COLS = QUERY_COLS + 2 * KV_COLS
OUT_COLS = 384
HIDDEN_COLS = 1024
ATTN_COLS = QKV_COLS + OUT_COLS
MLP_COLS = 3 * HIDDEN_COLS
LAYER_COLS = MLP_COLS + ATTN_COLS
REST_COLS = LAYER_COLS + ATTN_COLS
HIDDEN_TILE = 512
MLP_STRIP = 512
AHEAD = 3
WIDTH = 1536
HALF = WIDTH // 2
PARTS = 2
MIB = 1024 * 1024


def swap(value, axis):
    return lax.ppermute(value, axis, [(0, 1), (1, 0)])


def pick(index, first, second):
    return jnp.where(index == 0, first, second)


def norm_back(weighted, residual, inverse):
    scaled = residual * inverse
    return inverse * (weighted - scaled * jnp.mean(weighted * scaled, axis=-1, keepdims=True))


def vmem_whole():
    return pl.BlockSpec(memory_space=pltpu.VMEM)


def smem_whole():
    return pl.BlockSpec(memory_space=pltpu.SMEM)


def shape(rows, columns, dtype):
    return jax.ShapeDtypeStruct((rows, columns), dtype)


def half_of(core_ref, which):
    position = core_ref[0] if which == 0 else 1 - core_ref[0]
    return pl.ds(pl.multiple_of(position * HALF, HALF), HALF)


def nt_dot(left_side, right_side):
    return lax.dot_general(
        left_side, right_side, (((1,), (1,)), ((), ())), preferred_element_type=F32
    )


def tn_dot(left_side, right_side):
    return lax.dot_general(
        left_side, right_side, (((0,), (0,)), ((), ())), preferred_element_type=F32
    )


def nn_dot(left_side, right_side):
    return jnp.dot(left_side, right_side, preferred_element_type=F32)


def row_parts(rows):
    return [slice(rows // PARTS * part, rows // PARTS * (part + 1)) for part in range(PARTS)]


def part_shapes(rows):
    return [shape(rows // PARTS, HALF, BF16)] * (2 * PARTS)


def each_sum(core_ref, sum_refs):
    rows = sum_refs[0].shape[0] * PARTS
    for which in range(2):
        for part, at in enumerate(row_parts(rows)):
            yield at, half_of(core_ref, which), sum_refs[PARTS * which + part]


def write_partial(core_ref, left_ref, w_ref, columns, outs):
    keeps, gives = outs[:PARTS], outs[PARTS:]
    for which, refs in ((1, gives), (0, keeps)):
        weights = w_ref[half_of(core_ref, which), columns]
        for at, ref in zip(row_parts(left_ref.shape[0]), refs):
            ref[...] = nt_dot(left_ref[at, :], weights).astype(BF16)


def params(mib):
    return pltpu.CompilerParams(vmem_limit_bytes=mib * MIB)


def inverse_norm(rows):
    return lax.rsqrt(jnp.mean(rows * rows, axis=-1, keepdims=True) + EPSILON)


def causal_mask():
    row = lax.broadcasted_iota(jnp.int32, (128, 128), 0)
    return row >= lax.broadcasted_iota(jnp.int32, (128, 128), 1)


def two_heads(ref, rows, start):
    return jnp.concatenate(
        [
            ref[rows, start : start + HEAD_WIDTH],
            ref[rows, start + HEAD_WIDTH : start + 2 * HEAD_WIDTH],
        ],
        axis=0,
    )


def attention_weights_copy(w_any, w_ref, sem, column):
    return pltpu.make_async_copy(w_any.at[:, pl.ds(column, ATTN_COLS)], w_ref, sem)


def attention_forward_body(sequences, core_ref, first_ref, w_ref, qkv_ref, prob_ref, mix_ref, *parts):
    qkv_ref[...] = nn_dot(first_ref[...], w_ref[:, :QKV_COLS]).astype(BF16)
    mask = causal_mask()
    mask = jnp.concatenate([mask, mask], axis=0)
    for sequence in range(sequences):
        rows = slice(128 * sequence, 128 * (sequence + 1))
        for group in range(2):
            queries = two_heads(qkv_ref, rows, 2 * HEAD_WIDTH * group)
            key_at = QUERY_COLS + HEAD_WIDTH * group
            value_at = key_at + KV_COLS
            scores = nt_dot(queries, qkv_ref[rows, key_at : key_at + HEAD_WIDTH]) * SCORE_SCALE
            scores = jnp.where(mask, scores, BLOCKED)
            expanded = jnp.exp(scores - jnp.max(scores, axis=-1, keepdims=True))
            probability = expanded / jnp.sum(expanded, axis=-1, keepdims=True)
            prob_ref[2 * sequence + group] = probability
            mixed = nn_dot(
                probability.astype(BF16), qkv_ref[rows, value_at : value_at + HEAD_WIDTH]
            ).astype(BF16)
            at = 2 * HEAD_WIDTH * group
            mix_ref[rows, at : at + HEAD_WIDTH] = mixed[:128]
            mix_ref[rows, at + HEAD_WIDTH : at + 2 * HEAD_WIDTH] = mixed[128:]
    write_partial(core_ref, mix_ref, w_ref, slice(QKV_COLS, ATTN_COLS), parts)


def attention_first_kernel(sequences, column, core_ref, x_ref, w_any, first_ref, *rest):
    outs, w_ref, sem = rest[:-2], rest[-2], rest[-1]
    copy = attention_weights_copy(w_any, w_ref, sem, column)
    copy.start()
    rows = x_ref[...].astype(F32)
    first_ref[...] = (rows * inverse_norm(rows)).astype(BF16)
    copy.wait()
    attention_forward_body(sequences, core_ref, first_ref, w_ref, *outs)


def attention_next_kernel(sequences, column, core_ref, middle_ref, *rest):
    sums, (w_any, x_ref, first_ref) = rest[: 2 * PARTS], rest[2 * PARTS : 2 * PARTS + 3]
    outs, w_ref, sem = rest[2 * PARTS + 3 : -2], rest[-2], rest[-1]
    copy = attention_weights_copy(w_any, w_ref, sem, column)
    copy.start()
    for at, columns, part in each_sum(core_ref, sums):
        x_ref[at, columns] = (middle_ref[at, columns] + part[...].astype(F32)).astype(BF16)
    rows = x_ref[...].astype(F32)
    first_ref[...] = (rows * inverse_norm(rows)).astype(BF16)
    copy.wait()
    attention_forward_body(sequences, core_ref, first_ref, w_ref, *outs)


def in_hbm(value):
    return pltpu.with_memory_space_constraint(value, pltpu.HBM)


def hbm_whole():
    return pl.BlockSpec(memory_space=pltpu.HBM)


def attention_scratch():
    return [pltpu.VMEM((WIDTH, ATTN_COLS), BF16), pltpu.SemaphoreType.DMA(())]


def attention_forward(core, x, middle, sums, weights, column):
    rows = (x if middle is None else middle).shape[0]
    sequences = rows // 128
    outs = [
        shape(rows, WIDTH, BF16),
        shape(rows, QKV_COLS, BF16),
        jax.ShapeDtypeStruct((2 * sequences, 256, 128), F32),
        shape(rows, OUT_COLS, BF16),
    ] + part_shapes(rows)
    if middle is None:
        operands, kernel = (core, x), attention_first_kernel
    else:
        operands, kernel = (core, middle, *sums), attention_next_kernel
        outs = [shape(rows, WIDTH, BF16)] + outs
    results = pl.pallas_call(
        functools.partial(kernel, sequences, column),
        in_specs=[smem_whole()] + [vmem_whole()] * (len(operands) - 1) + [hbm_whole()],
        out_specs=[vmem_whole()] * len(outs),
        out_shape=outs,
        scratch_shapes=attention_scratch(),
        compiler_params=params(20),
        cost_estimate=pl.CostEstimate(
            flops=2 * rows * WIDTH * ATTN_COLS, bytes_accessed=8_000_000, transcendentals=0
        ),
        name="attention_forward",
    )(*operands, in_hbm(weights))
    return ([x] if middle is None else []) + list(results)


def column_tiles(first):
    return [pl.ds(first + HIDDEN_TILE * step, HIDDEN_TILE) for step in range(HIDDEN_STEPS)]


def weight_copies(w_any, w_ref, sems, regions):
    return [
        pltpu.make_async_copy(w_any.at[rows, columns], w_ref.at[rows, columns], sems.at[number])
        for number, (rows, columns) in enumerate(regions)
    ]


def sigmoid(values):
    return 0.5 * jnp.tanh(0.5 * values) + 0.5


def arrivals(copies):
    for copy in copies[:AHEAD]:
        copy.start()
    place = iter(range(len(copies)))

    def arrive():
        number = next(place)
        copies[number].wait()
        if number + AHEAD < len(copies):
            copies[number + AHEAD].start()

    return arrive


def mlp_forward_kernel(core_ref, x_ref, *rest):
    sums, (w_any, middle_any, second_any, gate_any, up_any, hidden_any) = rest[: 2 * PARTS], rest[2 * PARTS : 2 * PARTS + 6]
    outs = rest[2 * PARTS + 6 : -8]
    w_ref, middle_ref, second_ref, gate_ref, up_ref, hidden_ref, sems, out_sems = rest[-8:]
    whole = pl.ds(0, WIDTH)
    tiles = [(gate, up) for gate, up in zip(column_tiles(0), column_tiles(HIDDEN_COLS))]
    down = pl.ds(2 * HIDDEN_COLS, HIDDEN_COLS)
    regions = [(whole, columns) for pair in tiles for columns in pair]
    regions.append((whole, down))
    arrive = arrivals(weight_copies(w_any, w_ref, sems, regions))
    for at, columns, part in each_sum(core_ref, sums):
        middle_ref[at, columns] = x_ref[at, columns].astype(F32) + part[...].astype(F32)
    rows = middle_ref[...]
    second_ref[...] = (rows * inverse_norm(rows)).astype(BF16)
    outward = []

    def send(source, target):
        outward.append(pltpu.make_async_copy(source, target, out_sems.at[len(outward)]))
        outward[-1].start()

    send(middle_ref, middle_any)
    send(second_ref, second_any)
    for step, (gate, up) in enumerate(tiles):
        at = slice(HIDDEN_TILE * step, HIDDEN_TILE * (step + 1))
        arrive()
        gate_out = nn_dot(second_ref[...], w_ref[:, gate])
        arrive()
        up_out = nn_dot(second_ref[...], w_ref[:, up])
        gate_ref[:, at] = gate_out
        up_ref[:, at] = up_out
        hidden_ref[:, at] = (gate_out * sigmoid(gate_out) * up_out).astype(BF16)
    send(gate_ref, gate_any)
    send(up_ref, up_any)
    send(hidden_ref, hidden_any)
    arrive()
    write_partial(core_ref, hidden_ref, w_ref, down, outs)
    for copy in outward:
        copy.wait()


HIDDEN_STEPS = HIDDEN_COLS // HIDDEN_TILE


def mlp_scratch():
    return [pltpu.VMEM((WIDTH, MLP_COLS), BF16), pltpu.SemaphoreType.DMA((2 * HIDDEN_STEPS + 1,))]


def mlp_forward(core, x, sums, weights):
    rows = x.shape[0]
    saved = [
        shape(rows, WIDTH, F32),
        shape(rows, WIDTH, BF16),
        shape(rows, HIDDEN_COLS, F32),
        shape(rows, HIDDEN_COLS, F32),
        shape(rows, HIDDEN_COLS, BF16),
    ]
    return pl.pallas_call(
        mlp_forward_kernel,
        in_specs=[smem_whole()] + [vmem_whole()] * (1 + 2 * PARTS) + [hbm_whole()],
        out_specs=[hbm_whole()] * 5 + [vmem_whole()] * (2 * PARTS),
        out_shape=[pltpu.HBM(array.shape, array.dtype) for array in saved] + part_shapes(rows),
        scratch_shapes=mlp_scratch()[:1]
        + [pltpu.VMEM(out.shape, out.dtype) for out in saved]
        + mlp_scratch()[1:]
        + [pltpu.SemaphoreType.DMA((5,))],
        compiler_params=params(30),
        cost_estimate=pl.CostEstimate(
            flops=2 * rows * WIDTH * MLP_COLS, bytes_accessed=15_000_000, transcendentals=0
        ),
        name="mlp_forward",
    )(core, x, *sums, in_hbm(weights))


def mlp_backward_tiles(g_ref, gate_ref, up_ref, arrive, pair_grad_ref, w_ref):
    for step, down in enumerate(column_tiles(2 * HIDDEN_COLS)):
        at = slice(HIDDEN_TILE * step, HIDDEN_TILE * (step + 1))
        up_at = slice(HIDDEN_COLS + at.start, HIDDEN_COLS + at.stop)
        arrive()
        hidden_grad = nn_dot(g_ref[...], w_ref[:, down])
        gate_out = gate_ref[:, at]
        sigmoid_gate = sigmoid(gate_out)
        pair_grad_ref[:, at] = (
            hidden_grad
            * up_ref[:, at]
            * (sigmoid_gate * (1.0 + gate_out * (1.0 - sigmoid_gate)))
        ).astype(BF16)
        pair_grad_ref[:, up_at] = (hidden_grad * (gate_out * sigmoid_gate)).astype(BF16)


def mlp_backward_copies(w_any, w_ref, sems):
    regions = [(pl.ds(0, WIDTH), columns) for columns in column_tiles(2 * HIDDEN_COLS)]
    regions.append((pl.ds(0, WIDTH), pl.ds(0, 2 * HIDDEN_COLS)))
    return arrivals(weight_copies(w_any, w_ref, sems, regions))


def mlp_backward_kernel(core_ref, x_ref, middle_grad_ref, *rest):
    sums, (gate_ref, up_ref, w_any, g_ref, pair_grad_ref) = rest[: 2 * PARTS], rest[2 * PARTS : 2 * PARTS + 5]
    outs, (w_ref, sems, weighted) = rest[2 * PARTS + 5 : -3], rest[-3:]
    arrive = mlp_backward_copies(w_any, w_ref, sems)
    for at, columns, part in each_sum(core_ref, sums):
        weighted[at, columns] = part[...].astype(F32)
    rows = x_ref[...].astype(F32)
    g_ref[...] = (
        middle_grad_ref[...] + norm_back(weighted[...], rows, inverse_norm(rows))
    ).astype(BF16)
    mlp_backward_tiles(g_ref, gate_ref, up_ref, arrive, pair_grad_ref, w_ref)
    arrive()
    write_partial(core_ref, pair_grad_ref, w_ref, slice(0, 2 * HIDDEN_COLS), outs)


def mlp_backward(core, above, gate_out, up_out, weights):
    rows = gate_out.shape[0]
    return pl.pallas_call(
        mlp_backward_kernel,
        in_specs=[smem_whole()] + [vmem_whole()] * (4 + 2 * PARTS) + [hbm_whole()],
        out_specs=[vmem_whole()] * (2 + 2 * PARTS),
        out_shape=[shape(rows, WIDTH, BF16), shape(rows, 2 * HIDDEN_COLS, BF16)] + part_shapes(rows),
        scratch_shapes=mlp_scratch() + [pltpu.VMEM((rows, WIDTH), F32)],
        compiler_params=params(30),
        cost_estimate=pl.CostEstimate(
            flops=2 * rows * WIDTH * MLP_COLS, bytes_accessed=15_000_000, transcendentals=0
        ),
        name="mlp_backward",
    )(core, *above, gate_out, up_out, in_hbm(weights))


def mlp_last_kernel(core_ref, x_ref, *rest):
    sums, (g_ref, w_any, middle_any, second_any, hidden_any, pair_grad_ref) = rest[: 2 * PARTS], rest[2 * PARTS : 2 * PARTS + 6]
    outs = rest[2 * PARTS + 6 : -8]
    w_ref, middle_ref, second_ref, gate_ref, up_ref, hidden_ref, sems, out_sems = rest[-8:]
    whole = pl.ds(0, WIDTH)
    tiles = [(gate, up) for gate, up in zip(column_tiles(0), column_tiles(HIDDEN_COLS))]
    regions = [(whole, columns) for pair in tiles for columns in pair]
    regions += [(whole, columns) for columns in column_tiles(2 * HIDDEN_COLS)]
    arrive = arrivals(weight_copies(w_any, w_ref, sems, regions))
    for at, columns, part in each_sum(core_ref, sums):
        middle_ref[at, columns] = x_ref[at, columns].astype(F32) + part[...].astype(F32)
    rows = middle_ref[...]
    second_ref[...] = (rows * inverse_norm(rows)).astype(BF16)
    outward = []

    def send(source, target):
        outward.append(pltpu.make_async_copy(source, target, out_sems.at[len(outward)]))
        outward[-1].start()

    send(middle_ref, middle_any)
    send(second_ref, second_any)
    for step, (gate, up) in enumerate(tiles):
        at = slice(HIDDEN_TILE * step, HIDDEN_TILE * (step + 1))
        arrive()
        gate_out = nn_dot(second_ref[...], w_ref[:, gate])
        arrive()
        up_out = nn_dot(second_ref[...], w_ref[:, up])
        gate_ref[:, at] = gate_out
        up_ref[:, at] = up_out
        hidden_ref[:, at] = (gate_out * sigmoid(gate_out) * up_out).astype(BF16)
    send(hidden_ref, hidden_any)
    mlp_backward_tiles(g_ref, gate_ref, up_ref, arrive, pair_grad_ref, w_ref)
    write_partial(core_ref, pair_grad_ref, w_ref, slice(0, 2 * HIDDEN_COLS), outs)
    for copy in outward:
        copy.wait()


def mlp_last(core, x, sums, g, weights):
    rows = x.shape[0]
    saved = [
        shape(rows, WIDTH, F32),
        shape(rows, WIDTH, BF16),
        shape(rows, HIDDEN_COLS, BF16),
    ]
    inner = saved[:2] + [shape(rows, HIDDEN_COLS, F32)] * 2 + saved[2:]
    return pl.pallas_call(
        mlp_last_kernel,
        in_specs=[smem_whole()] + [vmem_whole()] * (2 + 2 * PARTS) + [hbm_whole()],
        out_specs=[hbm_whole()] * 3 + [vmem_whole()] * (1 + 2 * PARTS),
        out_shape=[pltpu.HBM(array.shape, array.dtype) for array in saved]
        + [shape(rows, 2 * HIDDEN_COLS, BF16)]
        + part_shapes(rows),
        scratch_shapes=mlp_scratch()[:1]
        + [pltpu.VMEM(array.shape, array.dtype) for array in inner]
        + [pltpu.SemaphoreType.DMA((3 * HIDDEN_STEPS,)), pltpu.SemaphoreType.DMA((3,))],
        compiler_params=params(30),
        cost_estimate=pl.CostEstimate(
            flops=4 * rows * WIDTH * MLP_COLS, bytes_accessed=15_000_000, transcendentals=0
        ),
        name="mlp_last",
    )(core, x, *sums, g, in_hbm(weights))


def mlp_down_kernel(core_ref, hidden_ref, w_any, *rest):
    outs, w_ref, sem = rest[:-2], rest[-2], rest[-1]
    copy = pltpu.make_async_copy(w_any.at[:, pl.ds(2 * HIDDEN_COLS, HIDDEN_COLS)], w_ref, sem)
    copy.start()
    copy.wait()
    write_partial(core_ref, hidden_ref, w_ref, slice(0, HIDDEN_COLS), outs)


def mlp_down(core, hidden, weights):
    rows = hidden.shape[0]
    return pl.pallas_call(
        mlp_down_kernel,
        in_specs=[smem_whole(), vmem_whole(), hbm_whole()],
        out_specs=[vmem_whole()] * (2 * PARTS),
        out_shape=part_shapes(rows),
        scratch_shapes=[pltpu.VMEM((WIDTH, HIDDEN_COLS), BF16), pltpu.SemaphoreType.DMA(())],
        compiler_params=params(30),
        cost_estimate=pl.CostEstimate(
            flops=2 * rows * WIDTH * HIDDEN_COLS, bytes_accessed=5_000_000, transcendentals=0
        ),
        name="mlp_down",
    )(core, hidden, in_hbm(weights))


def attention_backward_kernel(sequences, column, core_ref, g_ref, middle_ref, *rest):
    sums, (qkv_ref, prob_ref, w_any, middle_grad_ref, attn_in_ref, qkv_grad_ref) = rest[: 2 * PARTS], rest[2 * PARTS : 2 * PARTS + 6]
    outs, (mix_grad, w_ref, sem) = rest[2 * PARTS + 6 : -3], rest[-3:]
    copy = attention_weights_copy(w_any, w_ref, sem, column)
    copy.start()
    for at, columns, part in each_sum(core_ref, sums):
        middle_grad_ref[at, columns] = part[...].astype(F32)
    middle = middle_ref[...]
    middle_grad = g_ref[...].astype(F32) + norm_back(
        middle_grad_ref[...], middle, inverse_norm(middle)
    )
    middle_grad_ref[...] = middle_grad
    attn_in_ref[...] = middle_grad.astype(BF16)
    copy.wait()
    mix_grad[...] = nn_dot(attn_in_ref[...], w_ref[:, QKV_COLS:]).astype(BF16)
    for sequence in range(sequences):
        rows = slice(128 * sequence, 128 * (sequence + 1))
        for group in range(2):
            at = 2 * HEAD_WIDTH * group
            key_at = QUERY_COLS + HEAD_WIDTH * group
            value_at = key_at + KV_COLS
            grads = two_heads(mix_grad, rows, at)
            queries = two_heads(qkv_ref, rows, at)
            keys = qkv_ref[rows, key_at : key_at + HEAD_WIDTH]
            probability = prob_ref[2 * sequence + group]
            prob_grad = nt_dot(grads, qkv_ref[rows, value_at : value_at + HEAD_WIDTH])
            centred = jnp.sum(probability * prob_grad, axis=-1, keepdims=True)
            score_grad = (probability * (prob_grad - centred)).astype(BF16)
            query_grad = (nn_dot(score_grad, keys) * SCORE_SCALE).astype(BF16)
            qkv_grad_ref[rows, at : at + HEAD_WIDTH] = query_grad[:128]
            qkv_grad_ref[rows, at + HEAD_WIDTH : at + 2 * HEAD_WIDTH] = query_grad[128:]
            qkv_grad_ref[rows, key_at : key_at + HEAD_WIDTH] = (
                tn_dot(score_grad, queries) * SCORE_SCALE
            ).astype(BF16)
            qkv_grad_ref[rows, value_at : value_at + HEAD_WIDTH] = tn_dot(
                probability.astype(BF16), grads
            ).astype(BF16)
    write_partial(core_ref, qkv_grad_ref, w_ref, slice(0, QKV_COLS), outs)


def attention_backward(core, g, middle, sums, qkv, probability, weights, column):
    rows = g.shape[0]
    return pl.pallas_call(
        functools.partial(attention_backward_kernel, rows // 128, column),
        in_specs=[smem_whole()] + [vmem_whole()] * (4 + 2 * PARTS) + [hbm_whole()],
        out_specs=[vmem_whole()] * (3 + 2 * PARTS),
        out_shape=[
            shape(rows, WIDTH, F32),
            shape(rows, WIDTH, BF16),
            shape(rows, QKV_COLS, BF16),
        ]
        + part_shapes(rows),
        scratch_shapes=[pltpu.VMEM((rows, OUT_COLS), BF16)] + attention_scratch(),
        compiler_params=params(22),
        cost_estimate=pl.CostEstimate(
            flops=2 * rows * WIDTH * ATTN_COLS, bytes_accessed=12_000_000, transcendentals=0
        ),
        name="attention_backward",
    )(core, g, middle, *sums, qkv, probability, in_hbm(weights))


def write_products(start, products, out_any, slots, sems):
    copies = []
    for number, (left, right, columns) in enumerate(products):
        width = columns.stop - columns.start
        if number >= 2:
            copies[number - 2].wait()
        slot = slots.at[number % 2]
        slot[...] = tn_dot(left[...], right[:, columns]).astype(BF16)
        target = out_any.at[:, pl.ds(start, width)]
        copies.append(pltpu.make_async_copy(slot, target, sems.at[number % 2]))
        copies[-1].start()
        start += width
    for copy in copies[-2:]:
        copy.wait()


def strips(columns, width):
    return [slice(at, at + width) for at in range(0, columns, width)]


def mlp_weights_kernel(second_ref, g_ref, pair_grad_ref, hidden_ref, *rest):
    out_any, slots, sems = rest[-3:]
    products = [(second_ref, pair_grad_ref, at) for at in strips(2 * HIDDEN_COLS, MLP_STRIP)]
    products += [(g_ref, hidden_ref, at) for at in strips(HIDDEN_COLS, MLP_STRIP)]
    write_products(0, products, out_any, slots, sems)


def into_buffer(kernel, buffer, columns, strip, operands, flops, name, mib):
    aliases, specs = {}, [vmem_whole()] * len(operands)
    if buffer is not None:
        aliases = {len(operands): 0}
        specs, operands = specs + [hbm_whole()], operands + (in_hbm(buffer),)
    return pl.pallas_call(
        kernel,
        in_specs=specs,
        out_specs=hbm_whole(),
        out_shape=pltpu.HBM((WIDTH, columns), BF16),
        input_output_aliases=aliases,
        scratch_shapes=[pltpu.VMEM((2, WIDTH, strip), BF16), pltpu.SemaphoreType.DMA((2,))],
        compiler_params=params(mib),
        cost_estimate=pl.CostEstimate(flops=flops, bytes_accessed=flops // 250, transcendentals=0),
        name=name,
    )(*operands)


def mlp_weights(buffer, columns, second, g, pair_grad, hidden):
    return into_buffer(
        mlp_weights_kernel,
        buffer,
        columns,
        MLP_STRIP,
        (second, g, pair_grad, hidden),
        2 * second.shape[0] * WIDTH * MLP_COLS,
        "mlp_weights",
        18,
    )


def attention_weights_kernel(start, first_ref, attn_in_ref, qkv_grad_ref, mix_ref, *rest):
    out_any, slots, sems = rest[-3:]
    products = [(first_ref, qkv_grad_ref, at) for at in strips(QKV_COLS, OUT_COLS)]
    products += [(attn_in_ref, mix_ref, slice(0, OUT_COLS))]
    write_products(start, products, out_any, slots, sems)


def attention_weights(buffer, columns, start, first, attn_in, qkv_grad, mixture):
    return into_buffer(
        functools.partial(attention_weights_kernel, start),
        buffer,
        columns,
        OUT_COLS,
        (first, attn_in, qkv_grad, mixture),
        2 * first.shape[0] * WIDTH * ATTN_COLS,
        "attention_weights",
        14,
    )


def sum_four(partial, before=None, beside=None):
    keeps, gives = partial[:PARTS], partial[PARTS:]
    chips = [
        (keep.astype(F32) + swap(give, "section").astype(F32)).astype(BF16)
        for keep, give in zip(keeps, gives)
    ]
    if before is not None:
        chips, before = lax.optimization_barrier((chips, before))
    arrived = [swap(chip, "tensor") for chip in chips]
    if beside is not None:
        arrived[0], beside = lax.optimization_barrier((arrived[0], beside))
    totals = [
        (chip.astype(F32) + other.astype(F32)).astype(BF16)
        for chip, other in zip(chips, arrived)
    ]
    return totals + [swap(total, "section") for total in totals], before, beside


def pack_kernel(core_ref, attn_scale_ref, mlp_scale_ref, gate_ref, up_ref, down_ref, query_ref, key_ref, value_ref, out_ref, mine_ref, give_ref):
    is_first = core_ref[0] == 0

    def place(start, weight):
        width = weight.shape[1] // 2
        low, high = weight[:, :width], weight[:, width:]
        mine_ref[:, start : start + width] = jnp.where(is_first, low, high)
        give_ref[:, start : start + width] = jnp.where(is_first, high, low)

    def scaled(ref, scale_ref):
        return (ref[...].astype(F32) * scale_ref[...]).astype(BF16)

    place(0, scaled(gate_ref, mlp_scale_ref))
    place(HIDDEN_COLS, scaled(up_ref, mlp_scale_ref))
    place(2 * HIDDEN_COLS, down_ref[...])
    place(MLP_COLS, scaled(query_ref, attn_scale_ref))
    place(MLP_COLS + QUERY_COLS, scaled(key_ref, attn_scale_ref))
    place(MLP_COLS + QUERY_COLS + KV_COLS, scaled(value_ref, attn_scale_ref))
    place(MLP_COLS + QKV_COLS, out_ref[...])


def pack_shards(core, *shards):
    return pl.pallas_call(
        pack_kernel,
        in_specs=[smem_whole()] + [vmem_whole()] * len(shards),
        out_specs=[vmem_whole()] * 2,
        out_shape=[shape(48, LAYER_COLS, BF16)] * 2,
        compiler_params=params(30),
        name="pack_shards",
    )(core, *shards)


def combine_kernel(core_ref, keep_ref, arrived_ref, last_ref, zero_w_ref, one_w_ref, mine_ref, give_ref, terms_ref, zero, one):
    rest = (keep_ref[...].astype(F32) + arrived_ref[...].astype(F32)).astype(BF16)
    zero[:, :MLP_COLS] = rest[:, :MLP_COLS]
    zero[:, MLP_COLS:] = rest[:, LAYER_COLS:]
    one[:, :MLP_COLS] = last_ref[...]
    one[:, MLP_COLS:] = rest[:, MLP_COLS:LAYER_COLS]
    is_first = core_ref[0] == 0
    mine_ref[...] = jnp.where(is_first, zero[...], one[...])
    give_ref[...] = jnp.where(is_first, one[...], zero[...])
    row = 0
    for grad, weights in ((zero, zero_w_ref), (one, one_w_ref)):
        products = weights[...].astype(F32) * grad[...].astype(F32)
        for columns in (slice(MLP_COLS, MLP_COLS + QKV_COLS), slice(0, 2 * HIDDEN_COLS)):
            terms_ref[row, :] = jnp.sum(products[:, columns], axis=1)
            row += 1


def combine_grads(core, *operands):
    return pl.pallas_call(
        combine_kernel,
        in_specs=[smem_whole()] + [vmem_whole()] * len(operands),
        out_specs=[vmem_whole()] * 3,
        out_shape=[shape(48, LAYER_COLS, BF16)] * 2 + [shape(4, 48, F32)],
        scratch_shapes=[pltpu.VMEM((48, LAYER_COLS), BF16)] * 2,
        compiler_params=params(16),
        name="combine_grads",
    )(core, *operands)


def unpack_kernel(core_ref, attn_scale_ref, mlp_scale_ref, mine_ref, got_ref, gate_ref, up_ref, down_ref, query_ref, key_ref, value_ref, out_ref):
    is_first = core_ref[0] == 0

    def place(out, start, scale_ref):
        width = out.shape[1] // 2
        mine = mine_ref[:, start : start + width].astype(F32)
        got = got_ref[:, start : start + width].astype(F32)
        if scale_ref is not None:
            mine, got = mine * scale_ref[...], got * scale_ref[...]
        out[:, :width] = jnp.where(is_first, mine, got)
        out[:, width:] = jnp.where(is_first, got, mine)

    place(gate_ref, 0, mlp_scale_ref)
    place(up_ref, HIDDEN_COLS, mlp_scale_ref)
    place(down_ref, 2 * HIDDEN_COLS, None)
    place(query_ref, MLP_COLS, attn_scale_ref)
    place(key_ref, MLP_COLS + QUERY_COLS, attn_scale_ref)
    place(value_ref, MLP_COLS + QUERY_COLS + KV_COLS, attn_scale_ref)
    place(out_ref, MLP_COLS + QKV_COLS, None)


def unpack_grads(core, *operands):
    widths = [HIDDEN_COLS] * 3 + [QUERY_COLS, KV_COLS, KV_COLS, OUT_COLS]
    return pl.pallas_call(
        unpack_kernel,
        in_specs=[smem_whole()] + [vmem_whole()] * len(operands),
        out_specs=[vmem_whole()] * len(widths),
        out_shape=[shape(48, 2 * width, F32) for width in widths],
        compiler_params=params(16),
        name="unpack_grads",
    )(core, *operands)


def gather_rows(z_low, share):
    other = swap(share, "zl")
    pair = jnp.concatenate([pick(z_low, share, other), pick(z_low, other, share)], axis=0)
    return lax.all_gather(pair, ("y", "x"), axis=0, tiled=True)


def scatter_pair(grad):
    return lax.psum_scatter(grad, ("y", "x"), scatter_dimension=0, tiled=True)


def scatter_low(z_low, pair):
    keep = pick(z_low, pair[:48], pair[48:])
    give = pick(z_low, pair[48:], pair[:48])
    return (keep.astype(F32) + swap(give, "zl").astype(F32)).astype(BF16)


def to_ring_order(rows):
    lead = rows.shape[:-1]
    return jnp.swapaxes(rows.reshape(lead + (4, 2, 4, 48)), -3, -2).reshape(rows.shape)


def from_ring_order(rows):
    lead = rows.shape[:-1]
    return jnp.swapaxes(rows.reshape(lead + (4, 4, 2, 48)), -3, -2).reshape(rows.shape)


def join_positions(tensor, own):
    other = swap(own, "tensor")
    return jnp.concatenate(
        [pick(tensor, own, other), pick(tensor, other, own)], axis=1
    ).reshape(384, WIDTH)


def own_positions(tensor, rows):
    rows = rows.reshape(3, 128, 1536)
    return pick(tensor, rows[:, :64], rows[:, 64:])


def per_device(
    inputs, cotangent, plan, attn_gain, mlp_gain, w_query, key_weight, value_weight,
    w_out, w_gate, w_up, w_down,
):
    core = lax.axis_index("section")
    z_low = lax.axis_index("zl")
    tensor = lax.axis_index("tensor")

    attn_scale = attn_gain[0].astype(F32)[:, None]
    mlp_scale = mlp_gain[0].astype(F32)[:, None]

    core_ref = core.astype(jnp.int32).reshape(1)
    mine, give = pack_shards(
        core_ref, attn_scale, mlp_scale,
        w_gate[0], w_up[0], w_down[0].T, w_query[0], key_weight[0], value_weight[0], w_out[0].T,
    )
    got = swap(give, "section")
    layer_zero, layer_one = pick(core, mine, got), pick(core, got, mine)
    first_weights = gather_rows(
        z_low, jnp.concatenate([layer_zero, layer_one[:, MLP_COLS:]], axis=1)
    )
    last_weights = gather_rows(z_low, layer_one[:, :MLP_COLS])
    attn_weights = ((first_weights, MLP_COLS), (first_weights, LAYER_COLS))
    mlp_weights_of = (first_weights, last_weights)

    stream = join_positions(tensor, to_ring_order(inputs[:, 0][plan]))
    stream, late = lax.optimization_barrier((stream, cotangent))
    out_grad = join_positions(tensor, to_ring_order(late[:, 0][plan]))
    stream, out_grad = lax.optimization_barrier((stream, out_grad))

    def whole_rows(sums):
        own, other = jnp.concatenate(sums[:PARTS]), jnp.concatenate(sums[PARTS:])
        return jnp.concatenate([pick(core, own, other), pick(core, other, own)], axis=1).astype(F32)

    attn_zero, attn_one = attn_weights
    mlp_zero, mlp_one = mlp_weights_of

    x_zero = stream
    _, first_zero, qkv_zero, prob_zero, mix_zero, *partial = attention_forward(
        core_ref, x_zero, None, None, *attn_zero
    )
    sums, _, _ = sum_four(partial)
    middle_zero, second_zero, gate_zero, up_zero, hidden_zero, *partial = mlp_forward(
        core_ref, x_zero, sums, mlp_zero
    )
    sums, _, _ = sum_four(partial)
    x_one, first_one, qkv_one, prob_one, mix_one, *partial = attention_forward(
        core_ref, None, middle_zero, sums, *attn_one
    )
    sums, _, _ = sum_four(partial)

    middle_one, second_one, hidden_one, pair_grad, *partial = mlp_last(
        core_ref, x_one, sums, out_grad, mlp_one
    )
    one_mlp = mlp_weights(None, MLP_COLS, second_one, out_grad, pair_grad, hidden_one)
    sums, one_mlp, _ = sum_four(partial, before=one_mlp)
    last_pair = scatter_pair(one_mlp)
    middle_grad, attn_in, qkv_grad, *partial = attention_backward(
        core_ref, out_grad, middle_one, sums, qkv_one, prob_one, *attn_one
    )
    buffer = attention_weights(None, REST_COLS, MLP_COLS, first_one, attn_in, qkv_grad, mix_one)
    down_partial = mlp_down(core_ref, hidden_one, mlp_one)
    sums, _, (buffer, down_partial) = sum_four(partial, beside=(buffer, down_partial))

    grad_one, pair_grad, *partial = mlp_backward(
        core_ref, (x_one, middle_grad, *sums), gate_zero, up_zero, mlp_zero
    )
    buffer = mlp_weights(buffer, REST_COLS, second_zero, grad_one, pair_grad, hidden_zero)
    sums, _, buffer = sum_four(partial, beside=buffer)
    middle_grad, attn_in, qkv_grad, *partial = attention_backward(
        core_ref, grad_one, middle_zero, sums, qkv_zero, prob_zero, *attn_zero
    )
    buffer = attention_weights(
        buffer, REST_COLS, LAYER_COLS, first_zero, attn_in, qkv_grad, mix_zero
    )
    partial, buffer = lax.optimization_barrier((partial, buffer))
    rest_pair = scatter_pair(buffer)
    sums, _, _ = sum_four(partial)
    rows = x_zero.astype(F32)
    grad_zero = middle_grad + norm_back(whole_rows(sums), rows, inverse_norm(rows))
    down_sums, _, _ = sum_four(down_partial)
    result_one = (middle_one + whole_rows(down_sums)).astype(BF16)
    outputs = [own_positions(tensor, x_one), own_positions(tensor, result_one)]
    grads = [own_positions(tensor, grad_zero.astype(BF16)), own_positions(tensor, grad_one)]

    layer_outputs = from_ring_order(pick(core, outputs[0], outputs[1]))
    input_grads = from_ring_order(pick(core, grads[0], grads[1]))
    last_grad = scatter_low(z_low, last_pair)
    rest_pair, layer_outputs, input_grads, last_grad = lax.optimization_barrier(
        (rest_pair, layer_outputs, input_grads, last_grad)
    )
    keep = pick(z_low, rest_pair[:48], rest_pair[48:])
    arrived = swap(pick(z_low, rest_pair[48:], rest_pair[:48]), "zl")
    mine, give, terms = combine_grads(
        core_ref, keep, arrived, last_grad, layer_zero, layer_one
    )
    got = swap(give, "section")
    terms, got = lax.optimization_barrier((terms, got))
    terms = terms + swap(terms, "tensor")
    terms = pick(core, terms[:2], terms[2:]) + swap(pick(core, terms[2:], terms[:2]), "section")
    gate_grad, up_grad, down_grad, query_grad, key_grad, value_grad, out_weight_grad = unpack_grads(
        core_ref, attn_scale, mlp_scale, mine, got
    )
    return (
        layer_outputs[None, :, None],
        input_grads[None, :, None],
        (terms[0] / attn_scale[:, 0])[None],
        (terms[1] / mlp_scale[:, 0])[None],
        query_grad[None],
        key_grad[None],
        value_grad[None],
        out_weight_grad.T[None],
        gate_grad[None],
        up_grad[None],
        down_grad.T[None],
    )


def solution(mesh):
    split = Mesh(mesh.devices.reshape(2, 4, 2, 4, 2), ("section", "y", "zl", "x", "tensor"))
    dp = ("y", "zl", "x")
    rows = P("section", dp, "tensor")
    columns = P("section", "tensor", dp)
    return jax.shard_map(
        per_device,
        mesh=split,
        in_specs=(
            P(None, dp, "tensor", None),
            P(None, dp, "tensor", None),
            P(),
            P("section", dp),
            P("section", dp),
            rows,
            rows,
            rows,
            columns,
            rows,
            rows,
            columns,
        ),
        out_specs=(
            P("section", None, dp, "tensor", None),
            P("section", None, dp, "tensor", None),
            P("section", dp),
            P("section", dp),
            rows,
            rows,
            rows,
            columns,
            rows,
            rows,
            columns,
        ),
        check_vma=False,
    )
```

```python
import functools

import jax
import jax.numpy as jnp
from jax import lax
from jax.experimental import pallas as pl
from jax.experimental.pallas import tpu as pltpu
from jax.sharding import Mesh, PartitionSpec as P

HEAD_WIDTH = 96
EPSILON = 1e-05
BLOCKED = -1e30
SCORE_SCALE = HEAD_WIDTH ** (-0.5)
BF16 = jnp.bfloat16
F32 = jnp.float32

QUERY_COLS, KV_COLS = 384, 192
QKV_COLS = QUERY_COLS + 2 * KV_COLS
OUT_COLS = 384
HIDDEN_COLS = 1024
ATTN_COLS = QKV_COLS + OUT_COLS
MLP_COLS = 3 * HIDDEN_COLS
LAYER_COLS = MLP_COLS + ATTN_COLS
REST_COLS = LAYER_COLS + ATTN_COLS
HIDDEN_TILE = 512
MLP_STRIP = 512
AHEAD = 3
WIDTH = 1536
HALF = WIDTH // 2
PARTS = 2
MIB = 1024 * 1024


def swap(value, axis):
    return lax.ppermute(value, axis, [(0, 1), (1, 0)])


def pick(index, first, second):
    return jnp.where(index == 0, first, second)


def norm_back(weighted, residual, inverse):
    scaled = residual * inverse
    return inverse * (weighted - scaled * jnp.mean(weighted * scaled, axis=-1, keepdims=True))


def vmem_whole():
    return pl.BlockSpec(memory_space=pltpu.VMEM)


def smem_whole():
    return pl.BlockSpec(memory_space=pltpu.SMEM)


def shape(rows, columns, dtype):
    return jax.ShapeDtypeStruct((rows, columns), dtype)


def half_of(core_ref, which):
    position = core_ref[0] if which == 0 else 1 - core_ref[0]
    return pl.ds(pl.multiple_of(position * HALF, HALF), HALF)


def nt_dot(left_side, right_side):
    return lax.dot_general(
        left_side, right_side, (((1,), (1,)), ((), ())), preferred_element_type=F32
    )


def tn_dot(left_side, right_side):
    return lax.dot_general(
        left_side, right_side, (((0,), (0,)), ((), ())), preferred_element_type=F32
    )


def nn_dot(left_side, right_side):
    return jnp.dot(left_side, right_side, preferred_element_type=F32)


def row_parts(rows):
    return [slice(rows // PARTS * part, rows // PARTS * (part + 1)) for part in range(PARTS)]


def part_shapes(rows):
    return [shape(rows // PARTS, HALF, BF16)] * (2 * PARTS)


def each_sum(core_ref, sum_refs):
    rows = sum_refs[0].shape[0] * PARTS
    for which in range(2):
        for part, at in enumerate(row_parts(rows)):
            yield at, half_of(core_ref, which), sum_refs[PARTS * which + part]


def write_partial(core_ref, left_ref, w_ref, columns, outs):
    keeps, gives = outs[:PARTS], outs[PARTS:]
    for which, refs in ((1, gives), (0, keeps)):
        weights = w_ref[half_of(core_ref, which), columns]
        for at, ref in zip(row_parts(left_ref.shape[0]), refs):
            ref[...] = nt_dot(left_ref[at, :], weights).astype(BF16)


def params(mib):
    return pltpu.CompilerParams(vmem_limit_bytes=mib * MIB)


def inverse_norm(rows):
    return lax.rsqrt(jnp.mean(rows * rows, axis=-1, keepdims=True) + EPSILON)


def causal_mask():
    row = lax.broadcasted_iota(jnp.int32, (128, 128), 0)
    return row >= lax.broadcasted_iota(jnp.int32, (128, 128), 1)


def two_heads(ref, rows, start):
    return jnp.concatenate(
        [
            ref[rows, start : start + HEAD_WIDTH],
            ref[rows, start + HEAD_WIDTH : start + 2 * HEAD_WIDTH],
        ],
        axis=0,
    )


def attention_weights_copy(w_any, w_ref, sem, column):
    return pltpu.make_async_copy(w_any.at[:, pl.ds(column, ATTN_COLS)], w_ref, sem)


def attention_forward_body(sequences, core_ref, first_ref, w_ref, qkv_ref, prob_ref, mix_ref, *parts):
    qkv_ref[...] = nn_dot(first_ref[...], w_ref[:, :QKV_COLS]).astype(BF16)
    mask = causal_mask()
    mask = jnp.concatenate([mask, mask], axis=0)
    for sequence in range(sequences):
        rows = slice(128 * sequence, 128 * (sequence + 1))
        for group in range(2):
            queries = two_heads(qkv_ref, rows, 2 * HEAD_WIDTH * group)
            key_at = QUERY_COLS + HEAD_WIDTH * group
            value_at = key_at + KV_COLS
            scores = nt_dot(queries, qkv_ref[rows, key_at : key_at + HEAD_WIDTH]) * SCORE_SCALE
            scores = jnp.where(mask, scores, BLOCKED)
            expanded = jnp.exp(scores - jnp.max(scores, axis=-1, keepdims=True))
            probability = expanded / jnp.sum(expanded, axis=-1, keepdims=True)
            prob_ref[2 * sequence + group] = probability
            mixed = nn_dot(
                probability.astype(BF16), qkv_ref[rows, value_at : value_at + HEAD_WIDTH]
            ).astype(BF16)
            at = 2 * HEAD_WIDTH * group
            mix_ref[rows, at : at + HEAD_WIDTH] = mixed[:128]
            mix_ref[rows, at + HEAD_WIDTH : at + 2 * HEAD_WIDTH] = mixed[128:]
    write_partial(core_ref, mix_ref, w_ref, slice(QKV_COLS, ATTN_COLS), parts)


def attention_first_kernel(sequences, column, core_ref, x_ref, w_any, first_ref, *rest):
    outs, w_ref, sem = rest[:-2], rest[-2], rest[-1]
    copy = attention_weights_copy(w_any, w_ref, sem, column)
    copy.start()
    rows = x_ref[...].astype(F32)
    first_ref[...] = (rows * inverse_norm(rows)).astype(BF16)
    copy.wait()
    attention_forward_body(sequences, core_ref, first_ref, w_ref, *outs)


def attention_next_kernel(sequences, column, core_ref, middle_ref, *rest):
    sums, (w_any, x_ref, first_ref) = rest[: 2 * PARTS], rest[2 * PARTS : 2 * PARTS + 3]
    outs, w_ref, sem = rest[2 * PARTS + 3 : -2], rest[-2], rest[-1]
    copy = attention_weights_copy(w_any, w_ref, sem, column)
    copy.start()
    for at, columns, part in each_sum(core_ref, sums):
        x_ref[at, columns] = (middle_ref[at, columns] + part[...].astype(F32)).astype(BF16)
    rows = x_ref[...].astype(F32)
    first_ref[...] = (rows * inverse_norm(rows)).astype(BF16)
    copy.wait()
    attention_forward_body(sequences, core_ref, first_ref, w_ref, *outs)


def in_hbm(value):
    return pltpu.with_memory_space_constraint(value, pltpu.HBM)


def hbm_whole():
    return pl.BlockSpec(memory_space=pltpu.HBM)


def attention_scratch():
    return [pltpu.VMEM((WIDTH, ATTN_COLS), BF16), pltpu.SemaphoreType.DMA(())]


def attention_forward(core, x, middle, sums, weights, column):
    rows = (x if middle is None else middle).shape[0]
    sequences = rows // 128
    outs = [
        shape(rows, WIDTH, BF16),
        shape(rows, QKV_COLS, BF16),
        jax.ShapeDtypeStruct((2 * sequences, 256, 128), F32),
        shape(rows, OUT_COLS, BF16),
    ] + part_shapes(rows)
    if middle is None:
        operands, kernel = (core, x), attention_first_kernel
    else:
        operands, kernel = (core, middle, *sums), attention_next_kernel
        outs = [shape(rows, WIDTH, BF16)] + outs
    results = pl.pallas_call(
        functools.partial(kernel, sequences, column),
        in_specs=[smem_whole()] + [vmem_whole()] * (len(operands) - 1) + [hbm_whole()],
        out_specs=[vmem_whole()] * len(outs),
        out_shape=outs,
        scratch_shapes=attention_scratch(),
        compiler_params=params(20),
        cost_estimate=pl.CostEstimate(
            flops=2 * rows * WIDTH * ATTN_COLS, bytes_accessed=8_000_000, transcendentals=0
        ),
        name="attention_forward",
    )(*operands, in_hbm(weights))
    return ([x] if middle is None else []) + list(results)


def column_tiles(first):
    return [pl.ds(first + HIDDEN_TILE * step, HIDDEN_TILE) for step in range(HIDDEN_STEPS)]


def weight_copies(w_any, w_ref, sems, regions):
    return [
        pltpu.make_async_copy(w_any.at[rows, columns], w_ref.at[rows, columns], sems.at[number])
        for number, (rows, columns) in enumerate(regions)
    ]


def sigmoid(values):
    return 0.5 * jnp.tanh(0.5 * values) + 0.5


def arrivals(copies):
    for copy in copies[:AHEAD]:
        copy.start()
    place = iter(range(len(copies)))

    def arrive():
        number = next(place)
        copies[number].wait()
        if number + AHEAD < len(copies):
            copies[number + AHEAD].start()

    return arrive


def mlp_forward_kernel(core_ref, x_ref, *rest):
    sums, (w_any, middle_any, second_any, gate_any, up_any, hidden_any) = rest[: 2 * PARTS], rest[2 * PARTS : 2 * PARTS + 6]
    outs = rest[2 * PARTS + 6 : -8]
    w_ref, middle_ref, second_ref, gate_ref, up_ref, hidden_ref, sems, out_sems = rest[-8:]
    whole = pl.ds(0, WIDTH)
    tiles = [(gate, up) for gate, up in zip(column_tiles(0), column_tiles(HIDDEN_COLS))]
    down = pl.ds(2 * HIDDEN_COLS, HIDDEN_COLS)
    regions = [(whole, columns) for pair in tiles for columns in pair]
    regions.append((whole, down))
    arrive = arrivals(weight_copies(w_any, w_ref, sems, regions))
    for at, columns, part in each_sum(core_ref, sums):
        middle_ref[at, columns] = x_ref[at, columns].astype(F32) + part[...].astype(F32)
    rows = middle_ref[...]
    second_ref[...] = (rows * inverse_norm(rows)).astype(BF16)
    outward = []

    def send(source, target):
        outward.append(pltpu.make_async_copy(source, target, out_sems.at[len(outward)]))
        outward[-1].start()

    send(middle_ref, middle_any)
    send(second_ref, second_any)
    for step, (gate, up) in enumerate(tiles):
        at = slice(HIDDEN_TILE * step, HIDDEN_TILE * (step + 1))
        arrive()
        gate_out = nn_dot(second_ref[...], w_ref[:, gate])
        arrive()
        up_out = nn_dot(second_ref[...], w_ref[:, up])
        gate_ref[:, at] = gate_out
        up_ref[:, at] = up_out
        hidden_ref[:, at] = (gate_out * sigmoid(gate_out) * up_out).astype(BF16)
    send(gate_ref, gate_any)
    send(up_ref, up_any)
    send(hidden_ref, hidden_any)
    arrive()
    write_partial(core_ref, hidden_ref, w_ref, down, outs)
    for copy in outward:
        copy.wait()


HIDDEN_STEPS = HIDDEN_COLS // HIDDEN_TILE


def mlp_scratch():
    return [pltpu.VMEM((WIDTH, MLP_COLS), BF16), pltpu.SemaphoreType.DMA((2 * HIDDEN_STEPS + 1,))]


def mlp_forward(core, x, sums, weights):
    rows = x.shape[0]
    saved = [
        shape(rows, WIDTH, F32),
        shape(rows, WIDTH, BF16),
        shape(rows, HIDDEN_COLS, F32),
        shape(rows, HIDDEN_COLS, F32),
        shape(rows, HIDDEN_COLS, BF16),
    ]
    return pl.pallas_call(
        mlp_forward_kernel,
        in_specs=[smem_whole()] + [vmem_whole()] * (1 + 2 * PARTS) + [hbm_whole()],
        out_specs=[hbm_whole()] * 5 + [vmem_whole()] * (2 * PARTS),
        out_shape=[pltpu.HBM(array.shape, array.dtype) for array in saved] + part_shapes(rows),
        scratch_shapes=mlp_scratch()[:1]
        + [pltpu.VMEM(out.shape, out.dtype) for out in saved]
        + mlp_scratch()[1:]
        + [pltpu.SemaphoreType.DMA((5,))],
        compiler_params=params(30),
        cost_estimate=pl.CostEstimate(
            flops=2 * rows * WIDTH * MLP_COLS, bytes_accessed=15_000_000, transcendentals=0
        ),
        name="mlp_forward",
    )(core, x, *sums, in_hbm(weights))


def mlp_backward_tiles(g_ref, gate_ref, up_ref, arrive, pair_grad_ref, w_ref):
    for step, down in enumerate(column_tiles(2 * HIDDEN_COLS)):
        at = slice(HIDDEN_TILE * step, HIDDEN_TILE * (step + 1))
        up_at = slice(HIDDEN_COLS + at.start, HIDDEN_COLS + at.stop)
        arrive()
        hidden_grad = nn_dot(g_ref[...], w_ref[:, down])
        gate_out = gate_ref[:, at]
        sigmoid_gate = sigmoid(gate_out)
        pair_grad_ref[:, at] = (
            hidden_grad
            * up_ref[:, at]
            * (sigmoid_gate * (1.0 + gate_out * (1.0 - sigmoid_gate)))
        ).astype(BF16)
        pair_grad_ref[:, up_at] = (hidden_grad * (gate_out * sigmoid_gate)).astype(BF16)


def mlp_backward_copies(w_any, w_ref, sems):
    regions = [(pl.ds(0, WIDTH), columns) for columns in column_tiles(2 * HIDDEN_COLS)]
    regions.append((pl.ds(0, WIDTH), pl.ds(0, 2 * HIDDEN_COLS)))
    return arrivals(weight_copies(w_any, w_ref, sems, regions))


def mlp_backward_kernel(core_ref, x_ref, middle_grad_ref, *rest):
    sums, (gate_ref, up_ref, w_any, g_ref, pair_grad_ref) = rest[: 2 * PARTS], rest[2 * PARTS : 2 * PARTS + 5]
    outs, (w_ref, sems, weighted) = rest[2 * PARTS + 5 : -3], rest[-3:]
    arrive = mlp_backward_copies(w_any, w_ref, sems)
    for at, columns, part in each_sum(core_ref, sums):
        weighted[at, columns] = part[...].astype(F32)
    rows = x_ref[...].astype(F32)
    g_ref[...] = (
        middle_grad_ref[...] + norm_back(weighted[...], rows, inverse_norm(rows))
    ).astype(BF16)
    mlp_backward_tiles(g_ref, gate_ref, up_ref, arrive, pair_grad_ref, w_ref)
    arrive()
    write_partial(core_ref, pair_grad_ref, w_ref, slice(0, 2 * HIDDEN_COLS), outs)


def mlp_backward(core, above, gate_out, up_out, weights):
    rows = gate_out.shape[0]
    return pl.pallas_call(
        mlp_backward_kernel,
        in_specs=[smem_whole()] + [vmem_whole()] * (4 + 2 * PARTS) + [hbm_whole()],
        out_specs=[vmem_whole()] * (2 + 2 * PARTS),
        out_shape=[shape(rows, WIDTH, BF16), shape(rows, 2 * HIDDEN_COLS, BF16)] + part_shapes(rows),
        scratch_shapes=mlp_scratch() + [pltpu.VMEM((rows, WIDTH), F32)],
        compiler_params=params(30),
        cost_estimate=pl.CostEstimate(
            flops=2 * rows * WIDTH * MLP_COLS, bytes_accessed=15_000_000, transcendentals=0
        ),
        name="mlp_backward",
    )(core, *above, gate_out, up_out, in_hbm(weights))


def mlp_last_kernel(core_ref, x_ref, *rest):
    sums, (g_ref, w_any, middle_any, second_ref, hidden_ref, pair_grad_ref) = rest[: 2 * PARTS], rest[2 * PARTS : 2 * PARTS + 6]
    outs = rest[2 * PARTS + 6 : -6]
    w_ref, middle_ref, gate_ref, up_ref, sems, out_sem = rest[-6:]
    whole = pl.ds(0, WIDTH)
    tiles = [(gate, up) for gate, up in zip(column_tiles(0), column_tiles(HIDDEN_COLS))]
    regions = [(whole, columns) for pair in tiles for columns in pair]
    regions += [(whole, columns) for columns in column_tiles(2 * HIDDEN_COLS)]
    arrive = arrivals(weight_copies(w_any, w_ref, sems, regions))
    for at, columns, part in each_sum(core_ref, sums):
        middle_ref[at, columns] = x_ref[at, columns].astype(F32) + part[...].astype(F32)
    rows = middle_ref[...]
    second_ref[...] = (rows * inverse_norm(rows)).astype(BF16)
    outward = pltpu.make_async_copy(middle_ref, middle_any, out_sem)
    outward.start()
    for step, (gate, up) in enumerate(tiles):
        at = slice(HIDDEN_TILE * step, HIDDEN_TILE * (step + 1))
        arrive()
        gate_out = nn_dot(second_ref[...], w_ref[:, gate])
        arrive()
        up_out = nn_dot(second_ref[...], w_ref[:, up])
        gate_ref[:, at] = gate_out
        up_ref[:, at] = up_out
        hidden_ref[:, at] = (gate_out * sigmoid(gate_out) * up_out).astype(BF16)
    mlp_backward_tiles(g_ref, gate_ref, up_ref, arrive, pair_grad_ref, w_ref)
    write_partial(core_ref, pair_grad_ref, w_ref, slice(0, 2 * HIDDEN_COLS), outs)
    outward.wait()


def mlp_last(core, x, sums, g, weights):
    rows = x.shape[0]
    inner = [shape(rows, WIDTH, F32)] + [shape(rows, HIDDEN_COLS, F32)] * 2
    return pl.pallas_call(
        mlp_last_kernel,
        in_specs=[smem_whole()] + [vmem_whole()] * (2 + 2 * PARTS) + [hbm_whole()],
        out_specs=[hbm_whole()] + [vmem_whole()] * (3 + 2 * PARTS),
        out_shape=[
            pltpu.HBM((rows, WIDTH), F32),
            shape(rows, WIDTH, BF16),
            shape(rows, HIDDEN_COLS, BF16),
            shape(rows, 2 * HIDDEN_COLS, BF16),
        ]
        + part_shapes(rows),
        scratch_shapes=mlp_scratch()[:1]
        + [pltpu.VMEM(array.shape, array.dtype) for array in inner]
        + [pltpu.SemaphoreType.DMA((3 * HIDDEN_STEPS,)), pltpu.SemaphoreType.DMA(())],
        compiler_params=params(30),
        cost_estimate=pl.CostEstimate(
            flops=4 * rows * WIDTH * MLP_COLS, bytes_accessed=15_000_000, transcendentals=0
        ),
        name="mlp_last",
    )(core, x, *sums, g, in_hbm(weights))


def mlp_down_kernel(core_ref, hidden_ref, w_any, *rest):
    outs, w_ref, sem = rest[:-2], rest[-2], rest[-1]
    copy = pltpu.make_async_copy(w_any.at[:, pl.ds(2 * HIDDEN_COLS, HIDDEN_COLS)], w_ref, sem)
    copy.start()
    copy.wait()
    write_partial(core_ref, hidden_ref, w_ref, slice(0, HIDDEN_COLS), outs)


def mlp_down(core, hidden, weights):
    rows = hidden.shape[0]
    return pl.pallas_call(
        mlp_down_kernel,
        in_specs=[smem_whole(), vmem_whole(), hbm_whole()],
        out_specs=[vmem_whole()] * (2 * PARTS),
        out_shape=part_shapes(rows),
        scratch_shapes=[pltpu.VMEM((WIDTH, HIDDEN_COLS), BF16), pltpu.SemaphoreType.DMA(())],
        compiler_params=params(14),
        cost_estimate=pl.CostEstimate(
            flops=2 * rows * WIDTH * HIDDEN_COLS, bytes_accessed=5_000_000, transcendentals=0
        ),
        name="mlp_down",
    )(core, hidden, in_hbm(weights))


def attention_backward_kernel(sequences, column, core_ref, g_ref, middle_ref, *rest):
    sums, (qkv_ref, prob_ref, w_any, middle_grad_ref, attn_in_ref, qkv_grad_ref) = rest[: 2 * PARTS], rest[2 * PARTS : 2 * PARTS + 6]
    outs, (mix_grad, w_ref, sem) = rest[2 * PARTS + 6 : -3], rest[-3:]
    copy = attention_weights_copy(w_any, w_ref, sem, column)
    copy.start()
    for at, columns, part in each_sum(core_ref, sums):
        middle_grad_ref[at, columns] = part[...].astype(F32)
    middle = middle_ref[...]
    middle_grad = g_ref[...].astype(F32) + norm_back(
        middle_grad_ref[...], middle, inverse_norm(middle)
    )
    middle_grad_ref[...] = middle_grad
    attn_in_ref[...] = middle_grad.astype(BF16)
    copy.wait()
    mix_grad[...] = nn_dot(attn_in_ref[...], w_ref[:, QKV_COLS:]).astype(BF16)
    for sequence in range(sequences):
        rows = slice(128 * sequence, 128 * (sequence + 1))
        for group in range(2):
            at = 2 * HEAD_WIDTH * group
            key_at = QUERY_COLS + HEAD_WIDTH * group
            value_at = key_at + KV_COLS
            grads = two_heads(mix_grad, rows, at)
            queries = two_heads(qkv_ref, rows, at)
            keys = qkv_ref[rows, key_at : key_at + HEAD_WIDTH]
            probability = prob_ref[2 * sequence + group]
            prob_grad = nt_dot(grads, qkv_ref[rows, value_at : value_at + HEAD_WIDTH])
            centred = jnp.sum(probability * prob_grad, axis=-1, keepdims=True)
            score_grad = (probability * (prob_grad - centred)).astype(BF16)
            query_grad = (nn_dot(score_grad, keys) * SCORE_SCALE).astype(BF16)
            qkv_grad_ref[rows, at : at + HEAD_WIDTH] = query_grad[:128]
            qkv_grad_ref[rows, at + HEAD_WIDTH : at + 2 * HEAD_WIDTH] = query_grad[128:]
            qkv_grad_ref[rows, key_at : key_at + HEAD_WIDTH] = (
                tn_dot(score_grad, queries) * SCORE_SCALE
            ).astype(BF16)
            qkv_grad_ref[rows, value_at : value_at + HEAD_WIDTH] = tn_dot(
                probability.astype(BF16), grads
            ).astype(BF16)
    write_partial(core_ref, qkv_grad_ref, w_ref, slice(0, QKV_COLS), outs)


def attention_backward(core, g, middle, sums, qkv, probability, weights, column, near=True):
    rows = g.shape[0]
    place = shape if near else lambda *array: pltpu.HBM(array[:2], array[2])
    return pl.pallas_call(
        functools.partial(attention_backward_kernel, rows // 128, column),
        in_specs=[smem_whole()] + [vmem_whole()] * (4 + 2 * PARTS) + [hbm_whole()],
        out_specs=[vmem_whole()] * (3 + 2 * PARTS),
        out_shape=[
            place(rows, WIDTH, F32),
            shape(rows, WIDTH, BF16),
            shape(rows, QKV_COLS, BF16),
        ]
        + [place(*array.shape, array.dtype) for array in part_shapes(rows)],
        scratch_shapes=[pltpu.VMEM((rows, OUT_COLS), BF16)] + attention_scratch(),
        compiler_params=params(22),
        cost_estimate=pl.CostEstimate(
            flops=2 * rows * WIDTH * ATTN_COLS, bytes_accessed=12_000_000, transcendentals=0
        ),
        name="attention_backward",
    )(core, g, middle, *sums, qkv, probability, in_hbm(weights))


def write_products(start, products, out_any, slots, sems):
    copies = []
    for number, (left, right, columns) in enumerate(products):
        width = columns.stop - columns.start
        if number >= 2:
            copies[number - 2].wait()
        slot = slots.at[number % 2]
        slot[...] = tn_dot(left[...], right[:, columns]).astype(BF16)
        target = out_any.at[:, pl.ds(start, width)]
        copies.append(pltpu.make_async_copy(slot, target, sems.at[number % 2]))
        copies[-1].start()
        start += width
    for copy in copies[-2:]:
        copy.wait()


def strips(columns, width):
    return [slice(at, at + width) for at in range(0, columns, width)]


def mlp_weights_kernel(second_ref, g_ref, pair_grad_ref, hidden_ref, *rest):
    out_any, slots, sems = rest[-3:]
    products = [(second_ref, pair_grad_ref, at) for at in strips(2 * HIDDEN_COLS, MLP_STRIP)]
    products += [(g_ref, hidden_ref, at) for at in strips(HIDDEN_COLS, MLP_STRIP)]
    write_products(0, products, out_any, slots, sems)


def into_buffer(kernel, buffer, columns, strip, operands, flops, name, mib):
    aliases, specs = {}, [vmem_whole()] * len(operands)
    if buffer is not None:
        aliases = {len(operands): 0}
        specs, operands = specs + [hbm_whole()], operands + (in_hbm(buffer),)
    return pl.pallas_call(
        kernel,
        in_specs=specs,
        out_specs=hbm_whole(),
        out_shape=pltpu.HBM((WIDTH, columns), BF16),
        input_output_aliases=aliases,
        scratch_shapes=[pltpu.VMEM((2, WIDTH, strip), BF16), pltpu.SemaphoreType.DMA((2,))],
        compiler_params=params(mib),
        cost_estimate=pl.CostEstimate(flops=flops, bytes_accessed=flops // 250, transcendentals=0),
        name=name,
    )(*operands)


def mlp_weights(buffer, columns, second, g, pair_grad, hidden):
    return into_buffer(
        mlp_weights_kernel,
        buffer,
        columns,
        MLP_STRIP,
        (second, g, pair_grad, hidden),
        2 * second.shape[0] * WIDTH * MLP_COLS,
        "mlp_weights",
        18,
    )


def attention_weights_kernel(start, first_ref, attn_in_ref, qkv_grad_ref, mix_ref, *rest):
    out_any, slots, sems = rest[-3:]
    products = [(first_ref, qkv_grad_ref, at) for at in strips(QKV_COLS, OUT_COLS)]
    products += [(attn_in_ref, mix_ref, slice(0, OUT_COLS))]
    write_products(start, products, out_any, slots, sems)


def attention_weights(buffer, columns, start, first, attn_in, qkv_grad, mixture):
    return into_buffer(
        functools.partial(attention_weights_kernel, start),
        buffer,
        columns,
        OUT_COLS,
        (first, attn_in, qkv_grad, mixture),
        2 * first.shape[0] * WIDTH * ATTN_COLS,
        "attention_weights",
        14,
    )


def sum_four(partial, before=None, beside=None):
    keeps, gives = partial[:PARTS], partial[PARTS:]
    chips = [
        (keep.astype(F32) + swap(give, "section").astype(F32)).astype(BF16)
        for keep, give in zip(keeps, gives)
    ]
    if before is not None:
        chips[0], before = lax.optimization_barrier((chips[0], before))
    arrived = [swap(chip, "tensor") for chip in chips]
    if beside is not None:
        arrived[0], beside = lax.optimization_barrier((arrived[0], beside))
    totals = [
        (chip.astype(F32) + other.astype(F32)).astype(BF16)
        for chip, other in zip(chips, arrived)
    ]
    return totals + [swap(total, "section") for total in totals], before, beside


def pack_kernel(core_ref, attn_scale_ref, mlp_scale_ref, *rest):
    sources, (mine_ref, give_ref), shards, sems = rest[:7], rest[7:9], rest[9:16], rest[16]
    copies = [
        pltpu.make_async_copy(source, shard, sems.at[number])
        for number, (source, shard) in enumerate(zip(sources, shards))
    ]
    for copy in copies:
        copy.start()
    is_first = core_ref[0] == 0
    start = 0
    for copy, shard, scale_ref in zip(
        copies,
        shards,
        (mlp_scale_ref, mlp_scale_ref, None, attn_scale_ref, attn_scale_ref, attn_scale_ref, None),
    ):
        copy.wait()
        weight = shard[...]
        if scale_ref is not None:
            weight = (weight.astype(F32) * scale_ref[...]).astype(BF16)
        width = weight.shape[1] // 2
        low, high = weight[:, :width], weight[:, width:]
        mine_ref[:, start : start + width] = jnp.where(is_first, low, high)
        give_ref[:, start : start + width] = jnp.where(is_first, high, low)
        start += width


def pack_shards(core, attn_scale, mlp_scale, *shards):
    return pl.pallas_call(
        pack_kernel,
        in_specs=[smem_whole()] + [vmem_whole()] * 2 + [hbm_whole()] * len(shards),
        out_specs=[vmem_whole()] * 2,
        out_shape=[shape(48, LAYER_COLS, BF16)] * 2,
        scratch_shapes=[pltpu.VMEM(shard.shape, shard.dtype) for shard in shards]
        + [pltpu.SemaphoreType.DMA((len(shards),))],
        compiler_params=params(16),
        name="pack_shards",
    )(core, attn_scale, mlp_scale, *[in_hbm(shard) for shard in shards])


def combine_kernel(core_ref, keep_ref, arrived_ref, last_ref, zero_w_ref, one_w_ref, mine_ref, give_ref, terms_ref, zero, one):
    rest = (keep_ref[...].astype(F32) + arrived_ref[...].astype(F32)).astype(BF16)
    zero[:, :MLP_COLS] = rest[:, :MLP_COLS]
    zero[:, MLP_COLS:] = rest[:, LAYER_COLS:]
    one[:, :MLP_COLS] = last_ref[...]
    one[:, MLP_COLS:] = rest[:, MLP_COLS:LAYER_COLS]
    is_first = core_ref[0] == 0
    mine_ref[...] = jnp.where(is_first, zero[...], one[...])
    give_ref[...] = jnp.where(is_first, one[...], zero[...])
    row = 0
    for grad, weights in ((zero, zero_w_ref), (one, one_w_ref)):
        products = weights[...].astype(F32) * grad[...].astype(F32)
        for columns in (slice(MLP_COLS, MLP_COLS + QKV_COLS), slice(0, 2 * HIDDEN_COLS)):
            terms_ref[row, :] = jnp.sum(products[:, columns], axis=1)
            row += 1


def combine_grads(core, *operands):
    return pl.pallas_call(
        combine_kernel,
        in_specs=[smem_whole()] + [vmem_whole()] * len(operands),
        out_specs=[vmem_whole()] * 3,
        out_shape=[shape(48, LAYER_COLS, BF16)] * 2 + [shape(4, 48, F32)],
        scratch_shapes=[pltpu.VMEM((48, LAYER_COLS), BF16)] * 2,
        compiler_params=params(16),
        name="combine_grads",
    )(core, *operands)


def unpack_kernel(core_ref, attn_scale_ref, mlp_scale_ref, mine_ref, got_ref, gate_ref, up_ref, down_ref, query_ref, key_ref, value_ref, out_ref):
    is_first = core_ref[0] == 0

    def place(out, start, scale_ref):
        width = out.shape[1] // 2
        mine = mine_ref[:, start : start + width].astype(F32)
        got = got_ref[:, start : start + width].astype(F32)
        if scale_ref is not None:
            mine, got = mine * scale_ref[...], got * scale_ref[...]
        out[:, :width] = jnp.where(is_first, mine, got)
        out[:, width:] = jnp.where(is_first, got, mine)

    place(gate_ref, 0, mlp_scale_ref)
    place(up_ref, HIDDEN_COLS, mlp_scale_ref)
    place(down_ref, 2 * HIDDEN_COLS, None)
    place(query_ref, MLP_COLS, attn_scale_ref)
    place(key_ref, MLP_COLS + QUERY_COLS, attn_scale_ref)
    place(value_ref, MLP_COLS + QUERY_COLS + KV_COLS, attn_scale_ref)
    place(out_ref, MLP_COLS + QKV_COLS, None)


def unpack_grads(core, *operands):
    widths = [HIDDEN_COLS] * 3 + [QUERY_COLS, KV_COLS, KV_COLS, OUT_COLS]
    return pl.pallas_call(
        unpack_kernel,
        in_specs=[smem_whole()] + [vmem_whole()] * len(operands),
        out_specs=[vmem_whole()] * len(widths),
        out_shape=[shape(48, 2 * width, F32) for width in widths],
        compiler_params=params(16),
        name="unpack_grads",
    )(core, *operands)


def gather_rows(z_low, share):
    other = swap(share, "zl")
    pair = jnp.concatenate([pick(z_low, share, other), pick(z_low, other, share)], axis=0)
    return lax.all_gather(pair, ("y", "x"), axis=0, tiled=True)


def scatter_pair(grad):
    return lax.psum_scatter(grad, ("y", "x"), scatter_dimension=0, tiled=True)


def scatter_low(z_low, pair):
    keep = pick(z_low, pair[:48], pair[48:])
    give = pick(z_low, pair[48:], pair[:48])
    return (keep.astype(F32) + swap(give, "zl").astype(F32)).astype(BF16)


def to_ring_order(rows):
    lead = rows.shape[:-1]
    return jnp.swapaxes(rows.reshape(lead + (4, 2, 4, 48)), -3, -2).reshape(rows.shape)


def from_ring_order(rows):
    lead = rows.shape[:-1]
    return jnp.swapaxes(rows.reshape(lead + (4, 4, 2, 48)), -3, -2).reshape(rows.shape)


def join_positions(tensor, own):
    other = swap(own, "tensor")
    return jnp.concatenate(
        [pick(tensor, own, other), pick(tensor, other, own)], axis=1
    ).reshape(384, WIDTH)


def own_positions(tensor, rows):
    rows = rows.reshape(3, 128, 1536)
    return pick(tensor, rows[:, :64], rows[:, 64:])


def per_device(
    inputs, cotangent, plan, attn_gain, mlp_gain, w_query, key_weight, value_weight,
    w_out, w_gate, w_up, w_down,
):
    core = lax.axis_index("section")
    z_low = lax.axis_index("zl")
    tensor = lax.axis_index("tensor")

    attn_scale = attn_gain[0].astype(F32)[:, None]
    mlp_scale = mlp_gain[0].astype(F32)[:, None]

    core_ref = core.astype(jnp.int32).reshape(1)
    mine, give = pack_shards(
        core_ref, attn_scale, mlp_scale,
        w_gate[0], w_up[0], w_down[0].T, w_query[0], key_weight[0], value_weight[0], w_out[0].T,
    )
    got = swap(give, "section")
    layer_zero, layer_one = pick(core, mine, got), pick(core, got, mine)
    first_weights = gather_rows(
        z_low, jnp.concatenate([layer_zero, layer_one[:, MLP_COLS:]], axis=1)
    )
    last_weights = gather_rows(z_low, layer_one[:, :MLP_COLS])
    attn_weights = ((first_weights, MLP_COLS), (first_weights, LAYER_COLS))
    mlp_weights_of = (first_weights, last_weights)

    stream = join_positions(tensor, to_ring_order(inputs[:, 0][plan]))
    stream, late = lax.optimization_barrier((stream, cotangent))
    out_grad = join_positions(tensor, to_ring_order(late[:, 0][plan]))
    stream, out_grad = lax.optimization_barrier((stream, out_grad))

    def whole_rows(sums):
        own, other = jnp.concatenate(sums[:PARTS]), jnp.concatenate(sums[PARTS:])
        return jnp.concatenate([pick(core, own, other), pick(core, other, own)], axis=1).astype(F32)

    attn_zero, attn_one = attn_weights
    mlp_zero, mlp_one = mlp_weights_of

    x_zero = stream
    _, first_zero, qkv_zero, prob_zero, mix_zero, *partial = attention_forward(
        core_ref, x_zero, None, None, *attn_zero
    )
    sums, _, _ = sum_four(partial)
    middle_zero, second_zero, gate_zero, up_zero, hidden_zero, *partial = mlp_forward(
        core_ref, x_zero, sums, mlp_zero
    )
    sums, _, _ = sum_four(partial)
    x_one, first_one, qkv_one, prob_one, mix_one, *partial = attention_forward(
        core_ref, None, middle_zero, sums, *attn_one
    )
    sums, _, _ = sum_four(partial)

    middle_one, second_one, hidden_one, pair_grad, *partial = mlp_last(
        core_ref, x_one, sums, out_grad, mlp_one
    )
    one_mlp = mlp_weights(None, MLP_COLS, second_one, out_grad, pair_grad, hidden_one)
    sums, one_mlp, _ = sum_four(partial, before=one_mlp)
    last_pair = scatter_pair(one_mlp)
    middle_grad, attn_in, qkv_grad, *partial = attention_backward(
        core_ref, out_grad, middle_one, sums, qkv_one, prob_one, *attn_one
    )
    buffer = attention_weights(None, REST_COLS, MLP_COLS, first_one, attn_in, qkv_grad, mix_one)
    sums, _, buffer = sum_four(partial, beside=buffer)

    grad_one, pair_grad, *partial = mlp_backward(
        core_ref, (x_one, middle_grad, *sums), gate_zero, up_zero, mlp_zero
    )
    buffer = mlp_weights(buffer, REST_COLS, second_zero, grad_one, pair_grad, hidden_zero)
    sums, _, buffer = sum_four(partial, beside=buffer)
    hidden_one, sums[0] = lax.optimization_barrier((hidden_one, sums[0]))
    down_partial = mlp_down(core_ref, hidden_one, mlp_one)
    middle_grad, attn_in, qkv_grad, *partial = attention_backward(
        core_ref, grad_one, middle_zero, sums, qkv_zero, prob_zero, *attn_zero, near=False
    )
    buffer = attention_weights(
        buffer, REST_COLS, LAYER_COLS, first_zero, attn_in, qkv_grad, mix_zero
    )
    first_give, buffer = lax.optimization_barrier((partial[PARTS], buffer))
    partial = list(partial)
    partial[PARTS] = first_give
    rest_pair = scatter_pair(buffer)
    sums, _, _ = sum_four(partial)
    rows = x_zero.astype(F32)
    grad_zero = middle_grad + norm_back(whole_rows(sums), rows, inverse_norm(rows))
    down_sums, _, _ = sum_four(down_partial)
    result_one = (middle_one + whole_rows(down_sums)).astype(BF16)
    outputs = [own_positions(tensor, x_one), own_positions(tensor, result_one)]
    grads = [own_positions(tensor, grad_zero.astype(BF16)), own_positions(tensor, grad_one)]

    layer_outputs = from_ring_order(pick(core, outputs[0], outputs[1]))
    input_grads = from_ring_order(pick(core, grads[0], grads[1]))
    last_grad = scatter_low(z_low, last_pair)
    rest_pair, layer_outputs, input_grads, last_grad = lax.optimization_barrier(
        (rest_pair, layer_outputs, input_grads, last_grad)
    )
    keep = pick(z_low, rest_pair[:48], rest_pair[48:])
    arrived = swap(pick(z_low, rest_pair[48:], rest_pair[:48]), "zl")
    mine, give, terms = combine_grads(
        core_ref, keep, arrived, last_grad, layer_zero, layer_one
    )
    got = swap(give, "section")
    arrived = swap(terms, "tensor")
    gate_grad, up_grad, down_grad, query_grad, key_grad, value_grad, out_weight_grad = unpack_grads(
        core_ref, attn_scale, mlp_scale, mine, got
    )
    arrived, key_grad = lax.optimization_barrier((arrived, key_grad))
    terms = terms + arrived
    terms = pick(core, terms[:2], terms[2:]) + swap(pick(core, terms[2:], terms[:2]), "section")
    return (
        layer_outputs[None, :, None],
        input_grads[None, :, None],
        (terms[0] / attn_scale[:, 0])[None],
        (terms[1] / mlp_scale[:, 0])[None],
        query_grad[None],
        key_grad[None],
        value_grad[None],
        out_weight_grad.T[None],
        gate_grad[None],
        up_grad[None],
        down_grad.T[None],
    )


def solution(mesh):
    split = Mesh(mesh.devices.reshape(2, 4, 2, 4, 2), ("section", "y", "zl", "x", "tensor"))
    dp = ("y", "zl", "x")
    rows = P("section", dp, "tensor")
    columns = P("section", "tensor", dp)
    return jax.shard_map(
        per_device,
        mesh=split,
        in_specs=(
            P(None, dp, "tensor", None),
            P(None, dp, "tensor", None),
            P(),
            P("section", dp),
            P("section", dp),
            rows,
            rows,
            rows,
            columns,
            rows,
            rows,
            columns,
        ),
        out_specs=(
            P("section", None, dp, "tensor", None),
            P("section", None, dp, "tensor", None),
            P("section", dp),
            P("section", dp),
            rows,
            rows,
            rows,
            columns,
            rows,
            rows,
            columns,
        ),
        check_vma=False,
    )
```

```python
import functools

import jax
import jax.numpy as jnp
from jax import lax
from jax.experimental import pallas as pl
from jax.experimental.pallas import tpu as pltpu
from jax.sharding import Mesh, PartitionSpec as P

HEAD_WIDTH = 96
EPSILON = 1e-05
BLOCKED = -1e30
SCORE_SCALE = HEAD_WIDTH ** (-0.5)
BF16 = jnp.bfloat16
F32 = jnp.float32

QUERY_COLS, KV_COLS = 384, 192
QKV_COLS = QUERY_COLS + 2 * KV_COLS
OUT_COLS = 384
HIDDEN_COLS = 1024
ATTN_COLS = QKV_COLS + OUT_COLS
MLP_COLS = 3 * HIDDEN_COLS
LAYER_COLS = MLP_COLS + ATTN_COLS
REST_COLS = LAYER_COLS + ATTN_COLS
HIDDEN_TILE = 512
MLP_STRIP = 512
AHEAD = 3
WIDTH = 1536
HALF = WIDTH // 2
PARTS = 2
MIB = 1024 * 1024


def swap(value, axis):
    return lax.ppermute(value, axis, [(0, 1), (1, 0)])


def pick(index, first, second):
    return jnp.where(index == 0, first, second)


def norm_back(weighted, residual, inverse):
    scaled = residual * inverse
    return inverse * (weighted - scaled * jnp.mean(weighted * scaled, axis=-1, keepdims=True))


def vmem_whole():
    return pl.BlockSpec(memory_space=pltpu.VMEM)


def smem_whole():
    return pl.BlockSpec(memory_space=pltpu.SMEM)


def shape(rows, columns, dtype):
    return jax.ShapeDtypeStruct((rows, columns), dtype)


def half_of(core_ref, which):
    position = core_ref[0] if which == 0 else 1 - core_ref[0]
    return pl.ds(pl.multiple_of(position * HALF, HALF), HALF)


def nt_dot(left_side, right_side):
    return lax.dot_general(
        left_side, right_side, (((1,), (1,)), ((), ())), preferred_element_type=F32
    )


def tn_dot(left_side, right_side):
    return lax.dot_general(
        left_side, right_side, (((0,), (0,)), ((), ())), preferred_element_type=F32
    )


def nn_dot(left_side, right_side):
    return jnp.dot(left_side, right_side, preferred_element_type=F32)


def row_parts(rows):
    return [slice(rows // PARTS * part, rows // PARTS * (part + 1)) for part in range(PARTS)]


def part_shapes(rows):
    return [shape(rows // PARTS, HALF, BF16)] * (2 * PARTS)


class Outward:
    def __init__(self, sems):
        self.sems, self.copies = sems, []

    def send(self, source, target):
        self.copies.append(pltpu.make_async_copy(source, target, self.sems.at[len(self.copies)]))
        self.copies[-1].start()

    def wait(self):
        for copy in self.copies:
            copy.wait()


def far(array):
    return pltpu.HBM(array.shape, array.dtype)


def each_sum(core_ref, sum_refs):
    rows = sum_refs[0].shape[0] * PARTS
    for which in range(2):
        for part, at in enumerate(row_parts(rows)):
            yield at, half_of(core_ref, which), sum_refs[PARTS * which + part]


def write_partial(core_ref, left_ref, w_ref, columns, outs):
    keeps, gives = outs[:PARTS], outs[PARTS:]
    for which, refs in ((1, gives), (0, keeps)):
        product = nt_dot(left_ref[...], w_ref[half_of(core_ref, which), columns]).astype(BF16)
        for at, ref in zip(row_parts(left_ref.shape[0]), refs):
            ref[...] = product[at]


def params(mib):
    return pltpu.CompilerParams(vmem_limit_bytes=mib * MIB)


def inverse_norm(rows):
    return lax.rsqrt(jnp.mean(rows * rows, axis=-1, keepdims=True) + EPSILON)


def causal_mask():
    row = lax.broadcasted_iota(jnp.int32, (128, 128), 0)
    return row >= lax.broadcasted_iota(jnp.int32, (128, 128), 1)


def two_heads(ref, rows, start):
    return jnp.concatenate(
        [
            ref[rows, start : start + HEAD_WIDTH],
            ref[rows, start + HEAD_WIDTH : start + 2 * HEAD_WIDTH],
        ],
        axis=0,
    )


def attention_weights_copy(w_any, w_ref, sem, column):
    return pltpu.make_async_copy(w_any.at[:, pl.ds(column, ATTN_COLS)], w_ref, sem)


def attention_forward_body(sequences, core_ref, first_ref, w_ref, qkv_ref, prob_ref, mix_ref, *parts):
    qkv_ref[...] = nn_dot(first_ref[...], w_ref[:, :QKV_COLS]).astype(BF16)
    mask = causal_mask()
    mask = jnp.concatenate([mask, mask], axis=0)
    for sequence in range(sequences):
        rows = slice(128 * sequence, 128 * (sequence + 1))
        for group in range(2):
            queries = two_heads(qkv_ref, rows, 2 * HEAD_WIDTH * group)
            key_at = QUERY_COLS + HEAD_WIDTH * group
            value_at = key_at + KV_COLS
            scores = nt_dot(queries, qkv_ref[rows, key_at : key_at + HEAD_WIDTH]) * SCORE_SCALE
            scores = jnp.where(mask, scores, BLOCKED)
            expanded = jnp.exp(scores - jnp.max(scores, axis=-1, keepdims=True))
            probability = expanded / jnp.sum(expanded, axis=-1, keepdims=True)
            prob_ref[2 * sequence + group] = probability
            mixed = nn_dot(
                probability.astype(BF16), qkv_ref[rows, value_at : value_at + HEAD_WIDTH]
            ).astype(BF16)
            at = 2 * HEAD_WIDTH * group
            mix_ref[rows, at : at + HEAD_WIDTH] = mixed[:128]
            mix_ref[rows, at + HEAD_WIDTH : at + 2 * HEAD_WIDTH] = mixed[128:]
    write_partial(core_ref, mix_ref, w_ref, slice(QKV_COLS, ATTN_COLS), parts)


def attention_first_kernel(sequences, column, core_ref, x_ref, w_any, first_ref, *rest):
    outs, w_ref, sem = rest[:-2], rest[-2], rest[-1]
    copy = attention_weights_copy(w_any, w_ref, sem, column)
    copy.start()
    rows = x_ref[...].astype(F32)
    first_ref[...] = (rows * inverse_norm(rows)).astype(BF16)
    copy.wait()
    attention_forward_body(sequences, core_ref, first_ref, w_ref, *outs)


def attention_next_kernel(sequences, column, core_ref, middle_ref, *rest):
    sums, (w_any, x_ref, first_ref) = rest[: 2 * PARTS], rest[2 * PARTS : 2 * PARTS + 3]
    outs, w_ref, sem = rest[2 * PARTS + 3 : -2], rest[-2], rest[-1]
    copy = attention_weights_copy(w_any, w_ref, sem, column)
    copy.start()
    for at, columns, part in each_sum(core_ref, sums):
        x_ref[at, columns] = (middle_ref[at, columns] + part[...].astype(F32)).astype(BF16)
    rows = x_ref[...].astype(F32)
    first_ref[...] = (rows * inverse_norm(rows)).astype(BF16)
    copy.wait()
    attention_forward_body(sequences, core_ref, first_ref, w_ref, *outs)


def in_hbm(value):
    return pltpu.with_memory_space_constraint(value, pltpu.HBM)


def hbm_whole():
    return pl.BlockSpec(memory_space=pltpu.HBM)


def attention_scratch():
    return [pltpu.VMEM((WIDTH, ATTN_COLS), BF16), pltpu.SemaphoreType.DMA(())]


def attention_forward(core, x, middle, sums, weights, column):
    rows = (x if middle is None else middle).shape[0]
    sequences = rows // 128
    outs = [
        shape(rows, WIDTH, BF16),
        shape(rows, QKV_COLS, BF16),
        jax.ShapeDtypeStruct((2 * sequences, 256, 128), F32),
        shape(rows, OUT_COLS, BF16),
    ] + part_shapes(rows)
    if middle is None:
        operands, kernel = (core, x), attention_first_kernel
    else:
        operands, kernel = (core, middle, *sums), attention_next_kernel
        outs = [shape(rows, WIDTH, BF16)] + outs
    results = pl.pallas_call(
        functools.partial(kernel, sequences, column),
        in_specs=[smem_whole()] + [vmem_whole()] * (len(operands) - 1) + [hbm_whole()],
        out_specs=[vmem_whole()] * len(outs),
        out_shape=outs,
        scratch_shapes=attention_scratch(),
        compiler_params=params(20),
        cost_estimate=pl.CostEstimate(
            flops=2 * rows * WIDTH * ATTN_COLS, bytes_accessed=8_000_000, transcendentals=0
        ),
        name="attention_forward",
    )(*operands, in_hbm(weights))
    return ([x] if middle is None else []) + list(results)


def column_tiles(first):
    return [pl.ds(first + HIDDEN_TILE * step, HIDDEN_TILE) for step in range(HIDDEN_STEPS)]


def weight_copies(w_any, w_ref, sems, regions):
    return [
        pltpu.make_async_copy(w_any.at[rows, columns], w_ref.at[rows, columns], sems.at[number])
        for number, (rows, columns) in enumerate(regions)
    ]


def sigmoid(values):
    return 0.5 * jnp.tanh(0.5 * values) + 0.5


def arrivals(copies):
    for copy in copies[:AHEAD]:
        copy.start()
    place = iter(range(len(copies)))

    def arrive():
        number = next(place)
        copies[number].wait()
        if number + AHEAD < len(copies):
            copies[number + AHEAD].start()

    return arrive


def mlp_forward_kernel(core_ref, x_ref, *rest):
    sums, (w_any, middle_any, second_any, gate_any, up_any, hidden_any) = rest[: 2 * PARTS], rest[2 * PARTS : 2 * PARTS + 6]
    outs = rest[2 * PARTS + 6 : -8]
    w_ref, middle_ref, second_ref, gate_ref, up_ref, hidden_ref, sems, out_sems = rest[-8:]
    whole = pl.ds(0, WIDTH)
    tiles = [(gate, up) for gate, up in zip(column_tiles(0), column_tiles(HIDDEN_COLS))]
    down = pl.ds(2 * HIDDEN_COLS, HIDDEN_COLS)
    regions = [(whole, columns) for pair in tiles for columns in pair]
    regions.append((whole, down))
    arrive = arrivals(weight_copies(w_any, w_ref, sems, regions))
    for at, columns, part in each_sum(core_ref, sums):
        middle_ref[at, columns] = x_ref[at, columns].astype(F32) + part[...].astype(F32)
    rows = middle_ref[...]
    second_ref[...] = (rows * inverse_norm(rows)).astype(BF16)
    outward = Outward(out_sems)
    outward.send(middle_ref, middle_any)
    outward.send(second_ref, second_any)
    for step, (gate, up) in enumerate(tiles):
        at = slice(HIDDEN_TILE * step, HIDDEN_TILE * (step + 1))
        arrive()
        gate_out = nn_dot(second_ref[...], w_ref[:, gate])
        arrive()
        up_out = nn_dot(second_ref[...], w_ref[:, up])
        gate_ref[:, at] = gate_out
        up_ref[:, at] = up_out
        hidden_ref[:, at] = (gate_out * sigmoid(gate_out) * up_out).astype(BF16)
    outward.send(gate_ref, gate_any)
    outward.send(up_ref, up_any)
    outward.send(hidden_ref, hidden_any)
    arrive()
    write_partial(core_ref, hidden_ref, w_ref, down, outs)
    outward.wait()


HIDDEN_STEPS = HIDDEN_COLS // HIDDEN_TILE


def mlp_scratch():
    return [pltpu.VMEM((WIDTH, MLP_COLS), BF16), pltpu.SemaphoreType.DMA((2 * HIDDEN_STEPS + 1,))]


def mlp_forward(core, x, sums, weights):
    rows = x.shape[0]
    saved = [
        shape(rows, WIDTH, F32),
        shape(rows, WIDTH, BF16),
        shape(rows, HIDDEN_COLS, F32),
        shape(rows, HIDDEN_COLS, F32),
        shape(rows, HIDDEN_COLS, BF16),
    ]
    return pl.pallas_call(
        mlp_forward_kernel,
        in_specs=[smem_whole()] + [vmem_whole()] * (1 + 2 * PARTS) + [hbm_whole()],
        out_specs=[hbm_whole()] * 5 + [vmem_whole()] * (2 * PARTS),
        out_shape=[far(array) for array in saved] + part_shapes(rows),
        scratch_shapes=mlp_scratch()[:1]
        + [pltpu.VMEM(out.shape, out.dtype) for out in saved]
        + mlp_scratch()[1:]
        + [pltpu.SemaphoreType.DMA((5,))],
        compiler_params=params(24),
        cost_estimate=pl.CostEstimate(
            flops=2 * rows * WIDTH * MLP_COLS, bytes_accessed=15_000_000, transcendentals=0
        ),
        name="mlp_forward",
    )(core, x, *sums, in_hbm(weights))


def mlp_backward_tiles(g_ref, gate_ref, up_ref, arrive, pair_grad_ref, w_ref):
    for step, down in enumerate(column_tiles(2 * HIDDEN_COLS)):
        at = slice(HIDDEN_TILE * step, HIDDEN_TILE * (step + 1))
        up_at = slice(HIDDEN_COLS + at.start, HIDDEN_COLS + at.stop)
        arrive()
        hidden_grad = nn_dot(g_ref[...], w_ref[:, down])
        gate_out = gate_ref[:, at]
        sigmoid_gate = sigmoid(gate_out)
        pair_grad_ref[:, at] = (
            hidden_grad
            * up_ref[:, at]
            * (sigmoid_gate * (1.0 + gate_out * (1.0 - sigmoid_gate)))
        ).astype(BF16)
        pair_grad_ref[:, up_at] = (hidden_grad * (gate_out * sigmoid_gate)).astype(BF16)


def mlp_backward_copies(w_any, w_ref, sems):
    regions = [(pl.ds(0, WIDTH), columns) for columns in column_tiles(2 * HIDDEN_COLS)]
    regions.append((pl.ds(0, WIDTH), pl.ds(0, 2 * HIDDEN_COLS)))
    return arrivals(weight_copies(w_any, w_ref, sems, regions))


def mlp_backward_kernel(core_ref, x_ref, middle_grad_ref, *rest):
    sums, (gate_ref, up_ref, w_any, g_ref, pair_grad_ref) = rest[: 2 * PARTS], rest[2 * PARTS : 2 * PARTS + 5]
    outs, (w_ref, sems, weighted) = rest[2 * PARTS + 5 : -3], rest[-3:]
    arrive = mlp_backward_copies(w_any, w_ref, sems)
    for at, columns, part in each_sum(core_ref, sums):
        weighted[at, columns] = part[...].astype(F32)
    rows = x_ref[...].astype(F32)
    g_ref[...] = (
        middle_grad_ref[...] + norm_back(weighted[...], rows, inverse_norm(rows))
    ).astype(BF16)
    mlp_backward_tiles(g_ref, gate_ref, up_ref, arrive, pair_grad_ref, w_ref)
    arrive()
    write_partial(core_ref, pair_grad_ref, w_ref, slice(0, 2 * HIDDEN_COLS), outs)


def mlp_backward(core, above, gate_out, up_out, weights):
    rows = gate_out.shape[0]
    return pl.pallas_call(
        mlp_backward_kernel,
        in_specs=[smem_whole()] + [vmem_whole()] * (4 + 2 * PARTS) + [hbm_whole()],
        out_specs=[vmem_whole()] * (2 + 2 * PARTS),
        out_shape=[shape(rows, WIDTH, BF16), shape(rows, 2 * HIDDEN_COLS, BF16)] + part_shapes(rows),
        scratch_shapes=mlp_scratch() + [pltpu.VMEM((rows, WIDTH), F32)],
        compiler_params=params(24),
        cost_estimate=pl.CostEstimate(
            flops=2 * rows * WIDTH * MLP_COLS, bytes_accessed=15_000_000, transcendentals=0
        ),
        name="mlp_backward",
    )(core, *above, gate_out, up_out, in_hbm(weights))


def mlp_last_kernel(core_ref, x_ref, *rest):
    sums, (g_ref, w_any, middle_any, hidden_any, second_ref, hidden_ref, pair_grad_ref) = rest[: 2 * PARTS], rest[2 * PARTS : 2 * PARTS + 7]
    outs = rest[2 * PARTS + 7 : -6]
    w_ref, middle_ref, gate_ref, up_ref, sems, out_sems = rest[-6:]
    whole = pl.ds(0, WIDTH)
    tiles = [(gate, up) for gate, up in zip(column_tiles(0), column_tiles(HIDDEN_COLS))]
    regions = [(whole, columns) for pair in tiles for columns in pair]
    regions += [(whole, columns) for columns in column_tiles(2 * HIDDEN_COLS)]
    arrive = arrivals(weight_copies(w_any, w_ref, sems, regions))
    for at, columns, part in each_sum(core_ref, sums):
        middle_ref[at, columns] = x_ref[at, columns].astype(F32) + part[...].astype(F32)
    rows = middle_ref[...]
    second_ref[...] = (rows * inverse_norm(rows)).astype(BF16)
    outward = Outward(out_sems)
    outward.send(middle_ref, middle_any)
    for step, (gate, up) in enumerate(tiles):
        at = slice(HIDDEN_TILE * step, HIDDEN_TILE * (step + 1))
        arrive()
        gate_out = nn_dot(second_ref[...], w_ref[:, gate])
        arrive()
        up_out = nn_dot(second_ref[...], w_ref[:, up])
        gate_ref[:, at] = gate_out
        up_ref[:, at] = up_out
        hidden_ref[:, at] = (gate_out * sigmoid(gate_out) * up_out).astype(BF16)
    outward.send(hidden_ref, hidden_any)
    mlp_backward_tiles(g_ref, gate_ref, up_ref, arrive, pair_grad_ref, w_ref)
    write_partial(core_ref, pair_grad_ref, w_ref, slice(0, 2 * HIDDEN_COLS), outs)
    outward.wait()


def mlp_last(core, x, sums, g, weights):
    rows = x.shape[0]
    inner = [shape(rows, WIDTH, F32)] + [shape(rows, HIDDEN_COLS, F32)] * 2
    return pl.pallas_call(
        mlp_last_kernel,
        in_specs=[smem_whole()] + [vmem_whole()] * (2 + 2 * PARTS) + [hbm_whole()],
        out_specs=[hbm_whole()] * 2 + [vmem_whole()] * (3 + 2 * PARTS),
        out_shape=[
            pltpu.HBM((rows, WIDTH), F32),
            pltpu.HBM((rows, HIDDEN_COLS), BF16),
            shape(rows, WIDTH, BF16),
            shape(rows, HIDDEN_COLS, BF16),
            shape(rows, 2 * HIDDEN_COLS, BF16),
        ]
        + part_shapes(rows),
        scratch_shapes=mlp_scratch()[:1]
        + [pltpu.VMEM(array.shape, array.dtype) for array in inner]
        + [
            pltpu.SemaphoreType.DMA((3 * HIDDEN_STEPS,)),
            pltpu.SemaphoreType.DMA((2,)),
        ],
        compiler_params=params(24),
        cost_estimate=pl.CostEstimate(
            flops=4 * rows * WIDTH * MLP_COLS, bytes_accessed=15_000_000, transcendentals=0
        ),
        name="mlp_last",
    )(core, x, *sums, g, in_hbm(weights))


def mlp_down_kernel(core_ref, hidden_ref, w_any, *rest):
    outs, w_ref, sem = rest[:-2], rest[-2], rest[-1]
    copy = pltpu.make_async_copy(w_any.at[:, pl.ds(2 * HIDDEN_COLS, HIDDEN_COLS)], w_ref, sem)
    copy.start()
    copy.wait()
    write_partial(core_ref, hidden_ref, w_ref, slice(0, HIDDEN_COLS), outs)


def mlp_down(core, hidden, weights):
    rows = hidden.shape[0]
    return pl.pallas_call(
        mlp_down_kernel,
        in_specs=[smem_whole(), vmem_whole(), hbm_whole()],
        out_specs=[vmem_whole()] * (2 * PARTS),
        out_shape=part_shapes(rows),
        scratch_shapes=[pltpu.VMEM((WIDTH, HIDDEN_COLS), BF16), pltpu.SemaphoreType.DMA(())],
        compiler_params=params(14),
        cost_estimate=pl.CostEstimate(
            flops=2 * rows * WIDTH * HIDDEN_COLS, bytes_accessed=5_000_000, transcendentals=0
        ),
        name="mlp_down",
    )(core, hidden, in_hbm(weights))


def attention_backward_kernel(sequences, column, near, core_ref, g_ref, middle_ref, *rest):
    sums, rest = rest[: 2 * PARTS], rest[2 * PARTS :]
    (qkv_any, prob_any, w_any, middle_grad_out, attn_in_ref, qkv_grad_ref), rest = rest[:6], rest[6:]
    outs, (middle_grad_ref, qkv_ref, prob_ref, mix_grad, w_ref, sem, sems) = rest[:-7], rest[-7:]
    copies = [
        attention_weights_copy(w_any, w_ref, sem, column),
        pltpu.make_async_copy(qkv_any, qkv_ref, sems.at[0]),
        pltpu.make_async_copy(prob_any, prob_ref, sems.at[1]),
    ]
    for copy in copies:
        copy.start()
    for at, columns, part in each_sum(core_ref, sums):
        middle_grad_ref[at, columns] = part[...].astype(F32)
    middle = middle_ref[...]
    middle_grad = g_ref[...].astype(F32) + norm_back(
        middle_grad_ref[...], middle, inverse_norm(middle)
    )
    if near:
        middle_grad_out[...] = middle_grad
    else:
        middle_grad_ref[...] = middle_grad
        outward = pltpu.make_async_copy(middle_grad_ref, middle_grad_out, sems.at[2])
        outward.start()
    attn_in_ref[...] = middle_grad.astype(BF16)
    copies[0].wait()
    mix_grad[...] = nn_dot(attn_in_ref[...], w_ref[:, QKV_COLS:]).astype(BF16)
    for copy in copies[1:]:
        copy.wait()
    for sequence in range(sequences):
        rows = slice(128 * sequence, 128 * (sequence + 1))
        for group in range(2):
            at = 2 * HEAD_WIDTH * group
            key_at = QUERY_COLS + HEAD_WIDTH * group
            value_at = key_at + KV_COLS
            grads = two_heads(mix_grad, rows, at)
            queries = two_heads(qkv_ref, rows, at)
            keys = qkv_ref[rows, key_at : key_at + HEAD_WIDTH]
            probability = prob_ref[2 * sequence + group]
            prob_grad = nt_dot(grads, qkv_ref[rows, value_at : value_at + HEAD_WIDTH])
            centred = jnp.sum(probability * prob_grad, axis=-1, keepdims=True)
            score_grad = (probability * (prob_grad - centred)).astype(BF16)
            query_grad = (nn_dot(score_grad, keys) * SCORE_SCALE).astype(BF16)
            qkv_grad_ref[rows, at : at + HEAD_WIDTH] = query_grad[:128]
            qkv_grad_ref[rows, at + HEAD_WIDTH : at + 2 * HEAD_WIDTH] = query_grad[128:]
            qkv_grad_ref[rows, key_at : key_at + HEAD_WIDTH] = (
                tn_dot(score_grad, queries) * SCORE_SCALE
            ).astype(BF16)
            qkv_grad_ref[rows, value_at : value_at + HEAD_WIDTH] = tn_dot(
                probability.astype(BF16), grads
            ).astype(BF16)
    write_partial(core_ref, qkv_grad_ref, w_ref, slice(0, QKV_COLS), outs)
    if not near:
        outward.wait()


def attention_backward(core, g, middle, sums, qkv, probability, weights, column, near=True):
    rows = g.shape[0]
    residual, parts = shape(rows, WIDTH, F32), part_shapes(rows)
    return pl.pallas_call(
        functools.partial(attention_backward_kernel, rows // 128, column, near),
        in_specs=[smem_whole()] + [vmem_whole()] * (2 + 2 * PARTS) + [hbm_whole()] * 3,
        out_specs=[vmem_whole() if near else hbm_whole()] + [vmem_whole()] * (2 + 2 * PARTS),
        out_shape=[
            residual if near else far(residual),
            shape(rows, WIDTH, BF16),
            shape(rows, QKV_COLS, BF16),
        ]
        + [part if near else far(part) for part in parts],
        scratch_shapes=[
            pltpu.VMEM((rows, WIDTH), F32),
            pltpu.VMEM(qkv.shape, BF16),
            pltpu.VMEM(probability.shape, F32),
            pltpu.VMEM((rows, OUT_COLS), BF16),
        ]
        + attention_scratch()
        + [pltpu.SemaphoreType.DMA((3,))],
        compiler_params=params(24),
        cost_estimate=pl.CostEstimate(
            flops=2 * rows * WIDTH * ATTN_COLS, bytes_accessed=12_000_000, transcendentals=0
        ),
        name="attention_backward",
    )(core, g, middle, *sums, in_hbm(qkv), in_hbm(probability), in_hbm(weights))


def write_products(start, products, out_any, slots, sems):
    copies = []
    for number, (left, right, columns) in enumerate(products):
        width = columns.stop - columns.start
        if number >= 2:
            copies[number - 2].wait()
        slot = slots.at[number % 2]
        slot[...] = tn_dot(left[...], right[:, columns]).astype(BF16)
        target = out_any.at[:, pl.ds(start, width)]
        copies.append(pltpu.make_async_copy(slot, target, sems.at[number % 2]))
        copies[-1].start()
        start += width
    for copy in copies[-2:]:
        copy.wait()


def strips(columns, width):
    return [slice(at, at + width) for at in range(0, columns, width)]


def mlp_weights_kernel(second_ref, g_ref, pair_grad_ref, hidden_ref, *rest):
    out_any, slots, sems = rest[-3:]
    products = [(second_ref, pair_grad_ref, at) for at in strips(2 * HIDDEN_COLS, MLP_STRIP)]
    products += [(g_ref, hidden_ref, at) for at in strips(HIDDEN_COLS, MLP_STRIP)]
    write_products(0, products, out_any, slots, sems)


def into_buffer(kernel, buffer, columns, strip, operands, flops, name, mib):
    aliases, specs = {}, [vmem_whole()] * len(operands)
    if buffer is not None:
        aliases = {len(operands): 0}
        specs, operands = specs + [hbm_whole()], operands + (in_hbm(buffer),)
    return pl.pallas_call(
        kernel,
        in_specs=specs,
        out_specs=hbm_whole(),
        out_shape=pltpu.HBM((WIDTH, columns), BF16),
        input_output_aliases=aliases,
        scratch_shapes=[pltpu.VMEM((2, WIDTH, strip), BF16), pltpu.SemaphoreType.DMA((2,))],
        compiler_params=params(mib),
        cost_estimate=pl.CostEstimate(flops=flops, bytes_accessed=flops // 250, transcendentals=0),
        name=name,
    )(*operands)


def mlp_weights(buffer, columns, second, g, pair_grad, hidden):
    return into_buffer(
        mlp_weights_kernel,
        buffer,
        columns,
        MLP_STRIP,
        (second, g, pair_grad, hidden),
        2 * second.shape[0] * WIDTH * MLP_COLS,
        "mlp_weights",
        14,
    )


def attention_weights_kernel(start, first_ref, attn_in_ref, qkv_grad_ref, mix_ref, *rest):
    out_any, slots, sems = rest[-3:]
    products = [(first_ref, qkv_grad_ref, at) for at in strips(QKV_COLS, OUT_COLS)]
    products += [(attn_in_ref, mix_ref, slice(0, OUT_COLS))]
    write_products(start, products, out_any, slots, sems)


def attention_weights(buffer, columns, start, first, attn_in, qkv_grad, mixture):
    return into_buffer(
        functools.partial(attention_weights_kernel, start),
        buffer,
        columns,
        OUT_COLS,
        (first, attn_in, qkv_grad, mixture),
        2 * first.shape[0] * WIDTH * ATTN_COLS,
        "attention_weights",
        14,
    )


def sum_four(partial, before=None, beside=None):
    keeps, gives = partial[:PARTS], partial[PARTS:]
    chips = [
        (keep.astype(F32) + swap(give, "section").astype(F32)).astype(BF16)
        for keep, give in zip(keeps, gives)
    ]
    if before is not None:
        chips[0], before = lax.optimization_barrier((chips[0], before))
    arrived = [swap(chip, "tensor") for chip in chips]
    if beside is not None:
        arrived[0], beside = lax.optimization_barrier((arrived[0], beside))
    totals = [
        (chip.astype(F32) + other.astype(F32)).astype(BF16)
        for chip, other in zip(chips, arrived)
    ]
    return totals + [swap(total, "section") for total in totals], before, beside


def pack_kernel(core_ref, attn_scale_ref, mlp_scale_ref, *rest):
    sources, (mine_ref, give_ref), shards, sems = rest[:7], rest[7:9], rest[9:16], rest[16]
    copies = [
        pltpu.make_async_copy(source, shard, sems.at[number])
        for number, (source, shard) in enumerate(zip(sources, shards))
    ]
    for copy in copies:
        copy.start()
    is_first = core_ref[0] == 0
    start = 0
    for copy, shard, scale_ref in zip(
        copies,
        shards,
        (mlp_scale_ref, mlp_scale_ref, None, attn_scale_ref, attn_scale_ref, attn_scale_ref, None),
    ):
        copy.wait()
        weight = shard[...]
        if scale_ref is not None:
            weight = (weight.astype(F32) * scale_ref[...]).astype(BF16)
        width = weight.shape[1] // 2
        low, high = weight[:, :width], weight[:, width:]
        mine_ref[:, start : start + width] = jnp.where(is_first, low, high)
        give_ref[:, start : start + width] = jnp.where(is_first, high, low)
        start += width


def pack_shards(core, attn_scale, mlp_scale, *shards):
    return pl.pallas_call(
        pack_kernel,
        in_specs=[smem_whole()] + [vmem_whole()] * 2 + [hbm_whole()] * len(shards),
        out_specs=[vmem_whole()] * 2,
        out_shape=[shape(48, LAYER_COLS, BF16)] * 2,
        scratch_shapes=[pltpu.VMEM(shard.shape, shard.dtype) for shard in shards]
        + [pltpu.SemaphoreType.DMA((len(shards),))],
        compiler_params=params(16),
        name="pack_shards",
    )(core, attn_scale, mlp_scale, *[in_hbm(shard) for shard in shards])


def combine_kernel(core_ref, keep_ref, arrived_ref, last_ref, zero_w_ref, one_w_ref, mine_ref, give_ref, terms_ref, zero, one):
    rest = (keep_ref[...].astype(F32) + arrived_ref[...].astype(F32)).astype(BF16)
    zero[:, :MLP_COLS] = rest[:, :MLP_COLS]
    zero[:, MLP_COLS:] = rest[:, LAYER_COLS:]
    one[:, :MLP_COLS] = last_ref[...]
    one[:, MLP_COLS:] = rest[:, MLP_COLS:LAYER_COLS]
    is_first = core_ref[0] == 0
    mine_ref[...] = jnp.where(is_first, zero[...], one[...])
    give_ref[...] = jnp.where(is_first, one[...], zero[...])
    row = 0
    for grad, weights in ((zero, zero_w_ref), (one, one_w_ref)):
        products = weights[...].astype(F32) * grad[...].astype(F32)
        for columns in (slice(MLP_COLS, MLP_COLS + QKV_COLS), slice(0, 2 * HIDDEN_COLS)):
            terms_ref[row, :] = jnp.sum(products[:, columns], axis=1)
            row += 1


def combine_grads(core, *operands):
    return pl.pallas_call(
        combine_kernel,
        in_specs=[smem_whole()] + [vmem_whole()] * len(operands),
        out_specs=[vmem_whole()] * 3,
        out_shape=[shape(48, LAYER_COLS, BF16)] * 2 + [shape(4, 48, F32)],
        scratch_shapes=[pltpu.VMEM((48, LAYER_COLS), BF16)] * 2,
        compiler_params=params(16),
        name="combine_grads",
    )(core, *operands)


def unpack_kernel(core_ref, attn_scale_ref, mlp_scale_ref, mine_ref, got_ref, gate_ref, up_ref, down_ref, query_ref, key_ref, value_ref, out_ref):
    is_first = core_ref[0] == 0

    def place(out, start, scale_ref):
        width = out.shape[1] // 2
        mine = mine_ref[:, start : start + width].astype(F32)
        got = got_ref[:, start : start + width].astype(F32)
        if scale_ref is not None:
            mine, got = mine * scale_ref[...], got * scale_ref[...]
        out[:, :width] = jnp.where(is_first, mine, got)
        out[:, width:] = jnp.where(is_first, got, mine)

    place(gate_ref, 0, mlp_scale_ref)
    place(up_ref, HIDDEN_COLS, mlp_scale_ref)
    place(down_ref, 2 * HIDDEN_COLS, None)
    place(query_ref, MLP_COLS, attn_scale_ref)
    place(key_ref, MLP_COLS + QUERY_COLS, attn_scale_ref)
    place(value_ref, MLP_COLS + QUERY_COLS + KV_COLS, attn_scale_ref)
    place(out_ref, MLP_COLS + QKV_COLS, None)


def unpack_grads(core, *operands):
    widths = [HIDDEN_COLS] * 3 + [QUERY_COLS, KV_COLS, KV_COLS, OUT_COLS]
    return pl.pallas_call(
        unpack_kernel,
        in_specs=[smem_whole()] + [vmem_whole()] * len(operands),
        out_specs=[vmem_whole()] * len(widths),
        out_shape=[shape(48, 2 * width, F32) for width in widths],
        compiler_params=params(16),
        name="unpack_grads",
    )(core, *operands)


def gather_rows(z_low, share):
    other = swap(share, "zl")
    pair = jnp.concatenate([pick(z_low, share, other), pick(z_low, other, share)], axis=0)
    return lax.all_gather(pair, ("y", "x"), axis=0, tiled=True)


def scatter_pair(grad):
    return lax.psum_scatter(grad, ("y", "x"), scatter_dimension=0, tiled=True)


def scatter_low(z_low, pair):
    keep = pick(z_low, pair[:48], pair[48:])
    give = pick(z_low, pair[48:], pair[:48])
    return (keep.astype(F32) + swap(give, "zl").astype(F32)).astype(BF16)


def to_ring_order(rows):
    lead = rows.shape[:-1]
    return jnp.swapaxes(rows.reshape(lead + (4, 2, 4, 48)), -3, -2).reshape(rows.shape)


def from_ring_order(rows):
    lead = rows.shape[:-1]
    return jnp.swapaxes(rows.reshape(lead + (4, 4, 2, 48)), -3, -2).reshape(rows.shape)


def join_positions(tensor, own):
    other = swap(own, "tensor")
    return jnp.concatenate(
        [pick(tensor, own, other), pick(tensor, other, own)], axis=1
    ).reshape(384, WIDTH)


def own_positions(tensor, rows):
    rows = rows.reshape(3, 128, 1536)
    return pick(tensor, rows[:, :64], rows[:, 64:])


def per_device(
    inputs, cotangent, plan, attn_gain, mlp_gain, w_query, key_weight, value_weight,
    w_out, w_gate, w_up, w_down,
):
    core = lax.axis_index("section")
    z_low = lax.axis_index("zl")
    tensor = lax.axis_index("tensor")

    attn_scale = attn_gain[0].astype(F32)[:, None]
    mlp_scale = mlp_gain[0].astype(F32)[:, None]

    core_ref = core.astype(jnp.int32).reshape(1)
    mine, give = pack_shards(
        core_ref, attn_scale, mlp_scale,
        w_gate[0], w_up[0], w_down[0].T, w_query[0], key_weight[0], value_weight[0], w_out[0].T,
    )
    got = swap(give, "section")
    layer_zero, layer_one = pick(core, mine, got), pick(core, got, mine)
    first_weights = gather_rows(
        z_low, jnp.concatenate([layer_zero, layer_one[:, MLP_COLS:]], axis=1)
    )
    last_weights = gather_rows(z_low, layer_one[:, :MLP_COLS])
    attn_weights = ((first_weights, MLP_COLS), (first_weights, LAYER_COLS))
    mlp_weights_of = (first_weights, last_weights)

    stream = join_positions(tensor, to_ring_order(inputs[:, 0][plan]))
    stream, late = lax.optimization_barrier((stream, cotangent))
    out_grad = join_positions(tensor, to_ring_order(late[:, 0][plan]))
    stream, out_grad = lax.optimization_barrier((stream, out_grad))

    def whole_rows(sums):
        own, other = jnp.concatenate(sums[:PARTS]), jnp.concatenate(sums[PARTS:])
        return jnp.concatenate([pick(core, own, other), pick(core, other, own)], axis=1).astype(F32)

    attn_zero, attn_one = attn_weights
    mlp_zero, mlp_one = mlp_weights_of

    x_zero = stream
    _, first_zero, qkv_zero, prob_zero, mix_zero, *partial = attention_forward(
        core_ref, x_zero, None, None, *attn_zero
    )
    sums, _, _ = sum_four(partial)
    middle_zero, second_zero, gate_zero, up_zero, hidden_zero, *partial = mlp_forward(
        core_ref, x_zero, sums, mlp_zero
    )
    sums, _, _ = sum_four(partial)
    x_one, first_one, qkv_one, prob_one, mix_one, *partial = attention_forward(
        core_ref, None, middle_zero, sums, *attn_one
    )
    sums, _, _ = sum_four(partial)

    middle_one, hidden_far, second_one, hidden_one, pair_grad, *partial = mlp_last(
        core_ref, x_one, sums, out_grad, mlp_one
    )
    one_mlp = mlp_weights(None, MLP_COLS, second_one, out_grad, pair_grad, hidden_one)
    sums, one_mlp, _ = sum_four(partial, before=one_mlp)
    last_pair = scatter_pair(one_mlp)
    middle_grad, attn_in, qkv_grad, *partial = attention_backward(
        core_ref, out_grad, middle_one, sums, qkv_one, prob_one, *attn_one
    )
    buffer = attention_weights(None, REST_COLS, MLP_COLS, first_one, attn_in, qkv_grad, mix_one)
    sums, _, buffer = sum_four(partial, beside=buffer)

    grad_one, pair_grad, *partial = mlp_backward(
        core_ref, (x_one, middle_grad, *sums), gate_zero, up_zero, mlp_zero
    )
    buffer = mlp_weights(buffer, REST_COLS, second_zero, grad_one, pair_grad, hidden_zero)
    sums, _, buffer = sum_four(partial, beside=buffer)
    hidden_far, sums[0] = lax.optimization_barrier((hidden_far, sums[0]))
    down_partial = mlp_down(core_ref, hidden_far, mlp_one)
    middle_grad, attn_in, qkv_grad, *partial = attention_backward(
        core_ref, grad_one, middle_zero, sums, qkv_zero, prob_zero, *attn_zero, near=False
    )
    buffer = attention_weights(
        buffer, REST_COLS, LAYER_COLS, first_zero, attn_in, qkv_grad, mix_zero
    )
    first_give, buffer = lax.optimization_barrier((partial[PARTS], buffer))
    partial = list(partial)
    partial[PARTS] = first_give
    rest_pair = scatter_pair(buffer)
    sums, _, _ = sum_four(partial)
    rows = x_zero.astype(F32)
    grad_zero = middle_grad + norm_back(whole_rows(sums), rows, inverse_norm(rows))
    down_sums, _, _ = sum_four(down_partial)
    result_one = (middle_one + whole_rows(down_sums)).astype(BF16)
    outputs = [own_positions(tensor, x_one), own_positions(tensor, result_one)]
    grads = [own_positions(tensor, grad_zero.astype(BF16)), own_positions(tensor, grad_one)]

    layer_outputs = from_ring_order(pick(core, outputs[0], outputs[1]))
    input_grads = from_ring_order(pick(core, grads[0], grads[1]))
    last_grad = scatter_low(z_low, last_pair)
    rest_pair, layer_outputs, input_grads, last_grad = lax.optimization_barrier(
        (rest_pair, layer_outputs, input_grads, last_grad)
    )
    keep = pick(z_low, rest_pair[:48], rest_pair[48:])
    arrived = swap(pick(z_low, rest_pair[48:], rest_pair[:48]), "zl")
    mine, give, terms = combine_grads(
        core_ref, keep, arrived, last_grad, layer_zero, layer_one
    )
    got = swap(give, "section")
    arrived = swap(terms, "tensor")
    gate_grad, up_grad, down_grad, query_grad, key_grad, value_grad, out_weight_grad = unpack_grads(
        core_ref, attn_scale, mlp_scale, mine, got
    )
    arrived, key_grad = lax.optimization_barrier((arrived, key_grad))
    terms = terms + arrived
    terms = pick(core, terms[:2], terms[2:]) + swap(pick(core, terms[2:], terms[:2]), "section")
    return (
        layer_outputs[None, :, None],
        input_grads[None, :, None],
        (terms[0] / attn_scale[:, 0])[None],
        (terms[1] / mlp_scale[:, 0])[None],
        query_grad[None],
        key_grad[None],
        value_grad[None],
        out_weight_grad.T[None],
        gate_grad[None],
        up_grad[None],
        down_grad.T[None],
    )


def solution(mesh):
    split = Mesh(mesh.devices.reshape(2, 4, 2, 4, 2), ("section", "y", "zl", "x", "tensor"))
    dp = ("y", "zl", "x")
    rows = P("section", dp, "tensor")
    columns = P("section", "tensor", dp)
    return jax.shard_map(
        per_device,
        mesh=split,
        in_specs=(
            P(None, dp, "tensor", None),
            P(None, dp, "tensor", None),
            P(),
            P("section", dp),
            P("section", dp),
            rows,
            rows,
            rows,
            columns,
            rows,
            rows,
            columns,
        ),
        out_specs=(
            P("section", None, dp, "tensor", None),
            P("section", None, dp, "tensor", None),
            P("section", dp),
            P("section", dp),
            rows,
            rows,
            rows,
            columns,
            rows,
            rows,
            columns,
        ),
        check_vma=False,
    )
```

```python
import functools

import jax
import jax.numpy as jnp
from jax import lax
from jax.experimental import pallas as pl
from jax.experimental.pallas import tpu as pltpu
from jax.sharding import Mesh, PartitionSpec as P

HEAD_WIDTH = 96
EPSILON = 1e-05
BLOCKED = -1e30
SCORE_SCALE = HEAD_WIDTH ** (-0.5)
BF16 = jnp.bfloat16
F32 = jnp.float32

QUERY_COLS, KV_COLS = 384, 192
QKV_COLS = QUERY_COLS + 2 * KV_COLS
OUT_COLS = 384
HIDDEN_COLS = 1024
ATTN_COLS = QKV_COLS + OUT_COLS
MLP_COLS = 3 * HIDDEN_COLS
LAYER_COLS = MLP_COLS + ATTN_COLS
REST_COLS = LAYER_COLS + ATTN_COLS
HIDDEN_TILE = 512
AHEAD = 3
WIDTH = 1536
HALF = WIDTH // 2
PARTS = 2
MIB = 1024 * 1024


def swap(value, axis):
    return lax.ppermute(value, axis, [(0, 1), (1, 0)])


def pick(index, first, second):
    return jnp.where(index == 0, first, second)


def norm_back(weighted, residual, inverse):
    scaled = residual * inverse
    return inverse * (weighted - scaled * jnp.mean(weighted * scaled, axis=-1, keepdims=True))


def vmem_whole():
    return pl.BlockSpec(memory_space=pltpu.VMEM)


def smem_whole():
    return pl.BlockSpec(memory_space=pltpu.SMEM)


def shape(rows, columns, dtype):
    return jax.ShapeDtypeStruct((rows, columns), dtype)


def half_of(core_ref, which):
    position = core_ref[0] if which == 0 else 1 - core_ref[0]
    return pl.ds(pl.multiple_of(position * HALF, HALF), HALF)


def nt_dot(left_side, right_side):
    return lax.dot_general(
        left_side, right_side, (((1,), (1,)), ((), ())), preferred_element_type=F32
    )


def tn_dot(left_side, right_side):
    return lax.dot_general(
        left_side, right_side, (((0,), (0,)), ((), ())), preferred_element_type=F32
    )


def nn_dot(left_side, right_side):
    return jnp.dot(left_side, right_side, preferred_element_type=F32)


def row_parts(rows):
    return [slice(rows // PARTS * part, rows // PARTS * (part + 1)) for part in range(PARTS)]


def part_shapes(rows):
    return [shape(rows // PARTS, HALF, BF16)] * (2 * PARTS)


class Outward:
    def __init__(self, sems):
        self.sems, self.copies = sems, []

    def send(self, source, target):
        self.copies.append(pltpu.make_async_copy(source, target, self.sems.at[len(self.copies)]))
        self.copies[-1].start()

    def wait(self):
        for copy in self.copies:
            copy.wait()


def far(array):
    return pltpu.HBM(array.shape, array.dtype)


def each_sum(core_ref, sum_refs):
    rows = sum_refs[0].shape[0] * PARTS
    for which in range(2):
        for part, at in enumerate(row_parts(rows)):
            yield at, half_of(core_ref, which), sum_refs[PARTS * which + part]


def write_partial(core_ref, left_ref, w_ref, columns, outs):
    keeps, gives = outs[:PARTS], outs[PARTS:]
    for which, refs in ((1, gives), (0, keeps)):
        product = nt_dot(left_ref[...], w_ref[half_of(core_ref, which), columns]).astype(BF16)
        for at, ref in zip(row_parts(left_ref.shape[0]), refs):
            ref[...] = product[at]


def params(mib):
    return pltpu.CompilerParams(vmem_limit_bytes=mib * MIB)


def inverse_norm(rows):
    return lax.rsqrt(jnp.mean(rows * rows, axis=-1, keepdims=True) + EPSILON)


def causal_mask():
    row = lax.broadcasted_iota(jnp.int32, (128, 128), 0)
    return row >= lax.broadcasted_iota(jnp.int32, (128, 128), 1)


def two_heads(ref, rows, start):
    return jnp.concatenate(
        [
            ref[rows, start : start + HEAD_WIDTH],
            ref[rows, start + HEAD_WIDTH : start + 2 * HEAD_WIDTH],
        ],
        axis=0,
    )


def attention_weights_copy(w_any, w_ref, sem, column):
    return pltpu.make_async_copy(w_any.at[:, pl.ds(column, ATTN_COLS)], w_ref, sem)


def attention_forward_body(sequences, core_ref, outward, first_ref, w_ref, qkv_any, prob_ref, mix_ref, *rest):
    parts, qkv_ref = rest[:-1], rest[-1]
    qkv_ref[...] = nn_dot(first_ref[...], w_ref[:, :QKV_COLS]).astype(BF16)
    outward.send(qkv_ref, qkv_any)
    mask = causal_mask()
    mask = jnp.concatenate([mask, mask], axis=0)
    for sequence in range(sequences):
        rows = slice(128 * sequence, 128 * (sequence + 1))
        for group in range(2):
            queries = two_heads(qkv_ref, rows, 2 * HEAD_WIDTH * group)
            key_at = QUERY_COLS + HEAD_WIDTH * group
            value_at = key_at + KV_COLS
            scores = nt_dot(queries, qkv_ref[rows, key_at : key_at + HEAD_WIDTH]) * SCORE_SCALE
            scores = jnp.where(mask, scores, BLOCKED)
            expanded = jnp.exp(scores - jnp.max(scores, axis=-1, keepdims=True))
            probability = expanded / jnp.sum(expanded, axis=-1, keepdims=True)
            prob_ref[2 * sequence + group] = probability
            mixed = nn_dot(
                probability.astype(BF16), qkv_ref[rows, value_at : value_at + HEAD_WIDTH]
            ).astype(BF16)
            at = 2 * HEAD_WIDTH * group
            mix_ref[rows, at : at + HEAD_WIDTH] = mixed[:128]
            mix_ref[rows, at + HEAD_WIDTH : at + 2 * HEAD_WIDTH] = mixed[128:]
    write_partial(core_ref, mix_ref, w_ref, slice(QKV_COLS, ATTN_COLS), parts)
    outward.wait()


def attention_first_kernel(sequences, column, core_ref, x_ref, w_any, first_ref, *rest):
    outs, (w_ref, sem, sems) = rest[:-3], rest[-3:]
    copy = attention_weights_copy(w_any, w_ref, sem, column)
    copy.start()
    rows = x_ref[...].astype(F32)
    first_ref[...] = (rows * inverse_norm(rows)).astype(BF16)
    copy.wait()
    attention_forward_body(sequences, core_ref, Outward(sems), first_ref, w_ref, *outs)


def attention_next_kernel(sequences, column, core_ref, middle_ref, *rest):
    sums, (w_any, x_ref, first_ref) = rest[: 2 * PARTS], rest[2 * PARTS : 2 * PARTS + 3]
    outs, (w_ref, sem, sems) = rest[2 * PARTS + 3 : -3], rest[-3:]
    copy = attention_weights_copy(w_any, w_ref, sem, column)
    copy.start()
    for at, columns, part in each_sum(core_ref, sums):
        x_ref[at, columns] = (middle_ref[at, columns] + part[...].astype(F32)).astype(BF16)
    rows = x_ref[...].astype(F32)
    first_ref[...] = (rows * inverse_norm(rows)).astype(BF16)
    copy.wait()
    attention_forward_body(sequences, core_ref, Outward(sems), first_ref, w_ref, *outs)


def in_hbm(value):
    return pltpu.with_memory_space_constraint(value, pltpu.HBM)


def hbm_whole():
    return pl.BlockSpec(memory_space=pltpu.HBM)


def attention_scratch():
    return [pltpu.VMEM((WIDTH, ATTN_COLS), BF16), pltpu.SemaphoreType.DMA(())]


def attention_forward(core, x, middle, sums, weights, column):
    rows = (x if middle is None else middle).shape[0]
    sequences = rows // 128
    whole, qkv = shape(rows, WIDTH, BF16), shape(rows, QKV_COLS, BF16)
    outs = [
        whole,
        far(qkv),
        jax.ShapeDtypeStruct((2 * sequences, 256, 128), F32),
        shape(rows, OUT_COLS, BF16),
    ]
    specs = [vmem_whole(), hbm_whole(), vmem_whole(), vmem_whole()]
    if middle is None:
        operands, kernel = (core, x), attention_first_kernel
    else:
        operands, kernel = (core, middle, *sums), attention_next_kernel
        outs, specs = [whole] + outs, [vmem_whole()] + specs
    results = pl.pallas_call(
        functools.partial(kernel, sequences, column),
        in_specs=[smem_whole()] + [vmem_whole()] * (len(operands) - 1) + [hbm_whole()],
        out_specs=specs + [vmem_whole()] * (2 * PARTS),
        out_shape=outs + part_shapes(rows),
        scratch_shapes=[pltpu.VMEM(qkv.shape, BF16)]
        + attention_scratch()
        + [pltpu.SemaphoreType.DMA((1,))],
        compiler_params=params(20),
        cost_estimate=pl.CostEstimate(
            flops=2 * rows * WIDTH * ATTN_COLS, bytes_accessed=8_000_000, transcendentals=0
        ),
        name="attention_forward",
    )(*operands, in_hbm(weights))
    return results


def column_tiles(first):
    return [pl.ds(first + HIDDEN_TILE * step, HIDDEN_TILE) for step in range(HIDDEN_STEPS)]


def weight_copies(w_any, w_ref, sems, regions):
    return [
        pltpu.make_async_copy(w_any.at[rows, columns], w_ref.at[rows, columns], sems.at[number])
        for number, (rows, columns) in enumerate(regions)
    ]


def sigmoid(values):
    return 0.5 * jnp.tanh(0.5 * values) + 0.5


def arrivals(copies):
    for copy in copies[:AHEAD]:
        copy.start()
    place = iter(range(len(copies)))

    def arrive():
        number = next(place)
        copies[number].wait()
        if number + AHEAD < len(copies):
            copies[number + AHEAD].start()

    return arrive


def mlp_forward_kernel(core_ref, x_ref, *rest):
    sums, (w_any, middle_any, second_any, gate_any, up_any, hidden_any) = rest[: 2 * PARTS], rest[2 * PARTS : 2 * PARTS + 6]
    outs = rest[2 * PARTS + 6 : -8]
    w_ref, middle_ref, second_ref, gate_ref, up_ref, hidden_ref, sems, out_sems = rest[-8:]
    whole = pl.ds(0, WIDTH)
    tiles = [(gate, up) for gate, up in zip(column_tiles(0), column_tiles(HIDDEN_COLS))]
    down = pl.ds(2 * HIDDEN_COLS, HIDDEN_COLS)
    regions = [(whole, columns) for pair in tiles for columns in pair]
    regions.append((whole, down))
    arrive = arrivals(weight_copies(w_any, w_ref, sems, regions))
    for at, columns, part in each_sum(core_ref, sums):
        middle_ref[at, columns] = x_ref[at, columns].astype(F32) + part[...].astype(F32)
    rows = middle_ref[...]
    second_ref[...] = (rows * inverse_norm(rows)).astype(BF16)
    outward = Outward(out_sems)
    outward.send(middle_ref, middle_any)
    outward.send(second_ref, second_any)
    for step, (gate, up) in enumerate(tiles):
        at = slice(HIDDEN_TILE * step, HIDDEN_TILE * (step + 1))
        arrive()
        gate_out = nn_dot(second_ref[...], w_ref[:, gate])
        arrive()
        up_out = nn_dot(second_ref[...], w_ref[:, up])
        gate_ref[:, at] = gate_out
        up_ref[:, at] = up_out
        hidden_ref[:, at] = (gate_out * sigmoid(gate_out) * up_out).astype(BF16)
    outward.send(gate_ref, gate_any)
    outward.send(up_ref, up_any)
    outward.send(hidden_ref, hidden_any)
    arrive()
    write_partial(core_ref, hidden_ref, w_ref, down, outs)
    outward.wait()


HIDDEN_STEPS = HIDDEN_COLS // HIDDEN_TILE


def mlp_scratch():
    return [pltpu.VMEM((WIDTH, MLP_COLS), BF16), pltpu.SemaphoreType.DMA((2 * HIDDEN_STEPS + 1,))]


def mlp_forward(core, x, sums, weights):
    rows = x.shape[0]
    saved = [
        shape(rows, WIDTH, F32),
        shape(rows, WIDTH, BF16),
        shape(rows, HIDDEN_COLS, F32),
        shape(rows, HIDDEN_COLS, F32),
        shape(rows, HIDDEN_COLS, BF16),
    ]
    return pl.pallas_call(
        mlp_forward_kernel,
        in_specs=[smem_whole()] + [vmem_whole()] * (1 + 2 * PARTS) + [hbm_whole()],
        out_specs=[hbm_whole()] * 5 + [vmem_whole()] * (2 * PARTS),
        out_shape=[far(array) for array in saved] + part_shapes(rows),
        scratch_shapes=mlp_scratch()[:1]
        + [pltpu.VMEM(out.shape, out.dtype) for out in saved]
        + mlp_scratch()[1:]
        + [pltpu.SemaphoreType.DMA((5,))],
        compiler_params=params(24),
        cost_estimate=pl.CostEstimate(
            flops=2 * rows * WIDTH * MLP_COLS, bytes_accessed=15_000_000, transcendentals=0
        ),
        name="mlp_forward",
    )(core, x, *sums, in_hbm(weights))


def mlp_backward_tiles(g_ref, gate_ref, up_ref, arrive, pair_grad_ref, w_ref):
    for step, down in enumerate(column_tiles(2 * HIDDEN_COLS)):
        at = slice(HIDDEN_TILE * step, HIDDEN_TILE * (step + 1))
        up_at = slice(HIDDEN_COLS + at.start, HIDDEN_COLS + at.stop)
        arrive()
        hidden_grad = nn_dot(g_ref[...], w_ref[:, down])
        gate_out = gate_ref[:, at]
        sigmoid_gate = sigmoid(gate_out)
        pair_grad_ref[:, at] = (
            hidden_grad
            * up_ref[:, at]
            * (sigmoid_gate * (1.0 + gate_out * (1.0 - sigmoid_gate)))
        ).astype(BF16)
        pair_grad_ref[:, up_at] = (hidden_grad * (gate_out * sigmoid_gate)).astype(BF16)


def mlp_backward_copies(w_any, w_ref, sems):
    regions = [(pl.ds(0, WIDTH), columns) for columns in column_tiles(2 * HIDDEN_COLS)]
    regions.append((pl.ds(0, WIDTH), pl.ds(0, 2 * HIDDEN_COLS)))
    return arrivals(weight_copies(w_any, w_ref, sems, regions))


def mlp_backward_kernel(core_ref, x_ref, middle_grad_ref, *rest):
    sums, (gate_ref, up_ref, w_any, g_ref, pair_grad_ref) = rest[: 2 * PARTS], rest[2 * PARTS : 2 * PARTS + 5]
    outs, (w_ref, sems, weighted) = rest[2 * PARTS + 5 : -3], rest[-3:]
    arrive = mlp_backward_copies(w_any, w_ref, sems)
    for at, columns, part in each_sum(core_ref, sums):
        weighted[at, columns] = part[...].astype(F32)
    rows = x_ref[...].astype(F32)
    g_ref[...] = (
        middle_grad_ref[...] + norm_back(weighted[...], rows, inverse_norm(rows))
    ).astype(BF16)
    mlp_backward_tiles(g_ref, gate_ref, up_ref, arrive, pair_grad_ref, w_ref)
    arrive()
    write_partial(core_ref, pair_grad_ref, w_ref, slice(0, 2 * HIDDEN_COLS), outs)


def mlp_backward(core, above, gate_out, up_out, weights):
    rows = gate_out.shape[0]
    return pl.pallas_call(
        mlp_backward_kernel,
        in_specs=[smem_whole()] + [vmem_whole()] * (4 + 2 * PARTS) + [hbm_whole()],
        out_specs=[vmem_whole()] * (2 + 2 * PARTS),
        out_shape=[shape(rows, WIDTH, BF16), shape(rows, 2 * HIDDEN_COLS, BF16)] + part_shapes(rows),
        scratch_shapes=mlp_scratch() + [pltpu.VMEM((rows, WIDTH), F32)],
        compiler_params=params(24),
        cost_estimate=pl.CostEstimate(
            flops=2 * rows * WIDTH * MLP_COLS, bytes_accessed=15_000_000, transcendentals=0
        ),
        name="mlp_backward",
    )(core, *above, gate_out, up_out, in_hbm(weights))


def mlp_last_kernel(core_ref, x_ref, *rest):
    sums, (g_ref, w_any, middle_any, hidden_any, second_ref, hidden_ref, pair_grad_ref) = rest[: 2 * PARTS], rest[2 * PARTS : 2 * PARTS + 7]
    outs = rest[2 * PARTS + 7 : -6]
    w_ref, middle_ref, gate_ref, up_ref, sems, out_sems = rest[-6:]
    whole = pl.ds(0, WIDTH)
    tiles = [(gate, up) for gate, up in zip(column_tiles(0), column_tiles(HIDDEN_COLS))]
    regions = [(whole, columns) for pair in tiles for columns in pair]
    regions += [(whole, columns) for columns in column_tiles(2 * HIDDEN_COLS)]
    arrive = arrivals(weight_copies(w_any, w_ref, sems, regions))
    for at, columns, part in each_sum(core_ref, sums):
        middle_ref[at, columns] = x_ref[at, columns].astype(F32) + part[...].astype(F32)
    rows = middle_ref[...]
    second_ref[...] = (rows * inverse_norm(rows)).astype(BF16)
    outward = Outward(out_sems)
    outward.send(middle_ref, middle_any)
    for step, (gate, up) in enumerate(tiles):
        at = slice(HIDDEN_TILE * step, HIDDEN_TILE * (step + 1))
        arrive()
        gate_out = nn_dot(second_ref[...], w_ref[:, gate])
        arrive()
        up_out = nn_dot(second_ref[...], w_ref[:, up])
        gate_ref[:, at] = gate_out
        up_ref[:, at] = up_out
        hidden_ref[:, at] = (gate_out * sigmoid(gate_out) * up_out).astype(BF16)
    outward.send(hidden_ref, hidden_any)
    mlp_backward_tiles(g_ref, gate_ref, up_ref, arrive, pair_grad_ref, w_ref)
    write_partial(core_ref, pair_grad_ref, w_ref, slice(0, 2 * HIDDEN_COLS), outs)
    outward.wait()


def mlp_last(core, x, sums, g, weights):
    rows = x.shape[0]
    inner = [shape(rows, WIDTH, F32)] + [shape(rows, HIDDEN_COLS, F32)] * 2
    return pl.pallas_call(
        mlp_last_kernel,
        in_specs=[smem_whole()] + [vmem_whole()] * (2 + 2 * PARTS) + [hbm_whole()],
        out_specs=[hbm_whole()] * 2 + [vmem_whole()] * (3 + 2 * PARTS),
        out_shape=[
            pltpu.HBM((rows, WIDTH), F32),
            pltpu.HBM((rows, HIDDEN_COLS), BF16),
            shape(rows, WIDTH, BF16),
            shape(rows, HIDDEN_COLS, BF16),
            shape(rows, 2 * HIDDEN_COLS, BF16),
        ]
        + [far(part) for part in part_shapes(rows)],
        scratch_shapes=mlp_scratch()[:1]
        + [pltpu.VMEM(array.shape, array.dtype) for array in inner]
        + [
            pltpu.SemaphoreType.DMA((3 * HIDDEN_STEPS,)),
            pltpu.SemaphoreType.DMA((2,)),
        ],
        compiler_params=params(24),
        cost_estimate=pl.CostEstimate(
            flops=4 * rows * WIDTH * MLP_COLS, bytes_accessed=15_000_000, transcendentals=0
        ),
        name="mlp_last",
    )(core, x, *sums, g, in_hbm(weights))


def mlp_down_kernel(core_ref, hidden_ref, w_any, *rest):
    outs, w_ref, sem = rest[:-2], rest[-2], rest[-1]
    copy = pltpu.make_async_copy(w_any.at[:, pl.ds(2 * HIDDEN_COLS, HIDDEN_COLS)], w_ref, sem)
    copy.start()
    copy.wait()
    write_partial(core_ref, hidden_ref, w_ref, slice(0, HIDDEN_COLS), outs)


def mlp_down(core, hidden, weights):
    rows = hidden.shape[0]
    return pl.pallas_call(
        mlp_down_kernel,
        in_specs=[smem_whole(), vmem_whole(), hbm_whole()],
        out_specs=[vmem_whole()] * (2 * PARTS),
        out_shape=part_shapes(rows),
        scratch_shapes=[pltpu.VMEM((WIDTH, HIDDEN_COLS), BF16), pltpu.SemaphoreType.DMA(())],
        compiler_params=params(14),
        cost_estimate=pl.CostEstimate(
            flops=2 * rows * WIDTH * HIDDEN_COLS, bytes_accessed=5_000_000, transcendentals=0
        ),
        name="mlp_down",
    )(core, hidden, in_hbm(weights))


def attention_backward_kernel(sequences, column, near, core_ref, g_ref, middle_ref, *rest):
    sums, rest = rest[: 2 * PARTS], rest[2 * PARTS :]
    (qkv_any, prob_any, w_any, middle_grad_out, attn_in_ref, qkv_grad_ref), rest = rest[:6], rest[6:]
    outs, (middle_grad_ref, qkv_ref, prob_ref, mix_grad, w_ref, sem, sems) = rest[:-7], rest[-7:]
    copies = [
        attention_weights_copy(w_any, w_ref, sem, column),
        pltpu.make_async_copy(qkv_any, qkv_ref, sems.at[0]),
        pltpu.make_async_copy(prob_any, prob_ref, sems.at[1]),
    ]
    for copy in copies:
        copy.start()
    for at, columns, part in each_sum(core_ref, sums):
        middle_grad_ref[at, columns] = part[...].astype(F32)
    middle = middle_ref[...]
    middle_grad = g_ref[...].astype(F32) + norm_back(
        middle_grad_ref[...], middle, inverse_norm(middle)
    )
    if near:
        middle_grad_out[...] = middle_grad
    else:
        middle_grad_ref[...] = middle_grad
        outward = pltpu.make_async_copy(middle_grad_ref, middle_grad_out, sems.at[2])
        outward.start()
    attn_in_ref[...] = middle_grad.astype(BF16)
    copies[0].wait()
    mix_grad[...] = nn_dot(attn_in_ref[...], w_ref[:, QKV_COLS:]).astype(BF16)
    for copy in copies[1:]:
        copy.wait()
    for sequence in range(sequences):
        rows = slice(128 * sequence, 128 * (sequence + 1))
        for group in range(2):
            at = 2 * HEAD_WIDTH * group
            key_at = QUERY_COLS + HEAD_WIDTH * group
            value_at = key_at + KV_COLS
            grads = two_heads(mix_grad, rows, at)
            queries = two_heads(qkv_ref, rows, at)
            keys = qkv_ref[rows, key_at : key_at + HEAD_WIDTH]
            probability = prob_ref[2 * sequence + group]
            prob_grad = nt_dot(grads, qkv_ref[rows, value_at : value_at + HEAD_WIDTH])
            centred = jnp.sum(probability * prob_grad, axis=-1, keepdims=True)
            score_grad = (probability * (prob_grad - centred)).astype(BF16)
            query_grad = (nn_dot(score_grad, keys) * SCORE_SCALE).astype(BF16)
            qkv_grad_ref[rows, at : at + HEAD_WIDTH] = query_grad[:128]
            qkv_grad_ref[rows, at + HEAD_WIDTH : at + 2 * HEAD_WIDTH] = query_grad[128:]
            qkv_grad_ref[rows, key_at : key_at + HEAD_WIDTH] = (
                tn_dot(score_grad, queries) * SCORE_SCALE
            ).astype(BF16)
            qkv_grad_ref[rows, value_at : value_at + HEAD_WIDTH] = tn_dot(
                probability.astype(BF16), grads
            ).astype(BF16)
    if near:
        write_partial(core_ref, qkv_grad_ref, w_ref, slice(0, QKV_COLS), outs)
    else:
        outward.wait()


def attention_in_kernel(column, core_ref, qkv_grad_ref, w_any, *rest):
    outs, w_ref, sem = rest[:-2], rest[-2], rest[-1]
    copy = attention_weights_copy(w_any, w_ref, sem, column)
    copy.start()
    copy.wait()
    write_partial(core_ref, qkv_grad_ref, w_ref, slice(0, QKV_COLS), outs)


def attention_in(core, qkv_grad, weights, column):
    rows = qkv_grad.shape[0]
    return pl.pallas_call(
        functools.partial(attention_in_kernel, column),
        in_specs=[smem_whole(), vmem_whole(), hbm_whole()],
        out_specs=[vmem_whole()] * (2 * PARTS),
        out_shape=part_shapes(rows),
        scratch_shapes=attention_scratch(),
        compiler_params=params(14),
        cost_estimate=pl.CostEstimate(
            flops=2 * rows * WIDTH * QKV_COLS, bytes_accessed=5_000_000, transcendentals=0
        ),
        name="attention_in",
    )(core, qkv_grad, in_hbm(weights))


def attention_backward(core, g, middle, sums, qkv, probability, weights, column, near=True):
    rows = g.shape[0]
    residual, parts = shape(rows, WIDTH, F32), part_shapes(rows) if near else []
    return pl.pallas_call(
        functools.partial(attention_backward_kernel, rows // 128, column, near),
        in_specs=[smem_whole()] + [vmem_whole()] * (2 + 2 * PARTS) + [hbm_whole()] * 3,
        out_specs=[vmem_whole() if near else hbm_whole()] + [vmem_whole()] * (2 + len(parts)),
        out_shape=[
            residual if near else far(residual),
            shape(rows, WIDTH, BF16),
            shape(rows, QKV_COLS, BF16),
        ]
        + parts,
        scratch_shapes=[
            pltpu.VMEM((rows, WIDTH), F32),
            pltpu.VMEM(qkv.shape, BF16),
            pltpu.VMEM(probability.shape, F32),
            pltpu.VMEM((rows, OUT_COLS), BF16),
        ]
        + attention_scratch()
        + [pltpu.SemaphoreType.DMA((3,))],
        compiler_params=params(24),
        cost_estimate=pl.CostEstimate(
            flops=2 * rows * WIDTH * ATTN_COLS, bytes_accessed=12_000_000, transcendentals=0
        ),
        name="attention_backward",
    )(core, g, middle, *sums, in_hbm(qkv), in_hbm(probability), in_hbm(weights))


def write_products(start, pairs, out_any, slots, sems):
    _, height, width = slots.shape
    copies = []
    for number in range(WIDTH // height):
        features = pl.ds(height * number, height)
        if number >= 2:
            copies[number - 2].wait()
        slot = slots.at[number % 2]
        at = 0
        for left, right in pairs:
            columns = right.shape[1]
            slot[:, at : at + columns] = tn_dot(left[:, features], right[...]).astype(BF16)
            at += columns
        target = out_any.at[features, pl.ds(start, width)]
        copies.append(pltpu.make_async_copy(slot, target, sems.at[number % 2]))
        copies[-1].start()
    for copy in copies[-2:]:
        copy.wait()


def mlp_weights_kernel(second_ref, g_ref, pair_grad_ref, hidden_ref, *rest):
    out_any, slots, sems = rest[-3:]
    write_products(0, [(second_ref, pair_grad_ref), (g_ref, hidden_ref)], out_any, slots, sems)


def into_buffer(kernel, buffer, columns, slot, operands, flops, name, mib):
    aliases, specs = {}, [vmem_whole()] * len(operands)
    if buffer is not None:
        aliases = {len(operands): 0}
        specs, operands = specs + [hbm_whole()], operands + (in_hbm(buffer),)
    return pl.pallas_call(
        kernel,
        in_specs=specs,
        out_specs=hbm_whole(),
        out_shape=pltpu.HBM((WIDTH, columns), BF16),
        input_output_aliases=aliases,
        scratch_shapes=[pltpu.VMEM((2, *slot), BF16), pltpu.SemaphoreType.DMA((2,))],
        compiler_params=params(mib),
        cost_estimate=pl.CostEstimate(flops=flops, bytes_accessed=flops // 250, transcendentals=0),
        name=name,
    )(*operands)


def mlp_weights(buffer, columns, second, g, pair_grad, hidden):
    return into_buffer(
        mlp_weights_kernel,
        buffer,
        columns,
        (512, MLP_COLS),
        (second, g, pair_grad, hidden),
        2 * second.shape[0] * WIDTH * MLP_COLS,
        "mlp_weights",
        18,
    )


def attention_weights_kernel(start, first_ref, attn_in_ref, qkv_grad_ref, mix_ref, *rest):
    out_any, slots, sems = rest[-3:]
    pairs = [(first_ref, qkv_grad_ref), (attn_in_ref, mix_ref)]
    write_products(start, pairs, out_any, slots, sems)


def attention_weights(buffer, columns, start, first, attn_in, qkv_grad, mixture):
    return into_buffer(
        functools.partial(attention_weights_kernel, start),
        buffer,
        columns,
        (768, ATTN_COLS),
        (first, attn_in, qkv_grad, mixture),
        2 * first.shape[0] * WIDTH * ATTN_COLS,
        "attention_weights",
        14,
    )


def sum_four(partial, before=None, beside=None):
    keeps, gives = list(partial[:PARTS]), list(partial[PARTS:])
    if before is not None:
        keeps, before = lax.optimization_barrier((keeps, before))
    chips = [
        (keep.astype(F32) + swap(give, "section").astype(F32)).astype(BF16)
        for keep, give in zip(keeps, gives)
    ]
    arrived = [swap(chip, "tensor") for chip in chips]
    if beside is not None:
        arrived[0], beside = lax.optimization_barrier((arrived[0], beside))
    totals = [
        (chip.astype(F32) + other.astype(F32)).astype(BF16)
        for chip, other in zip(chips, arrived)
    ]
    return totals + [swap(total, "section") for total in totals], before, beside


def row_scales(gain_ref):
    row = lax.broadcasted_iota(jnp.int32, (48, 48), 0)
    column = lax.broadcasted_iota(jnp.int32, (48, 48), 1)
    return jnp.where(row == column, gain_ref[...].astype(F32), 0.0).astype(BF16)


def pack_kernel(core_ref, attn_gain_ref, mlp_gain_ref, *rest):
    sources, (mine_ref, give_ref), shards, sems = rest[:7], rest[7:9], rest[9:16], rest[16]
    copies = [
        pltpu.make_async_copy(source, shard, sems.at[number])
        for number, (source, shard) in enumerate(zip(sources, shards))
    ]
    for copy in copies:
        copy.start()
    is_first = core_ref[0] == 0
    attn_scale, mlp_scale = row_scales(attn_gain_ref), row_scales(mlp_gain_ref)
    start = 0
    for copy, shard, scale in zip(
        copies,
        shards,
        (mlp_scale, mlp_scale, None, attn_scale, attn_scale, attn_scale, None),
    ):
        copy.wait()
        weight = shard[...]
        if scale is not None:
            weight = nn_dot(scale, weight).astype(BF16)
        width = weight.shape[1] // 2
        low, high = weight[:, :width], weight[:, width:]
        mine_ref[:, start : start + width] = jnp.where(is_first, low, high)
        give_ref[:, start : start + width] = jnp.where(is_first, high, low)
        start += width


def pack_shards(core, attn_gain, mlp_gain, *shards):
    return pl.pallas_call(
        pack_kernel,
        in_specs=[smem_whole()] + [vmem_whole()] * 2 + [hbm_whole()] * len(shards),
        out_specs=[vmem_whole()] * 2,
        out_shape=[shape(48, LAYER_COLS, BF16)] * 2,
        scratch_shapes=[pltpu.VMEM(shard.shape, shard.dtype) for shard in shards]
        + [pltpu.SemaphoreType.DMA((len(shards),))],
        compiler_params=params(16),
        name="pack_shards",
    )(core, attn_gain, mlp_gain, *[in_hbm(shard) for shard in shards])


def combine_kernel(core_ref, keep_ref, arrived_ref, last_ref, zero_w_ref, one_w_ref, mine_ref, give_ref, terms_ref, zero, one):
    rest = (keep_ref[...].astype(F32) + arrived_ref[...].astype(F32)).astype(BF16)
    zero[:, :MLP_COLS] = rest[:, :MLP_COLS]
    zero[:, MLP_COLS:] = rest[:, LAYER_COLS:]
    one[:, :MLP_COLS] = last_ref[...]
    one[:, MLP_COLS:] = rest[:, MLP_COLS:LAYER_COLS]
    is_first = core_ref[0] == 0
    mine_ref[...] = jnp.where(is_first, zero[...], one[...])
    give_ref[...] = jnp.where(is_first, one[...], zero[...])
    row = 0
    for grad, weights in ((zero, zero_w_ref), (one, one_w_ref)):
        products = weights[...].astype(F32) * grad[...].astype(F32)
        for columns in (slice(MLP_COLS, MLP_COLS + QKV_COLS), slice(0, 2 * HIDDEN_COLS)):
            terms_ref[row, :] = jnp.sum(products[:, columns], axis=1)
            row += 1


def combine_grads(core, *operands):
    return pl.pallas_call(
        combine_kernel,
        in_specs=[smem_whole()] + [vmem_whole()] * len(operands),
        out_specs=[vmem_whole()] * 3,
        out_shape=[shape(48, LAYER_COLS, BF16)] * 2 + [shape(4, 48, F32)],
        scratch_shapes=[pltpu.VMEM((48, LAYER_COLS), BF16)] * 2,
        compiler_params=params(16),
        name="combine_grads",
    )(core, *operands)


def unpack_kernel(core_ref, attn_scale_ref, mlp_scale_ref, mine_ref, got_ref, gate_ref, up_ref, down_ref, query_ref, key_ref, value_ref, out_ref):
    is_first = core_ref[0] == 0

    def place(out, start, scale_ref):
        width = out.shape[1] // 2
        mine = mine_ref[:, start : start + width].astype(F32)
        got = got_ref[:, start : start + width].astype(F32)
        if scale_ref is not None:
            mine, got = mine * scale_ref[...], got * scale_ref[...]
        out[:, :width] = jnp.where(is_first, mine, got)
        out[:, width:] = jnp.where(is_first, got, mine)

    place(gate_ref, 0, mlp_scale_ref)
    place(up_ref, HIDDEN_COLS, mlp_scale_ref)
    place(down_ref, 2 * HIDDEN_COLS, None)
    place(query_ref, MLP_COLS, attn_scale_ref)
    place(key_ref, MLP_COLS + QUERY_COLS, attn_scale_ref)
    place(value_ref, MLP_COLS + QUERY_COLS + KV_COLS, attn_scale_ref)
    place(out_ref, MLP_COLS + QKV_COLS, None)


def unpack_grads(core, *operands):
    widths = [HIDDEN_COLS] * 3 + [QUERY_COLS, KV_COLS, KV_COLS, OUT_COLS]
    return pl.pallas_call(
        unpack_kernel,
        in_specs=[smem_whole()] + [vmem_whole()] * len(operands),
        out_specs=[vmem_whole()] * len(widths),
        out_shape=[shape(48, 2 * width, F32) for width in widths],
        compiler_params=params(16),
        name="unpack_grads",
    )(core, *operands)


def gather_rows(z_low, share):
    other = swap(share, "zl")
    pair = jnp.concatenate([pick(z_low, share, other), pick(z_low, other, share)], axis=0)
    return lax.all_gather(pair, ("y", "x"), axis=0, tiled=True)


def scatter_pair(grad):
    return lax.psum_scatter(grad, ("y", "x"), scatter_dimension=0, tiled=True)


def scatter_low(z_low, pair):
    keep = pick(z_low, pair[:48], pair[48:])
    give = pick(z_low, pair[48:], pair[:48])
    return (keep.astype(F32) + swap(give, "zl").astype(F32)).astype(BF16)


def to_ring_order(rows):
    lead = rows.shape[:-1]
    return jnp.swapaxes(rows.reshape(lead + (4, 2, 4, 48)), -3, -2).reshape(rows.shape)


def from_ring_order(rows):
    lead = rows.shape[:-1]
    return jnp.swapaxes(rows.reshape(lead + (4, 4, 2, 48)), -3, -2).reshape(rows.shape)


def join_positions(tensor, own):
    other = swap(own, "tensor")
    return jnp.concatenate(
        [pick(tensor, own, other), pick(tensor, other, own)], axis=1
    ).reshape(384, WIDTH)


def own_positions(tensor, rows):
    rows = rows.reshape(3, 128, 1536)
    return pick(tensor, rows[:, :64], rows[:, 64:])


def per_device(
    inputs, cotangent, plan, attn_gain, mlp_gain, w_query, key_weight, value_weight,
    w_out, w_gate, w_up, w_down,
):
    core = lax.axis_index("section")
    z_low = lax.axis_index("zl")
    tensor = lax.axis_index("tensor")

    attn_scale = attn_gain[0].astype(F32)[:, None]
    mlp_scale = mlp_gain[0].astype(F32)[:, None]

    core_ref = core.astype(jnp.int32).reshape(1)
    mine, give = pack_shards(
        core_ref, attn_gain, mlp_gain,
        w_gate[0], w_up[0], w_down[0].T, w_query[0], key_weight[0], value_weight[0], w_out[0].T,
    )
    got = swap(give, "section")
    layer_zero, layer_one = pick(core, mine, got), pick(core, got, mine)
    first_weights = gather_rows(
        z_low, jnp.concatenate([layer_zero, layer_one[:, MLP_COLS:]], axis=1)
    )
    last_weights = gather_rows(z_low, layer_one[:, :MLP_COLS])
    attn_weights = ((first_weights, MLP_COLS), (first_weights, LAYER_COLS))
    mlp_weights_of = (first_weights, last_weights)

    stream = join_positions(tensor, to_ring_order(inputs[:, 0][plan]))
    stream, late = lax.optimization_barrier((stream, cotangent))
    out_grad = join_positions(tensor, to_ring_order(late[:, 0][plan]))
    stream, out_grad = lax.optimization_barrier((stream, out_grad))

    def whole_rows(sums):
        own, other = jnp.concatenate(sums[:PARTS]), jnp.concatenate(sums[PARTS:])
        return jnp.concatenate([pick(core, own, other), pick(core, other, own)], axis=1).astype(F32)

    attn_zero, attn_one = attn_weights
    mlp_zero, mlp_one = mlp_weights_of

    x_zero = stream
    first_zero, qkv_zero, prob_zero, mix_zero, *partial = attention_forward(
        core_ref, x_zero, None, None, *attn_zero
    )
    sums, _, _ = sum_four(partial)
    middle_zero, second_zero, gate_zero, up_zero, hidden_zero, *partial = mlp_forward(
        core_ref, x_zero, sums, mlp_zero
    )
    sums, _, _ = sum_four(partial)
    x_one, first_one, qkv_one, prob_one, mix_one, *partial = attention_forward(
        core_ref, None, middle_zero, sums, *attn_one
    )
    sums, _, _ = sum_four(partial)

    middle_one, hidden_far, second_one, hidden_one, pair_grad, *partial = mlp_last(
        core_ref, x_one, sums, out_grad, mlp_one
    )
    one_mlp = mlp_weights(None, MLP_COLS, second_one, out_grad, pair_grad, hidden_one)
    sums, one_mlp, _ = sum_four(partial, before=one_mlp)
    last_pair = scatter_pair(one_mlp)
    middle_grad, attn_in, qkv_grad, *partial = attention_backward(
        core_ref, out_grad, middle_one, sums, qkv_one, prob_one, *attn_one
    )
    buffer = attention_weights(None, REST_COLS, MLP_COLS, first_one, attn_in, qkv_grad, mix_one)
    sums, _, buffer = sum_four(partial, beside=buffer)

    grad_one, pair_grad, *partial = mlp_backward(
        core_ref, (x_one, middle_grad, *sums), gate_zero, up_zero, mlp_zero
    )
    buffer = mlp_weights(buffer, REST_COLS, second_zero, grad_one, pair_grad, hidden_zero)
    sums, _, buffer = sum_four(partial, beside=buffer)
    hidden_far, sums[0] = lax.optimization_barrier((hidden_far, sums[0]))
    down_partial = mlp_down(core_ref, hidden_far, mlp_one)
    middle_grad, attn_in, qkv_grad = attention_backward(
        core_ref, grad_one, middle_zero, sums, qkv_zero, prob_zero, *attn_zero, near=False
    )
    buffer = attention_weights(
        buffer, REST_COLS, LAYER_COLS, first_zero, attn_in, qkv_grad, mix_zero
    )
    rest_pair = scatter_pair(buffer)
    qkv_grad, buffer = lax.optimization_barrier((qkv_grad, buffer))
    sums, _, _ = sum_four(attention_in(core_ref, qkv_grad, *attn_zero))
    rows = x_zero.astype(F32)
    grad_zero = middle_grad + norm_back(whole_rows(sums), rows, inverse_norm(rows))
    down_sums, _, _ = sum_four(down_partial)
    result_one = (middle_one + whole_rows(down_sums)).astype(BF16)
    outputs = [own_positions(tensor, x_one), own_positions(tensor, result_one)]
    grads = [own_positions(tensor, grad_zero.astype(BF16)), own_positions(tensor, grad_one)]

    layer_outputs = from_ring_order(pick(core, outputs[0], outputs[1]))
    input_grads = from_ring_order(pick(core, grads[0], grads[1]))
    last_grad = scatter_low(z_low, last_pair)
    rest_pair, layer_outputs, input_grads, last_grad = lax.optimization_barrier(
        (rest_pair, layer_outputs, input_grads, last_grad)
    )
    keep = pick(z_low, rest_pair[:48], rest_pair[48:])
    arrived = swap(pick(z_low, rest_pair[48:], rest_pair[:48]), "zl")
    mine, give, terms = combine_grads(
        core_ref, keep, arrived, last_grad, layer_zero, layer_one
    )
    got = swap(give, "section")
    across = lax.ppermute(terms, ("section", "tensor"), [(0, 3), (1, 2), (2, 1), (3, 0)])
    arrived = swap(terms, "tensor") + swap(terms, "section") + across
    gate_grad, up_grad, down_grad, query_grad, key_grad, value_grad, out_weight_grad = unpack_grads(
        core_ref, attn_scale, mlp_scale, mine, got
    )
    arrived, key_grad = lax.optimization_barrier((arrived, key_grad))
    terms = terms + arrived
    terms = pick(core, terms[:2], terms[2:])
    return (
        layer_outputs[None, :, None],
        input_grads[None, :, None],
        (terms[0] / attn_scale[:, 0])[None],
        (terms[1] / mlp_scale[:, 0])[None],
        query_grad[None],
        key_grad[None],
        value_grad[None],
        out_weight_grad.T[None],
        gate_grad[None],
        up_grad[None],
        down_grad.T[None],
    )


def solution(mesh):
    split = Mesh(mesh.devices.reshape(2, 4, 2, 4, 2), ("section", "y", "zl", "x", "tensor"))
    dp = ("y", "zl", "x")
    rows = P("section", dp, "tensor")
    columns = P("section", "tensor", dp)
    return jax.shard_map(
        per_device,
        mesh=split,
        in_specs=(
            P(None, dp, "tensor", None),
            P(None, dp, "tensor", None),
            P(),
            P("section", dp),
            P("section", dp),
            rows,
            rows,
            rows,
            columns,
            rows,
            rows,
            columns,
        ),
        out_specs=(
            P("section", None, dp, "tensor", None),
            P("section", None, dp, "tensor", None),
            P("section", dp),
            P("section", dp),
            rows,
            rows,
            rows,
            columns,
            rows,
            rows,
            columns,
        ),
        check_vma=False,
    )
```

```python
import functools

import jax
import jax.numpy as jnp
from jax import lax
from jax.experimental import pallas as pl
from jax.experimental.pallas import tpu as pltpu
from jax.sharding import Mesh, PartitionSpec as P

HEAD_WIDTH = 96
EPSILON = 1e-05
BLOCKED = -1e30
SCORE_SCALE = HEAD_WIDTH ** (-0.5)
BF16 = jnp.bfloat16
F32 = jnp.float32

QUERY_COLS, KV_COLS = 384, 192
QKV_COLS = QUERY_COLS + 2 * KV_COLS
OUT_COLS = 384
HIDDEN_COLS = 1024
ATTN_COLS = QKV_COLS + OUT_COLS
MLP_COLS = 3 * HIDDEN_COLS
LAYER_COLS = MLP_COLS + ATTN_COLS
REST_COLS = LAYER_COLS + ATTN_COLS
HIDDEN_TILE = 512
AHEAD = 3
WIDTH = 1536
HALF = WIDTH // 2
PARTS = 2
MIB = 1024 * 1024


def swap(value, axis):
    return lax.ppermute(value, axis, [(0, 1), (1, 0)])


def pick(index, first, second):
    return jnp.where(index == 0, first, second)


def norm_back(weighted, residual, inverse):
    scaled = residual * inverse
    return inverse * (weighted - scaled * jnp.mean(weighted * scaled, axis=-1, keepdims=True))


def vmem_whole():
    return pl.BlockSpec(memory_space=pltpu.VMEM)


def smem_whole():
    return pl.BlockSpec(memory_space=pltpu.SMEM)


def shape(rows, columns, dtype):
    return jax.ShapeDtypeStruct((rows, columns), dtype)


def half_of(core_ref, which):
    position = core_ref[0] if which == 0 else 1 - core_ref[0]
    return pl.ds(pl.multiple_of(position * HALF, HALF), HALF)


def nt_dot(left_side, right_side):
    return lax.dot_general(
        left_side, right_side, (((1,), (1,)), ((), ())), preferred_element_type=F32
    )


def tn_dot(left_side, right_side):
    return lax.dot_general(
        left_side, right_side, (((0,), (0,)), ((), ())), preferred_element_type=F32
    )


def nn_dot(left_side, right_side):
    return jnp.dot(left_side, right_side, preferred_element_type=F32)


def row_parts(rows):
    return [slice(rows // PARTS * part, rows // PARTS * (part + 1)) for part in range(PARTS)]


def part_shapes(rows):
    return [shape(rows // PARTS, HALF, BF16)] * (2 * PARTS)


class Outward:
    def __init__(self, sems):
        self.sems, self.copies = sems, []

    def send(self, source, target):
        self.copies.append(pltpu.make_async_copy(source, target, self.sems.at[len(self.copies)]))
        self.copies[-1].start()

    def wait(self):
        for copy in self.copies:
            copy.wait()


def far(array):
    return pltpu.HBM(array.shape, array.dtype)


def each_sum(core_ref, sum_refs):
    rows = sum_refs[0].shape[0] * PARTS
    for which in range(2):
        for part, at in enumerate(row_parts(rows)):
            yield at, half_of(core_ref, which), sum_refs[PARTS * which + part]


def write_partial(core_ref, left_ref, w_ref, columns, outs):
    keeps, gives = outs[:PARTS], outs[PARTS:]
    for which, refs in ((1, gives), (0, keeps)):
        product = nt_dot(left_ref[...], w_ref[half_of(core_ref, which), columns]).astype(BF16)
        for at, ref in zip(row_parts(left_ref.shape[0]), refs):
            ref[...] = product[at]


def params(mib):
    return pltpu.CompilerParams(vmem_limit_bytes=mib * MIB)


def inverse_norm(rows):
    return lax.rsqrt(jnp.mean(rows * rows, axis=-1, keepdims=True) + EPSILON)


def causal_mask():
    row = lax.broadcasted_iota(jnp.int32, (128, 128), 0)
    return row >= lax.broadcasted_iota(jnp.int32, (128, 128), 1)


def two_heads(ref, rows, start):
    return jnp.concatenate(
        [
            ref[rows, start : start + HEAD_WIDTH],
            ref[rows, start + HEAD_WIDTH : start + 2 * HEAD_WIDTH],
        ],
        axis=0,
    )


def ahead_copy(w_any, w_ref, sem, column):
    return pltpu.make_async_copy(w_any.at[:, pl.ds(column, w_ref.shape[1])], w_ref, sem)


def attention_forward_body(sequences, core_ref, outward, first_ref, w_ref, qkv_any, prob_ref, mix_ref, *rest):
    parts, qkv_ref = rest[:-1], rest[-1]
    qkv_ref[...] = nn_dot(first_ref[...], w_ref[:, :QKV_COLS]).astype(BF16)
    outward.send(qkv_ref, qkv_any)
    mask = causal_mask()
    mask = jnp.concatenate([mask, mask], axis=0)
    for sequence in range(sequences):
        rows = slice(128 * sequence, 128 * (sequence + 1))
        for group in range(2):
            queries = two_heads(qkv_ref, rows, 2 * HEAD_WIDTH * group)
            key_at = QUERY_COLS + HEAD_WIDTH * group
            value_at = key_at + KV_COLS
            scores = nt_dot(queries, qkv_ref[rows, key_at : key_at + HEAD_WIDTH]) * SCORE_SCALE
            scores = jnp.where(mask, scores, BLOCKED)
            expanded = jnp.exp(scores - jnp.max(scores, axis=-1, keepdims=True))
            probability = expanded / jnp.sum(expanded, axis=-1, keepdims=True)
            prob_ref[2 * sequence + group] = probability
            mixed = nn_dot(
                probability.astype(BF16), qkv_ref[rows, value_at : value_at + HEAD_WIDTH]
            ).astype(BF16)
            at = 2 * HEAD_WIDTH * group
            mix_ref[rows, at : at + HEAD_WIDTH] = mixed[:128]
            mix_ref[rows, at + HEAD_WIDTH : at + 2 * HEAD_WIDTH] = mixed[128:]
    write_partial(core_ref, mix_ref, w_ref, slice(QKV_COLS, ATTN_COLS), parts)
    outward.wait()


def attention_first_kernel(sequences, column, core_ref, x_ref, w_any, next_ref, first_ref, *rest):
    outs, (w_ref, sem, sems) = rest[:-3], rest[-3:]
    copy = ahead_copy(w_any, w_ref, sem, column)
    copy.start()
    rows = x_ref[...].astype(F32)
    first_ref[...] = (rows * inverse_norm(rows)).astype(BF16)
    copy.wait()
    ahead = ahead_copy(w_any, next_ref, sem, 0)
    ahead.start()
    attention_forward_body(sequences, core_ref, Outward(sems), first_ref, w_ref, *outs)
    ahead.wait()


def attention_next_kernel(sequences, core_ref, middle_ref, *rest):
    sums, (w_ref, x_ref, first_ref) = rest[: 2 * PARTS], rest[2 * PARTS : 2 * PARTS + 3]
    outs, sems = rest[2 * PARTS + 3 : -1], rest[-1]
    for at, columns, part in each_sum(core_ref, sums):
        x_ref[at, columns] = (middle_ref[at, columns] + part[...].astype(F32)).astype(BF16)
    rows = x_ref[...].astype(F32)
    first_ref[...] = (rows * inverse_norm(rows)).astype(BF16)
    attention_forward_body(sequences, core_ref, Outward(sems), first_ref, w_ref, *outs)


def in_hbm(value):
    return pltpu.with_memory_space_constraint(value, pltpu.HBM)


def hbm_whole():
    return pl.BlockSpec(memory_space=pltpu.HBM)


def attention_scratch():
    return [pltpu.VMEM((WIDTH, ATTN_COLS), BF16), pltpu.SemaphoreType.DMA(())]


def attention_outs(rows):
    outs = [
        shape(rows, WIDTH, BF16),
        far(shape(rows, QKV_COLS, BF16)),
        jax.ShapeDtypeStruct((rows // 64, 256, 128), F32),
        shape(rows, OUT_COLS, BF16),
    ]
    return outs + part_shapes(rows), [vmem_whole(), hbm_whole()] + [vmem_whole()] * (2 + 2 * PARTS)


def attention_cost(rows):
    return pl.CostEstimate(
        flops=2 * rows * WIDTH * ATTN_COLS, bytes_accessed=8_000_000, transcendentals=0
    )


def attention_first(core, x, weights, column):
    rows = x.shape[0]
    outs, specs = attention_outs(rows)
    return pl.pallas_call(
        functools.partial(attention_first_kernel, rows // 128, column),
        in_specs=[smem_whole(), vmem_whole(), hbm_whole()],
        out_specs=[vmem_whole()] + specs,
        out_shape=[shape(WIDTH, MLP_COLS, BF16)] + outs,
        scratch_shapes=[pltpu.VMEM((rows, QKV_COLS), BF16)]
        + attention_scratch()
        + [pltpu.SemaphoreType.DMA((1,))],
        compiler_params=params(26),
        cost_estimate=attention_cost(rows),
        name="attention_first",
    )(core, x, in_hbm(weights))


def attention_next(core, middle, sums, weights):
    rows = middle.shape[0]
    outs, specs = attention_outs(rows)
    return pl.pallas_call(
        functools.partial(attention_next_kernel, rows // 128),
        in_specs=[smem_whole()] + [vmem_whole()] * (2 + 2 * PARTS),
        out_specs=[vmem_whole()] + specs,
        out_shape=[shape(rows, WIDTH, BF16)] + outs,
        scratch_shapes=[pltpu.VMEM((rows, QKV_COLS), BF16), pltpu.SemaphoreType.DMA((1,))],
        compiler_params=params(16),
        cost_estimate=attention_cost(rows),
        name="attention_next",
    )(core, middle, *sums, weights)


def column_tiles(first):
    return [pl.ds(first + HIDDEN_TILE * step, HIDDEN_TILE) for step in range(HIDDEN_STEPS)]


def weight_copies(w_any, w_ref, sems, regions):
    return [
        pltpu.make_async_copy(w_any.at[rows, columns], w_ref.at[rows, columns], sems.at[number])
        for number, (rows, columns) in enumerate(regions)
    ]


def sigmoid(values):
    return 0.5 * jnp.tanh(0.5 * values) + 0.5


def arrivals(copies):
    for copy in copies[:AHEAD]:
        copy.start()
    place = iter(range(len(copies)))

    def arrive():
        number = next(place)
        copies[number].wait()
        if number + AHEAD < len(copies):
            copies[number + AHEAD].start()

    return arrive


def mlp_forward_kernel(column, core_ref, x_ref, *rest):
    sums, rest = rest[: 2 * PARTS], rest[2 * PARTS :]
    (w_ref, w_any, middle_any, second_any, gate_any, up_any, hidden_any, next_ref), rest = rest[:8], rest[8:]
    outs, (middle_ref, second_ref, gate_ref, up_ref, hidden_ref, out_sems, sem) = rest[:-7], rest[-7:]
    tiles = [(gate, up) for gate, up in zip(column_tiles(0), column_tiles(HIDDEN_COLS))]
    down = pl.ds(2 * HIDDEN_COLS, HIDDEN_COLS)
    ahead = ahead_copy(w_any, next_ref, sem, column)
    ahead.start()
    for at, columns, part in each_sum(core_ref, sums):
        middle_ref[at, columns] = x_ref[at, columns].astype(F32) + part[...].astype(F32)
    rows = middle_ref[...]
    second_ref[...] = (rows * inverse_norm(rows)).astype(BF16)
    outward = Outward(out_sems)
    outward.send(middle_ref, middle_any)
    outward.send(second_ref, second_any)
    for step, (gate, up) in enumerate(tiles):
        at = slice(HIDDEN_TILE * step, HIDDEN_TILE * (step + 1))
        gate_out = nn_dot(second_ref[...], w_ref[:, gate])
        up_out = nn_dot(second_ref[...], w_ref[:, up])
        gate_ref[:, at] = gate_out
        up_ref[:, at] = up_out
        hidden_ref[:, at] = (gate_out * sigmoid(gate_out) * up_out).astype(BF16)
    outward.send(gate_ref, gate_any)
    outward.send(up_ref, up_any)
    outward.send(hidden_ref, hidden_any)
    write_partial(core_ref, hidden_ref, w_ref, down, outs)
    outward.wait()
    ahead.wait()


HIDDEN_STEPS = HIDDEN_COLS // HIDDEN_TILE


def mlp_scratch():
    return [pltpu.VMEM((WIDTH, MLP_COLS), BF16), pltpu.SemaphoreType.DMA((2 * HIDDEN_STEPS + 1,))]


def mlp_cost(rows):
    return pl.CostEstimate(
        flops=2 * rows * WIDTH * MLP_COLS, bytes_accessed=15_000_000, transcendentals=0
    )


def mlp_forward(core, x, sums, near_weights, weights, column):
    rows = x.shape[0]
    saved = [
        shape(rows, WIDTH, F32),
        shape(rows, WIDTH, BF16),
        shape(rows, HIDDEN_COLS, F32),
        shape(rows, HIDDEN_COLS, F32),
        shape(rows, HIDDEN_COLS, BF16),
    ]
    return pl.pallas_call(
        functools.partial(mlp_forward_kernel, column),
        in_specs=[smem_whole()] + [vmem_whole()] * (2 + 2 * PARTS) + [hbm_whole()],
        out_specs=[hbm_whole()] * 5 + [vmem_whole()] * (1 + 2 * PARTS),
        out_shape=[far(array) for array in saved]
        + [shape(WIDTH, ATTN_COLS, BF16)]
        + part_shapes(rows),
        scratch_shapes=[pltpu.VMEM(out.shape, out.dtype) for out in saved]
        + [pltpu.SemaphoreType.DMA((5,)), pltpu.SemaphoreType.DMA(())],
        compiler_params=params(24),
        cost_estimate=mlp_cost(rows),
        name="mlp_forward",
    )(core, x, *sums, near_weights, in_hbm(weights))


def mlp_backward_tiles(g_ref, gate_ref, up_ref, arrive, pair_grad_ref, w_ref):
    for step, down in enumerate(column_tiles(2 * HIDDEN_COLS)):
        at = slice(HIDDEN_TILE * step, HIDDEN_TILE * (step + 1))
        up_at = slice(HIDDEN_COLS + at.start, HIDDEN_COLS + at.stop)
        arrive()
        hidden_grad = nn_dot(g_ref[...], w_ref[:, down])
        gate_out = gate_ref[:, at]
        sigmoid_gate = sigmoid(gate_out)
        pair_grad_ref[:, at] = (
            hidden_grad
            * up_ref[:, at]
            * (sigmoid_gate * (1.0 + gate_out * (1.0 - sigmoid_gate)))
        ).astype(BF16)
        pair_grad_ref[:, up_at] = (hidden_grad * (gate_out * sigmoid_gate)).astype(BF16)


def mlp_backward_copies(w_any, w_ref, sems):
    regions = [(pl.ds(0, WIDTH), columns) for columns in column_tiles(2 * HIDDEN_COLS)]
    regions.append((pl.ds(0, WIDTH), pl.ds(0, 2 * HIDDEN_COLS)))
    return arrivals(weight_copies(w_any, w_ref, sems, regions))


def mlp_backward_kernel(core_ref, x_ref, middle_grad_ref, *rest):
    sums, (gate_ref, up_ref, w_any, g_ref, pair_grad_ref) = rest[: 2 * PARTS], rest[2 * PARTS : 2 * PARTS + 5]
    outs, (w_ref, sems, weighted) = rest[2 * PARTS + 5 : -3], rest[-3:]
    arrive = mlp_backward_copies(w_any, w_ref, sems)
    for at, columns, part in each_sum(core_ref, sums):
        weighted[at, columns] = part[...].astype(F32)
    rows = x_ref[...].astype(F32)
    g_ref[...] = (
        middle_grad_ref[...] + norm_back(weighted[...], rows, inverse_norm(rows))
    ).astype(BF16)
    mlp_backward_tiles(g_ref, gate_ref, up_ref, arrive, pair_grad_ref, w_ref)
    arrive()
    write_partial(core_ref, pair_grad_ref, w_ref, slice(0, 2 * HIDDEN_COLS), outs)


def mlp_backward(core, above, gate_out, up_out, weights):
    rows = gate_out.shape[0]
    return pl.pallas_call(
        mlp_backward_kernel,
        in_specs=[smem_whole()] + [vmem_whole()] * (4 + 2 * PARTS) + [hbm_whole()],
        out_specs=[vmem_whole()] * (2 + 2 * PARTS),
        out_shape=[shape(rows, WIDTH, BF16), shape(rows, 2 * HIDDEN_COLS, BF16)] + part_shapes(rows),
        scratch_shapes=mlp_scratch() + [pltpu.VMEM((rows, WIDTH), F32)],
        compiler_params=params(24),
        cost_estimate=pl.CostEstimate(
            flops=2 * rows * WIDTH * MLP_COLS, bytes_accessed=15_000_000, transcendentals=0
        ),
        name="mlp_backward",
    )(core, *above, gate_out, up_out, in_hbm(weights))


def mlp_last_kernel(core_ref, x_ref, *rest):
    sums, (g_ref, w_any, middle_any, hidden_any, second_ref, hidden_ref, pair_grad_ref) = rest[: 2 * PARTS], rest[2 * PARTS : 2 * PARTS + 7]
    outs = rest[2 * PARTS + 7 : -6]
    w_ref, middle_ref, gate_ref, up_ref, sems, out_sems = rest[-6:]
    whole = pl.ds(0, WIDTH)
    tiles = [(gate, up) for gate, up in zip(column_tiles(0), column_tiles(HIDDEN_COLS))]
    regions = [(whole, columns) for pair in tiles for columns in pair]
    regions += [(whole, columns) for columns in column_tiles(2 * HIDDEN_COLS)]
    arrive = arrivals(weight_copies(w_any, w_ref, sems, regions))
    for at, columns, part in each_sum(core_ref, sums):
        middle_ref[at, columns] = x_ref[at, columns].astype(F32) + part[...].astype(F32)
    rows = middle_ref[...]
    second_ref[...] = (rows * inverse_norm(rows)).astype(BF16)
    outward = Outward(out_sems)
    outward.send(middle_ref, middle_any)
    for step, (gate, up) in enumerate(tiles):
        at = slice(HIDDEN_TILE * step, HIDDEN_TILE * (step + 1))
        arrive()
        gate_out = nn_dot(second_ref[...], w_ref[:, gate])
        arrive()
        up_out = nn_dot(second_ref[...], w_ref[:, up])
        gate_ref[:, at] = gate_out
        up_ref[:, at] = up_out
        hidden_ref[:, at] = (gate_out * sigmoid(gate_out) * up_out).astype(BF16)
    outward.send(hidden_ref, hidden_any)
    mlp_backward_tiles(g_ref, gate_ref, up_ref, arrive, pair_grad_ref, w_ref)
    write_partial(core_ref, pair_grad_ref, w_ref, slice(0, 2 * HIDDEN_COLS), outs)
    outward.wait()


def mlp_last(core, x, sums, g, weights):
    rows = x.shape[0]
    inner = [shape(rows, WIDTH, F32)] + [shape(rows, HIDDEN_COLS, F32)] * 2
    return pl.pallas_call(
        mlp_last_kernel,
        in_specs=[smem_whole()] + [vmem_whole()] * (2 + 2 * PARTS) + [hbm_whole()],
        out_specs=[hbm_whole()] * 2 + [vmem_whole()] * (3 + 2 * PARTS),
        out_shape=[
            pltpu.HBM((rows, WIDTH), F32),
            pltpu.HBM((rows, HIDDEN_COLS), BF16),
            shape(rows, WIDTH, BF16),
            shape(rows, HIDDEN_COLS, BF16),
            shape(rows, 2 * HIDDEN_COLS, BF16),
        ]
        + [far(part) for part in part_shapes(rows)],
        scratch_shapes=mlp_scratch()[:1]
        + [pltpu.VMEM(array.shape, array.dtype) for array in inner]
        + [
            pltpu.SemaphoreType.DMA((3 * HIDDEN_STEPS,)),
            pltpu.SemaphoreType.DMA((2,)),
        ],
        compiler_params=params(24),
        cost_estimate=pl.CostEstimate(
            flops=4 * rows * WIDTH * MLP_COLS, bytes_accessed=15_000_000, transcendentals=0
        ),
        name="mlp_last",
    )(core, x, *sums, g, in_hbm(weights))


def mlp_down_kernel(core_ref, hidden_ref, w_any, *rest):
    outs, w_ref, sem = rest[:-2], rest[-2], rest[-1]
    copy = pltpu.make_async_copy(w_any.at[:, pl.ds(2 * HIDDEN_COLS, HIDDEN_COLS)], w_ref, sem)
    copy.start()
    copy.wait()
    write_partial(core_ref, hidden_ref, w_ref, slice(0, HIDDEN_COLS), outs)


def mlp_down(core, hidden, weights):
    rows = hidden.shape[0]
    return pl.pallas_call(
        mlp_down_kernel,
        in_specs=[smem_whole(), vmem_whole(), hbm_whole()],
        out_specs=[vmem_whole()] * (2 * PARTS),
        out_shape=part_shapes(rows),
        scratch_shapes=[pltpu.VMEM((WIDTH, HIDDEN_COLS), BF16), pltpu.SemaphoreType.DMA(())],
        compiler_params=params(14),
        cost_estimate=pl.CostEstimate(
            flops=2 * rows * WIDTH * HIDDEN_COLS, bytes_accessed=5_000_000, transcendentals=0
        ),
        name="mlp_down",
    )(core, hidden, in_hbm(weights))


def attention_backward_kernel(sequences, column, near, core_ref, g_ref, middle_ref, *rest):
    sums, rest = rest[: 2 * PARTS], rest[2 * PARTS :]
    (qkv_any, prob_any, w_any, middle_grad_out, attn_in_ref, qkv_grad_ref), rest = rest[:6], rest[6:]
    outs, (middle_grad_ref, qkv_ref, prob_ref, mix_grad, w_ref, sem, sems) = rest[:-7], rest[-7:]
    copies = [
        ahead_copy(w_any, w_ref, sem, column),
        pltpu.make_async_copy(qkv_any, qkv_ref, sems.at[0]),
        pltpu.make_async_copy(prob_any, prob_ref, sems.at[1]),
    ]
    for copy in copies:
        copy.start()
    for at, columns, part in each_sum(core_ref, sums):
        middle_grad_ref[at, columns] = part[...].astype(F32)
    middle = middle_ref[...]
    middle_grad = g_ref[...].astype(F32) + norm_back(
        middle_grad_ref[...], middle, inverse_norm(middle)
    )
    if near:
        middle_grad_out[...] = middle_grad
    else:
        middle_grad_ref[...] = middle_grad
        outward = pltpu.make_async_copy(middle_grad_ref, middle_grad_out, sems.at[2])
        outward.start()
    attn_in_ref[...] = middle_grad.astype(BF16)
    copies[0].wait()
    mix_grad[...] = nn_dot(attn_in_ref[...], w_ref[:, QKV_COLS:]).astype(BF16)
    for copy in copies[1:]:
        copy.wait()
    for sequence in range(sequences):
        rows = slice(128 * sequence, 128 * (sequence + 1))
        for group in range(2):
            at = 2 * HEAD_WIDTH * group
            key_at = QUERY_COLS + HEAD_WIDTH * group
            value_at = key_at + KV_COLS
            grads = two_heads(mix_grad, rows, at)
            queries = two_heads(qkv_ref, rows, at)
            keys = qkv_ref[rows, key_at : key_at + HEAD_WIDTH]
            probability = prob_ref[2 * sequence + group]
            prob_grad = nt_dot(grads, qkv_ref[rows, value_at : value_at + HEAD_WIDTH])
            centred = jnp.sum(probability * prob_grad, axis=-1, keepdims=True)
            score_grad = (probability * (prob_grad - centred)).astype(BF16)
            query_grad = (nn_dot(score_grad, keys) * SCORE_SCALE).astype(BF16)
            qkv_grad_ref[rows, at : at + HEAD_WIDTH] = query_grad[:128]
            qkv_grad_ref[rows, at + HEAD_WIDTH : at + 2 * HEAD_WIDTH] = query_grad[128:]
            qkv_grad_ref[rows, key_at : key_at + HEAD_WIDTH] = (
                tn_dot(score_grad, queries) * SCORE_SCALE
            ).astype(BF16)
            qkv_grad_ref[rows, value_at : value_at + HEAD_WIDTH] = tn_dot(
                probability.astype(BF16), grads
            ).astype(BF16)
    if near:
        write_partial(core_ref, qkv_grad_ref, w_ref, slice(0, QKV_COLS), outs)
    else:
        outward.wait()


def attention_in_kernel(column, core_ref, qkv_grad_ref, w_any, *rest):
    outs, w_ref, sem = rest[:-2], rest[-2], rest[-1]
    copy = ahead_copy(w_any, w_ref, sem, column)
    copy.start()
    copy.wait()
    write_partial(core_ref, qkv_grad_ref, w_ref, slice(0, QKV_COLS), outs)


def attention_in(core, qkv_grad, weights, column):
    rows = qkv_grad.shape[0]
    return pl.pallas_call(
        functools.partial(attention_in_kernel, column),
        in_specs=[smem_whole(), vmem_whole(), hbm_whole()],
        out_specs=[vmem_whole()] * (2 * PARTS),
        out_shape=part_shapes(rows),
        scratch_shapes=attention_scratch(),
        compiler_params=params(14),
        cost_estimate=pl.CostEstimate(
            flops=2 * rows * WIDTH * QKV_COLS, bytes_accessed=5_000_000, transcendentals=0
        ),
        name="attention_in",
    )(core, qkv_grad, in_hbm(weights))


def attention_backward(core, g, middle, sums, qkv, probability, weights, column, near=True):
    rows = g.shape[0]
    residual, parts = shape(rows, WIDTH, F32), part_shapes(rows) if near else []
    return pl.pallas_call(
        functools.partial(attention_backward_kernel, rows // 128, column, near),
        in_specs=[smem_whole()] + [vmem_whole()] * (2 + 2 * PARTS) + [hbm_whole()] * 3,
        out_specs=[vmem_whole() if near else hbm_whole()] + [vmem_whole()] * (2 + len(parts)),
        out_shape=[
            residual if near else far(residual),
            shape(rows, WIDTH, BF16),
            shape(rows, QKV_COLS, BF16),
        ]
        + parts,
        scratch_shapes=[
            pltpu.VMEM((rows, WIDTH), F32),
            pltpu.VMEM(qkv.shape, BF16),
            pltpu.VMEM(probability.shape, F32),
            pltpu.VMEM((rows, OUT_COLS), BF16),
        ]
        + attention_scratch()
        + [pltpu.SemaphoreType.DMA((3,))],
        compiler_params=params(24),
        cost_estimate=pl.CostEstimate(
            flops=2 * rows * WIDTH * ATTN_COLS, bytes_accessed=12_000_000, transcendentals=0
        ),
        name="attention_backward",
    )(core, g, middle, *sums, in_hbm(qkv), in_hbm(probability), in_hbm(weights))


def write_products(start, pairs, out_any, slots, sems):
    _, height, width = slots.shape
    copies = []
    for number in range(WIDTH // height):
        features = pl.ds(height * number, height)
        if number >= 2:
            copies[number - 2].wait()
        slot = slots.at[number % 2]
        at = 0
        for left, right in pairs:
            columns = right.shape[1]
            slot[:, at : at + columns] = tn_dot(left[:, features], right[...]).astype(BF16)
            at += columns
        target = out_any.at[features, pl.ds(start, width)]
        copies.append(pltpu.make_async_copy(slot, target, sems.at[number % 2]))
        copies[-1].start()
    for copy in copies[-2:]:
        copy.wait()


def mlp_weights_kernel(second_ref, g_ref, pair_grad_ref, hidden_ref, *rest):
    out_any, slots, sems = rest[-3:]
    write_products(0, [(second_ref, pair_grad_ref), (g_ref, hidden_ref)], out_any, slots, sems)


def into_buffer(kernel, buffer, columns, slot, operands, flops, name, mib):
    aliases, specs = {}, [vmem_whole()] * len(operands)
    if buffer is not None:
        aliases = {len(operands): 0}
        specs, operands = specs + [hbm_whole()], operands + (in_hbm(buffer),)
    return pl.pallas_call(
        kernel,
        in_specs=specs,
        out_specs=hbm_whole(),
        out_shape=pltpu.HBM((WIDTH, columns), BF16),
        input_output_aliases=aliases,
        scratch_shapes=[pltpu.VMEM((2, *slot), BF16), pltpu.SemaphoreType.DMA((2,))],
        compiler_params=params(mib),
        cost_estimate=pl.CostEstimate(flops=flops, bytes_accessed=flops // 250, transcendentals=0),
        name=name,
    )(*operands)


def mlp_weights(buffer, columns, second, g, pair_grad, hidden):
    return into_buffer(
        mlp_weights_kernel,
        buffer,
        columns,
        (512, MLP_COLS),
        (second, g, pair_grad, hidden),
        2 * second.shape[0] * WIDTH * MLP_COLS,
        "mlp_weights",
        18,
    )


def attention_weights_kernel(start, first_ref, attn_in_ref, qkv_grad_ref, mix_ref, *rest):
    out_any, slots, sems = rest[-3:]
    pairs = [(first_ref, qkv_grad_ref), (attn_in_ref, mix_ref)]
    write_products(start, pairs, out_any, slots, sems)


def attention_weights(buffer, columns, start, first, attn_in, qkv_grad, mixture):
    return into_buffer(
        functools.partial(attention_weights_kernel, start),
        buffer,
        columns,
        (768, ATTN_COLS),
        (first, attn_in, qkv_grad, mixture),
        2 * first.shape[0] * WIDTH * ATTN_COLS,
        "attention_weights",
        14,
    )


def sum_four(partial, before=None, beside=None):
    keeps, gives = list(partial[:PARTS]), list(partial[PARTS:])
    if before is not None:
        keeps, before = lax.optimization_barrier((keeps, before))
    chips = [
        (keep.astype(F32) + swap(give, "section").astype(F32)).astype(BF16)
        for keep, give in zip(keeps, gives)
    ]
    arrived = [swap(chip, "tensor") for chip in chips]
    if beside is not None:
        arrived[0], beside = lax.optimization_barrier((arrived[0], beside))
    totals = [
        (chip.astype(F32) + other.astype(F32)).astype(BF16)
        for chip, other in zip(chips, arrived)
    ]
    return totals + [swap(total, "section") for total in totals], before, beside


def row_scales(gain_ref):
    row = lax.broadcasted_iota(jnp.int32, (48, 48), 0)
    column = lax.broadcasted_iota(jnp.int32, (48, 48), 1)
    return jnp.where(row == column, gain_ref[...].astype(F32), 0.0).astype(BF16)


def pack_kernel(core_ref, attn_gain_ref, mlp_gain_ref, *rest):
    sources, (mine_ref, give_ref), shards, sems = rest[:7], rest[7:9], rest[9:16], rest[16]
    copies = [
        pltpu.make_async_copy(source, shard, sems.at[number])
        for number, (source, shard) in enumerate(zip(sources, shards))
    ]
    for copy in copies:
        copy.start()
    is_first = core_ref[0] == 0
    attn_scale, mlp_scale = row_scales(attn_gain_ref), row_scales(mlp_gain_ref)
    start = 0
    for copy, shard, scale in zip(
        copies,
        shards,
        (mlp_scale, mlp_scale, None, attn_scale, attn_scale, attn_scale, None),
    ):
        copy.wait()
        weight = shard[...]
        if scale is not None:
            weight = nn_dot(scale, weight).astype(BF16)
        width = weight.shape[1] // 2
        low, high = weight[:, :width], weight[:, width:]
        mine_ref[:, start : start + width] = jnp.where(is_first, low, high)
        give_ref[:, start : start + width] = jnp.where(is_first, high, low)
        start += width


def pack_shards(core, attn_gain, mlp_gain, *shards):
    return pl.pallas_call(
        pack_kernel,
        in_specs=[smem_whole()] + [vmem_whole()] * 2 + [hbm_whole()] * len(shards),
        out_specs=[vmem_whole()] * 2,
        out_shape=[shape(48, LAYER_COLS, BF16)] * 2,
        scratch_shapes=[pltpu.VMEM(shard.shape, shard.dtype) for shard in shards]
        + [pltpu.SemaphoreType.DMA((len(shards),))],
        compiler_params=params(16),
        name="pack_shards",
    )(core, attn_gain, mlp_gain, *[in_hbm(shard) for shard in shards])


def combine_kernel(core_ref, keep_ref, arrived_ref, last_ref, zero_w_ref, one_w_ref, mine_ref, give_ref, terms_ref, zero, one):
    rest = (keep_ref[...].astype(F32) + arrived_ref[...].astype(F32)).astype(BF16)
    zero[:, :MLP_COLS] = rest[:, :MLP_COLS]
    zero[:, MLP_COLS:] = rest[:, LAYER_COLS:]
    one[:, :MLP_COLS] = last_ref[...]
    one[:, MLP_COLS:] = rest[:, MLP_COLS:LAYER_COLS]
    is_first = core_ref[0] == 0
    mine_ref[...] = jnp.where(is_first, zero[...], one[...])
    give_ref[...] = jnp.where(is_first, one[...], zero[...])
    row = 0
    for grad, weights in ((zero, zero_w_ref), (one, one_w_ref)):
        products = weights[...].astype(F32) * grad[...].astype(F32)
        for columns in (slice(MLP_COLS, MLP_COLS + QKV_COLS), slice(0, 2 * HIDDEN_COLS)):
            terms_ref[row, :] = jnp.sum(products[:, columns], axis=1)
            row += 1


def combine_grads(core, *operands):
    return pl.pallas_call(
        combine_kernel,
        in_specs=[smem_whole()] + [vmem_whole()] * len(operands),
        out_specs=[vmem_whole()] * 3,
        out_shape=[shape(48, LAYER_COLS, BF16)] * 2 + [shape(4, 48, F32)],
        scratch_shapes=[pltpu.VMEM((48, LAYER_COLS), BF16)] * 2,
        compiler_params=params(16),
        name="combine_grads",
    )(core, *operands)


def unpack_kernel(core_ref, attn_scale_ref, mlp_scale_ref, mine_ref, got_ref, gate_ref, up_ref, down_ref, query_ref, key_ref, value_ref, out_ref):
    is_first = core_ref[0] == 0

    def place(out, start, scale_ref):
        width = out.shape[1] // 2
        mine = mine_ref[:, start : start + width].astype(F32)
        got = got_ref[:, start : start + width].astype(F32)
        if scale_ref is not None:
            mine, got = mine * scale_ref[...], got * scale_ref[...]
        out[:, :width] = jnp.where(is_first, mine, got)
        out[:, width:] = jnp.where(is_first, got, mine)

    place(gate_ref, 0, mlp_scale_ref)
    place(up_ref, HIDDEN_COLS, mlp_scale_ref)
    place(down_ref, 2 * HIDDEN_COLS, None)
    place(query_ref, MLP_COLS, attn_scale_ref)
    place(key_ref, MLP_COLS + QUERY_COLS, attn_scale_ref)
    place(value_ref, MLP_COLS + QUERY_COLS + KV_COLS, attn_scale_ref)
    place(out_ref, MLP_COLS + QKV_COLS, None)


def unpack_grads(core, *operands):
    widths = [HIDDEN_COLS] * 3 + [QUERY_COLS, KV_COLS, KV_COLS, OUT_COLS]
    return pl.pallas_call(
        unpack_kernel,
        in_specs=[smem_whole()] + [vmem_whole()] * len(operands),
        out_specs=[vmem_whole()] * len(widths),
        out_shape=[shape(48, 2 * width, F32) for width in widths],
        compiler_params=params(16),
        name="unpack_grads",
    )(core, *operands)


def gather_rows(z_low, share):
    other = swap(share, "zl")
    pair = jnp.concatenate([pick(z_low, share, other), pick(z_low, other, share)], axis=0)
    return lax.all_gather(pair, ("y", "x"), axis=0, tiled=True)


def scatter_pair(grad):
    return lax.psum_scatter(grad, ("y", "x"), scatter_dimension=0, tiled=True)


def scatter_low(z_low, pair):
    keep = pick(z_low, pair[:48], pair[48:])
    give = pick(z_low, pair[48:], pair[:48])
    return (keep.astype(F32) + swap(give, "zl").astype(F32)).astype(BF16)


def to_ring_order(rows):
    lead = rows.shape[:-1]
    return jnp.swapaxes(rows.reshape(lead + (4, 2, 4, 48)), -3, -2).reshape(rows.shape)


def from_ring_order(rows):
    lead = rows.shape[:-1]
    return jnp.swapaxes(rows.reshape(lead + (4, 4, 2, 48)), -3, -2).reshape(rows.shape)


def join_positions(tensor, own):
    other = swap(own, "tensor")
    return jnp.concatenate(
        [pick(tensor, own, other), pick(tensor, other, own)], axis=1
    ).reshape(384, WIDTH)


def own_positions(tensor, rows):
    rows = rows.reshape(3, 128, 1536)
    return pick(tensor, rows[:, :64], rows[:, 64:])


def per_device(
    inputs, cotangent, plan, attn_gain, mlp_gain, w_query, key_weight, value_weight,
    w_out, w_gate, w_up, w_down,
):
    core = lax.axis_index("section")
    z_low = lax.axis_index("zl")
    tensor = lax.axis_index("tensor")

    attn_scale = attn_gain[0].astype(F32)[:, None]
    mlp_scale = mlp_gain[0].astype(F32)[:, None]

    core_ref = core.astype(jnp.int32).reshape(1)
    mine, give = pack_shards(
        core_ref, attn_gain, mlp_gain,
        w_gate[0], w_up[0], w_down[0].T, w_query[0], key_weight[0], value_weight[0], w_out[0].T,
    )
    got = swap(give, "section")
    layer_zero, layer_one = pick(core, mine, got), pick(core, got, mine)
    first_weights = gather_rows(
        z_low, jnp.concatenate([layer_zero, layer_one[:, MLP_COLS:]], axis=1)
    )
    last_weights = gather_rows(z_low, layer_one[:, :MLP_COLS])
    attn_weights = ((first_weights, MLP_COLS), (first_weights, LAYER_COLS))
    mlp_weights_of = (first_weights, last_weights)

    stream = join_positions(tensor, to_ring_order(inputs[:, 0][plan]))
    stream, late = lax.optimization_barrier((stream, cotangent))
    out_grad = join_positions(tensor, to_ring_order(late[:, 0][plan]))
    stream, out_grad = lax.optimization_barrier((stream, out_grad))

    def whole_rows(sums):
        own, other = jnp.concatenate(sums[:PARTS]), jnp.concatenate(sums[PARTS:])
        return jnp.concatenate([pick(core, own, other), pick(core, other, own)], axis=1).astype(F32)

    attn_zero, attn_one = attn_weights
    mlp_zero, mlp_one = mlp_weights_of

    x_zero = stream
    near, first_zero, qkv_zero, prob_zero, mix_zero, *partial = attention_first(
        core_ref, x_zero, first_weights, MLP_COLS
    )
    sums, _, _ = sum_four(partial)
    middle_zero, second_zero, gate_zero, up_zero, hidden_zero, near, *partial = mlp_forward(
        core_ref, x_zero, sums, near, first_weights, LAYER_COLS
    )
    sums, _, _ = sum_four(partial)
    x_one, first_one, qkv_one, prob_one, mix_one, *partial = attention_next(
        core_ref, middle_zero, sums, near
    )
    sums, _, _ = sum_four(partial)

    middle_one, hidden_far, second_one, hidden_one, pair_grad, *partial = mlp_last(
        core_ref, x_one, sums, out_grad, mlp_one
    )
    one_mlp = mlp_weights(None, MLP_COLS, second_one, out_grad, pair_grad, hidden_one)
    sums, one_mlp, _ = sum_four(partial, before=one_mlp)
    last_pair = scatter_pair(one_mlp)
    middle_grad, attn_in, qkv_grad, *partial = attention_backward(
        core_ref, out_grad, middle_one, sums, qkv_one, prob_one, *attn_one
    )
    buffer = attention_weights(None, REST_COLS, MLP_COLS, first_one, attn_in, qkv_grad, mix_one)
    sums, _, buffer = sum_four(partial, beside=buffer)

    grad_one, pair_grad, *partial = mlp_backward(
        core_ref, (x_one, middle_grad, *sums), gate_zero, up_zero, mlp_zero
    )
    buffer = mlp_weights(buffer, REST_COLS, second_zero, grad_one, pair_grad, hidden_zero)
    sums, _, buffer = sum_four(partial, beside=buffer)
    hidden_far, sums[0] = lax.optimization_barrier((hidden_far, sums[0]))
    down_partial = mlp_down(core_ref, hidden_far, mlp_one)
    middle_grad, attn_in, qkv_grad = attention_backward(
        core_ref, grad_one, middle_zero, sums, qkv_zero, prob_zero, *attn_zero, near=False
    )
    buffer = attention_weights(
        buffer, REST_COLS, LAYER_COLS, first_zero, attn_in, qkv_grad, mix_zero
    )
    rest_pair = scatter_pair(buffer)
    qkv_grad, buffer = lax.optimization_barrier((qkv_grad, buffer))
    sums, _, _ = sum_four(attention_in(core_ref, qkv_grad, *attn_zero))
    rows = x_zero.astype(F32)
    grad_zero = middle_grad + norm_back(whole_rows(sums), rows, inverse_norm(rows))
    down_sums, _, _ = sum_four(down_partial)
    result_one = (middle_one + whole_rows(down_sums)).astype(BF16)
    outputs = [own_positions(tensor, x_one), own_positions(tensor, result_one)]
    grads = [own_positions(tensor, grad_zero.astype(BF16)), own_positions(tensor, grad_one)]

    layer_outputs = from_ring_order(pick(core, outputs[0], outputs[1]))
    input_grads = from_ring_order(pick(core, grads[0], grads[1]))
    last_grad = scatter_low(z_low, last_pair)
    rest_pair, layer_outputs, input_grads, last_grad = lax.optimization_barrier(
        (rest_pair, layer_outputs, input_grads, last_grad)
    )
    keep = pick(z_low, rest_pair[:48], rest_pair[48:])
    arrived = swap(pick(z_low, rest_pair[48:], rest_pair[:48]), "zl")
    mine, give, terms = combine_grads(
        core_ref, keep, arrived, last_grad, layer_zero, layer_one
    )
    got = swap(give, "section")
    arrived = swap(terms, "tensor")
    gate_grad, up_grad, down_grad, query_grad, key_grad, value_grad, out_weight_grad = unpack_grads(
        core_ref, attn_scale, mlp_scale, mine, got
    )
    arrived, key_grad = lax.optimization_barrier((arrived, key_grad))
    terms = terms + arrived
    terms = pick(core, terms[:2], terms[2:]) + swap(pick(core, terms[2:], terms[:2]), "section")
    return (
        layer_outputs[None, :, None],
        input_grads[None, :, None],
        (terms[0] / attn_scale[:, 0])[None],
        (terms[1] / mlp_scale[:, 0])[None],
        query_grad[None],
        key_grad[None],
        value_grad[None],
        out_weight_grad.T[None],
        gate_grad[None],
        up_grad[None],
        down_grad.T[None],
    )


def solution(mesh):
    split = Mesh(mesh.devices.reshape(2, 4, 2, 4, 2), ("section", "y", "zl", "x", "tensor"))
    dp = ("y", "zl", "x")
    rows = P("section", dp, "tensor")
    columns = P("section", "tensor", dp)
    return jax.shard_map(
        per_device,
        mesh=split,
        in_specs=(
            P(None, dp, "tensor", None),
            P(None, dp, "tensor", None),
            P(),
            P("section", dp),
            P("section", dp),
            rows,
            rows,
            rows,
            columns,
            rows,
            rows,
            columns,
        ),
        out_specs=(
            P("section", None, dp, "tensor", None),
            P("section", None, dp, "tensor", None),
            P("section", dp),
            P("section", dp),
            rows,
            rows,
            rows,
            columns,
            rows,
            rows,
            columns,
        ),
        check_vma=False,
    )
```

```python
import functools

import jax
import jax.numpy as jnp
from jax import lax
from jax.experimental import pallas as pl
from jax.experimental.pallas import tpu as pltpu
from jax.sharding import Mesh, PartitionSpec as P

HEAD_WIDTH = 96
EPSILON = 1e-05
BLOCKED = -1e30
SCORE_SCALE = HEAD_WIDTH ** (-0.5)
BF16 = jnp.bfloat16
F32 = jnp.float32

QUERY_COLS, KV_COLS = 384, 192
QKV_COLS = QUERY_COLS + 2 * KV_COLS
OUT_COLS = 384
HIDDEN_COLS = 1024
ATTN_COLS = QKV_COLS + OUT_COLS
MLP_COLS = 3 * HIDDEN_COLS
LAYER_COLS = MLP_COLS + ATTN_COLS
REST_COLS = LAYER_COLS + ATTN_COLS
HIDDEN_TILE = 512
AHEAD = 3
WIDTH = 1536
HALF = WIDTH // 2
PARTS = 2
MIB = 1024 * 1024


def swap(value, axis):
    return lax.ppermute(value, axis, [(0, 1), (1, 0)])


def pick(index, first, second):
    return jnp.where(index == 0, first, second)


def norm_back(weighted, residual, inverse):
    scaled = residual * inverse
    return inverse * (weighted - scaled * jnp.mean(weighted * scaled, axis=-1, keepdims=True))


def vmem_whole():
    return pl.BlockSpec(memory_space=pltpu.VMEM)


def smem_whole():
    return pl.BlockSpec(memory_space=pltpu.SMEM)


def shape(rows, columns, dtype):
    return jax.ShapeDtypeStruct((rows, columns), dtype)


def half_of(core_ref, which):
    position = core_ref[0] if which == 0 else 1 - core_ref[0]
    return pl.ds(pl.multiple_of(position * HALF, HALF), HALF)


def nt_dot(left_side, right_side):
    return lax.dot_general(
        left_side, right_side, (((1,), (1,)), ((), ())), preferred_element_type=F32
    )


def tn_dot(left_side, right_side):
    return lax.dot_general(
        left_side, right_side, (((0,), (0,)), ((), ())), preferred_element_type=F32
    )


def nn_dot(left_side, right_side):
    return jnp.dot(left_side, right_side, preferred_element_type=F32)


def row_parts(rows):
    return [slice(rows // PARTS * part, rows // PARTS * (part + 1)) for part in range(PARTS)]


def part_shapes(rows):
    return [shape(rows // PARTS, HALF, BF16)] * (2 * PARTS)


class Outward:
    def __init__(self, sems):
        self.sems, self.copies = sems, []

    def send(self, source, target):
        self.copies.append(pltpu.make_async_copy(source, target, self.sems.at[len(self.copies)]))
        self.copies[-1].start()

    def wait(self):
        for copy in self.copies:
            copy.wait()


def far(array):
    return pltpu.HBM(array.shape, array.dtype)


def each_sum(core_ref, sum_refs):
    rows = sum_refs[0].shape[0] * PARTS
    for which in range(2):
        for part, at in enumerate(row_parts(rows)):
            yield at, half_of(core_ref, which), sum_refs[PARTS * which + part]


def write_partial(core_ref, left_ref, w_ref, columns, outs):
    keeps, gives = outs[:PARTS], outs[PARTS:]
    for which, refs in ((1, gives), (0, keeps)):
        product = nt_dot(left_ref[...], w_ref[half_of(core_ref, which), columns]).astype(BF16)
        for at, ref in zip(row_parts(left_ref.shape[0]), refs):
            ref[...] = product[at]


def params(mib):
    return pltpu.CompilerParams(vmem_limit_bytes=mib * MIB)


def inverse_norm(rows):
    return lax.rsqrt(jnp.mean(rows * rows, axis=-1, keepdims=True) + EPSILON)


def causal_mask():
    row = lax.broadcasted_iota(jnp.int32, (128, 128), 0)
    return row >= lax.broadcasted_iota(jnp.int32, (128, 128), 1)


def two_heads(ref, rows, start):
    return jnp.concatenate(
        [
            ref[rows, start : start + HEAD_WIDTH],
            ref[rows, start + HEAD_WIDTH : start + 2 * HEAD_WIDTH],
        ],
        axis=0,
    )


def ahead_copy(w_any, w_ref, sem, column):
    return pltpu.make_async_copy(w_any.at[:, pl.ds(column, w_ref.shape[1])], w_ref, sem)


def attention_forward_body(sequences, core_ref, outward, first_ref, w_ref, qkv_any, prob_ref, mix_ref, *rest):
    parts, qkv_ref = rest[:-1], rest[-1]
    qkv_ref[...] = nn_dot(first_ref[...], w_ref[:, :QKV_COLS]).astype(BF16)
    outward.send(qkv_ref, qkv_any)
    mask = causal_mask()
    mask = jnp.concatenate([mask, mask], axis=0)
    for sequence in range(sequences):
        rows = slice(128 * sequence, 128 * (sequence + 1))
        for group in range(2):
            queries = two_heads(qkv_ref, rows, 2 * HEAD_WIDTH * group)
            key_at = QUERY_COLS + HEAD_WIDTH * group
            value_at = key_at + KV_COLS
            scores = nt_dot(queries, qkv_ref[rows, key_at : key_at + HEAD_WIDTH]) * SCORE_SCALE
            scores = jnp.where(mask, scores, BLOCKED)
            expanded = jnp.exp(scores - jnp.max(scores, axis=-1, keepdims=True))
            probability = expanded / jnp.sum(expanded, axis=-1, keepdims=True)
            prob_ref[2 * sequence + group] = probability
            mixed = nn_dot(
                probability.astype(BF16), qkv_ref[rows, value_at : value_at + HEAD_WIDTH]
            ).astype(BF16)
            at = 2 * HEAD_WIDTH * group
            mix_ref[rows, at : at + HEAD_WIDTH] = mixed[:128]
            mix_ref[rows, at + HEAD_WIDTH : at + 2 * HEAD_WIDTH] = mixed[128:]
    write_partial(core_ref, mix_ref, w_ref, slice(QKV_COLS, ATTN_COLS), parts)
    outward.wait()


def attention_first_kernel(sequences, column, core_ref, x_ref, w_any, first_ref, *rest):
    outs, (w_ref, sem, sems) = rest[:-3], rest[-3:]
    copy = ahead_copy(w_any, w_ref, sem, column)
    copy.start()
    rows = x_ref[...].astype(F32)
    first_ref[...] = (rows * inverse_norm(rows)).astype(BF16)
    copy.wait()
    attention_forward_body(sequences, core_ref, Outward(sems), first_ref, w_ref, *outs)


def attention_next_kernel(sequences, core_ref, middle_ref, *rest):
    sums, (w_ref, _, x_any, first_any) = rest[: 2 * PARTS], rest[2 * PARTS : 2 * PARTS + 4]
    outs, (x_ref, first_ref, sems) = rest[2 * PARTS + 4 : -3], rest[-3:]
    outward = Outward(sems)
    for at, columns, part in each_sum(core_ref, sums):
        x_ref[at, columns] = (middle_ref[at, columns] + part[...].astype(F32)).astype(BF16)
    outward.send(x_ref, x_any)
    rows = x_ref[...].astype(F32)
    first_ref[...] = (rows * inverse_norm(rows)).astype(BF16)
    outward.send(first_ref, first_any)
    attention_forward_body(sequences, core_ref, outward, first_ref, w_ref, *outs)


def in_hbm(value):
    return pltpu.with_memory_space_constraint(value, pltpu.HBM)


def hbm_whole():
    return pl.BlockSpec(memory_space=pltpu.HBM)


def attention_scratch():
    return [pltpu.VMEM((WIDTH, ATTN_COLS), BF16), pltpu.SemaphoreType.DMA(())]


def attention_outs(rows):
    outs = [
        shape(rows, WIDTH, BF16),
        far(shape(rows, QKV_COLS, BF16)),
        jax.ShapeDtypeStruct((rows // 64, 256, 128), F32),
        shape(rows, OUT_COLS, BF16),
    ]
    return outs + part_shapes(rows), [vmem_whole(), hbm_whole()] + [vmem_whole()] * (2 + 2 * PARTS)


def attention_cost(rows):
    return pl.CostEstimate(
        flops=2 * rows * WIDTH * ATTN_COLS, bytes_accessed=8_000_000, transcendentals=0
    )


def fetch_kernel(column, w_any, *rest):
    out_ref, token_ref, sem = rest[-3:]
    copy = ahead_copy(w_any, out_ref, sem, column)
    copy.start()
    token_ref[...] = jnp.zeros_like(token_ref)
    copy.wait()


TOKEN = jax.ShapeDtypeStruct((8, 128), F32)


def fetch(weights, column, columns, *after):
    return pl.pallas_call(
        functools.partial(fetch_kernel, column),
        in_specs=[hbm_whole()] * (1 + len(after)),
        out_specs=[vmem_whole()] * 2,
        out_shape=[shape(WIDTH, columns, BF16), TOKEN],
        scratch_shapes=[pltpu.SemaphoreType.DMA(())],
        compiler_params=params(12),
        cost_estimate=pl.CostEstimate(
            flops=0, bytes_accessed=2 * WIDTH * columns * 2, transcendentals=0
        ),
        name="fetch",
    )(in_hbm(weights), *[in_hbm(value) for value in after])


def attention_first(core, x, weights, column):
    rows = x.shape[0]
    outs, specs = attention_outs(rows)
    return pl.pallas_call(
        functools.partial(attention_first_kernel, rows // 128, column),
        in_specs=[smem_whole(), vmem_whole(), hbm_whole()],
        out_specs=specs,
        out_shape=outs,
        scratch_shapes=[pltpu.VMEM((rows, QKV_COLS), BF16)]
        + attention_scratch()
        + [pltpu.SemaphoreType.DMA((1,))],
        compiler_params=params(20),
        cost_estimate=attention_cost(rows),
        name="attention_first",
    )(core, x, in_hbm(weights))


def attention_next(core, middle, sums, weights, token):
    rows = middle.shape[0]
    outs, specs = attention_outs(rows)
    whole = shape(rows, WIDTH, BF16)
    return pl.pallas_call(
        functools.partial(attention_next_kernel, rows // 128),
        in_specs=[smem_whole()] + [vmem_whole()] * (2 + 2 * PARTS) + [hbm_whole()],
        out_specs=[hbm_whole()] * 2 + specs[1:],
        out_shape=[far(whole)] * 2 + outs[1:],
        scratch_shapes=[
            pltpu.VMEM((rows, QKV_COLS), BF16),
            pltpu.VMEM(whole.shape, BF16),
            pltpu.VMEM(whole.shape, BF16),
            pltpu.SemaphoreType.DMA((3,)),
        ],
        compiler_params=params(16),
        cost_estimate=attention_cost(rows),
        name="attention_next",
    )(core, middle, *sums, weights, token)


def column_tiles(first):
    return [pl.ds(first + HIDDEN_TILE * step, HIDDEN_TILE) for step in range(HIDDEN_STEPS)]


def sigmoid(values):
    return 0.5 * jnp.tanh(0.5 * values) + 0.5


def arrivals(copies):
    for copy in copies[:AHEAD]:
        copy.start()
    place = iter(range(len(copies)))

    def arrive():
        number = next(place)
        copies[number].wait()
        if number + AHEAD < len(copies):
            copies[number + AHEAD].start()

    return arrive


def mlp_forward_kernel(core_ref, x_ref, *rest):
    sums, rest = rest[: 2 * PARTS], rest[2 * PARTS :]
    (w_ref, _, middle_any, second_any, gate_any, up_any, hidden_any), rest = rest[:7], rest[7:]
    outs, (middle_ref, second_ref, gate_ref, up_ref, hidden_ref, out_sems) = rest[:-6], rest[-6:]
    tiles = [(gate, up) for gate, up in zip(column_tiles(0), column_tiles(HIDDEN_COLS))]
    down = pl.ds(2 * HIDDEN_COLS, HIDDEN_COLS)
    for at, columns, part in each_sum(core_ref, sums):
        middle_ref[at, columns] = x_ref[at, columns].astype(F32) + part[...].astype(F32)
    rows = middle_ref[...]
    second_ref[...] = (rows * inverse_norm(rows)).astype(BF16)
    outward = Outward(out_sems)
    outward.send(middle_ref, middle_any)
    outward.send(second_ref, second_any)
    for step, (gate, up) in enumerate(tiles):
        at = slice(HIDDEN_TILE * step, HIDDEN_TILE * (step + 1))
        gate_out = nn_dot(second_ref[...], w_ref[:, gate])
        up_out = nn_dot(second_ref[...], w_ref[:, up])
        gate_ref[:, at] = gate_out
        up_ref[:, at] = up_out
        hidden_ref[:, at] = (gate_out * sigmoid(gate_out) * up_out).astype(BF16)
        for ref, target in ((gate_ref, gate_any), (up_ref, up_any), (hidden_ref, hidden_any)):
            outward.send(ref.at[:, at], target.at[:, at])
    write_partial(core_ref, hidden_ref, w_ref, down, outs)
    outward.wait()


HIDDEN_STEPS = HIDDEN_COLS // HIDDEN_TILE


def mlp_cost(rows):
    return pl.CostEstimate(
        flops=2 * rows * WIDTH * MLP_COLS, bytes_accessed=15_000_000, transcendentals=0
    )


def mlp_forward(core, x, sums, weights, token):
    rows = x.shape[0]
    saved = [
        shape(rows, WIDTH, F32),
        shape(rows, WIDTH, BF16),
        shape(rows, HIDDEN_COLS, F32),
        shape(rows, HIDDEN_COLS, F32),
        shape(rows, HIDDEN_COLS, BF16),
    ]
    return pl.pallas_call(
        mlp_forward_kernel,
        in_specs=[smem_whole()] + [vmem_whole()] * (2 + 2 * PARTS) + [hbm_whole()],
        out_specs=[hbm_whole()] * 5 + [vmem_whole()] * (2 * PARTS),
        out_shape=[far(array) for array in saved] + part_shapes(rows),
        scratch_shapes=[pltpu.VMEM(out.shape, out.dtype) for out in saved]
        + [pltpu.SemaphoreType.DMA((2 + 3 * HIDDEN_STEPS,))],
        compiler_params=params(24),
        cost_estimate=mlp_cost(rows),
        name="mlp_forward",
    )(core, x, *sums, weights, token)


def mlp_grads(hidden_grad, gate_out, up_out):
    sigmoid_gate = sigmoid(gate_out)
    gate_grad = hidden_grad * up_out * (sigmoid_gate * (1.0 + gate_out * (1.0 - sigmoid_gate)))
    return gate_grad.astype(BF16), (hidden_grad * (gate_out * sigmoid_gate)).astype(BF16)


def mlp_backward_kernel(core_ref, x_ref, middle_grad_ref, *rest):
    sums, rest = rest[: 2 * PARTS], rest[2 * PARTS :]
    (gate_ref, up_ref, w_ref, _, g_ref, pair_grad_ref), rest = rest[:6], rest[6:]
    outs, weighted = rest[:-1], rest[-1]
    for at, columns, part in each_sum(core_ref, sums):
        weighted[at, columns] = part[...].astype(F32)
    rows = x_ref[...].astype(F32)
    g_ref[...] = (
        middle_grad_ref[...] + norm_back(weighted[...], rows, inverse_norm(rows))
    ).astype(BF16)
    for step, down in enumerate(column_tiles(2 * HIDDEN_COLS)):
        at = slice(HIDDEN_TILE * step, HIDDEN_TILE * (step + 1))
        up_at = slice(HIDDEN_COLS + at.start, HIDDEN_COLS + at.stop)
        hidden_grad = nn_dot(g_ref[...], w_ref[:, down])
        pair_grad_ref[:, at], pair_grad_ref[:, up_at] = mlp_grads(
            hidden_grad, gate_ref[:, at], up_ref[:, at]
        )
    write_partial(core_ref, pair_grad_ref, w_ref, slice(0, 2 * HIDDEN_COLS), outs)


def mlp_backward(core, above, gate_out, up_out, weights, token):
    rows = gate_out.shape[0]
    return pl.pallas_call(
        mlp_backward_kernel,
        in_specs=[smem_whole()] + [vmem_whole()] * (5 + 2 * PARTS) + [hbm_whole()],
        out_specs=[vmem_whole()] * (2 + 2 * PARTS),
        out_shape=[shape(rows, WIDTH, BF16), shape(rows, 2 * HIDDEN_COLS, BF16)]
        + part_shapes(rows),
        scratch_shapes=[pltpu.VMEM((rows, WIDTH), F32)],
        compiler_params=params(26),
        cost_estimate=mlp_cost(rows),
        name="mlp_backward",
    )(core, *above, gate_out, up_out, weights, token)


def mlp_ahead_kernel(g_ref, w_any, hidden_grad_ref, pair_ref, token_ref, down_ref, sems):
    down = ahead_copy(w_any, down_ref, sems.at[0], 2 * HIDDEN_COLS)
    pair = ahead_copy(w_any, pair_ref, sems.at[1], 0)
    down.start()
    pair.start()
    token_ref[...] = jnp.zeros_like(token_ref)
    down.wait()
    hidden_grad_ref[...] = nn_dot(g_ref[...], down_ref[...])
    pair.wait()


def mlp_ahead(g, weights):
    rows = g.shape[0]
    return pl.pallas_call(
        mlp_ahead_kernel,
        in_specs=[vmem_whole(), hbm_whole()],
        out_specs=[vmem_whole()] * 3,
        out_shape=[
            shape(rows, HIDDEN_COLS, F32),
            shape(WIDTH, 2 * HIDDEN_COLS, BF16),
            TOKEN,
        ],
        scratch_shapes=[pltpu.VMEM((WIDTH, HIDDEN_COLS), BF16), pltpu.SemaphoreType.DMA((2,))],
        compiler_params=params(15),
        cost_estimate=pl.CostEstimate(
            flops=2 * rows * WIDTH * HIDDEN_COLS, bytes_accessed=14_000_000, transcendentals=0
        ),
        name="mlp_ahead",
    )(g, in_hbm(weights))


def mlp_last_kernel(core_ref, x_ref, *rest):
    sums, rest = rest[: 2 * PARTS], rest[2 * PARTS :]
    (hidden_grad_ref, w_ref, _, middle_any, hidden_any, second_ref, hidden_ref, pair_grad_ref), rest = rest[:8], rest[8:]
    outs, (middle_ref, out_sems) = rest[:-2], rest[-2:]
    for at, columns, part in each_sum(core_ref, sums):
        middle_ref[at, columns] = x_ref[at, columns].astype(F32) + part[...].astype(F32)
    rows = middle_ref[...]
    second_ref[...] = (rows * inverse_norm(rows)).astype(BF16)
    outward = Outward(out_sems)
    outward.send(middle_ref, middle_any)
    for step, (gate, up) in enumerate(zip(column_tiles(0), column_tiles(HIDDEN_COLS))):
        at = slice(HIDDEN_TILE * step, HIDDEN_TILE * (step + 1))
        up_at = slice(HIDDEN_COLS + at.start, HIDDEN_COLS + at.stop)
        gate_out = nn_dot(second_ref[...], w_ref[:, gate])
        up_out = nn_dot(second_ref[...], w_ref[:, up])
        hidden_ref[:, at] = (gate_out * sigmoid(gate_out) * up_out).astype(BF16)
        pair_grad_ref[:, at], pair_grad_ref[:, up_at] = mlp_grads(
            hidden_grad_ref[:, at], gate_out, up_out
        )
    outward.send(hidden_ref, hidden_any)
    write_partial(core_ref, pair_grad_ref, w_ref, slice(0, 2 * HIDDEN_COLS), outs)
    outward.wait()


def mlp_last(core, x, sums, hidden_grad, pair_weights, token):
    rows = x.shape[0]
    return pl.pallas_call(
        mlp_last_kernel,
        in_specs=[smem_whole()] + [vmem_whole()] * (3 + 2 * PARTS) + [hbm_whole()],
        out_specs=[hbm_whole()] * 2 + [vmem_whole()] * (3 + 2 * PARTS),
        out_shape=[
            pltpu.HBM((rows, WIDTH), F32),
            pltpu.HBM((rows, HIDDEN_COLS), BF16),
            shape(rows, WIDTH, BF16),
            shape(rows, HIDDEN_COLS, BF16),
            shape(rows, 2 * HIDDEN_COLS, BF16),
        ]
        + [far(part) for part in part_shapes(rows)],
        scratch_shapes=[pltpu.VMEM((rows, WIDTH), F32), pltpu.SemaphoreType.DMA((2,))],
        compiler_params=params(28),
        cost_estimate=mlp_cost(rows),
        name="mlp_last",
    )(core, x, *sums, hidden_grad, pair_weights, token)


def mlp_down_kernel(core_ref, hidden_ref, w_any, *rest):
    outs, w_ref, sem = rest[:-2], rest[-2], rest[-1]
    copy = pltpu.make_async_copy(w_any.at[:, pl.ds(2 * HIDDEN_COLS, HIDDEN_COLS)], w_ref, sem)
    copy.start()
    copy.wait()
    write_partial(core_ref, hidden_ref, w_ref, slice(0, HIDDEN_COLS), outs)


def mlp_down(core, hidden, weights):
    rows = hidden.shape[0]
    return pl.pallas_call(
        mlp_down_kernel,
        in_specs=[smem_whole(), vmem_whole(), hbm_whole()],
        out_specs=[vmem_whole()] * (2 * PARTS),
        out_shape=part_shapes(rows),
        scratch_shapes=[pltpu.VMEM((WIDTH, HIDDEN_COLS), BF16), pltpu.SemaphoreType.DMA(())],
        compiler_params=params(14),
        cost_estimate=pl.CostEstimate(
            flops=2 * rows * WIDTH * HIDDEN_COLS, bytes_accessed=5_000_000, transcendentals=0
        ),
        name="mlp_down",
    )(core, hidden, in_hbm(weights))


def attention_backward_kernel(sequences, near, core_ref, g_ref, middle_ref, *rest):
    sums, rest = rest[: 2 * PARTS], rest[2 * PARTS :]
    (w_ref, qkv_any, prob_any, _, middle_grad_out, attn_in_ref, qkv_grad_ref), rest = rest[:7], rest[7:]
    outs, (middle_grad_ref, qkv_ref, prob_ref, mix_grad, sems) = rest[:-5], rest[-5:]
    copies = [
        pltpu.make_async_copy(qkv_any, qkv_ref, sems.at[0]),
        pltpu.make_async_copy(prob_any, prob_ref, sems.at[1]),
    ]
    for copy in copies:
        copy.start()
    for at, columns, part in each_sum(core_ref, sums):
        middle_grad_ref[at, columns] = part[...].astype(F32)
    middle = middle_ref[...]
    middle_grad = g_ref[...].astype(F32) + norm_back(
        middle_grad_ref[...], middle, inverse_norm(middle)
    )
    if near:
        middle_grad_out[...] = middle_grad
    else:
        middle_grad_ref[...] = middle_grad
        outward = pltpu.make_async_copy(middle_grad_ref, middle_grad_out, sems.at[2])
        outward.start()
    attn_in_ref[...] = middle_grad.astype(BF16)
    mix_grad[...] = nn_dot(attn_in_ref[...], w_ref[:, QKV_COLS:]).astype(BF16)
    for copy in copies:
        copy.wait()
    for sequence in range(sequences):
        rows = slice(128 * sequence, 128 * (sequence + 1))
        for group in range(2):
            at = 2 * HEAD_WIDTH * group
            key_at = QUERY_COLS + HEAD_WIDTH * group
            value_at = key_at + KV_COLS
            grads = two_heads(mix_grad, rows, at)
            queries = two_heads(qkv_ref, rows, at)
            keys = qkv_ref[rows, key_at : key_at + HEAD_WIDTH]
            probability = prob_ref[2 * sequence + group]
            prob_grad = nt_dot(grads, qkv_ref[rows, value_at : value_at + HEAD_WIDTH])
            centred = jnp.sum(probability * prob_grad, axis=-1, keepdims=True)
            score_grad = (probability * (prob_grad - centred)).astype(BF16)
            query_grad = (nn_dot(score_grad, keys) * SCORE_SCALE).astype(BF16)
            qkv_grad_ref[rows, at : at + HEAD_WIDTH] = query_grad[:128]
            qkv_grad_ref[rows, at + HEAD_WIDTH : at + 2 * HEAD_WIDTH] = query_grad[128:]
            qkv_grad_ref[rows, key_at : key_at + HEAD_WIDTH] = (
                tn_dot(score_grad, queries) * SCORE_SCALE
            ).astype(BF16)
            qkv_grad_ref[rows, value_at : value_at + HEAD_WIDTH] = tn_dot(
                probability.astype(BF16), grads
            ).astype(BF16)
    if near:
        write_partial(core_ref, qkv_grad_ref, w_ref, slice(0, QKV_COLS), outs)
    else:
        outward.wait()


def attention_in_kernel(core_ref, qkv_grad_ref, w_ref, *outs):
    write_partial(core_ref, qkv_grad_ref, w_ref, slice(0, QKV_COLS), outs)


def attention_in(core, qkv_grad, weights):
    rows = qkv_grad.shape[0]
    return pl.pallas_call(
        attention_in_kernel,
        in_specs=[smem_whole()] + [vmem_whole()] * 2,
        out_specs=[vmem_whole()] * (2 * PARTS),
        out_shape=part_shapes(rows),
        compiler_params=params(14),
        cost_estimate=pl.CostEstimate(
            flops=2 * rows * WIDTH * QKV_COLS, bytes_accessed=5_000_000, transcendentals=0
        ),
        name="attention_in",
    )(core, qkv_grad, weights)


def attention_backward(core, g, middle, sums, qkv, probability, weights, token, near):
    rows = g.shape[0]
    residual, parts = shape(rows, WIDTH, F32), part_shapes(rows) if near else []
    return pl.pallas_call(
        functools.partial(attention_backward_kernel, rows // 128, near),
        in_specs=[smem_whole()] + [vmem_whole()] * (3 + 2 * PARTS) + [hbm_whole()] * 3,
        out_specs=[vmem_whole() if near else hbm_whole()] + [vmem_whole()] * (2 + len(parts)),
        out_shape=[
            residual if near else far(residual),
            shape(rows, WIDTH, BF16),
            shape(rows, QKV_COLS, BF16),
        ]
        + parts,
        scratch_shapes=[
            pltpu.VMEM((rows, WIDTH), F32),
            pltpu.VMEM(qkv.shape, BF16),
            pltpu.VMEM(probability.shape, F32),
            pltpu.VMEM((rows, OUT_COLS), BF16),
            pltpu.SemaphoreType.DMA((3,)),
        ],
        compiler_params=params(24),
        cost_estimate=attention_cost(rows),
        name="attention_backward",
    )(core, g, middle, *sums, weights, in_hbm(qkv), in_hbm(probability), token)


def write_products(start, pairs, out_any, slots, sems):
    _, height, width = slots.shape
    copies = []
    for number in range(WIDTH // height):
        features = pl.ds(height * number, height)
        if number >= 2:
            copies[number - 2].wait()
        slot = slots.at[number % 2]
        at = 0
        for left, right in pairs:
            columns = right.shape[1]
            slot[:, at : at + columns] = tn_dot(left[:, features], right[...]).astype(BF16)
            at += columns
        target = out_any.at[features, pl.ds(start, width)]
        copies.append(pltpu.make_async_copy(slot, target, sems.at[number % 2]))
        copies[-1].start()
    for copy in copies[-2:]:
        copy.wait()


def mlp_weights_kernel(second_ref, g_ref, pair_grad_ref, hidden_ref, *rest):
    out_any, slots, sems = rest[-3:]
    write_products(0, [(second_ref, pair_grad_ref), (g_ref, hidden_ref)], out_any, slots, sems)


def into_buffer(kernel, buffer, columns, slot, operands, flops, name, mib):
    aliases, specs = {}, [vmem_whole()] * len(operands)
    if buffer is not None:
        aliases = {len(operands): 0}
        specs, operands = specs + [hbm_whole()], operands + (in_hbm(buffer),)
    return pl.pallas_call(
        kernel,
        in_specs=specs,
        out_specs=hbm_whole(),
        out_shape=pltpu.HBM((WIDTH, columns), BF16),
        input_output_aliases=aliases,
        scratch_shapes=[pltpu.VMEM((2, *slot), BF16), pltpu.SemaphoreType.DMA((2,))],
        compiler_params=params(mib),
        cost_estimate=pl.CostEstimate(flops=flops, bytes_accessed=flops // 250, transcendentals=0),
        name=name,
    )(*operands)


def mlp_weights(buffer, columns, second, g, pair_grad, hidden):
    return into_buffer(
        mlp_weights_kernel,
        buffer,
        columns,
        (512, MLP_COLS),
        (second, g, pair_grad, hidden),
        2 * second.shape[0] * WIDTH * MLP_COLS,
        "mlp_weights",
        18,
    )


def attention_weights_kernel(start, first_ref, attn_in_ref, qkv_grad_ref, mix_ref, *rest):
    out_any, slots, sems = rest[-3:]
    pairs = [(first_ref, qkv_grad_ref), (attn_in_ref, mix_ref)]
    write_products(start, pairs, out_any, slots, sems)


def attention_weights(buffer, columns, start, first, attn_in, qkv_grad, mixture):
    return into_buffer(
        functools.partial(attention_weights_kernel, start),
        buffer,
        columns,
        (768, ATTN_COLS),
        (first, attn_in, qkv_grad, mixture),
        2 * first.shape[0] * WIDTH * ATTN_COLS,
        "attention_weights",
        14,
    )


def sum_four(partial, before=None, beside=None):
    keeps, gives = list(partial[:PARTS]), list(partial[PARTS:])
    if before is not None:
        keeps, before = lax.optimization_barrier((keeps, before))
    chips = [
        (keep.astype(F32) + swap(give, "section").astype(F32)).astype(BF16)
        for keep, give in zip(keeps, gives)
    ]
    arrived = [swap(chip, "tensor") for chip in chips]
    if beside is not None:
        arrived[0], beside = lax.optimization_barrier((arrived[0], beside))
    totals = [
        (chip.astype(F32) + other.astype(F32)).astype(BF16)
        for chip, other in zip(chips, arrived)
    ]
    return totals + [swap(total, "section") for total in totals], *([] if before is None else [before]), beside


def row_scales(gain_ref):
    row = lax.broadcasted_iota(jnp.int32, (48, 48), 0)
    column = lax.broadcasted_iota(jnp.int32, (48, 48), 1)
    return jnp.where(row == column, gain_ref[...].astype(F32), 0.0).astype(BF16)


def pack_kernel(core_ref, attn_gain_ref, mlp_gain_ref, *rest):
    sources, (mine_ref, give_ref), shards, sems = rest[:7], rest[7:9], rest[9:16], rest[16]
    copies = [
        pltpu.make_async_copy(source, shard, sems.at[number])
        for number, (source, shard) in enumerate(zip(sources, shards))
    ]
    for copy in copies:
        copy.start()
    is_first = core_ref[0] == 0
    attn_scale, mlp_scale = row_scales(attn_gain_ref), row_scales(mlp_gain_ref)
    start = 0
    for copy, shard, scale in zip(
        copies,
        shards,
        (mlp_scale, mlp_scale, None, attn_scale, attn_scale, attn_scale, None),
    ):
        copy.wait()
        weight = shard[...]
        if scale is not None:
            weight = nn_dot(scale, weight).astype(BF16)
        width = weight.shape[1] // 2
        low, high = weight[:, :width], weight[:, width:]
        mine_ref[:, start : start + width] = jnp.where(is_first, low, high)
        give_ref[:, start : start + width] = jnp.where(is_first, high, low)
        start += width


def pack_shards(core, attn_gain, mlp_gain, *shards):
    return pl.pallas_call(
        pack_kernel,
        in_specs=[smem_whole()] + [vmem_whole()] * 2 + [hbm_whole()] * len(shards),
        out_specs=[vmem_whole()] * 2,
        out_shape=[shape(48, LAYER_COLS, BF16)] * 2,
        scratch_shapes=[pltpu.VMEM(shard.shape, shard.dtype) for shard in shards]
        + [pltpu.SemaphoreType.DMA((len(shards),))],
        compiler_params=params(16),
        name="pack_shards",
    )(core, attn_gain, mlp_gain, *[in_hbm(shard) for shard in shards])


def combine_kernel(core_ref, keep_ref, arrived_ref, last_ref, zero_w_ref, one_w_ref, mine_ref, give_ref, terms_ref, zero, one):
    rest = (keep_ref[...].astype(F32) + arrived_ref[...].astype(F32)).astype(BF16)
    zero[:, :MLP_COLS] = rest[:, :MLP_COLS]
    zero[:, MLP_COLS:] = rest[:, LAYER_COLS:]
    one[:, :MLP_COLS] = last_ref[...]
    one[:, MLP_COLS:] = rest[:, MLP_COLS:LAYER_COLS]
    is_first = core_ref[0] == 0
    mine_ref[...] = jnp.where(is_first, zero[...], one[...])
    give_ref[...] = jnp.where(is_first, one[...], zero[...])
    row = 0
    for grad, weights in ((zero, zero_w_ref), (one, one_w_ref)):
        products = weights[...].astype(F32) * grad[...].astype(F32)
        for columns in (slice(MLP_COLS, MLP_COLS + QKV_COLS), slice(0, 2 * HIDDEN_COLS)):
            terms_ref[row, :] = jnp.sum(products[:, columns], axis=1)
            row += 1


def combine_grads(core, *operands):
    return pl.pallas_call(
        combine_kernel,
        in_specs=[smem_whole()] + [vmem_whole()] * len(operands),
        out_specs=[vmem_whole()] * 3,
        out_shape=[shape(48, LAYER_COLS, BF16)] * 2 + [shape(4, 48, F32)],
        scratch_shapes=[pltpu.VMEM((48, LAYER_COLS), BF16)] * 2,
        compiler_params=params(16),
        name="combine_grads",
    )(core, *operands)


def unpack_kernel(core_ref, attn_scale_ref, mlp_scale_ref, mine_ref, got_ref, gate_ref, up_ref, down_ref, query_ref, key_ref, value_ref, out_ref):
    is_first = core_ref[0] == 0

    def place(out, start, scale_ref):
        width = out.shape[1] // 2
        mine = mine_ref[:, start : start + width].astype(F32)
        got = got_ref[:, start : start + width].astype(F32)
        if scale_ref is not None:
            mine, got = mine * scale_ref[...], got * scale_ref[...]
        out[:, :width] = jnp.where(is_first, mine, got)
        out[:, width:] = jnp.where(is_first, got, mine)

    place(gate_ref, 0, mlp_scale_ref)
    place(up_ref, HIDDEN_COLS, mlp_scale_ref)
    place(down_ref, 2 * HIDDEN_COLS, None)
    place(query_ref, MLP_COLS, attn_scale_ref)
    place(key_ref, MLP_COLS + QUERY_COLS, attn_scale_ref)
    place(value_ref, MLP_COLS + QUERY_COLS + KV_COLS, attn_scale_ref)
    place(out_ref, MLP_COLS + QKV_COLS, None)


def unpack_grads(core, *operands):
    widths = [HIDDEN_COLS] * 3 + [QUERY_COLS, KV_COLS, KV_COLS, OUT_COLS]
    return pl.pallas_call(
        unpack_kernel,
        in_specs=[smem_whole()] + [vmem_whole()] * len(operands),
        out_specs=[vmem_whole()] * len(widths),
        out_shape=[shape(48, 2 * width, F32) for width in widths],
        compiler_params=params(16),
        name="unpack_grads",
    )(core, *operands)


def gather_rows(z_low, share):
    other = swap(share, "zl")
    pair = jnp.concatenate([pick(z_low, share, other), pick(z_low, other, share)], axis=0)
    return lax.all_gather(pair, ("y", "x"), axis=0, tiled=True)


def scatter_pair(grad):
    return lax.psum_scatter(grad, ("y", "x"), scatter_dimension=0, tiled=True)


def scatter_low(z_low, pair):
    keep = pick(z_low, pair[:48], pair[48:])
    give = pick(z_low, pair[48:], pair[:48])
    return (keep.astype(F32) + swap(give, "zl").astype(F32)).astype(BF16)


def to_ring_order(rows):
    lead = rows.shape[:-1]
    return jnp.swapaxes(rows.reshape(lead + (4, 2, 4, 48)), -3, -2).reshape(rows.shape)


def from_ring_order(rows):
    lead = rows.shape[:-1]
    return jnp.swapaxes(rows.reshape(lead + (4, 4, 2, 48)), -3, -2).reshape(rows.shape)


def join_positions(tensor, own):
    other = swap(own, "tensor")
    return jnp.concatenate(
        [pick(tensor, own, other), pick(tensor, other, own)], axis=1
    ).reshape(384, WIDTH)


def own_positions(tensor, rows):
    rows = rows.reshape(3, 128, 1536)
    return pick(tensor, rows[:, :64], rows[:, 64:])


def per_device(
    inputs, cotangent, plan, attn_gain, mlp_gain, w_query, key_weight, value_weight,
    w_out, w_gate, w_up, w_down,
):
    core = lax.axis_index("section")
    z_low = lax.axis_index("zl")
    tensor = lax.axis_index("tensor")

    attn_scale = attn_gain[0].astype(F32)[:, None]
    mlp_scale = mlp_gain[0].astype(F32)[:, None]

    core_ref = core.astype(jnp.int32).reshape(1)
    mine, give = pack_shards(
        core_ref, attn_gain, mlp_gain,
        w_gate[0], w_up[0], w_down[0].T, w_query[0], key_weight[0], value_weight[0], w_out[0].T,
    )
    got = swap(give, "section")
    layer_zero, layer_one = pick(core, mine, got), pick(core, got, mine)
    first_weights = gather_rows(
        z_low, jnp.concatenate([layer_zero, layer_one[:, MLP_COLS:]], axis=1)
    )
    last_weights = gather_rows(z_low, layer_one[:, :MLP_COLS])

    stream = join_positions(tensor, to_ring_order(inputs[:, 0][plan]))
    stream, late = lax.optimization_barrier((stream, cotangent))
    out_grad = join_positions(tensor, to_ring_order(late[:, 0][plan]))
    stream, out_grad = lax.optimization_barrier((stream, out_grad))

    def whole_rows(sums):
        own, other = jnp.concatenate(sums[:PARTS]), jnp.concatenate(sums[PARTS:])
        return jnp.concatenate([pick(core, own, other), pick(core, other, own)], axis=1).astype(F32)

    x_zero = stream
    first_zero, qkv_zero, prob_zero, mix_zero, *partial = attention_first(
        core_ref, x_zero, first_weights, MLP_COLS
    )
    near, token = fetch(first_weights, 0, MLP_COLS)
    sums, token = sum_four(partial, beside=token)
    middle_zero, second_zero, gate_zero, up_zero, hidden_zero, *partial = mlp_forward(
        core_ref, x_zero, sums, near, token
    )
    near, token = fetch(first_weights, LAYER_COLS, ATTN_COLS)
    sums, token = sum_four(partial, beside=token)
    x_one, first_one, qkv_one, prob_one, mix_one, *partial = attention_next(
        core_ref, middle_zero, sums, near, token
    )
    hidden_grad, near, token = mlp_ahead(out_grad, last_weights)
    sums, token = sum_four(partial, beside=token)

    middle_one, hidden_far, second_one, hidden_one, pair_grad, *partial = mlp_last(
        core_ref, x_one, sums, hidden_grad, near, token
    )
    one_mlp = mlp_weights(None, MLP_COLS, second_one, out_grad, pair_grad, hidden_one)
    near, token = fetch(first_weights, LAYER_COLS, ATTN_COLS, one_mlp)
    sums, one_mlp, token = sum_four(partial, before=one_mlp, beside=token)
    last_pair = scatter_pair(one_mlp)
    middle_grad, attn_in, qkv_grad, *partial = attention_backward(
        core_ref, out_grad, middle_one, sums, qkv_one, prob_one, near, token, True
    )
    buffer = attention_weights(None, REST_COLS, MLP_COLS, first_one, attn_in, qkv_grad, mix_one)
    near, token = fetch(first_weights, 0, MLP_COLS, buffer)
    sums, (buffer, token) = sum_four(partial, beside=(buffer, token))

    grad_one, pair_grad, *partial = mlp_backward(
        core_ref, (x_one, middle_grad, *sums), gate_zero, up_zero, near, token
    )
    buffer = mlp_weights(buffer, REST_COLS, second_zero, grad_one, pair_grad, hidden_zero)
    near, token = fetch(first_weights, MLP_COLS, ATTN_COLS, buffer)
    sums, (buffer, token) = sum_four(partial, beside=(buffer, token))
    hidden_far, sums[0] = lax.optimization_barrier((hidden_far, sums[0]))
    down_partial = mlp_down(core_ref, hidden_far, last_weights)
    middle_grad, attn_in, qkv_grad = attention_backward(
        core_ref, grad_one, middle_zero, sums, qkv_zero, prob_zero, near, token, False
    )
    buffer = attention_weights(
        buffer, REST_COLS, LAYER_COLS, first_zero, attn_in, qkv_grad, mix_zero
    )
    rest_pair = scatter_pair(buffer)
    qkv_grad, buffer = lax.optimization_barrier((qkv_grad, buffer))
    sums, _ = sum_four(attention_in(core_ref, qkv_grad, near))
    rows = x_zero.astype(F32)
    grad_zero = middle_grad + norm_back(whole_rows(sums), rows, inverse_norm(rows))
    down_sums, _ = sum_four(down_partial)
    result_one = (middle_one + whole_rows(down_sums)).astype(BF16)
    outputs = [own_positions(tensor, x_one), own_positions(tensor, result_one)]
    grads = [own_positions(tensor, grad_zero.astype(BF16)), own_positions(tensor, grad_one)]

    layer_outputs = from_ring_order(pick(core, outputs[0], outputs[1]))
    input_grads = from_ring_order(pick(core, grads[0], grads[1]))
    last_grad = scatter_low(z_low, last_pair)
    rest_pair, layer_outputs, input_grads, last_grad = lax.optimization_barrier(
        (rest_pair, layer_outputs, input_grads, last_grad)
    )
    keep = pick(z_low, rest_pair[:48], rest_pair[48:])
    arrived = swap(pick(z_low, rest_pair[48:], rest_pair[:48]), "zl")
    mine, give, terms = combine_grads(
        core_ref, keep, arrived, last_grad, layer_zero, layer_one
    )
    got = swap(give, "section")
    arrived = swap(terms, "tensor")
    gate_grad, up_grad, down_grad, query_grad, key_grad, value_grad, out_weight_grad = unpack_grads(
        core_ref, attn_scale, mlp_scale, mine, got
    )
    arrived, key_grad = lax.optimization_barrier((arrived, key_grad))
    terms = terms + arrived
    terms = pick(core, terms[:2], terms[2:]) + swap(pick(core, terms[2:], terms[:2]), "section")
    return (
        layer_outputs[None, :, None],
        input_grads[None, :, None],
        (terms[0] / attn_scale[:, 0])[None],
        (terms[1] / mlp_scale[:, 0])[None],
        query_grad[None],
        key_grad[None],
        value_grad[None],
        out_weight_grad.T[None],
        gate_grad[None],
        up_grad[None],
        down_grad.T[None],
    )


def solution(mesh):
    split = Mesh(mesh.devices.reshape(2, 4, 2, 4, 2), ("section", "y", "zl", "x", "tensor"))
    dp = ("y", "zl", "x")
    rows = P("section", dp, "tensor")
    columns = P("section", "tensor", dp)
    return jax.shard_map(
        per_device,
        mesh=split,
        in_specs=(
            P(None, dp, "tensor", None),
            P(None, dp, "tensor", None),
            P(),
            P("section", dp),
            P("section", dp),
            rows,
            rows,
            rows,
            columns,
            rows,
            rows,
            columns,
        ),
        out_specs=(
            P("section", None, dp, "tensor", None),
            P("section", None, dp, "tensor", None),
            P("section", dp),
            P("section", dp),
            rows,
            rows,
            rows,
            columns,
            rows,
            rows,
            columns,
        ),
        check_vma=False,
    )
```

```python
import functools

import jax
import jax.numpy as jnp
from jax import lax
from jax.experimental import pallas as pl
from jax.experimental.pallas import tpu as pltpu
from jax.sharding import Mesh, PartitionSpec as P

HEAD_WIDTH = 96
EPSILON = 1e-05
BLOCKED = -1e30
SCORE_SCALE = HEAD_WIDTH ** (-0.5)
BF16 = jnp.bfloat16
F32 = jnp.float32

QUERY_COLS, KV_COLS = 384, 192
QKV_COLS = QUERY_COLS + 2 * KV_COLS
OUT_COLS = 384
HIDDEN_COLS = 1024
ATTN_COLS = QKV_COLS + OUT_COLS
MLP_COLS = 3 * HIDDEN_COLS
LAYER_COLS = MLP_COLS + ATTN_COLS
REST_COLS = LAYER_COLS + ATTN_COLS
HIDDEN_TILE = 512
AHEAD = 3
WIDTH = 1536
HALF = WIDTH // 2
PARTS = 2
MIB = 1024 * 1024


def swap(value, axis):
    return lax.ppermute(value, axis, [(0, 1), (1, 0)])


def pick(index, first, second):
    return jnp.where(index == 0, first, second)


def norm_back(weighted, residual, inverse):
    scaled = residual * inverse
    return inverse * (weighted - scaled * jnp.mean(weighted * scaled, axis=-1, keepdims=True))


def vmem_whole():
    return pl.BlockSpec(memory_space=pltpu.VMEM)


def smem_whole():
    return pl.BlockSpec(memory_space=pltpu.SMEM)


def shape(rows, columns, dtype):
    return jax.ShapeDtypeStruct((rows, columns), dtype)


def half_of(core_ref, which):
    position = core_ref[0] if which == 0 else 1 - core_ref[0]
    return pl.ds(pl.multiple_of(position * HALF, HALF), HALF)


def nt_dot(left_side, right_side):
    return lax.dot_general(
        left_side, right_side, (((1,), (1,)), ((), ())), preferred_element_type=F32
    )


def tn_dot(left_side, right_side):
    return lax.dot_general(
        left_side, right_side, (((0,), (0,)), ((), ())), preferred_element_type=F32
    )


def nn_dot(left_side, right_side):
    return jnp.dot(left_side, right_side, preferred_element_type=F32)


def row_parts(rows):
    return [slice(rows // PARTS * part, rows // PARTS * (part + 1)) for part in range(PARTS)]


def part_shapes(rows):
    return [shape(rows // PARTS, HALF, BF16)] * (2 * PARTS)


class Outward:
    def __init__(self, sems):
        self.sems, self.copies = sems, []

    def send(self, source, target):
        self.copies.append(pltpu.make_async_copy(source, target, self.sems.at[len(self.copies)]))
        self.copies[-1].start()

    def wait(self):
        for copy in self.copies:
            copy.wait()


def far(array):
    return pltpu.HBM(array.shape, array.dtype)


def each_sum(core_ref, sum_refs):
    rows = sum_refs[0].shape[0] * PARTS
    for which in range(2):
        for part, at in enumerate(row_parts(rows)):
            yield at, half_of(core_ref, which), sum_refs[PARTS * which + part]


def write_half(core_ref, which, left_ref, w_ref, columns, outs):
    product = nt_dot(left_ref[...], w_ref[half_of(core_ref, which), columns]).astype(BF16)
    refs = outs[PARTS * which : PARTS * (which + 1)]
    for at, ref in zip(row_parts(left_ref.shape[0]), refs):
        ref[...] = product[at]


def write_partial(core_ref, left_ref, w_ref, columns, outs):
    for which in (1, 0):
        write_half(core_ref, which, left_ref, w_ref, columns, outs)


def params(mib):
    return pltpu.CompilerParams(vmem_limit_bytes=mib * MIB)


def inverse_norm(rows):
    return lax.rsqrt(jnp.mean(rows * rows, axis=-1, keepdims=True) + EPSILON)


def causal_mask():
    row = lax.broadcasted_iota(jnp.int32, (128, 128), 0)
    return row >= lax.broadcasted_iota(jnp.int32, (128, 128), 1)


def two_heads(ref, rows, start):
    return jnp.concatenate(
        [
            ref[rows, start : start + HEAD_WIDTH],
            ref[rows, start + HEAD_WIDTH : start + 2 * HEAD_WIDTH],
        ],
        axis=0,
    )


def ahead_copy(w_any, w_ref, sem, column):
    return pltpu.make_async_copy(w_any.at[:, pl.ds(column, w_ref.shape[1])], w_ref, sem)


def attention_forward_body(sequences, core_ref, outward, first_ref, w_ref, qkv_any, prob_any, mix_ref, *rest):
    parts, (qkv_ref, prob_ref) = rest[:-2], rest[-2:]
    qkv_ref[...] = nn_dot(first_ref[...], w_ref[:, :QKV_COLS]).astype(BF16)
    outward.send(qkv_ref, qkv_any)
    mask = causal_mask()
    mask = jnp.concatenate([mask, mask], axis=0)
    for sequence in range(sequences):
        rows = slice(128 * sequence, 128 * (sequence + 1))
        for group in range(2):
            queries = two_heads(qkv_ref, rows, 2 * HEAD_WIDTH * group)
            key_at = QUERY_COLS + HEAD_WIDTH * group
            value_at = key_at + KV_COLS
            scores = nt_dot(queries, qkv_ref[rows, key_at : key_at + HEAD_WIDTH]) * SCORE_SCALE
            scores = jnp.where(mask, scores, BLOCKED)
            expanded = jnp.exp(scores - jnp.max(scores, axis=-1, keepdims=True))
            probability = expanded / jnp.sum(expanded, axis=-1, keepdims=True)
            prob_ref[2 * sequence + group] = probability
            mixed = nn_dot(
                probability.astype(BF16), qkv_ref[rows, value_at : value_at + HEAD_WIDTH]
            ).astype(BF16)
            at = 2 * HEAD_WIDTH * group
            mix_ref[rows, at : at + HEAD_WIDTH] = mixed[:128]
            mix_ref[rows, at + HEAD_WIDTH : at + 2 * HEAD_WIDTH] = mixed[128:]
        both = pl.ds(2 * sequence, 2)
        outward.send(prob_ref.at[both], prob_any.at[both])
    write_partial(core_ref, mix_ref, w_ref, slice(QKV_COLS, ATTN_COLS), parts)
    outward.wait()


def attention_first_kernel(sequences, column, core_ref, x_ref, w_any, first_any, *rest):
    outs, (first_ref, w_ref, sem, sems) = rest[:-4], rest[-4:]
    copy = ahead_copy(w_any, w_ref, sem, column)
    copy.start()
    rows = x_ref[...].astype(F32)
    first_ref[...] = (rows * inverse_norm(rows)).astype(BF16)
    copy.wait()
    outward = Outward(sems)
    outward.send(first_ref, first_any)
    attention_forward_body(sequences, core_ref, outward, first_ref, w_ref, *outs)


def attention_next_kernel(sequences, core_ref, middle_ref, *rest):
    sums, (w_ref, _, x_any, first_any) = rest[: 2 * PARTS], rest[2 * PARTS : 2 * PARTS + 4]
    outs, (x_ref, first_ref, sems) = rest[2 * PARTS + 4 : -3], rest[-3:]
    outward = Outward(sems)
    for at, columns, part in each_sum(core_ref, sums):
        x_ref[at, columns] = (middle_ref[at, columns] + part[...].astype(F32)).astype(BF16)
    outward.send(x_ref, x_any)
    rows = x_ref[...].astype(F32)
    first_ref[...] = (rows * inverse_norm(rows)).astype(BF16)
    outward.send(first_ref, first_any)
    attention_forward_body(sequences, core_ref, outward, first_ref, w_ref, *outs)


def in_hbm(value):
    return pltpu.with_memory_space_constraint(value, pltpu.HBM)


def hbm_whole():
    return pl.BlockSpec(memory_space=pltpu.HBM)


def attention_scratch():
    return [pltpu.VMEM((WIDTH, ATTN_COLS), BF16), pltpu.SemaphoreType.DMA(())]


def attention_outs(rows):
    outs = [
        shape(rows, WIDTH, BF16),
        far(shape(rows, QKV_COLS, BF16)),
        pltpu.HBM((rows // 64, 256, 128), F32),
        shape(rows, OUT_COLS, BF16),
    ]
    return outs + part_shapes(rows), [vmem_whole(), hbm_whole(), hbm_whole()] + [vmem_whole()] * (1 + 2 * PARTS)


def attention_cost(rows):
    return pl.CostEstimate(
        flops=2 * rows * WIDTH * ATTN_COLS, bytes_accessed=8_000_000, transcendentals=0
    )


def fetch_kernel(column, w_any, *rest):
    out_ref, token_ref, sem = rest[-3:]
    copy = ahead_copy(w_any, out_ref, sem, column)
    copy.start()
    token_ref[...] = jnp.zeros_like(token_ref)
    copy.wait()


TOKEN = jax.ShapeDtypeStruct((8, 128), F32)


def fetch(weights, column, columns, *after):
    return pl.pallas_call(
        functools.partial(fetch_kernel, column),
        in_specs=[hbm_whole()] * (1 + len(after)),
        out_specs=[vmem_whole()] * 2,
        out_shape=[shape(WIDTH, columns, BF16), TOKEN],
        scratch_shapes=[pltpu.SemaphoreType.DMA(())],
        compiler_params=params(12),
        cost_estimate=pl.CostEstimate(
            flops=0, bytes_accessed=2 * WIDTH * columns * 2, transcendentals=0
        ),
        name="fetch",
    )(in_hbm(weights), *[in_hbm(value) for value in after])


def attention_first(core, x, weights, column):
    rows = x.shape[0]
    outs, specs = attention_outs(rows)
    return pl.pallas_call(
        functools.partial(attention_first_kernel, rows // 128, column),
        in_specs=[smem_whole(), vmem_whole(), hbm_whole()],
        out_specs=[hbm_whole()] + specs[1:],
        out_shape=[far(outs[0])] + outs[1:],
        scratch_shapes=[
            pltpu.VMEM((rows, QKV_COLS), BF16),
            pltpu.VMEM((rows // 64, 256, 128), F32),
            pltpu.VMEM((rows, WIDTH), BF16),
        ]
        + attention_scratch()
        + [pltpu.SemaphoreType.DMA((2 + rows // 128,))],
        compiler_params=params(20),
        cost_estimate=attention_cost(rows),
        name="attention_first",
    )(core, x, in_hbm(weights))


def attention_next(core, middle, sums, weights, token):
    rows = middle.shape[0]
    outs, specs = attention_outs(rows)
    whole = shape(rows, WIDTH, BF16)
    return pl.pallas_call(
        functools.partial(attention_next_kernel, rows // 128),
        in_specs=[smem_whole()] + [vmem_whole()] * (2 + 2 * PARTS) + [hbm_whole()],
        out_specs=[hbm_whole()] * 2 + specs[1:],
        out_shape=[far(whole)] * 2 + outs[1:],
        scratch_shapes=[
            pltpu.VMEM((rows, QKV_COLS), BF16),
            pltpu.VMEM((rows // 64, 256, 128), F32),
            pltpu.VMEM(whole.shape, BF16),
            pltpu.VMEM(whole.shape, BF16),
            pltpu.SemaphoreType.DMA((3 + rows // 128,)),
        ],
        compiler_params=params(16),
        cost_estimate=attention_cost(rows),
        name="attention_next",
    )(core, middle, *sums, weights, token)


def column_tiles(first):
    return [pl.ds(first + HIDDEN_TILE * step, HIDDEN_TILE) for step in range(HIDDEN_STEPS)]


def sigmoid(values):
    return 0.5 * jnp.tanh(0.5 * values) + 0.5


def arrivals(copies):
    for copy in copies[:AHEAD]:
        copy.start()
    place = iter(range(len(copies)))

    def arrive():
        number = next(place)
        copies[number].wait()
        if number + AHEAD < len(copies):
            copies[number + AHEAD].start()

    return arrive


def mlp_forward_kernel(core_ref, x_ref, *rest):
    sums, rest = rest[: 2 * PARTS], rest[2 * PARTS :]
    (w_ref, _, middle_any, second_any, gate_any, up_any, hidden_any), rest = rest[:7], rest[7:]
    outs, (middle_ref, second_ref, gate_ref, up_ref, hidden_ref, out_sems) = rest[:-6], rest[-6:]
    tiles = [(gate, up) for gate, up in zip(column_tiles(0), column_tiles(HIDDEN_COLS))]
    down = pl.ds(2 * HIDDEN_COLS, HIDDEN_COLS)
    for at, columns, part in each_sum(core_ref, sums):
        middle_ref[at, columns] = x_ref[at, columns].astype(F32) + part[...].astype(F32)
    rows = middle_ref[...]
    second_ref[...] = (rows * inverse_norm(rows)).astype(BF16)
    outward = Outward(out_sems)
    outward.send(middle_ref, middle_any)
    outward.send(second_ref, second_any)
    for step, (gate, up) in enumerate(tiles):
        at = slice(HIDDEN_TILE * step, HIDDEN_TILE * (step + 1))
        gate_out = nn_dot(second_ref[...], w_ref[:, gate])
        up_out = nn_dot(second_ref[...], w_ref[:, up])
        gate_ref[:, at] = gate_out
        up_ref[:, at] = up_out
        hidden_ref[:, at] = (gate_out * sigmoid(gate_out) * up_out).astype(BF16)
        for ref, target in ((gate_ref, gate_any), (up_ref, up_any), (hidden_ref, hidden_any)):
            outward.send(ref.at[:, at], target.at[:, at])
    write_partial(core_ref, hidden_ref, w_ref, down, outs)
    outward.wait()


HIDDEN_STEPS = HIDDEN_COLS // HIDDEN_TILE


def mlp_cost(rows):
    return pl.CostEstimate(
        flops=2 * rows * WIDTH * MLP_COLS, bytes_accessed=15_000_000, transcendentals=0
    )


def mlp_forward(core, x, sums, weights, token):
    rows = x.shape[0]
    saved = [
        shape(rows, WIDTH, F32),
        shape(rows, WIDTH, BF16),
        shape(rows, HIDDEN_COLS, F32),
        shape(rows, HIDDEN_COLS, F32),
        shape(rows, HIDDEN_COLS, BF16),
    ]
    return pl.pallas_call(
        mlp_forward_kernel,
        in_specs=[smem_whole()] + [vmem_whole()] * (2 + 2 * PARTS) + [hbm_whole()],
        out_specs=[hbm_whole()] * 5 + [vmem_whole()] * (2 * PARTS),
        out_shape=[far(array) for array in saved] + part_shapes(rows),
        scratch_shapes=[pltpu.VMEM(out.shape, out.dtype) for out in saved]
        + [pltpu.SemaphoreType.DMA((2 + 3 * HIDDEN_STEPS,))],
        compiler_params=params(24),
        cost_estimate=mlp_cost(rows),
        name="mlp_forward",
    )(core, x, *sums, weights, token)


def mlp_grads(hidden_grad, gate_out, up_out):
    sigmoid_gate = sigmoid(gate_out)
    gate_grad = hidden_grad * up_out * (sigmoid_gate * (1.0 + gate_out * (1.0 - sigmoid_gate)))
    return gate_grad.astype(BF16), (hidden_grad * (gate_out * sigmoid_gate)).astype(BF16)


def mlp_backward_kernel(core_ref, x_ref, middle_grad_ref, *rest):
    sums, rest = rest[: 2 * PARTS], rest[2 * PARTS :]
    (gate_ref, up_ref, w_ref, _, g_ref, pair_grad_ref), rest = rest[:6], rest[6:]
    outs, weighted = rest[:-1], rest[-1]
    for at, columns, part in each_sum(core_ref, sums):
        weighted[at, columns] = part[...].astype(F32)
    rows = x_ref[...].astype(F32)
    g_ref[...] = (
        middle_grad_ref[...] + norm_back(weighted[...], rows, inverse_norm(rows))
    ).astype(BF16)
    for step, down in enumerate(column_tiles(2 * HIDDEN_COLS)):
        at = slice(HIDDEN_TILE * step, HIDDEN_TILE * (step + 1))
        up_at = slice(HIDDEN_COLS + at.start, HIDDEN_COLS + at.stop)
        hidden_grad = nn_dot(g_ref[...], w_ref[:, down])
        pair_grad_ref[:, at], pair_grad_ref[:, up_at] = mlp_grads(
            hidden_grad, gate_ref[:, at], up_ref[:, at]
        )
    write_partial(core_ref, pair_grad_ref, w_ref, slice(0, 2 * HIDDEN_COLS), outs)


def mlp_backward(core, above, gate_out, up_out, weights, token):
    rows = gate_out.shape[0]
    return pl.pallas_call(
        mlp_backward_kernel,
        in_specs=[smem_whole()] + [vmem_whole()] * (5 + 2 * PARTS) + [hbm_whole()],
        out_specs=[vmem_whole()] * (2 + 2 * PARTS),
        out_shape=[shape(rows, WIDTH, BF16), shape(rows, 2 * HIDDEN_COLS, BF16)]
        + part_shapes(rows),
        scratch_shapes=[pltpu.VMEM((rows, WIDTH), F32)],
        compiler_params=params(26),
        cost_estimate=mlp_cost(rows),
        name="mlp_backward",
    )(core, *above, gate_out, up_out, weights, token)


def mlp_ahead_kernel(g_ref, w_any, hidden_grad_ref, pair_ref, token_ref, down_ref, sems):
    down = ahead_copy(w_any, down_ref, sems.at[0], 2 * HIDDEN_COLS)
    pair = ahead_copy(w_any, pair_ref, sems.at[1], 0)
    down.start()
    pair.start()
    token_ref[...] = jnp.zeros_like(token_ref)
    down.wait()
    hidden_grad_ref[...] = nn_dot(g_ref[...], down_ref[...])
    pair.wait()


def mlp_ahead(g, weights):
    rows = g.shape[0]
    return pl.pallas_call(
        mlp_ahead_kernel,
        in_specs=[vmem_whole(), hbm_whole()],
        out_specs=[vmem_whole()] * 3,
        out_shape=[
            shape(rows, HIDDEN_COLS, F32),
            shape(WIDTH, 2 * HIDDEN_COLS, BF16),
            TOKEN,
        ],
        scratch_shapes=[pltpu.VMEM((WIDTH, HIDDEN_COLS), BF16), pltpu.SemaphoreType.DMA((2,))],
        compiler_params=params(15),
        cost_estimate=pl.CostEstimate(
            flops=2 * rows * WIDTH * HIDDEN_COLS, bytes_accessed=14_000_000, transcendentals=0
        ),
        name="mlp_ahead",
    )(g, in_hbm(weights))


def mlp_last_kernel(core_ref, x_ref, *rest):
    sums, rest = rest[: 2 * PARTS], rest[2 * PARTS :]
    (hidden_grad_ref, w_ref, _, middle_any, hidden_any, second_ref, hidden_ref, pair_grad_ref), rest = rest[:8], rest[8:]
    middle_ref, out_sems = rest
    for at, columns, part in each_sum(core_ref, sums):
        middle_ref[at, columns] = x_ref[at, columns].astype(F32) + part[...].astype(F32)
    rows = middle_ref[...]
    second_ref[...] = (rows * inverse_norm(rows)).astype(BF16)
    outward = Outward(out_sems)
    outward.send(middle_ref, middle_any)
    for step, (gate, up) in enumerate(zip(column_tiles(0), column_tiles(HIDDEN_COLS))):
        at = slice(HIDDEN_TILE * step, HIDDEN_TILE * (step + 1))
        up_at = slice(HIDDEN_COLS + at.start, HIDDEN_COLS + at.stop)
        gate_out = nn_dot(second_ref[...], w_ref[:, gate])
        up_out = nn_dot(second_ref[...], w_ref[:, up])
        hidden_ref[:, at] = (gate_out * sigmoid(gate_out) * up_out).astype(BF16)
        pair_grad_ref[:, at], pair_grad_ref[:, up_at] = mlp_grads(
            hidden_grad_ref[:, at], gate_out, up_out
        )
    outward.send(hidden_ref, hidden_any)
    outward.wait()


def mlp_last(core, x, sums, hidden_grad, pair_weights, token):
    rows = x.shape[0]
    return pl.pallas_call(
        mlp_last_kernel,
        in_specs=[smem_whole()] + [vmem_whole()] * (3 + 2 * PARTS) + [hbm_whole()],
        out_specs=[hbm_whole()] * 2 + [vmem_whole()] * 3,
        out_shape=[
            pltpu.HBM((rows, WIDTH), F32),
            pltpu.HBM((rows, HIDDEN_COLS), BF16),
            shape(rows, WIDTH, BF16),
            shape(rows, HIDDEN_COLS, BF16),
            shape(rows, 2 * HIDDEN_COLS, BF16),
        ],
        scratch_shapes=[pltpu.VMEM((rows, WIDTH), F32), pltpu.SemaphoreType.DMA((2,))],
        compiler_params=params(28),
        cost_estimate=mlp_cost(rows),
        name="mlp_last",
    )(core, x, *sums, hidden_grad, pair_weights, token)


def mlp_in_kernel(core_ref, pair_grad_ref, w_any, _, *rest):
    outs, w_ref, sems = rest[:-2], rest[-2], rest[-1]
    copies = []
    for which in (1, 0):
        half = half_of(core_ref, which)
        source = w_any.at[half, pl.ds(0, 2 * HIDDEN_COLS)]
        copies.append(pltpu.make_async_copy(source, w_ref.at[half, :], sems.at[which]))
        copies[-1].start()
    for copy, which in zip(copies, (1, 0)):
        copy.wait()
        write_half(core_ref, which, pair_grad_ref, w_ref, slice(0, 2 * HIDDEN_COLS), outs)


def mlp_in(core, pair_grad, weights, token):
    rows = pair_grad.shape[0]
    return pl.pallas_call(
        mlp_in_kernel,
        in_specs=[smem_whole(), vmem_whole()] + [hbm_whole()] * 2,
        out_specs=[vmem_whole()] * (2 * PARTS),
        out_shape=part_shapes(rows),
        scratch_shapes=[
            pltpu.VMEM((WIDTH, 2 * HIDDEN_COLS), BF16),
            pltpu.SemaphoreType.DMA((2,)),
        ],
        compiler_params=params(18),
        cost_estimate=pl.CostEstimate(
            flops=4 * rows * WIDTH * HIDDEN_COLS, bytes_accessed=9_000_000, transcendentals=0
        ),
        name="mlp_in",
    )(core, pair_grad, in_hbm(weights), token)


def mlp_down_kernel(core_ref, hidden_ref, w_any, *rest):
    outs, w_ref, sem = rest[:-2], rest[-2], rest[-1]
    copy = pltpu.make_async_copy(w_any.at[:, pl.ds(2 * HIDDEN_COLS, HIDDEN_COLS)], w_ref, sem)
    copy.start()
    copy.wait()
    write_partial(core_ref, hidden_ref, w_ref, slice(0, HIDDEN_COLS), outs)


def mlp_down(core, hidden, weights):
    rows = hidden.shape[0]
    return pl.pallas_call(
        mlp_down_kernel,
        in_specs=[smem_whole(), vmem_whole(), hbm_whole()],
        out_specs=[vmem_whole()] * (2 * PARTS),
        out_shape=part_shapes(rows),
        scratch_shapes=[pltpu.VMEM((WIDTH, HIDDEN_COLS), BF16), pltpu.SemaphoreType.DMA(())],
        compiler_params=params(14),
        cost_estimate=pl.CostEstimate(
            flops=2 * rows * WIDTH * HIDDEN_COLS, bytes_accessed=5_000_000, transcendentals=0
        ),
        name="mlp_down",
    )(core, hidden, in_hbm(weights))


def attention_backward_kernel(sequences, near, core_ref, g_ref, middle_ref, *rest):
    sums, rest = rest[: 2 * PARTS], rest[2 * PARTS :]
    (w_ref, qkv_any, prob_any, _, middle_grad_out, attn_in_ref, qkv_grad_ref), rest = rest[:7], rest[7:]
    outs, (middle_grad_ref, qkv_ref, prob_ref, mix_grad, sems) = rest[:-5], rest[-5:]
    copies = [
        pltpu.make_async_copy(qkv_any, qkv_ref, sems.at[0]),
        pltpu.make_async_copy(prob_any, prob_ref, sems.at[1]),
    ]
    for copy in copies:
        copy.start()
    for at, columns, part in each_sum(core_ref, sums):
        middle_grad_ref[at, columns] = part[...].astype(F32)
    middle = middle_ref[...]
    middle_grad = g_ref[...].astype(F32) + norm_back(
        middle_grad_ref[...], middle, inverse_norm(middle)
    )
    if near:
        middle_grad_out[...] = middle_grad
    else:
        middle_grad_ref[...] = middle_grad
        outward = pltpu.make_async_copy(middle_grad_ref, middle_grad_out, sems.at[2])
        outward.start()
    attn_in_ref[...] = middle_grad.astype(BF16)
    mix_grad[...] = nn_dot(attn_in_ref[...], w_ref[:, QKV_COLS:]).astype(BF16)
    for copy in copies:
        copy.wait()
    for sequence in range(sequences):
        rows = slice(128 * sequence, 128 * (sequence + 1))
        for group in range(2):
            at = 2 * HEAD_WIDTH * group
            key_at = QUERY_COLS + HEAD_WIDTH * group
            value_at = key_at + KV_COLS
            grads = two_heads(mix_grad, rows, at)
            queries = two_heads(qkv_ref, rows, at)
            keys = qkv_ref[rows, key_at : key_at + HEAD_WIDTH]
            probability = prob_ref[2 * sequence + group]
            prob_grad = nt_dot(grads, qkv_ref[rows, value_at : value_at + HEAD_WIDTH])
            centred = jnp.sum(probability * prob_grad, axis=-1, keepdims=True)
            score_grad = (probability * (prob_grad - centred)).astype(BF16)
            query_grad = (nn_dot(score_grad, keys) * SCORE_SCALE).astype(BF16)
            qkv_grad_ref[rows, at : at + HEAD_WIDTH] = query_grad[:128]
            qkv_grad_ref[rows, at + HEAD_WIDTH : at + 2 * HEAD_WIDTH] = query_grad[128:]
            qkv_grad_ref[rows, key_at : key_at + HEAD_WIDTH] = (
                tn_dot(score_grad, queries) * SCORE_SCALE
            ).astype(BF16)
            qkv_grad_ref[rows, value_at : value_at + HEAD_WIDTH] = tn_dot(
                probability.astype(BF16), grads
            ).astype(BF16)
    if near:
        write_partial(core_ref, qkv_grad_ref, w_ref, slice(0, QKV_COLS), outs)
    else:
        outward.wait()


def attention_in_kernel(core_ref, qkv_grad_ref, w_ref, _, *outs):
    write_partial(core_ref, qkv_grad_ref, w_ref, slice(0, QKV_COLS), outs)


def attention_in(core, qkv_grad, weights, token):
    rows = qkv_grad.shape[0]
    return pl.pallas_call(
        attention_in_kernel,
        in_specs=[smem_whole()] + [vmem_whole()] * 2 + [hbm_whole()],
        out_specs=[vmem_whole()] * (2 * PARTS),
        out_shape=part_shapes(rows),
        compiler_params=params(14),
        cost_estimate=pl.CostEstimate(
            flops=2 * rows * WIDTH * QKV_COLS, bytes_accessed=5_000_000, transcendentals=0
        ),
        name="attention_in",
    )(core, qkv_grad, weights, token)


def attention_backward(core, g, middle, sums, qkv, probability, weights, token, near):
    rows = g.shape[0]
    residual, parts = shape(rows, WIDTH, F32), part_shapes(rows) if near else []
    return pl.pallas_call(
        functools.partial(attention_backward_kernel, rows // 128, near),
        in_specs=[smem_whole()] + [vmem_whole()] * (3 + 2 * PARTS) + [hbm_whole()] * 3,
        out_specs=[vmem_whole() if near else hbm_whole()] + [vmem_whole()] * (2 + len(parts)),
        out_shape=[
            residual if near else far(residual),
            shape(rows, WIDTH, BF16),
            shape(rows, QKV_COLS, BF16),
        ]
        + parts,
        scratch_shapes=[
            pltpu.VMEM((rows, WIDTH), F32),
            pltpu.VMEM(qkv.shape, BF16),
            pltpu.VMEM(probability.shape, F32),
            pltpu.VMEM((rows, OUT_COLS), BF16),
            pltpu.SemaphoreType.DMA((3,)),
        ],
        compiler_params=params(24),
        cost_estimate=attention_cost(rows),
        name="attention_backward",
    )(core, g, middle, *sums, weights, in_hbm(qkv), in_hbm(probability), token)


def write_products(start, pairs, out_any, slots, sems):
    _, height, width = slots.shape
    copies = []
    for number in range(WIDTH // height):
        features = pl.ds(height * number, height)
        if number >= 2:
            copies[number - 2].wait()
        slot = slots.at[number % 2]
        at = 0
        for left, right in pairs:
            columns = right.shape[1]
            slot[:, at : at + columns] = tn_dot(left[:, features], right[...]).astype(BF16)
            at += columns
        target = out_any.at[features, pl.ds(start, width)]
        copies.append(pltpu.make_async_copy(slot, target, sems.at[number % 2]))
        copies[-1].start()
    for copy in copies[-2:]:
        copy.wait()


def mlp_weights_kernel(second_ref, g_ref, pair_grad_ref, hidden_ref, *rest):
    out_any, token_ref, slots, sems = rest[-4:]
    token_ref[...] = jnp.zeros_like(token_ref)
    write_products(0, [(second_ref, pair_grad_ref), (g_ref, hidden_ref)], out_any, slots, sems)


def into_buffer(kernel, buffer, columns, slot, operands, flops, name, mib):
    aliases, specs = {}, [vmem_whole()] * len(operands)
    if buffer is not None:
        aliases = {len(operands): 0}
        specs, operands = specs + [hbm_whole()], operands + (in_hbm(buffer),)
    return pl.pallas_call(
        kernel,
        in_specs=specs,
        out_specs=[hbm_whole(), vmem_whole()],
        out_shape=[pltpu.HBM((WIDTH, columns), BF16), TOKEN],
        input_output_aliases=aliases,
        scratch_shapes=[pltpu.VMEM((2, *slot), BF16), pltpu.SemaphoreType.DMA((2,))],
        compiler_params=params(mib),
        cost_estimate=pl.CostEstimate(flops=flops, bytes_accessed=flops // 250, transcendentals=0),
        name=name,
    )(*operands)


def mlp_weights(buffer, columns, second, g, pair_grad, hidden):
    return into_buffer(
        mlp_weights_kernel,
        buffer,
        columns,
        (512, MLP_COLS),
        (second, g, pair_grad, hidden),
        2 * second.shape[0] * WIDTH * MLP_COLS,
        "mlp_weights",
        18,
    )


def attention_weights_kernel(start, first_ref, attn_in_ref, qkv_grad_ref, mix_ref, *rest):
    out_any, token_ref, slots, sems = rest[-4:]
    token_ref[...] = jnp.zeros_like(token_ref)
    pairs = [(first_ref, qkv_grad_ref), (attn_in_ref, mix_ref)]
    write_products(start, pairs, out_any, slots, sems)


def attention_weights(buffer, columns, start, first, attn_in, qkv_grad, mixture):
    return into_buffer(
        functools.partial(attention_weights_kernel, start),
        buffer,
        columns,
        (768, ATTN_COLS),
        (first, attn_in, qkv_grad, mixture),
        2 * first.shape[0] * WIDTH * ATTN_COLS,
        "attention_weights",
        14,
    )


def sum_four(partial, beside=None):
    keeps, gives = list(partial[:PARTS]), list(partial[PARTS:])
    chips = [
        (keep.astype(F32) + swap(give, "section").astype(F32)).astype(BF16)
        for keep, give in zip(keeps, gives)
    ]
    arrived = [swap(chip, "tensor") for chip in chips]
    if beside is not None:
        arrived[-1], beside = lax.optimization_barrier((arrived[-1], beside))
    totals = [
        (chip.astype(F32) + other.astype(F32)).astype(BF16)
        for chip, other in zip(chips, arrived)
    ]
    return totals + [swap(total, "section") for total in totals], beside


def row_scales(gain_ref):
    row = lax.broadcasted_iota(jnp.int32, (48, 48), 0)
    column = lax.broadcasted_iota(jnp.int32, (48, 48), 1)
    return jnp.where(row == column, gain_ref[...].astype(F32), 0.0).astype(BF16)


def pack_kernel(core_ref, attn_gain_ref, mlp_gain_ref, *rest):
    sources, (mine_ref, give_ref), shards, sems = rest[:7], rest[7:9], rest[9:16], rest[16]
    copies = [
        pltpu.make_async_copy(source, shard, sems.at[number])
        for number, (source, shard) in enumerate(zip(sources, shards))
    ]
    for copy in copies:
        copy.start()
    is_first = core_ref[0] == 0
    attn_scale, mlp_scale = row_scales(attn_gain_ref), row_scales(mlp_gain_ref)
    start = 0
    for copy, shard, scale in zip(
        copies,
        shards,
        (mlp_scale, mlp_scale, None, attn_scale, attn_scale, attn_scale, None),
    ):
        copy.wait()
        weight = shard[...]
        if scale is not None:
            weight = nn_dot(scale, weight).astype(BF16)
        width = weight.shape[1] // 2
        low, high = weight[:, :width], weight[:, width:]
        mine_ref[:, start : start + width] = jnp.where(is_first, low, high)
        give_ref[:, start : start + width] = jnp.where(is_first, high, low)
        start += width


def pack_shards(core, attn_gain, mlp_gain, *shards):
    return pl.pallas_call(
        pack_kernel,
        in_specs=[smem_whole()] + [vmem_whole()] * 2 + [hbm_whole()] * len(shards),
        out_specs=[vmem_whole()] * 2,
        out_shape=[shape(48, LAYER_COLS, BF16)] * 2,
        scratch_shapes=[pltpu.VMEM(shard.shape, shard.dtype) for shard in shards]
        + [pltpu.SemaphoreType.DMA((len(shards),))],
        compiler_params=params(16),
        name="pack_shards",
    )(core, attn_gain, mlp_gain, *[in_hbm(shard) for shard in shards])


def combine_kernel(core_ref, keep_ref, arrived_ref, last_ref, zero_w_ref, one_w_ref, mine_ref, give_ref, terms_ref, zero, one):
    rest = (keep_ref[...].astype(F32) + arrived_ref[...].astype(F32)).astype(BF16)
    zero[:, :MLP_COLS] = rest[:, :MLP_COLS]
    zero[:, MLP_COLS:] = rest[:, LAYER_COLS:]
    one[:, :MLP_COLS] = last_ref[...]
    one[:, MLP_COLS:] = rest[:, MLP_COLS:LAYER_COLS]
    is_first = core_ref[0] == 0
    mine_ref[...] = jnp.where(is_first, zero[...], one[...])
    give_ref[...] = jnp.where(is_first, one[...], zero[...])
    row = 0
    for grad, weights in ((zero, zero_w_ref), (one, one_w_ref)):
        products = weights[...].astype(F32) * grad[...].astype(F32)
        for columns in (slice(MLP_COLS, MLP_COLS + QKV_COLS), slice(0, 2 * HIDDEN_COLS)):
            terms_ref[row, :] = jnp.sum(products[:, columns], axis=1)
            row += 1


def combine_grads(core, *operands):
    return pl.pallas_call(
        combine_kernel,
        in_specs=[smem_whole()] + [vmem_whole()] * len(operands),
        out_specs=[vmem_whole()] * 3,
        out_shape=[shape(48, LAYER_COLS, BF16)] * 2 + [shape(4, 48, F32)],
        scratch_shapes=[pltpu.VMEM((48, LAYER_COLS), BF16)] * 2,
        compiler_params=params(16),
        name="combine_grads",
    )(core, *operands)


def unpack_kernel(core_ref, attn_scale_ref, mlp_scale_ref, mine_ref, got_ref, gate_ref, up_ref, down_ref, query_ref, key_ref, value_ref, out_ref):
    is_first = core_ref[0] == 0

    def place(out, start, scale_ref):
        width = out.shape[1] // 2
        mine = mine_ref[:, start : start + width].astype(F32)
        got = got_ref[:, start : start + width].astype(F32)
        if scale_ref is not None:
            mine, got = mine * scale_ref[...], got * scale_ref[...]
        out[:, :width] = jnp.where(is_first, mine, got)
        out[:, width:] = jnp.where(is_first, got, mine)

    place(gate_ref, 0, mlp_scale_ref)
    place(up_ref, HIDDEN_COLS, mlp_scale_ref)
    place(down_ref, 2 * HIDDEN_COLS, None)
    place(query_ref, MLP_COLS, attn_scale_ref)
    place(key_ref, MLP_COLS + QUERY_COLS, attn_scale_ref)
    place(value_ref, MLP_COLS + QUERY_COLS + KV_COLS, attn_scale_ref)
    place(out_ref, MLP_COLS + QKV_COLS, None)


def unpack_grads(core, *operands):
    widths = [HIDDEN_COLS] * 3 + [QUERY_COLS, KV_COLS, KV_COLS, OUT_COLS]
    return pl.pallas_call(
        unpack_kernel,
        in_specs=[smem_whole()] + [vmem_whole()] * len(operands),
        out_specs=[vmem_whole()] * len(widths),
        out_shape=[shape(48, 2 * width, F32) for width in widths],
        compiler_params=params(16),
        name="unpack_grads",
    )(core, *operands)


def gather_rows(z_low, share):
    other = swap(share, "zl")
    pair = jnp.concatenate([pick(z_low, share, other), pick(z_low, other, share)], axis=0)
    return lax.all_gather(pair, ("y", "x"), axis=0, tiled=True)


def scatter_pair(grad):
    return lax.psum_scatter(grad, ("y", "x"), scatter_dimension=0, tiled=True)


def scatter_low(z_low, pair):
    keep = pick(z_low, pair[:48], pair[48:])
    give = pick(z_low, pair[48:], pair[:48])
    return (keep.astype(F32) + swap(give, "zl").astype(F32)).astype(BF16)


def to_ring_order(rows):
    lead = rows.shape[:-1]
    return jnp.swapaxes(rows.reshape(lead + (4, 2, 4, 48)), -3, -2).reshape(rows.shape)


def from_ring_order(rows):
    lead = rows.shape[:-1]
    return jnp.swapaxes(rows.reshape(lead + (4, 4, 2, 48)), -3, -2).reshape(rows.shape)


def join_positions(tensor, own):
    other = swap(own, "tensor")
    return jnp.concatenate(
        [pick(tensor, own, other), pick(tensor, other, own)], axis=1
    ).reshape(384, WIDTH)


def own_positions(tensor, rows):
    rows = rows.reshape(3, 128, 1536)
    return pick(tensor, rows[:, :64], rows[:, 64:])


def per_device(
    inputs, cotangent, plan, attn_gain, mlp_gain, w_query, key_weight, value_weight,
    w_out, w_gate, w_up, w_down,
):
    core = lax.axis_index("section")
    z_low = lax.axis_index("zl")
    tensor = lax.axis_index("tensor")

    attn_scale = attn_gain[0].astype(F32)[:, None]
    mlp_scale = mlp_gain[0].astype(F32)[:, None]

    core_ref = core.astype(jnp.int32).reshape(1)
    mine, give = pack_shards(
        core_ref, attn_gain, mlp_gain,
        w_gate[0], w_up[0], w_down[0].T, w_query[0], key_weight[0], value_weight[0], w_out[0].T,
    )
    got = swap(give, "section")
    layer_zero, layer_one = pick(core, mine, got), pick(core, got, mine)
    first_weights = gather_rows(
        z_low, jnp.concatenate([layer_zero, layer_one[:, MLP_COLS:]], axis=1)
    )
    last_weights = gather_rows(z_low, layer_one[:, :MLP_COLS])

    stream = join_positions(tensor, to_ring_order(inputs[:, 0][plan]))
    stream, late = lax.optimization_barrier((stream, cotangent))
    out_grad = join_positions(tensor, to_ring_order(late[:, 0][plan]))
    stream, out_grad = lax.optimization_barrier((stream, out_grad))

    def whole_rows(sums):
        own, other = jnp.concatenate(sums[:PARTS]), jnp.concatenate(sums[PARTS:])
        return jnp.concatenate([pick(core, own, other), pick(core, other, own)], axis=1).astype(F32)

    x_zero = stream
    first_zero, qkv_zero, prob_zero, mix_zero, *partial = attention_first(
        core_ref, x_zero, first_weights, MLP_COLS
    )
    near, token = fetch(first_weights, 0, MLP_COLS)
    sums, token = sum_four(partial, beside=token)
    middle_zero, second_zero, gate_zero, up_zero, hidden_zero, *partial = mlp_forward(
        core_ref, x_zero, sums, near, token
    )
    near, token = fetch(first_weights, LAYER_COLS, ATTN_COLS)
    sums, token = sum_four(partial, beside=token)
    x_one, first_one, qkv_one, prob_one, mix_one, *partial = attention_next(
        core_ref, middle_zero, sums, near, token
    )
    hidden_grad, near, token = mlp_ahead(out_grad, last_weights)
    sums, token = sum_four(partial, beside=token)

    middle_one, hidden_far, second_one, hidden_one, pair_grad = mlp_last(
        core_ref, x_one, sums, hidden_grad, near, token
    )
    one_mlp, done = mlp_weights(None, MLP_COLS, second_one, out_grad, pair_grad, hidden_one)
    last_pair = scatter_pair(one_mlp)
    partial = mlp_in(core_ref, pair_grad, last_weights, done)
    near, token = fetch(first_weights, LAYER_COLS, ATTN_COLS, one_mlp)
    sums, token = sum_four(partial, beside=token)
    middle_grad, attn_in, qkv_grad, *partial = attention_backward(
        core_ref, out_grad, middle_one, sums, qkv_one, prob_one, near, token, True
    )
    buffer, _ = attention_weights(None, REST_COLS, MLP_COLS, first_one, attn_in, qkv_grad, mix_one)
    near, token = fetch(first_weights, 0, MLP_COLS, buffer)
    sums, (buffer, token) = sum_four(partial, beside=(buffer, token))

    grad_one, pair_grad, *partial = mlp_backward(
        core_ref, (x_one, middle_grad, *sums), gate_zero, up_zero, near, token
    )
    buffer, _ = mlp_weights(buffer, REST_COLS, second_zero, grad_one, pair_grad, hidden_zero)
    near, token = fetch(first_weights, MLP_COLS, ATTN_COLS, buffer)
    sums, (buffer, token) = sum_four(partial, beside=(buffer, token))
    hidden_far, sums[0] = lax.optimization_barrier((hidden_far, sums[0]))
    down_partial = mlp_down(core_ref, hidden_far, last_weights)
    middle_grad, attn_in, qkv_grad = attention_backward(
        core_ref, grad_one, middle_zero, sums, qkv_zero, prob_zero, near, token, False
    )
    buffer, done = attention_weights(
        buffer, REST_COLS, LAYER_COLS, first_zero, attn_in, qkv_grad, mix_zero
    )
    rest_pair = scatter_pair(buffer)
    sums, _ = sum_four(attention_in(core_ref, qkv_grad, near, done))
    rows = x_zero.astype(F32)
    grad_zero = middle_grad + norm_back(whole_rows(sums), rows, inverse_norm(rows))
    down_sums, _ = sum_four(down_partial)
    result_one = (middle_one + whole_rows(down_sums)).astype(BF16)
    outputs = [own_positions(tensor, x_one), own_positions(tensor, result_one)]
    grads = [own_positions(tensor, grad_zero.astype(BF16)), own_positions(tensor, grad_one)]

    layer_outputs = from_ring_order(pick(core, outputs[0], outputs[1]))
    input_grads = from_ring_order(pick(core, grads[0], grads[1]))
    last_grad = scatter_low(z_low, last_pair)
    rest_pair, layer_outputs, input_grads, last_grad = lax.optimization_barrier(
        (rest_pair, layer_outputs, input_grads, last_grad)
    )
    keep = pick(z_low, rest_pair[:48], rest_pair[48:])
    arrived = swap(pick(z_low, rest_pair[48:], rest_pair[:48]), "zl")
    mine, give, terms = combine_grads(
        core_ref, keep, arrived, last_grad, layer_zero, layer_one
    )
    got = swap(give, "section")
    arrived = swap(terms, "tensor")
    gate_grad, up_grad, down_grad, query_grad, key_grad, value_grad, out_weight_grad = unpack_grads(
        core_ref, attn_scale, mlp_scale, mine, got
    )
    arrived, key_grad = lax.optimization_barrier((arrived, key_grad))
    terms = terms + arrived
    terms = pick(core, terms[:2], terms[2:]) + swap(pick(core, terms[2:], terms[:2]), "section")
    return (
        layer_outputs[None, :, None],
        input_grads[None, :, None],
        (terms[0] / attn_scale[:, 0])[None],
        (terms[1] / mlp_scale[:, 0])[None],
        query_grad[None],
        key_grad[None],
        value_grad[None],
        out_weight_grad.T[None],
        gate_grad[None],
        up_grad[None],
        down_grad.T[None],
    )


def solution(mesh):
    split = Mesh(mesh.devices.reshape(2, 4, 2, 4, 2), ("section", "y", "zl", "x", "tensor"))
    dp = ("y", "zl", "x")
    rows = P("section", dp, "tensor")
    columns = P("section", "tensor", dp)
    return jax.shard_map(
        per_device,
        mesh=split,
        in_specs=(
            P(None, dp, "tensor", None),
            P(None, dp, "tensor", None),
            P(),
            P("section", dp),
            P("section", dp),
            rows,
            rows,
            rows,
            columns,
            rows,
            rows,
            columns,
        ),
        out_specs=(
            P("section", None, dp, "tensor", None),
            P("section", None, dp, "tensor", None),
            P("section", dp),
            P("section", dp),
            rows,
            rows,
            rows,
            columns,
            rows,
            rows,
            columns,
        ),
        check_vma=False,
    )
```

```python
import functools

import jax
import jax.numpy as jnp
from jax import lax
from jax.experimental import pallas as pl
from jax.experimental.pallas import tpu as pltpu
from jax.sharding import Mesh, PartitionSpec as P

HEAD_WIDTH = 96
EPSILON = 1e-05
BLOCKED = -1e30
SCORE_SCALE = HEAD_WIDTH ** (-0.5)
BF16 = jnp.bfloat16
F32 = jnp.float32

QUERY_COLS, KV_COLS = 384, 192
QKV_COLS = QUERY_COLS + 2 * KV_COLS
OUT_COLS = 384
HIDDEN_COLS = 1024
ATTN_COLS = QKV_COLS + OUT_COLS
MLP_COLS = 3 * HIDDEN_COLS
LAYER_COLS = MLP_COLS + ATTN_COLS
REST_COLS = LAYER_COLS + ATTN_COLS
HIDDEN_TILE = 512
AHEAD = 3
WIDTH = 1536
HALF = WIDTH // 2
PARTS = 2
MIB = 1024 * 1024


def swap(value, axis):
    return lax.ppermute(value, axis, [(0, 1), (1, 0)])


def pick(index, first, second):
    return jnp.where(index == 0, first, second)


def norm_back(weighted, residual, inverse):
    scaled = residual * inverse
    return inverse * (weighted - scaled * jnp.mean(weighted * scaled, axis=-1, keepdims=True))


def vmem_whole():
    return pl.BlockSpec(memory_space=pltpu.VMEM)


def smem_whole():
    return pl.BlockSpec(memory_space=pltpu.SMEM)


def shape(rows, columns, dtype):
    return jax.ShapeDtypeStruct((rows, columns), dtype)


def half_of(core_ref, which):
    position = core_ref[0] if which == 0 else 1 - core_ref[0]
    return pl.ds(pl.multiple_of(position * HALF, HALF), HALF)


def nt_dot(left_side, right_side):
    return lax.dot_general(
        left_side, right_side, (((1,), (1,)), ((), ())), preferred_element_type=F32
    )


def tn_dot(left_side, right_side):
    return lax.dot_general(
        left_side, right_side, (((0,), (0,)), ((), ())), preferred_element_type=F32
    )


def nn_dot(left_side, right_side):
    return jnp.dot(left_side, right_side, preferred_element_type=F32)


def row_parts(rows):
    return [slice(rows // PARTS * part, rows // PARTS * (part + 1)) for part in range(PARTS)]


def part_shapes(rows):
    return [shape(rows // PARTS, HALF, BF16)] * (2 * PARTS)


class Outward:
    def __init__(self, sems):
        self.sems, self.copies = sems, []

    def send(self, source, target):
        self.copies.append(pltpu.make_async_copy(source, target, self.sems.at[len(self.copies)]))
        self.copies[-1].start()

    def wait(self):
        for copy in self.copies:
            copy.wait()


def far(array):
    return pltpu.HBM(array.shape, array.dtype)


def each_sum(core_ref, sum_refs):
    rows = sum_refs[0].shape[0] * PARTS
    for which in range(2):
        for part, at in enumerate(row_parts(rows)):
            yield at, half_of(core_ref, which), sum_refs[PARTS * which + part]


def write_half(core_ref, which, left_ref, w_ref, columns, outs):
    product = nt_dot(left_ref[...], w_ref[half_of(core_ref, which), columns]).astype(BF16)
    refs = outs[PARTS * which : PARTS * (which + 1)]
    for at, ref in zip(row_parts(left_ref.shape[0]), refs):
        ref[...] = product[at]


def write_partial(core_ref, left_ref, w_ref, columns, outs):
    for which in (1, 0):
        write_half(core_ref, which, left_ref, w_ref, columns, outs)


def params(mib):
    return pltpu.CompilerParams(vmem_limit_bytes=mib * MIB)


def inverse_norm(rows):
    return lax.rsqrt(jnp.mean(rows * rows, axis=-1, keepdims=True) + EPSILON)


def causal_mask():
    row = lax.broadcasted_iota(jnp.int32, (128, 128), 0)
    return row >= lax.broadcasted_iota(jnp.int32, (128, 128), 1)


def two_heads(ref, rows, start):
    return jnp.concatenate(
        [
            ref[rows, start : start + HEAD_WIDTH],
            ref[rows, start + HEAD_WIDTH : start + 2 * HEAD_WIDTH],
        ],
        axis=0,
    )


def ahead_copy(w_any, w_ref, sem, column):
    return pltpu.make_async_copy(w_any.at[:, pl.ds(column, w_ref.shape[1])], w_ref, sem)


def attention_forward_body(sequences, core_ref, outward, first_ref, w_ref, qkv_any, prob_any, mix_ref, *rest):
    parts, (qkv_ref, prob_ref) = rest[:-2], rest[-2:]
    qkv_ref[...] = nn_dot(first_ref[...], w_ref[:, :QKV_COLS]).astype(BF16)
    outward.send(qkv_ref, qkv_any)
    mask = causal_mask()
    mask = jnp.concatenate([mask, mask], axis=0)
    for sequence in range(sequences):
        rows = slice(128 * sequence, 128 * (sequence + 1))
        for group in range(2):
            queries = two_heads(qkv_ref, rows, 2 * HEAD_WIDTH * group)
            key_at = QUERY_COLS + HEAD_WIDTH * group
            value_at = key_at + KV_COLS
            scores = nt_dot(queries, qkv_ref[rows, key_at : key_at + HEAD_WIDTH]) * SCORE_SCALE
            scores = jnp.where(mask, scores, BLOCKED)
            expanded = jnp.exp(scores - jnp.max(scores, axis=-1, keepdims=True))
            probability = expanded / jnp.sum(expanded, axis=-1, keepdims=True)
            prob_ref[2 * sequence + group] = probability
            mixed = nn_dot(
                probability.astype(BF16), qkv_ref[rows, value_at : value_at + HEAD_WIDTH]
            ).astype(BF16)
            at = 2 * HEAD_WIDTH * group
            mix_ref[rows, at : at + HEAD_WIDTH] = mixed[:128]
            mix_ref[rows, at + HEAD_WIDTH : at + 2 * HEAD_WIDTH] = mixed[128:]
        both = pl.ds(2 * sequence, 2)
        outward.send(prob_ref.at[both], prob_any.at[both])
    write_partial(core_ref, mix_ref, w_ref, slice(QKV_COLS, ATTN_COLS), parts)
    outward.wait()


def attention_first_kernel(sequences, column, core_ref, x_ref, w_any, first_any, *rest):
    outs, (first_ref, w_ref, sem, sems) = rest[:-4], rest[-4:]
    copy = ahead_copy(w_any, w_ref, sem, column)
    copy.start()
    rows = x_ref[...].astype(F32)
    first_ref[...] = (rows * inverse_norm(rows)).astype(BF16)
    copy.wait()
    outward = Outward(sems)
    outward.send(first_ref, first_any)
    attention_forward_body(sequences, core_ref, outward, first_ref, w_ref, *outs)


def attention_next_kernel(sequences, core_ref, middle_ref, *rest):
    sums, (w_ref, _, x_any, first_any) = rest[: 2 * PARTS], rest[2 * PARTS : 2 * PARTS + 4]
    outs, (x_ref, first_ref, sems) = rest[2 * PARTS + 4 : -3], rest[-3:]
    outward = Outward(sems)
    for at, columns, part in each_sum(core_ref, sums):
        x_ref[at, columns] = (middle_ref[at, columns] + part[...].astype(F32)).astype(BF16)
    outward.send(x_ref, x_any)
    rows = x_ref[...].astype(F32)
    first_ref[...] = (rows * inverse_norm(rows)).astype(BF16)
    outward.send(first_ref, first_any)
    attention_forward_body(sequences, core_ref, outward, first_ref, w_ref, *outs)


def in_hbm(value):
    return pltpu.with_memory_space_constraint(value, pltpu.HBM)


def hbm_whole():
    return pl.BlockSpec(memory_space=pltpu.HBM)


def attention_scratch():
    return [pltpu.VMEM((WIDTH, ATTN_COLS), BF16), pltpu.SemaphoreType.DMA(())]


def attention_outs(rows):
    outs = [
        shape(rows, WIDTH, BF16),
        far(shape(rows, QKV_COLS, BF16)),
        pltpu.HBM((rows // 64, 256, 128), F32),
        shape(rows, OUT_COLS, BF16),
    ]
    return outs + part_shapes(rows), [vmem_whole(), hbm_whole(), hbm_whole()] + [vmem_whole()] * (1 + 2 * PARTS)


def attention_cost(rows):
    return pl.CostEstimate(
        flops=2 * rows * WIDTH * ATTN_COLS, bytes_accessed=8_000_000, transcendentals=0
    )


def fetch_kernel(column, w_any, *rest):
    out_ref, token_ref, sem = rest[-3:]
    copy = ahead_copy(w_any, out_ref, sem, column)
    copy.start()
    token_ref[...] = jnp.zeros_like(token_ref)
    copy.wait()


TOKEN = jax.ShapeDtypeStruct((8, 128), F32)


def fetch(weights, column, columns, *after):
    return pl.pallas_call(
        functools.partial(fetch_kernel, column),
        in_specs=[hbm_whole()] * (1 + len(after)),
        out_specs=[vmem_whole()] * 2,
        out_shape=[shape(WIDTH, columns, BF16), TOKEN],
        scratch_shapes=[pltpu.SemaphoreType.DMA(())],
        compiler_params=params(12),
        cost_estimate=pl.CostEstimate(
            flops=0, bytes_accessed=2 * WIDTH * columns * 2, transcendentals=0
        ),
        name="fetch",
    )(in_hbm(weights), *[in_hbm(value) for value in after])


def attention_first(core, x, weights, column):
    rows = x.shape[0]
    outs, specs = attention_outs(rows)
    return pl.pallas_call(
        functools.partial(attention_first_kernel, rows // 128, column),
        in_specs=[smem_whole(), vmem_whole(), hbm_whole()],
        out_specs=[hbm_whole()] + specs[1:],
        out_shape=[far(outs[0])] + outs[1:],
        scratch_shapes=[
            pltpu.VMEM((rows, QKV_COLS), BF16),
            pltpu.VMEM((rows // 64, 256, 128), F32),
            pltpu.VMEM((rows, WIDTH), BF16),
        ]
        + attention_scratch()
        + [pltpu.SemaphoreType.DMA((2 + rows // 128,))],
        compiler_params=params(20),
        cost_estimate=attention_cost(rows),
        name="attention_first",
    )(core, x, in_hbm(weights))


def attention_next(core, middle, sums, weights, token):
    rows = middle.shape[0]
    outs, specs = attention_outs(rows)
    whole = shape(rows, WIDTH, BF16)
    return pl.pallas_call(
        functools.partial(attention_next_kernel, rows // 128),
        in_specs=[smem_whole()] + [vmem_whole()] * (2 + 2 * PARTS) + [hbm_whole()],
        out_specs=[hbm_whole()] * 2 + specs[1:],
        out_shape=[far(whole)] * 2 + outs[1:],
        scratch_shapes=[
            pltpu.VMEM((rows, QKV_COLS), BF16),
            pltpu.VMEM((rows // 64, 256, 128), F32),
            pltpu.VMEM(whole.shape, BF16),
            pltpu.VMEM(whole.shape, BF16),
            pltpu.SemaphoreType.DMA((3 + rows // 128,)),
        ],
        compiler_params=params(16),
        cost_estimate=attention_cost(rows),
        name="attention_next",
    )(core, middle, *sums, weights, token)


def column_tiles(first):
    return [pl.ds(first + HIDDEN_TILE * step, HIDDEN_TILE) for step in range(HIDDEN_STEPS)]


def sigmoid(values):
    return 0.5 * jnp.tanh(0.5 * values) + 0.5


def arrivals(copies):
    for copy in copies[:AHEAD]:
        copy.start()
    place = iter(range(len(copies)))

    def arrive():
        number = next(place)
        copies[number].wait()
        if number + AHEAD < len(copies):
            copies[number + AHEAD].start()

    return arrive


def mlp_forward_kernel(core_ref, x_ref, *rest):
    sums, rest = rest[: 2 * PARTS], rest[2 * PARTS :]
    (w_ref, _, middle_any, second_any, gate_any, up_any, hidden_any), rest = rest[:7], rest[7:]
    outs, (middle_ref, second_ref, gate_ref, up_ref, hidden_ref, out_sems) = rest[:-6], rest[-6:]
    tiles = [(gate, up) for gate, up in zip(column_tiles(0), column_tiles(HIDDEN_COLS))]
    down = pl.ds(2 * HIDDEN_COLS, HIDDEN_COLS)
    for at, columns, part in each_sum(core_ref, sums):
        middle_ref[at, columns] = x_ref[at, columns].astype(F32) + part[...].astype(F32)
    rows = middle_ref[...]
    second_ref[...] = (rows * inverse_norm(rows)).astype(BF16)
    outward = Outward(out_sems)
    outward.send(middle_ref, middle_any)
    outward.send(second_ref, second_any)
    for step, (gate, up) in enumerate(tiles):
        at = slice(HIDDEN_TILE * step, HIDDEN_TILE * (step + 1))
        gate_out = nn_dot(second_ref[...], w_ref[:, gate])
        up_out = nn_dot(second_ref[...], w_ref[:, up])
        gate_ref[:, at] = gate_out
        up_ref[:, at] = up_out
        hidden_ref[:, at] = (gate_out * sigmoid(gate_out) * up_out).astype(BF16)
        for ref, target in ((gate_ref, gate_any), (up_ref, up_any), (hidden_ref, hidden_any)):
            outward.send(ref.at[:, at], target.at[:, at])
    write_partial(core_ref, hidden_ref, w_ref, down, outs)
    outward.wait()


HIDDEN_STEPS = HIDDEN_COLS // HIDDEN_TILE


def mlp_cost(rows):
    return pl.CostEstimate(
        flops=2 * rows * WIDTH * MLP_COLS, bytes_accessed=15_000_000, transcendentals=0
    )


def mlp_forward(core, x, sums, weights, token):
    rows = x.shape[0]
    saved = [
        shape(rows, WIDTH, F32),
        shape(rows, WIDTH, BF16),
        shape(rows, HIDDEN_COLS, F32),
        shape(rows, HIDDEN_COLS, F32),
        shape(rows, HIDDEN_COLS, BF16),
    ]
    return pl.pallas_call(
        mlp_forward_kernel,
        in_specs=[smem_whole()] + [vmem_whole()] * (2 + 2 * PARTS) + [hbm_whole()],
        out_specs=[hbm_whole()] * 5 + [vmem_whole()] * (2 * PARTS),
        out_shape=[far(array) for array in saved] + part_shapes(rows),
        scratch_shapes=[pltpu.VMEM(out.shape, out.dtype) for out in saved]
        + [pltpu.SemaphoreType.DMA((2 + 3 * HIDDEN_STEPS,))],
        compiler_params=params(24),
        cost_estimate=mlp_cost(rows),
        name="mlp_forward",
    )(core, x, *sums, weights, token)


def mlp_grads(hidden_grad, gate_out, up_out):
    sigmoid_gate = sigmoid(gate_out)
    gate_grad = hidden_grad * up_out * (sigmoid_gate * (1.0 + gate_out * (1.0 - sigmoid_gate)))
    return gate_grad.astype(BF16), (hidden_grad * (gate_out * sigmoid_gate)).astype(BF16)


def mlp_backward_kernel(core_ref, x_ref, middle_grad_ref, *rest):
    sums, rest = rest[: 2 * PARTS], rest[2 * PARTS :]
    (gate_ref, up_ref, w_ref, _, g_ref, pair_grad_ref), rest = rest[:6], rest[6:]
    outs, weighted = rest[:-1], rest[-1]
    for at, columns, part in each_sum(core_ref, sums):
        weighted[at, columns] = part[...].astype(F32)
    rows = x_ref[...].astype(F32)
    g_ref[...] = (
        middle_grad_ref[...] + norm_back(weighted[...], rows, inverse_norm(rows))
    ).astype(BF16)
    for step, down in enumerate(column_tiles(2 * HIDDEN_COLS)):
        at = slice(HIDDEN_TILE * step, HIDDEN_TILE * (step + 1))
        up_at = slice(HIDDEN_COLS + at.start, HIDDEN_COLS + at.stop)
        hidden_grad = nn_dot(g_ref[...], w_ref[:, down])
        pair_grad_ref[:, at], pair_grad_ref[:, up_at] = mlp_grads(
            hidden_grad, gate_ref[:, at], up_ref[:, at]
        )
    write_partial(core_ref, pair_grad_ref, w_ref, slice(0, 2 * HIDDEN_COLS), outs)


def mlp_backward(core, above, gate_out, up_out, weights, token):
    rows = gate_out.shape[0]
    return pl.pallas_call(
        mlp_backward_kernel,
        in_specs=[smem_whole()] + [vmem_whole()] * (5 + 2 * PARTS) + [hbm_whole()],
        out_specs=[vmem_whole()] * (2 + 2 * PARTS),
        out_shape=[shape(rows, WIDTH, BF16), shape(rows, 2 * HIDDEN_COLS, BF16)]
        + part_shapes(rows),
        scratch_shapes=[pltpu.VMEM((rows, WIDTH), F32)],
        compiler_params=params(26),
        cost_estimate=mlp_cost(rows),
        name="mlp_backward",
    )(core, *above, gate_out, up_out, weights, token)


def mlp_ahead_kernel(g_ref, w_any, hidden_grad_ref, pair_ref, token_ref, down_ref, sems):
    down = ahead_copy(w_any, down_ref, sems.at[0], 2 * HIDDEN_COLS)
    pair = ahead_copy(w_any, pair_ref, sems.at[1], 0)
    down.start()
    pair.start()
    token_ref[...] = jnp.zeros_like(token_ref)
    down.wait()
    hidden_grad_ref[...] = nn_dot(g_ref[...], down_ref[...])
    pair.wait()


def mlp_ahead(g, weights):
    rows = g.shape[0]
    return pl.pallas_call(
        mlp_ahead_kernel,
        in_specs=[vmem_whole(), hbm_whole()],
        out_specs=[vmem_whole()] * 3,
        out_shape=[
            shape(rows, HIDDEN_COLS, F32),
            shape(WIDTH, 2 * HIDDEN_COLS, BF16),
            TOKEN,
        ],
        scratch_shapes=[pltpu.VMEM((WIDTH, HIDDEN_COLS), BF16), pltpu.SemaphoreType.DMA((2,))],
        compiler_params=params(15),
        cost_estimate=pl.CostEstimate(
            flops=2 * rows * WIDTH * HIDDEN_COLS, bytes_accessed=14_000_000, transcendentals=0
        ),
        name="mlp_ahead",
    )(g, in_hbm(weights))


def mlp_last_kernel(core_ref, x_ref, *rest):
    sums, rest = rest[: 2 * PARTS], rest[2 * PARTS :]
    (hidden_grad_ref, w_ref, _, middle_any, hidden_any, second_ref, hidden_ref, pair_grad_ref), rest = rest[:8], rest[8:]
    middle_ref, out_sems = rest
    for at, columns, part in each_sum(core_ref, sums):
        middle_ref[at, columns] = x_ref[at, columns].astype(F32) + part[...].astype(F32)
    rows = middle_ref[...]
    second_ref[...] = (rows * inverse_norm(rows)).astype(BF16)
    outward = Outward(out_sems)
    outward.send(middle_ref, middle_any)
    for step, (gate, up) in enumerate(zip(column_tiles(0), column_tiles(HIDDEN_COLS))):
        at = slice(HIDDEN_TILE * step, HIDDEN_TILE * (step + 1))
        up_at = slice(HIDDEN_COLS + at.start, HIDDEN_COLS + at.stop)
        gate_out = nn_dot(second_ref[...], w_ref[:, gate])
        up_out = nn_dot(second_ref[...], w_ref[:, up])
        hidden_ref[:, at] = (gate_out * sigmoid(gate_out) * up_out).astype(BF16)
        pair_grad_ref[:, at], pair_grad_ref[:, up_at] = mlp_grads(
            hidden_grad_ref[:, at], gate_out, up_out
        )
    outward.send(hidden_ref, hidden_any)
    outward.wait()


def mlp_last(core, x, sums, hidden_grad, pair_weights, token):
    rows = x.shape[0]
    return pl.pallas_call(
        mlp_last_kernel,
        in_specs=[smem_whole()] + [vmem_whole()] * (3 + 2 * PARTS) + [hbm_whole()],
        out_specs=[hbm_whole()] * 2 + [vmem_whole()] * 3,
        out_shape=[
            pltpu.HBM((rows, WIDTH), F32),
            pltpu.HBM((rows, HIDDEN_COLS), BF16),
            shape(rows, WIDTH, BF16),
            shape(rows, HIDDEN_COLS, BF16),
            shape(rows, 2 * HIDDEN_COLS, BF16),
        ],
        scratch_shapes=[pltpu.VMEM((rows, WIDTH), F32), pltpu.SemaphoreType.DMA((2,))],
        compiler_params=params(28),
        cost_estimate=mlp_cost(rows),
        name="mlp_last",
    )(core, x, *sums, hidden_grad, pair_weights, token)


def mlp_in_kernel(core_ref, pair_grad_ref, w_any, _, *rest):
    outs, w_ref, sems = rest[:-2], rest[-2], rest[-1]
    copies = []
    for which in (1, 0):
        half = half_of(core_ref, which)
        source = w_any.at[half, pl.ds(0, 2 * HIDDEN_COLS)]
        copies.append(pltpu.make_async_copy(source, w_ref.at[half, :], sems.at[which]))
        copies[-1].start()
    for copy, which in zip(copies, (1, 0)):
        copy.wait()
        write_half(core_ref, which, pair_grad_ref, w_ref, slice(0, 2 * HIDDEN_COLS), outs)


def mlp_in(core, pair_grad, weights, token):
    rows = pair_grad.shape[0]
    return pl.pallas_call(
        mlp_in_kernel,
        in_specs=[smem_whole(), vmem_whole()] + [hbm_whole()] * 2,
        out_specs=[vmem_whole()] * (2 * PARTS),
        out_shape=part_shapes(rows),
        scratch_shapes=[
            pltpu.VMEM((WIDTH, 2 * HIDDEN_COLS), BF16),
            pltpu.SemaphoreType.DMA((2,)),
        ],
        compiler_params=params(18),
        cost_estimate=pl.CostEstimate(
            flops=4 * rows * WIDTH * HIDDEN_COLS, bytes_accessed=9_000_000, transcendentals=0
        ),
        name="mlp_in",
    )(core, pair_grad, in_hbm(weights), token)


def mlp_down_kernel(core_ref, hidden_ref, w_any, *rest):
    outs, w_ref, sem = rest[:-2], rest[-2], rest[-1]
    copy = pltpu.make_async_copy(w_any.at[:, pl.ds(2 * HIDDEN_COLS, HIDDEN_COLS)], w_ref, sem)
    copy.start()
    copy.wait()
    write_partial(core_ref, hidden_ref, w_ref, slice(0, HIDDEN_COLS), outs)


def mlp_down(core, hidden, weights):
    rows = hidden.shape[0]
    return pl.pallas_call(
        mlp_down_kernel,
        in_specs=[smem_whole(), vmem_whole(), hbm_whole()],
        out_specs=[vmem_whole()] * (2 * PARTS),
        out_shape=part_shapes(rows),
        scratch_shapes=[pltpu.VMEM((WIDTH, HIDDEN_COLS), BF16), pltpu.SemaphoreType.DMA(())],
        compiler_params=params(14),
        cost_estimate=pl.CostEstimate(
            flops=2 * rows * WIDTH * HIDDEN_COLS, bytes_accessed=5_000_000, transcendentals=0
        ),
        name="mlp_down",
    )(core, hidden, in_hbm(weights))


def attention_backward_kernel(sequences, near, core_ref, g_ref, middle_ref, *rest):
    sums, rest = rest[: 2 * PARTS], rest[2 * PARTS :]
    (w_ref, qkv_any, prob_any, _, middle_grad_out, attn_in_ref, qkv_grad_ref), rest = rest[:7], rest[7:]
    outs, (middle_grad_ref, qkv_ref, prob_ref, mix_grad, sems) = rest[:-5], rest[-5:]
    copies = [
        pltpu.make_async_copy(qkv_any, qkv_ref, sems.at[0]),
        pltpu.make_async_copy(prob_any, prob_ref, sems.at[1]),
    ]
    for copy in copies:
        copy.start()
    for at, columns, part in each_sum(core_ref, sums):
        middle_grad_ref[at, columns] = part[...].astype(F32)
    middle = middle_ref[...]
    middle_grad = g_ref[...].astype(F32) + norm_back(
        middle_grad_ref[...], middle, inverse_norm(middle)
    )
    if near:
        middle_grad_out[...] = middle_grad
    else:
        middle_grad_ref[...] = middle_grad
        outward = pltpu.make_async_copy(middle_grad_ref, middle_grad_out, sems.at[2])
        outward.start()
    attn_in_ref[...] = middle_grad.astype(BF16)
    mix_grad[...] = nn_dot(attn_in_ref[...], w_ref[:, QKV_COLS:]).astype(BF16)
    for copy in copies:
        copy.wait()
    for sequence in range(sequences):
        rows = slice(128 * sequence, 128 * (sequence + 1))
        for group in range(2):
            at = 2 * HEAD_WIDTH * group
            key_at = QUERY_COLS + HEAD_WIDTH * group
            value_at = key_at + KV_COLS
            grads = two_heads(mix_grad, rows, at)
            queries = two_heads(qkv_ref, rows, at)
            keys = qkv_ref[rows, key_at : key_at + HEAD_WIDTH]
            probability = prob_ref[2 * sequence + group]
            prob_grad = nt_dot(grads, qkv_ref[rows, value_at : value_at + HEAD_WIDTH])
            centred = jnp.sum(probability * prob_grad, axis=-1, keepdims=True)
            score_grad = (probability * (prob_grad - centred)).astype(BF16)
            query_grad = (nn_dot(score_grad, keys) * SCORE_SCALE).astype(BF16)
            qkv_grad_ref[rows, at : at + HEAD_WIDTH] = query_grad[:128]
            qkv_grad_ref[rows, at + HEAD_WIDTH : at + 2 * HEAD_WIDTH] = query_grad[128:]
            qkv_grad_ref[rows, key_at : key_at + HEAD_WIDTH] = (
                tn_dot(score_grad, queries) * SCORE_SCALE
            ).astype(BF16)
            qkv_grad_ref[rows, value_at : value_at + HEAD_WIDTH] = tn_dot(
                probability.astype(BF16), grads
            ).astype(BF16)
    if near:
        write_partial(core_ref, qkv_grad_ref, w_ref, slice(0, QKV_COLS), outs)
    else:
        outward.wait()


def attention_in_kernel(core_ref, qkv_grad_ref, w_ref, _, *outs):
    write_partial(core_ref, qkv_grad_ref, w_ref, slice(0, QKV_COLS), outs)


def attention_in(core, qkv_grad, weights, token):
    rows = qkv_grad.shape[0]
    return pl.pallas_call(
        attention_in_kernel,
        in_specs=[smem_whole()] + [vmem_whole()] * 2 + [hbm_whole()],
        out_specs=[vmem_whole()] * (2 * PARTS),
        out_shape=part_shapes(rows),
        compiler_params=params(14),
        cost_estimate=pl.CostEstimate(
            flops=2 * rows * WIDTH * QKV_COLS, bytes_accessed=5_000_000, transcendentals=0
        ),
        name="attention_in",
    )(core, qkv_grad, weights, token)


def attention_backward(core, g, middle, sums, qkv, probability, weights, token, near):
    rows = g.shape[0]
    residual, parts = shape(rows, WIDTH, F32), part_shapes(rows) if near else []
    return pl.pallas_call(
        functools.partial(attention_backward_kernel, rows // 128, near),
        in_specs=[smem_whole()] + [vmem_whole()] * (3 + 2 * PARTS) + [hbm_whole()] * 3,
        out_specs=[vmem_whole() if near else hbm_whole()] + [vmem_whole()] * (2 + len(parts)),
        out_shape=[
            residual if near else far(residual),
            shape(rows, WIDTH, BF16),
            shape(rows, QKV_COLS, BF16),
        ]
        + parts,
        scratch_shapes=[
            pltpu.VMEM((rows, WIDTH), F32),
            pltpu.VMEM(qkv.shape, BF16),
            pltpu.VMEM(probability.shape, F32),
            pltpu.VMEM((rows, OUT_COLS), BF16),
            pltpu.SemaphoreType.DMA((3,)),
        ],
        compiler_params=params(24),
        cost_estimate=attention_cost(rows),
        name="attention_backward",
    )(core, g, middle, *sums, weights, in_hbm(qkv), in_hbm(probability), token)


def write_products(start, pairs, out_any, slots, sems):
    _, height, width = slots.shape
    copies = []
    for number in range(WIDTH // height):
        features = pl.ds(height * number, height)
        if number >= 2:
            copies[number - 2].wait()
        slot = slots.at[number % 2]
        at = 0
        for left, right in pairs:
            columns = right.shape[1]
            slot[:, at : at + columns] = tn_dot(left[:, features], right[...]).astype(BF16)
            at += columns
        target = out_any.at[features, pl.ds(start, width)]
        copies.append(pltpu.make_async_copy(slot, target, sems.at[number % 2]))
        copies[-1].start()
    for copy in copies[-2:]:
        copy.wait()


def mlp_weights_kernel(second_ref, g_ref, pair_grad_ref, hidden_ref, *rest):
    out_any, token_ref, slots, sems = rest[-4:]
    token_ref[...] = jnp.zeros_like(token_ref)
    write_products(0, [(second_ref, pair_grad_ref), (g_ref, hidden_ref)], out_any, slots, sems)


def into_buffer(kernel, buffer, columns, slot, operands, flops, name, mib):
    aliases, specs = {}, [vmem_whole()] * len(operands)
    if buffer is not None:
        aliases = {len(operands): 0}
        specs, operands = specs + [hbm_whole()], operands + (in_hbm(buffer),)
    return pl.pallas_call(
        kernel,
        in_specs=specs,
        out_specs=[hbm_whole(), vmem_whole()],
        out_shape=[pltpu.HBM((WIDTH, columns), BF16), TOKEN],
        input_output_aliases=aliases,
        scratch_shapes=[pltpu.VMEM((2, *slot), BF16), pltpu.SemaphoreType.DMA((2,))],
        compiler_params=params(mib),
        cost_estimate=pl.CostEstimate(flops=flops, bytes_accessed=flops // 250, transcendentals=0),
        name=name,
    )(*operands)


def mlp_weights(buffer, columns, second, g, pair_grad, hidden):
    return into_buffer(
        mlp_weights_kernel,
        buffer,
        columns,
        (512, MLP_COLS),
        (second, g, pair_grad, hidden),
        2 * second.shape[0] * WIDTH * MLP_COLS,
        "mlp_weights",
        18,
    )


def attention_weights_kernel(start, first_ref, attn_in_ref, qkv_grad_ref, mix_ref, *rest):
    out_any, token_ref, slots, sems = rest[-4:]
    token_ref[...] = jnp.zeros_like(token_ref)
    pairs = [(first_ref, qkv_grad_ref), (attn_in_ref, mix_ref)]
    write_products(start, pairs, out_any, slots, sems)


def attention_weights(buffer, columns, start, first, attn_in, qkv_grad, mixture):
    return into_buffer(
        functools.partial(attention_weights_kernel, start),
        buffer,
        columns,
        (768, ATTN_COLS),
        (first, attn_in, qkv_grad, mixture),
        2 * first.shape[0] * WIDTH * ATTN_COLS,
        "attention_weights",
        14,
    )


def sum_four(partial, beside=None, within=None):
    keeps, gives = list(partial[:PARTS]), list(partial[PARTS:])
    chips = [
        (keep.astype(F32) + swap(give, "section").astype(F32)).astype(BF16)
        for keep, give in zip(keeps, gives)
    ]
    arrived = [swap(chip, "tensor") for chip in chips]
    if beside is not None:
        arrived[-1], beside = lax.optimization_barrier((arrived[-1], beside))
    totals = [
        (chip.astype(F32) + other.astype(F32)).astype(BF16)
        for chip, other in zip(chips, arrived)
    ]
    if within is not None:

        def tie(value):
            totals[0], value = lax.optimization_barrier((totals[0], value))
            return value

        beside = within(tie)
    return totals + [swap(total, "section") for total in totals], beside


def row_scales(gain_ref):
    row = lax.broadcasted_iota(jnp.int32, (48, 48), 0)
    column = lax.broadcasted_iota(jnp.int32, (48, 48), 1)
    return jnp.where(row == column, gain_ref[...].astype(F32), 0.0).astype(BF16)


def pack_kernel(core_ref, *rest):
    sources, (mine_ref, give_ref), shards, sems = rest[:9], rest[9:11], rest[11:20], rest[20]
    copies = [
        pltpu.make_async_copy(source, shard, sems.at[number])
        for number, (source, shard) in enumerate(zip(sources, shards))
    ]
    for copy in copies:
        copy.start()
    is_first = core_ref[0] == 0
    (attn_gain_ref, mlp_gain_ref), shards = shards[:2], shards[2:]
    for copy in copies[:2]:
        copy.wait()
    attn_scale, mlp_scale = row_scales(attn_gain_ref), row_scales(mlp_gain_ref)
    start = 0
    for copy, shard, scale in zip(
        copies[2:],
        shards,
        (mlp_scale, mlp_scale, None, attn_scale, attn_scale, attn_scale, None),
    ):
        copy.wait()
        weight = shard[...]
        if scale is not None:
            weight = nn_dot(scale, weight).astype(BF16)
        width = weight.shape[1] // 2
        low, high = weight[:, :width], weight[:, width:]
        mine_ref[:, start : start + width] = jnp.where(is_first, low, high)
        give_ref[:, start : start + width] = jnp.where(is_first, high, low)
        start += width


def pack_shards(core, *shards):
    return pl.pallas_call(
        pack_kernel,
        in_specs=[smem_whole()] + [hbm_whole()] * len(shards),
        out_specs=[vmem_whole()] * 2,
        out_shape=[shape(48, LAYER_COLS, BF16)] * 2,
        scratch_shapes=[pltpu.VMEM(shard.shape, shard.dtype) for shard in shards]
        + [pltpu.SemaphoreType.DMA((len(shards),))],
        compiler_params=params(16),
        name="pack_shards",
    )(core, *[in_hbm(shard) for shard in shards])


def combine_kernel(core_ref, keep_ref, arrived_ref, last_ref, zero_w_ref, one_w_ref, mine_ref, give_ref, terms_ref, zero, one):
    rest = (keep_ref[...].astype(F32) + arrived_ref[...].astype(F32)).astype(BF16)
    zero[:, :MLP_COLS] = rest[:, :MLP_COLS]
    zero[:, MLP_COLS:] = rest[:, LAYER_COLS:]
    one[:, :MLP_COLS] = last_ref[...]
    one[:, MLP_COLS:] = rest[:, MLP_COLS:LAYER_COLS]
    is_first = core_ref[0] == 0
    mine_ref[...] = jnp.where(is_first, zero[...], one[...])
    give_ref[...] = jnp.where(is_first, one[...], zero[...])
    row = 0
    for grad, weights in ((zero, zero_w_ref), (one, one_w_ref)):
        products = weights[...].astype(F32) * grad[...].astype(F32)
        for columns in (slice(MLP_COLS, MLP_COLS + QKV_COLS), slice(0, 2 * HIDDEN_COLS)):
            terms_ref[row, :] = jnp.sum(products[:, columns], axis=1)
            row += 1


def combine_grads(core, *operands):
    return pl.pallas_call(
        combine_kernel,
        in_specs=[smem_whole()] + [vmem_whole()] * len(operands),
        out_specs=[vmem_whole()] * 3,
        out_shape=[shape(48, LAYER_COLS, BF16)] * 2 + [shape(4, 48, F32)],
        scratch_shapes=[pltpu.VMEM((48, LAYER_COLS), BF16)] * 2,
        compiler_params=params(16),
        name="combine_grads",
    )(core, *operands)


def unpack_kernel(core_ref, attn_scale_ref, mlp_scale_ref, mine_ref, got_ref, gate_ref, up_ref, down_ref, query_ref, key_ref, value_ref, out_ref):
    is_first = core_ref[0] == 0

    def place(out, start, scale_ref):
        width = out.shape[1] // 2
        mine = mine_ref[:, start : start + width].astype(F32)
        got = got_ref[:, start : start + width].astype(F32)
        if scale_ref is not None:
            mine, got = mine * scale_ref[...], got * scale_ref[...]
        out[:, :width] = jnp.where(is_first, mine, got)
        out[:, width:] = jnp.where(is_first, got, mine)

    place(gate_ref, 0, mlp_scale_ref)
    place(up_ref, HIDDEN_COLS, mlp_scale_ref)
    place(down_ref, 2 * HIDDEN_COLS, None)
    place(query_ref, MLP_COLS, attn_scale_ref)
    place(key_ref, MLP_COLS + QUERY_COLS, attn_scale_ref)
    place(value_ref, MLP_COLS + QUERY_COLS + KV_COLS, attn_scale_ref)
    place(out_ref, MLP_COLS + QKV_COLS, None)


def unpack_grads(core, *operands):
    widths = [HIDDEN_COLS] * 3 + [QUERY_COLS, KV_COLS, KV_COLS, OUT_COLS]
    return pl.pallas_call(
        unpack_kernel,
        in_specs=[smem_whole()] + [vmem_whole()] * len(operands),
        out_specs=[vmem_whole()] * len(widths),
        out_shape=[shape(48, 2 * width, F32) for width in widths],
        compiler_params=params(16),
        name="unpack_grads",
    )(core, *operands)


def gather_rows(z_low, share):
    other = swap(share, "zl")
    pair = jnp.concatenate([pick(z_low, share, other), pick(z_low, other, share)], axis=0)
    return lax.all_gather(pair, ("y", "x"), axis=0, tiled=True)


def scatter_pair(grad):
    return lax.psum_scatter(grad, ("y", "x"), scatter_dimension=0, tiled=True)


def scatter_low(z_low, pair):
    keep = pick(z_low, pair[:48], pair[48:])
    give = pick(z_low, pair[48:], pair[:48])
    return (keep.astype(F32) + swap(give, "zl").astype(F32)).astype(BF16)


def to_ring_order(rows):
    lead = rows.shape[:-1]
    return jnp.swapaxes(rows.reshape(lead + (4, 2, 4, 48)), -3, -2).reshape(rows.shape)


def from_ring_order(rows):
    lead = rows.shape[:-1]
    return jnp.swapaxes(rows.reshape(lead + (4, 4, 2, 48)), -3, -2).reshape(rows.shape)


def join_positions(tensor, own):
    other = swap(own, "tensor")
    return jnp.concatenate(
        [pick(tensor, own, other), pick(tensor, other, own)], axis=1
    ).reshape(384, WIDTH)


def own_positions(tensor, rows):
    rows = rows.reshape(3, 128, 1536)
    return pick(tensor, rows[:, :64], rows[:, 64:])


def per_device(
    inputs, cotangent, plan, attn_gain, mlp_gain, w_query, key_weight, value_weight,
    w_out, w_gate, w_up, w_down,
):
    core = lax.axis_index("section")
    z_low = lax.axis_index("zl")
    tensor = lax.axis_index("tensor")

    attn_scale = attn_gain[0].astype(F32)[:, None]
    mlp_scale = mlp_gain[0].astype(F32)[:, None]

    core_ref = core.astype(jnp.int32).reshape(1)
    mine, give = pack_shards(
        core_ref, attn_gain, mlp_gain,
        w_gate[0], w_up[0], w_down[0].T, w_query[0], key_weight[0], value_weight[0], w_out[0].T,
    )
    got = swap(give, "section")
    layer_zero, layer_one = pick(core, mine, got), pick(core, got, mine)
    first_weights = gather_rows(
        z_low, jnp.concatenate([layer_zero, layer_one[:, MLP_COLS:]], axis=1)
    )
    last_weights = gather_rows(z_low, layer_one[:, :MLP_COLS])

    stream = join_positions(tensor, to_ring_order(inputs[:, 0][plan]))
    stream, late = lax.optimization_barrier((stream, cotangent))
    out_grad = join_positions(tensor, to_ring_order(late[:, 0][plan]))
    stream, out_grad = lax.optimization_barrier((stream, out_grad))

    def whole_rows(sums):
        own, other = jnp.concatenate(sums[:PARTS]), jnp.concatenate(sums[PARTS:])
        return jnp.concatenate([pick(core, own, other), pick(core, other, own)], axis=1).astype(F32)

    x_zero = stream
    first_zero, qkv_zero, prob_zero, mix_zero, *partial = attention_first(
        core_ref, x_zero, first_weights, MLP_COLS
    )
    near, token = fetch(first_weights, 0, MLP_COLS)
    sums, token = sum_four(partial, beside=token)
    middle_zero, second_zero, gate_zero, up_zero, hidden_zero, *partial = mlp_forward(
        core_ref, x_zero, sums, near, token
    )
    near, token = fetch(first_weights, LAYER_COLS, ATTN_COLS)
    sums, token = sum_four(partial, beside=token)
    x_one, first_one, qkv_one, prob_one, mix_one, *partial = attention_next(
        core_ref, middle_zero, sums, near, token
    )
    sums, ahead = sum_four(partial, within=lambda tie: mlp_ahead(out_grad, tie(last_weights)))
    hidden_grad, near, token = ahead

    middle_one, hidden_far, second_one, hidden_one, pair_grad = mlp_last(
        core_ref, x_one, sums, hidden_grad, near, token
    )
    one_mlp, done = mlp_weights(None, MLP_COLS, second_one, out_grad, pair_grad, hidden_one)
    last_pair = scatter_pair(one_mlp)
    partial = mlp_in(core_ref, pair_grad, last_weights, done)
    near, token = fetch(first_weights, LAYER_COLS, ATTN_COLS, one_mlp)
    sums, token = sum_four(partial, beside=token)
    middle_grad, attn_in, qkv_grad, *partial = attention_backward(
        core_ref, out_grad, middle_one, sums, qkv_one, prob_one, near, token, True
    )
    buffer, _ = attention_weights(None, REST_COLS, MLP_COLS, first_one, attn_in, qkv_grad, mix_one)
    near, token = fetch(first_weights, 0, MLP_COLS, buffer)
    sums, (buffer, token) = sum_four(partial, beside=(buffer, token))

    grad_one, pair_grad, *partial = mlp_backward(
        core_ref, (x_one, middle_grad, *sums), gate_zero, up_zero, near, token
    )
    buffer, _ = mlp_weights(buffer, REST_COLS, second_zero, grad_one, pair_grad, hidden_zero)
    near, token = fetch(first_weights, MLP_COLS, ATTN_COLS, buffer)
    sums, (buffer, token) = sum_four(partial, beside=(buffer, token))
    hidden_far, sums[0] = lax.optimization_barrier((hidden_far, sums[0]))
    down_partial = mlp_down(core_ref, hidden_far, last_weights)
    middle_grad, attn_in, qkv_grad = attention_backward(
        core_ref, grad_one, middle_zero, sums, qkv_zero, prob_zero, near, token, False
    )
    buffer, done = attention_weights(
        buffer, REST_COLS, LAYER_COLS, first_zero, attn_in, qkv_grad, mix_zero
    )
    rest_pair = scatter_pair(buffer)
    sums, _ = sum_four(attention_in(core_ref, qkv_grad, near, done))
    rows = x_zero.astype(F32)
    grad_zero = middle_grad + norm_back(whole_rows(sums), rows, inverse_norm(rows))
    down_sums, _ = sum_four(down_partial)
    result_one = (middle_one + whole_rows(down_sums)).astype(BF16)
    outputs = [own_positions(tensor, x_one), own_positions(tensor, result_one)]
    grads = [own_positions(tensor, grad_zero.astype(BF16)), own_positions(tensor, grad_one)]

    layer_outputs = from_ring_order(pick(core, outputs[0], outputs[1]))
    input_grads = from_ring_order(pick(core, grads[0], grads[1]))
    last_grad = scatter_low(z_low, last_pair)
    rest_pair, layer_outputs, input_grads, last_grad = lax.optimization_barrier(
        (rest_pair, layer_outputs, input_grads, last_grad)
    )
    keep = pick(z_low, rest_pair[:48], rest_pair[48:])
    arrived = swap(pick(z_low, rest_pair[48:], rest_pair[:48]), "zl")
    mine, give, terms = combine_grads(
        core_ref, keep, arrived, last_grad, layer_zero, layer_one
    )
    got = swap(give, "section")
    arrived = swap(terms, "tensor")
    gate_grad, up_grad, down_grad, query_grad, key_grad, value_grad, out_weight_grad = unpack_grads(
        core_ref, attn_scale, mlp_scale, mine, got
    )
    arrived, key_grad = lax.optimization_barrier((arrived, key_grad))
    terms = terms + arrived
    terms = pick(core, terms[:2], terms[2:]) + swap(pick(core, terms[2:], terms[:2]), "section")
    return (
        layer_outputs[None, :, None],
        input_grads[None, :, None],
        (terms[0] / attn_scale[:, 0])[None],
        (terms[1] / mlp_scale[:, 0])[None],
        query_grad[None],
        key_grad[None],
        value_grad[None],
        out_weight_grad.T[None],
        gate_grad[None],
        up_grad[None],
        down_grad.T[None],
    )


def solution(mesh):
    split = Mesh(mesh.devices.reshape(2, 4, 2, 4, 2), ("section", "y", "zl", "x", "tensor"))
    dp = ("y", "zl", "x")
    rows = P("section", dp, "tensor")
    columns = P("section", "tensor", dp)
    return jax.shard_map(
        per_device,
        mesh=split,
        in_specs=(
            P(None, dp, "tensor", None),
            P(None, dp, "tensor", None),
            P(),
            P("section", dp),
            P("section", dp),
            rows,
            rows,
            rows,
            columns,
            rows,
            rows,
            columns,
        ),
        out_specs=(
            P("section", None, dp, "tensor", None),
            P("section", None, dp, "tensor", None),
            P("section", dp),
            P("section", dp),
            rows,
            rows,
            rows,
            columns,
            rows,
            rows,
            columns,
        ),
        check_vma=False,
    )
```

```python
import functools

import jax
import jax.numpy as jnp
from jax import lax
from jax.experimental import pallas as pl
from jax.experimental.pallas import tpu as pltpu
from jax.sharding import Mesh, PartitionSpec as P

HEAD_WIDTH = 96
EPSILON = 1e-05
BLOCKED = -1e30
SCORE_SCALE = HEAD_WIDTH ** (-0.5)
BF16 = jnp.bfloat16
F32 = jnp.float32

QUERY_COLS, KV_COLS = 384, 192
QKV_COLS = QUERY_COLS + 2 * KV_COLS
OUT_COLS = 384
HIDDEN_COLS = 1024
ATTN_COLS = QKV_COLS + OUT_COLS
MLP_COLS = 3 * HIDDEN_COLS
LAYER_COLS = MLP_COLS + ATTN_COLS
REST_COLS = LAYER_COLS + ATTN_COLS
HIDDEN_TILE = 512
AHEAD = 3
WIDTH = 1536
HALF = WIDTH // 2
PARTS = 2
MIB = 1024 * 1024


def swap(value, axis):
    return lax.ppermute(value, axis, [(0, 1), (1, 0)])


def pick(index, first, second):
    return jnp.where(index == 0, first, second)


def norm_back(weighted, residual, inverse):
    scaled = residual * inverse
    return inverse * (weighted - scaled * jnp.mean(weighted * scaled, axis=-1, keepdims=True))


def vmem_whole():
    return pl.BlockSpec(memory_space=pltpu.VMEM)


def smem_whole():
    return pl.BlockSpec(memory_space=pltpu.SMEM)


def shape(rows, columns, dtype):
    return jax.ShapeDtypeStruct((rows, columns), dtype)


def half_of(core_ref, which):
    position = core_ref[0] if which == 0 else 1 - core_ref[0]
    return pl.ds(pl.multiple_of(position * HALF, HALF), HALF)


def nt_dot(left_side, right_side):
    return lax.dot_general(
        left_side, right_side, (((1,), (1,)), ((), ())), preferred_element_type=F32
    )


def tn_dot(left_side, right_side):
    return lax.dot_general(
        left_side, right_side, (((0,), (0,)), ((), ())), preferred_element_type=F32
    )


def nn_dot(left_side, right_side):
    return jnp.dot(left_side, right_side, preferred_element_type=F32)


def row_parts(rows):
    return [slice(rows // PARTS * part, rows // PARTS * (part + 1)) for part in range(PARTS)]


def part_shapes(rows):
    return [shape(rows // PARTS, HALF, BF16)] * (2 * PARTS)


class Outward:
    def __init__(self, sems):
        self.sems, self.copies = sems, []

    def send(self, source, target):
        self.copies.append(pltpu.make_async_copy(source, target, self.sems.at[len(self.copies)]))
        self.copies[-1].start()

    def wait(self):
        for copy in self.copies:
            copy.wait()


def far(array):
    return pltpu.HBM(array.shape, array.dtype)


def each_sum(core_ref, sum_refs):
    rows = sum_refs[0].shape[0] * PARTS
    for which in range(2):
        for part, at in enumerate(row_parts(rows)):
            yield at, half_of(core_ref, which), sum_refs[PARTS * which + part]


def write_half(core_ref, which, left_ref, w_ref, columns, outs):
    product = nt_dot(left_ref[...], w_ref[half_of(core_ref, which), columns]).astype(BF16)
    refs = outs[PARTS * which : PARTS * (which + 1)]
    for at, ref in zip(row_parts(left_ref.shape[0]), refs):
        ref[...] = product[at]


def write_partial(core_ref, left_ref, w_ref, columns, outs):
    for which in (1, 0):
        write_half(core_ref, which, left_ref, w_ref, columns, outs)


def params(mib):
    return pltpu.CompilerParams(vmem_limit_bytes=mib * MIB)


def inverse_norm(rows):
    return lax.rsqrt(jnp.mean(rows * rows, axis=-1, keepdims=True) + EPSILON)


def causal_mask():
    row = lax.broadcasted_iota(jnp.int32, (128, 128), 0)
    return row >= lax.broadcasted_iota(jnp.int32, (128, 128), 1)


def two_heads(ref, rows, start):
    return jnp.concatenate(
        [
            ref[rows, start : start + HEAD_WIDTH],
            ref[rows, start + HEAD_WIDTH : start + 2 * HEAD_WIDTH],
        ],
        axis=0,
    )


def ahead_copy(w_any, w_ref, sem, column):
    return pltpu.make_async_copy(w_any.at[:, pl.ds(column, w_ref.shape[1])], w_ref, sem)


def attention_forward_body(sequences, core_ref, outward, first_ref, w_ref, qkv_any, prob_any, mix_ref, *rest):
    parts, (qkv_ref, prob_ref) = rest[:-2], rest[-2:]
    qkv_ref[...] = nn_dot(first_ref[...], w_ref[:, :QKV_COLS]).astype(BF16)
    outward.send(qkv_ref, qkv_any)
    mask = causal_mask()
    mask = jnp.concatenate([mask, mask], axis=0)
    for sequence in range(sequences):
        rows = slice(128 * sequence, 128 * (sequence + 1))
        for group in range(2):
            queries = two_heads(qkv_ref, rows, 2 * HEAD_WIDTH * group)
            key_at = QUERY_COLS + HEAD_WIDTH * group
            value_at = key_at + KV_COLS
            scores = nt_dot(queries, qkv_ref[rows, key_at : key_at + HEAD_WIDTH]) * SCORE_SCALE
            scores = jnp.where(mask, scores, BLOCKED)
            expanded = jnp.exp(scores - jnp.max(scores, axis=-1, keepdims=True))
            probability = expanded / jnp.sum(expanded, axis=-1, keepdims=True)
            prob_ref[2 * sequence + group] = probability
            mixed = nn_dot(
                probability.astype(BF16), qkv_ref[rows, value_at : value_at + HEAD_WIDTH]
            ).astype(BF16)
            at = 2 * HEAD_WIDTH * group
            mix_ref[rows, at : at + HEAD_WIDTH] = mixed[:128]
            mix_ref[rows, at + HEAD_WIDTH : at + 2 * HEAD_WIDTH] = mixed[128:]
        both = pl.ds(2 * sequence, 2)
        outward.send(prob_ref.at[both], prob_any.at[both])
    write_partial(core_ref, mix_ref, w_ref, slice(QKV_COLS, ATTN_COLS), parts)
    outward.wait()


def attention_first_kernel(sequences, column, core_ref, x_ref, w_any, first_any, *rest):
    outs, (first_ref, w_ref, sem, sems) = rest[:-4], rest[-4:]
    copy = ahead_copy(w_any, w_ref, sem, column)
    copy.start()
    rows = x_ref[...].astype(F32)
    first_ref[...] = (rows * inverse_norm(rows)).astype(BF16)
    copy.wait()
    outward = Outward(sems)
    outward.send(first_ref, first_any)
    attention_forward_body(sequences, core_ref, outward, first_ref, w_ref, *outs)


def attention_next_kernel(sequences, core_ref, middle_ref, *rest):
    sums, (w_ref, _, x_any, first_any) = rest[: 2 * PARTS], rest[2 * PARTS : 2 * PARTS + 4]
    outs, (x_ref, first_ref, sems) = rest[2 * PARTS + 4 : -3], rest[-3:]
    outward = Outward(sems)
    for at, columns, part in each_sum(core_ref, sums):
        x_ref[at, columns] = (middle_ref[at, columns] + part[...].astype(F32)).astype(BF16)
    outward.send(x_ref, x_any)
    rows = x_ref[...].astype(F32)
    first_ref[...] = (rows * inverse_norm(rows)).astype(BF16)
    outward.send(first_ref, first_any)
    attention_forward_body(sequences, core_ref, outward, first_ref, w_ref, *outs)


def in_hbm(value):
    return pltpu.with_memory_space_constraint(value, pltpu.HBM)


def hbm_whole():
    return pl.BlockSpec(memory_space=pltpu.HBM)


def attention_scratch():
    return [pltpu.VMEM((WIDTH, ATTN_COLS), BF16), pltpu.SemaphoreType.DMA(())]


def attention_outs(rows):
    outs = [
        shape(rows, WIDTH, BF16),
        far(shape(rows, QKV_COLS, BF16)),
        pltpu.HBM((rows // 64, 256, 128), F32),
        shape(rows, OUT_COLS, BF16),
    ]
    return outs + part_shapes(rows), [vmem_whole(), hbm_whole(), hbm_whole()] + [vmem_whole()] * (1 + 2 * PARTS)


def attention_cost(rows):
    return pl.CostEstimate(
        flops=2 * rows * WIDTH * ATTN_COLS, bytes_accessed=8_000_000, transcendentals=0
    )


def fetch_kernel(column, w_any, *rest):
    out_ref, token_ref, sem = rest[-3:]
    copy = ahead_copy(w_any, out_ref, sem, column)
    copy.start()
    token_ref[...] = jnp.zeros_like(token_ref)
    copy.wait()


TOKEN = jax.ShapeDtypeStruct((8, 128), F32)


def fetch(weights, column, columns, *after):
    return pl.pallas_call(
        functools.partial(fetch_kernel, column),
        in_specs=[hbm_whole()] * (1 + len(after)),
        out_specs=[vmem_whole()] * 2,
        out_shape=[shape(WIDTH, columns, BF16), TOKEN],
        scratch_shapes=[pltpu.SemaphoreType.DMA(())],
        compiler_params=params(12),
        cost_estimate=pl.CostEstimate(
            flops=0, bytes_accessed=2 * WIDTH * columns * 2, transcendentals=0
        ),
        name="fetch",
    )(in_hbm(weights), *[in_hbm(value) for value in after])


def attention_first(core, x, weights, column):
    rows = x.shape[0]
    outs, specs = attention_outs(rows)
    return pl.pallas_call(
        functools.partial(attention_first_kernel, rows // 128, column),
        in_specs=[smem_whole(), vmem_whole(), hbm_whole()],
        out_specs=[hbm_whole()] + specs[1:],
        out_shape=[far(outs[0])] + outs[1:],
        scratch_shapes=[
            pltpu.VMEM((rows, QKV_COLS), BF16),
            pltpu.VMEM((rows // 64, 256, 128), F32),
            pltpu.VMEM((rows, WIDTH), BF16),
        ]
        + attention_scratch()
        + [pltpu.SemaphoreType.DMA((2 + rows // 128,))],
        compiler_params=params(20),
        cost_estimate=attention_cost(rows),
        name="attention_first",
    )(core, x, in_hbm(weights))


def attention_next(core, middle, sums, weights, token):
    rows = middle.shape[0]
    outs, specs = attention_outs(rows)
    whole = shape(rows, WIDTH, BF16)
    return pl.pallas_call(
        functools.partial(attention_next_kernel, rows // 128),
        in_specs=[smem_whole()] + [vmem_whole()] * (2 + 2 * PARTS) + [hbm_whole()],
        out_specs=[hbm_whole()] * 2 + specs[1:],
        out_shape=[far(whole)] * 2 + outs[1:],
        scratch_shapes=[
            pltpu.VMEM((rows, QKV_COLS), BF16),
            pltpu.VMEM((rows // 64, 256, 128), F32),
            pltpu.VMEM(whole.shape, BF16),
            pltpu.VMEM(whole.shape, BF16),
            pltpu.SemaphoreType.DMA((3 + rows // 128,)),
        ],
        compiler_params=params(16),
        cost_estimate=attention_cost(rows),
        name="attention_next",
    )(core, middle, *sums, weights, token)


def column_tiles(first):
    return [pl.ds(first + HIDDEN_TILE * step, HIDDEN_TILE) for step in range(HIDDEN_STEPS)]


def sigmoid(values):
    return 0.5 * jnp.tanh(0.5 * values) + 0.5


def arrivals(copies):
    for copy in copies[:AHEAD]:
        copy.start()
    place = iter(range(len(copies)))

    def arrive():
        number = next(place)
        copies[number].wait()
        if number + AHEAD < len(copies):
            copies[number + AHEAD].start()

    return arrive


def mlp_forward_kernel(core_ref, x_ref, *rest):
    sums, rest = rest[: 2 * PARTS], rest[2 * PARTS :]
    (w_ref, _, middle_any, second_any, gate_any, up_any, hidden_any), rest = rest[:7], rest[7:]
    outs, (middle_ref, second_ref, gate_ref, up_ref, hidden_ref, out_sems) = rest[:-6], rest[-6:]
    tiles = [(gate, up) for gate, up in zip(column_tiles(0), column_tiles(HIDDEN_COLS))]
    down = pl.ds(2 * HIDDEN_COLS, HIDDEN_COLS)
    for at, columns, part in each_sum(core_ref, sums):
        middle_ref[at, columns] = x_ref[at, columns].astype(F32) + part[...].astype(F32)
    rows = middle_ref[...]
    second_ref[...] = (rows * inverse_norm(rows)).astype(BF16)
    outward = Outward(out_sems)
    outward.send(middle_ref, middle_any)
    outward.send(second_ref, second_any)
    for step, (gate, up) in enumerate(tiles):
        at = slice(HIDDEN_TILE * step, HIDDEN_TILE * (step + 1))
        gate_out = nn_dot(second_ref[...], w_ref[:, gate])
        up_out = nn_dot(second_ref[...], w_ref[:, up])
        gate_ref[:, at] = gate_out
        up_ref[:, at] = up_out
        hidden_ref[:, at] = (gate_out * sigmoid(gate_out) * up_out).astype(BF16)
        for ref, target in ((gate_ref, gate_any), (up_ref, up_any), (hidden_ref, hidden_any)):
            outward.send(ref.at[:, at], target.at[:, at])
    write_partial(core_ref, hidden_ref, w_ref, down, outs)
    outward.wait()


HIDDEN_STEPS = HIDDEN_COLS // HIDDEN_TILE


def mlp_cost(rows):
    return pl.CostEstimate(
        flops=2 * rows * WIDTH * MLP_COLS, bytes_accessed=15_000_000, transcendentals=0
    )


def mlp_forward(core, x, sums, weights, token):
    rows = x.shape[0]
    saved = [
        shape(rows, WIDTH, F32),
        shape(rows, WIDTH, BF16),
        shape(rows, HIDDEN_COLS, F32),
        shape(rows, HIDDEN_COLS, F32),
        shape(rows, HIDDEN_COLS, BF16),
    ]
    return pl.pallas_call(
        mlp_forward_kernel,
        in_specs=[smem_whole()] + [vmem_whole()] * (2 + 2 * PARTS) + [hbm_whole()],
        out_specs=[hbm_whole()] * 5 + [vmem_whole()] * (2 * PARTS),
        out_shape=[far(array) for array in saved] + part_shapes(rows),
        scratch_shapes=[pltpu.VMEM(out.shape, out.dtype) for out in saved]
        + [pltpu.SemaphoreType.DMA((2 + 3 * HIDDEN_STEPS,))],
        compiler_params=params(24),
        cost_estimate=mlp_cost(rows),
        name="mlp_forward",
    )(core, x, *sums, weights, token)


def mlp_grads(hidden_grad, gate_out, up_out):
    sigmoid_gate = sigmoid(gate_out)
    gate_grad = hidden_grad * up_out * (sigmoid_gate * (1.0 + gate_out * (1.0 - sigmoid_gate)))
    return gate_grad.astype(BF16), (hidden_grad * (gate_out * sigmoid_gate)).astype(BF16)


def mlp_backward_kernel(core_ref, x_ref, middle_grad_ref, *rest):
    sums, rest = rest[: 2 * PARTS], rest[2 * PARTS :]
    (gate_ref, up_ref, w_ref, _, g_ref, pair_grad_ref), rest = rest[:6], rest[6:]
    outs, weighted = rest[:-1], rest[-1]
    for at, columns, part in each_sum(core_ref, sums):
        weighted[at, columns] = part[...].astype(F32)
    rows = x_ref[...].astype(F32)
    g_ref[...] = (
        middle_grad_ref[...] + norm_back(weighted[...], rows, inverse_norm(rows))
    ).astype(BF16)
    for step, down in enumerate(column_tiles(2 * HIDDEN_COLS)):
        at = slice(HIDDEN_TILE * step, HIDDEN_TILE * (step + 1))
        up_at = slice(HIDDEN_COLS + at.start, HIDDEN_COLS + at.stop)
        hidden_grad = nn_dot(g_ref[...], w_ref[:, down])
        pair_grad_ref[:, at], pair_grad_ref[:, up_at] = mlp_grads(
            hidden_grad, gate_ref[:, at], up_ref[:, at]
        )
    write_partial(core_ref, pair_grad_ref, w_ref, slice(0, 2 * HIDDEN_COLS), outs)


def mlp_backward(core, above, gate_out, up_out, weights, token):
    rows = gate_out.shape[0]
    return pl.pallas_call(
        mlp_backward_kernel,
        in_specs=[smem_whole()] + [vmem_whole()] * (5 + 2 * PARTS) + [hbm_whole()],
        out_specs=[vmem_whole()] * (2 + 2 * PARTS),
        out_shape=[shape(rows, WIDTH, BF16), shape(rows, 2 * HIDDEN_COLS, BF16)]
        + part_shapes(rows),
        scratch_shapes=[pltpu.VMEM((rows, WIDTH), F32)],
        compiler_params=params(26),
        cost_estimate=mlp_cost(rows),
        name="mlp_backward",
    )(core, *above, gate_out, up_out, weights, token)


def mlp_ahead_kernel(g_ref, w_any, hidden_grad_ref, pair_ref, token_ref, down_ref, sems):
    down = ahead_copy(w_any, down_ref, sems.at[0], 2 * HIDDEN_COLS)
    pair = ahead_copy(w_any, pair_ref, sems.at[1], 0)
    down.start()
    pair.start()
    token_ref[...] = jnp.zeros_like(token_ref)
    down.wait()
    hidden_grad_ref[...] = nn_dot(g_ref[...], down_ref[...])
    pair.wait()


def mlp_ahead(g, weights):
    rows = g.shape[0]
    return pl.pallas_call(
        mlp_ahead_kernel,
        in_specs=[vmem_whole(), hbm_whole()],
        out_specs=[vmem_whole()] * 3,
        out_shape=[
            shape(rows, HIDDEN_COLS, F32),
            shape(WIDTH, 2 * HIDDEN_COLS, BF16),
            TOKEN,
        ],
        scratch_shapes=[pltpu.VMEM((WIDTH, HIDDEN_COLS), BF16), pltpu.SemaphoreType.DMA((2,))],
        compiler_params=params(15),
        cost_estimate=pl.CostEstimate(
            flops=2 * rows * WIDTH * HIDDEN_COLS, bytes_accessed=14_000_000, transcendentals=0
        ),
        name="mlp_ahead",
    )(g, in_hbm(weights))


def mlp_last_kernel(core_ref, x_ref, *rest):
    sums, rest = rest[: 2 * PARTS], rest[2 * PARTS :]
    (hidden_grad_ref, w_ref, _, middle_any, hidden_any, second_ref, hidden_ref, pair_grad_ref), rest = rest[:8], rest[8:]
    middle_ref, out_sems = rest
    for at, columns, part in each_sum(core_ref, sums):
        middle_ref[at, columns] = x_ref[at, columns].astype(F32) + part[...].astype(F32)
    rows = middle_ref[...]
    second_ref[...] = (rows * inverse_norm(rows)).astype(BF16)
    outward = Outward(out_sems)
    outward.send(middle_ref, middle_any)
    for step, (gate, up) in enumerate(zip(column_tiles(0), column_tiles(HIDDEN_COLS))):
        at = slice(HIDDEN_TILE * step, HIDDEN_TILE * (step + 1))
        up_at = slice(HIDDEN_COLS + at.start, HIDDEN_COLS + at.stop)
        gate_out = nn_dot(second_ref[...], w_ref[:, gate])
        up_out = nn_dot(second_ref[...], w_ref[:, up])
        hidden_ref[:, at] = (gate_out * sigmoid(gate_out) * up_out).astype(BF16)
        pair_grad_ref[:, at], pair_grad_ref[:, up_at] = mlp_grads(
            hidden_grad_ref[:, at], gate_out, up_out
        )
    outward.send(hidden_ref, hidden_any)
    outward.wait()


def mlp_last(core, x, sums, hidden_grad, pair_weights, token):
    rows = x.shape[0]
    return pl.pallas_call(
        mlp_last_kernel,
        in_specs=[smem_whole()] + [vmem_whole()] * (3 + 2 * PARTS) + [hbm_whole()],
        out_specs=[hbm_whole()] * 2 + [vmem_whole()] * 3,
        out_shape=[
            pltpu.HBM((rows, WIDTH), F32),
            pltpu.HBM((rows, HIDDEN_COLS), BF16),
            shape(rows, WIDTH, BF16),
            shape(rows, HIDDEN_COLS, BF16),
            shape(rows, 2 * HIDDEN_COLS, BF16),
        ],
        scratch_shapes=[pltpu.VMEM((rows, WIDTH), F32), pltpu.SemaphoreType.DMA((2,))],
        compiler_params=params(28),
        cost_estimate=mlp_cost(rows),
        name="mlp_last",
    )(core, x, *sums, hidden_grad, pair_weights, token)


def mlp_in_kernel(core_ref, pair_grad_any, w_any, _, *rest):
    outs, (pair_grad_ref, w_ref, sems) = rest[:-3], rest[-3:]
    fetched = pltpu.make_async_copy(pair_grad_any, pair_grad_ref, sems.at[4])
    fetched.start()
    quarter = HALF // 2
    pieces = []
    for number, (which, part) in enumerate(((1, 0), (1, 1), (0, 0), (0, 1))):
        position = core_ref[0] if which == 0 else 1 - core_ref[0]
        features = pl.ds(pl.multiple_of(position * HALF + part * quarter, quarter), quarter)
        source = w_any.at[features, pl.ds(0, 2 * HIDDEN_COLS)]
        copy = pltpu.make_async_copy(source, w_ref.at[number], sems.at[number])
        copy.start()
        pieces.append((copy, which, slice(part * quarter, (part + 1) * quarter)))
    fetched.wait()
    for number, (copy, which, columns) in enumerate(pieces):
        copy.wait()
        product = nt_dot(pair_grad_ref[...], w_ref[number]).astype(BF16)
        refs = outs[PARTS * which : PARTS * (which + 1)]
        for at, ref in zip(row_parts(product.shape[0]), refs):
            ref[:, columns] = product[at]


def mlp_in(core, pair_grad, weights, token):
    rows = pair_grad.shape[0]
    return pl.pallas_call(
        mlp_in_kernel,
        in_specs=[smem_whole()] + [hbm_whole()] * 3,
        out_specs=[vmem_whole()] * (2 * PARTS),
        out_shape=part_shapes(rows),
        scratch_shapes=[
            pltpu.VMEM(pair_grad.shape, BF16),
            pltpu.VMEM((4, HALF // 2, 2 * HIDDEN_COLS), BF16),
            pltpu.SemaphoreType.DMA((5,)),
        ],
        compiler_params=params(18),
        cost_estimate=pl.CostEstimate(
            flops=4 * rows * WIDTH * HIDDEN_COLS, bytes_accessed=9_000_000, transcendentals=0
        ),
        name="mlp_in",
    )(core, in_hbm(pair_grad), in_hbm(weights), token)


def mlp_down_kernel(core_ref, hidden_ref, w_any, *rest):
    outs, w_ref, sem = rest[:-2], rest[-2], rest[-1]
    copy = pltpu.make_async_copy(w_any.at[:, pl.ds(2 * HIDDEN_COLS, HIDDEN_COLS)], w_ref, sem)
    copy.start()
    copy.wait()
    write_partial(core_ref, hidden_ref, w_ref, slice(0, HIDDEN_COLS), outs)


def mlp_down(core, hidden, weights):
    rows = hidden.shape[0]
    return pl.pallas_call(
        mlp_down_kernel,
        in_specs=[smem_whole(), vmem_whole(), hbm_whole()],
        out_specs=[vmem_whole()] * (2 * PARTS),
        out_shape=part_shapes(rows),
        scratch_shapes=[pltpu.VMEM((WIDTH, HIDDEN_COLS), BF16), pltpu.SemaphoreType.DMA(())],
        compiler_params=params(14),
        cost_estimate=pl.CostEstimate(
            flops=2 * rows * WIDTH * HIDDEN_COLS, bytes_accessed=5_000_000, transcendentals=0
        ),
        name="mlp_down",
    )(core, hidden, in_hbm(weights))


def attention_backward_kernel(sequences, near, core_ref, g_ref, middle_ref, *rest):
    sums, rest = rest[: 2 * PARTS], rest[2 * PARTS :]
    (w_ref, qkv_any, prob_any, _, middle_grad_out, attn_in_ref, qkv_grad_ref), rest = rest[:7], rest[7:]
    outs, (middle_grad_ref, qkv_ref, prob_ref, mix_grad, sems) = rest[:-5], rest[-5:]
    copies = [
        pltpu.make_async_copy(qkv_any, qkv_ref, sems.at[0]),
        pltpu.make_async_copy(prob_any, prob_ref, sems.at[1]),
    ]
    for copy in copies:
        copy.start()
    for at, columns, part in each_sum(core_ref, sums):
        middle_grad_ref[at, columns] = part[...].astype(F32)
    middle = middle_ref[...]
    middle_grad = g_ref[...].astype(F32) + norm_back(
        middle_grad_ref[...], middle, inverse_norm(middle)
    )
    if near:
        middle_grad_out[...] = middle_grad
    else:
        middle_grad_ref[...] = middle_grad
        outward = pltpu.make_async_copy(middle_grad_ref, middle_grad_out, sems.at[2])
        outward.start()
    attn_in_ref[...] = middle_grad.astype(BF16)
    mix_grad[...] = nn_dot(attn_in_ref[...], w_ref[:, QKV_COLS:]).astype(BF16)
    for copy in copies:
        copy.wait()
    for sequence in range(sequences):
        rows = slice(128 * sequence, 128 * (sequence + 1))
        for group in range(2):
            at = 2 * HEAD_WIDTH * group
            key_at = QUERY_COLS + HEAD_WIDTH * group
            value_at = key_at + KV_COLS
            grads = two_heads(mix_grad, rows, at)
            queries = two_heads(qkv_ref, rows, at)
            keys = qkv_ref[rows, key_at : key_at + HEAD_WIDTH]
            probability = prob_ref[2 * sequence + group]
            prob_grad = nt_dot(grads, qkv_ref[rows, value_at : value_at + HEAD_WIDTH])
            centred = jnp.sum(probability * prob_grad, axis=-1, keepdims=True)
            score_grad = (probability * (prob_grad - centred)).astype(BF16)
            query_grad = (nn_dot(score_grad, keys) * SCORE_SCALE).astype(BF16)
            qkv_grad_ref[rows, at : at + HEAD_WIDTH] = query_grad[:128]
            qkv_grad_ref[rows, at + HEAD_WIDTH : at + 2 * HEAD_WIDTH] = query_grad[128:]
            qkv_grad_ref[rows, key_at : key_at + HEAD_WIDTH] = (
                tn_dot(score_grad, queries) * SCORE_SCALE
            ).astype(BF16)
            qkv_grad_ref[rows, value_at : value_at + HEAD_WIDTH] = tn_dot(
                probability.astype(BF16), grads
            ).astype(BF16)
    if near:
        write_partial(core_ref, qkv_grad_ref, w_ref, slice(0, QKV_COLS), outs)
    else:
        outward.wait()


def attention_in_kernel(core_ref, qkv_grad_ref, w_ref, _, *outs):
    write_partial(core_ref, qkv_grad_ref, w_ref, slice(0, QKV_COLS), outs)


def attention_in(core, qkv_grad, weights, token):
    rows = qkv_grad.shape[0]
    return pl.pallas_call(
        attention_in_kernel,
        in_specs=[smem_whole()] + [vmem_whole()] * 2 + [hbm_whole()],
        out_specs=[vmem_whole()] * (2 * PARTS),
        out_shape=part_shapes(rows),
        compiler_params=params(14),
        cost_estimate=pl.CostEstimate(
            flops=2 * rows * WIDTH * QKV_COLS, bytes_accessed=5_000_000, transcendentals=0
        ),
        name="attention_in",
    )(core, qkv_grad, weights, token)


def attention_backward(core, g, middle, sums, qkv, probability, weights, token, near):
    rows = g.shape[0]
    residual, parts = shape(rows, WIDTH, F32), part_shapes(rows) if near else []
    return pl.pallas_call(
        functools.partial(attention_backward_kernel, rows // 128, near),
        in_specs=[smem_whole()] + [vmem_whole()] * (3 + 2 * PARTS) + [hbm_whole()] * 3,
        out_specs=[vmem_whole() if near else hbm_whole()] + [vmem_whole()] * (2 + len(parts)),
        out_shape=[
            residual if near else far(residual),
            shape(rows, WIDTH, BF16),
            shape(rows, QKV_COLS, BF16),
        ]
        + parts,
        scratch_shapes=[
            pltpu.VMEM((rows, WIDTH), F32),
            pltpu.VMEM(qkv.shape, BF16),
            pltpu.VMEM(probability.shape, F32),
            pltpu.VMEM((rows, OUT_COLS), BF16),
            pltpu.SemaphoreType.DMA((3,)),
        ],
        compiler_params=params(24),
        cost_estimate=attention_cost(rows),
        name="attention_backward",
    )(core, g, middle, *sums, weights, in_hbm(qkv), in_hbm(probability), token)


def write_products(start, pairs, out_any, slots, sems):
    _, height, width = slots.shape
    copies = []
    for number in range(WIDTH // height):
        features = pl.ds(height * number, height)
        if number >= 2:
            copies[number - 2].wait()
        slot = slots.at[number % 2]
        at = 0
        for left, right in pairs:
            columns = right.shape[1]
            slot[:, at : at + columns] = tn_dot(left[:, features], right[...]).astype(BF16)
            at += columns
        target = out_any.at[features, pl.ds(start, width)]
        copies.append(pltpu.make_async_copy(slot, target, sems.at[number % 2]))
        copies[-1].start()
    for copy in copies[-2:]:
        copy.wait()


def mlp_weights_kernel(second_ref, g_ref, pair_grad_ref, hidden_ref, *rest):
    out_any, token_ref, slots, sems = rest[-4:]
    token_ref[...] = jnp.zeros_like(token_ref)
    write_products(0, [(second_ref, pair_grad_ref), (g_ref, hidden_ref)], out_any, slots, sems)


def into_buffer(kernel, buffer, columns, slot, operands, flops, name, mib):
    aliases, specs = {}, [vmem_whole()] * len(operands)
    if buffer is not None:
        aliases = {len(operands): 0}
        specs, operands = specs + [hbm_whole()], operands + (in_hbm(buffer),)
    return pl.pallas_call(
        kernel,
        in_specs=specs,
        out_specs=[hbm_whole(), vmem_whole()],
        out_shape=[pltpu.HBM((WIDTH, columns), BF16), TOKEN],
        input_output_aliases=aliases,
        scratch_shapes=[pltpu.VMEM((2, *slot), BF16), pltpu.SemaphoreType.DMA((2,))],
        compiler_params=params(mib),
        cost_estimate=pl.CostEstimate(flops=flops, bytes_accessed=flops // 250, transcendentals=0),
        name=name,
    )(*operands)


def mlp_weights(buffer, columns, second, g, pair_grad, hidden):
    return into_buffer(
        mlp_weights_kernel,
        buffer,
        columns,
        (512, MLP_COLS),
        (second, g, pair_grad, hidden),
        2 * second.shape[0] * WIDTH * MLP_COLS,
        "mlp_weights",
        18,
    )


def attention_weights_kernel(start, first_ref, attn_in_ref, qkv_grad_ref, mix_ref, *rest):
    out_any, token_ref, slots, sems = rest[-4:]
    token_ref[...] = jnp.zeros_like(token_ref)
    pairs = [(first_ref, qkv_grad_ref), (attn_in_ref, mix_ref)]
    write_products(start, pairs, out_any, slots, sems)


def attention_weights(buffer, columns, start, first, attn_in, qkv_grad, mixture):
    return into_buffer(
        functools.partial(attention_weights_kernel, start),
        buffer,
        columns,
        (768, ATTN_COLS),
        (first, attn_in, qkv_grad, mixture),
        2 * first.shape[0] * WIDTH * ATTN_COLS,
        "attention_weights",
        14,
    )


def sum_four(partial, beside=None, within=None):
    keeps, gives = list(partial[:PARTS]), list(partial[PARTS:])
    chips = [
        (keep.astype(F32) + swap(give, "section").astype(F32)).astype(BF16)
        for keep, give in zip(keeps, gives)
    ]
    arrived = [swap(chip, "tensor") for chip in chips]
    if beside is not None:
        arrived[-1], beside = lax.optimization_barrier((arrived[-1], beside))
    totals = [
        (chip.astype(F32) + other.astype(F32)).astype(BF16)
        for chip, other in zip(chips, arrived)
    ]
    if within is not None:

        def tie(value):
            totals[0], value = lax.optimization_barrier((totals[0], value))
            return value

        beside = within(tie)
    return totals + [swap(total, "section") for total in totals], beside


def row_scales(gain_row):
    row = lax.broadcasted_iota(jnp.int32, (48, 48), 0)
    column = lax.broadcasted_iota(jnp.int32, (48, 48), 1)
    return jnp.where(row == column, gain_row, 0.0).astype(BF16)


def pack_kernel(core_ref, *rest):
    sources, (mine_ref, give_ref), shards, sems = rest[:8], rest[8:10], rest[10:18], rest[18]
    copies = [
        pltpu.make_async_copy(source, shard, sems.at[number])
        for number, (source, shard) in enumerate(zip(sources, shards))
    ]
    for copy in copies:
        copy.start()
    is_first = core_ref[0] == 0
    gains_ref, shards = shards[0], shards[1:]
    copies[0].wait()
    attn_scale, mlp_scale = row_scales(gains_ref[0:1, :]), row_scales(gains_ref[1:2, :])
    start = 0
    for copy, shard, scale in zip(
        copies[1:],
        shards,
        (mlp_scale, mlp_scale, None, attn_scale, attn_scale, attn_scale, None),
    ):
        copy.wait()
        weight = shard[...]
        if scale is not None:
            weight = nn_dot(scale, weight).astype(BF16)
        width = weight.shape[1] // 2
        low, high = weight[:, :width], weight[:, width:]
        mine_ref[:, start : start + width] = jnp.where(is_first, low, high)
        give_ref[:, start : start + width] = jnp.where(is_first, high, low)
        start += width


def pack_shards(core, *shards):
    return pl.pallas_call(
        pack_kernel,
        in_specs=[smem_whole()] + [hbm_whole()] * len(shards),
        out_specs=[vmem_whole()] * 2,
        out_shape=[shape(48, LAYER_COLS, BF16)] * 2,
        scratch_shapes=[pltpu.VMEM(shard.shape, shard.dtype) for shard in shards]
        + [pltpu.SemaphoreType.DMA((len(shards),))],
        compiler_params=params(16),
        name="pack_shards",
    )(core, *[in_hbm(shard) for shard in shards])


def combine_kernel(core_ref, keep_ref, arrived_ref, last_ref, zero_w_ref, one_w_ref, mine_ref, give_ref, terms_ref, zero, one):
    rest = (keep_ref[...].astype(F32) + arrived_ref[...].astype(F32)).astype(BF16)
    zero[:, :MLP_COLS] = rest[:, :MLP_COLS]
    zero[:, MLP_COLS:] = rest[:, LAYER_COLS:]
    one[:, :MLP_COLS] = last_ref[...]
    one[:, MLP_COLS:] = rest[:, MLP_COLS:LAYER_COLS]
    is_first = core_ref[0] == 0
    mine_ref[...] = jnp.where(is_first, zero[...], one[...])
    give_ref[...] = jnp.where(is_first, one[...], zero[...])
    row = 0
    for grad, weights in ((zero, zero_w_ref), (one, one_w_ref)):
        products = weights[...].astype(F32) * grad[...].astype(F32)
        for columns in (slice(MLP_COLS, MLP_COLS + QKV_COLS), slice(0, 2 * HIDDEN_COLS)):
            terms_ref[row, :] = jnp.sum(products[:, columns], axis=1)
            row += 1


def combine_grads(core, *operands):
    return pl.pallas_call(
        combine_kernel,
        in_specs=[smem_whole()] + [vmem_whole()] * len(operands),
        out_specs=[vmem_whole()] * 3,
        out_shape=[shape(48, LAYER_COLS, BF16)] * 2 + [shape(4, 48, F32)],
        scratch_shapes=[pltpu.VMEM((48, LAYER_COLS), BF16)] * 2,
        compiler_params=params(16),
        name="combine_grads",
    )(core, *operands)


def unpack_kernel(core_ref, attn_scale_ref, mlp_scale_ref, mine_ref, got_ref, gate_ref, up_ref, down_ref, query_ref, key_ref, value_ref, out_ref):
    is_first = core_ref[0] == 0

    def place(out, start, scale_ref):
        width = out.shape[1] // 2
        mine = mine_ref[:, start : start + width].astype(F32)
        got = got_ref[:, start : start + width].astype(F32)
        if scale_ref is not None:
            mine, got = mine * scale_ref[...], got * scale_ref[...]
        out[:, :width] = jnp.where(is_first, mine, got)
        out[:, width:] = jnp.where(is_first, got, mine)

    place(gate_ref, 0, mlp_scale_ref)
    place(up_ref, HIDDEN_COLS, mlp_scale_ref)
    place(down_ref, 2 * HIDDEN_COLS, None)
    place(query_ref, MLP_COLS, attn_scale_ref)
    place(key_ref, MLP_COLS + QUERY_COLS, attn_scale_ref)
    place(value_ref, MLP_COLS + QUERY_COLS + KV_COLS, attn_scale_ref)
    place(out_ref, MLP_COLS + QKV_COLS, None)


def unpack_grads(core, *operands):
    widths = [HIDDEN_COLS] * 3 + [QUERY_COLS, KV_COLS, KV_COLS, OUT_COLS]
    return pl.pallas_call(
        unpack_kernel,
        in_specs=[smem_whole()] + [vmem_whole()] * len(operands),
        out_specs=[vmem_whole()] * len(widths),
        out_shape=[shape(48, 2 * width, F32) for width in widths],
        compiler_params=params(16),
        name="unpack_grads",
    )(core, *operands)


def gather_rows(z_low, share):
    other = swap(share, "zl")
    pair = jnp.concatenate([pick(z_low, share, other), pick(z_low, other, share)], axis=0)
    return lax.all_gather(pair, ("y", "x"), axis=0, tiled=True)


def scatter_pair(grad):
    return lax.psum_scatter(grad, ("y", "x"), scatter_dimension=0, tiled=True)


def scatter_low(z_low, pair):
    keep = pick(z_low, pair[:48], pair[48:])
    give = pick(z_low, pair[48:], pair[:48])
    return (keep.astype(F32) + swap(give, "zl").astype(F32)).astype(BF16)


def to_ring_order(rows):
    lead = rows.shape[:-1]
    return jnp.swapaxes(rows.reshape(lead + (4, 2, 4, 48)), -3, -2).reshape(rows.shape)


def from_ring_order(rows):
    lead = rows.shape[:-1]
    return jnp.swapaxes(rows.reshape(lead + (4, 4, 2, 48)), -3, -2).reshape(rows.shape)


def join_positions(tensor, own):
    other = swap(own, "tensor")
    return jnp.concatenate(
        [pick(tensor, own, other), pick(tensor, other, own)], axis=1
    ).reshape(384, WIDTH)


def own_positions(tensor, rows):
    rows = rows.reshape(3, 128, 1536)
    return pick(tensor, rows[:, :64], rows[:, 64:])


def per_device(
    inputs, cotangent, plan, attn_gain, mlp_gain, w_query, key_weight, value_weight,
    w_out, w_gate, w_up, w_down,
):
    core = lax.axis_index("section")
    z_low = lax.axis_index("zl")
    tensor = lax.axis_index("tensor")

    attn_scale = attn_gain[0].astype(F32)[:, None]
    mlp_scale = mlp_gain[0].astype(F32)[:, None]

    core_ref = core.astype(jnp.int32).reshape(1)
    mine, give = pack_shards(
        core_ref, jnp.concatenate([attn_gain, mlp_gain]).astype(F32),
        w_gate[0], w_up[0], w_down[0].T, w_query[0], key_weight[0], value_weight[0], w_out[0].T,
    )
    got = swap(give, "section")
    layer_zero, layer_one = pick(core, mine, got), pick(core, got, mine)
    first_weights = gather_rows(
        z_low, jnp.concatenate([layer_zero, layer_one[:, MLP_COLS:]], axis=1)
    )
    last_weights = gather_rows(z_low, layer_one[:, :MLP_COLS])

    stream = join_positions(tensor, to_ring_order(inputs[:, 0][plan]))
    stream, late = lax.optimization_barrier((stream, cotangent))
    out_grad = join_positions(tensor, to_ring_order(late[:, 0][plan]))
    stream, out_grad = lax.optimization_barrier((stream, out_grad))

    def whole_rows(sums):
        own, other = jnp.concatenate(sums[:PARTS]), jnp.concatenate(sums[PARTS:])
        return jnp.concatenate([pick(core, own, other), pick(core, other, own)], axis=1).astype(F32)

    x_zero = stream
    first_zero, qkv_zero, prob_zero, mix_zero, *partial = attention_first(
        core_ref, x_zero, first_weights, MLP_COLS
    )
    near, token = fetch(first_weights, 0, MLP_COLS)
    sums, token = sum_four(partial, beside=token)
    middle_zero, second_zero, gate_zero, up_zero, hidden_zero, *partial = mlp_forward(
        core_ref, x_zero, sums, near, token
    )
    near, token = fetch(first_weights, LAYER_COLS, ATTN_COLS)
    sums, token = sum_four(partial, beside=token)
    x_one, first_one, qkv_one, prob_one, mix_one, *partial = attention_next(
        core_ref, middle_zero, sums, near, token
    )
    sums, ahead = sum_four(partial, within=lambda tie: mlp_ahead(out_grad, tie(last_weights)))
    hidden_grad, near, token = ahead

    middle_one, hidden_far, second_one, hidden_one, pair_grad = mlp_last(
        core_ref, x_one, sums, hidden_grad, near, token
    )
    one_mlp, done = mlp_weights(None, MLP_COLS, second_one, out_grad, pair_grad, hidden_one)
    last_pair = scatter_pair(one_mlp)
    partial = mlp_in(core_ref, pair_grad, last_weights, done)
    near, token = fetch(first_weights, LAYER_COLS, ATTN_COLS, one_mlp)
    sums, token = sum_four(partial, beside=token)
    middle_grad, attn_in, qkv_grad, *partial = attention_backward(
        core_ref, out_grad, middle_one, sums, qkv_one, prob_one, near, token, True
    )
    buffer, _ = attention_weights(None, REST_COLS, MLP_COLS, first_one, attn_in, qkv_grad, mix_one)
    near, token = fetch(first_weights, 0, MLP_COLS, buffer)
    sums, (buffer, token) = sum_four(partial, beside=(buffer, token))

    grad_one, pair_grad, *partial = mlp_backward(
        core_ref, (x_one, middle_grad, *sums), gate_zero, up_zero, near, token
    )
    buffer, _ = mlp_weights(buffer, REST_COLS, second_zero, grad_one, pair_grad, hidden_zero)
    near, token = fetch(first_weights, MLP_COLS, ATTN_COLS, buffer)
    sums, (buffer, token) = sum_four(partial, beside=(buffer, token))
    hidden_far, sums[0] = lax.optimization_barrier((hidden_far, sums[0]))
    down_partial = mlp_down(core_ref, hidden_far, last_weights)
    middle_grad, attn_in, qkv_grad = attention_backward(
        core_ref, grad_one, middle_zero, sums, qkv_zero, prob_zero, near, token, False
    )
    buffer, done = attention_weights(
        buffer, REST_COLS, LAYER_COLS, first_zero, attn_in, qkv_grad, mix_zero
    )
    rest_pair = scatter_pair(buffer)
    sums, _ = sum_four(attention_in(core_ref, qkv_grad, near, done))
    rows = x_zero.astype(F32)
    grad_zero = middle_grad + norm_back(whole_rows(sums), rows, inverse_norm(rows))
    down_sums, _ = sum_four(down_partial)
    result_one = (middle_one + whole_rows(down_sums)).astype(BF16)
    outputs = [own_positions(tensor, x_one), own_positions(tensor, result_one)]
    grads = [own_positions(tensor, grad_zero.astype(BF16)), own_positions(tensor, grad_one)]

    layer_outputs = from_ring_order(pick(core, outputs[0], outputs[1]))
    input_grads = from_ring_order(pick(core, grads[0], grads[1]))
    last_grad = scatter_low(z_low, last_pair)
    rest_pair, layer_outputs, input_grads, last_grad = lax.optimization_barrier(
        (rest_pair, layer_outputs, input_grads, last_grad)
    )
    keep = pick(z_low, rest_pair[:48], rest_pair[48:])
    arrived = swap(pick(z_low, rest_pair[48:], rest_pair[:48]), "zl")
    mine, give, terms = combine_grads(
        core_ref, keep, arrived, last_grad, layer_zero, layer_one
    )
    got = swap(give, "section")
    arrived = swap(terms, "tensor")
    gate_grad, up_grad, down_grad, query_grad, key_grad, value_grad, out_weight_grad = unpack_grads(
        core_ref, attn_scale, mlp_scale, mine, got
    )
    arrived, key_grad = lax.optimization_barrier((arrived, key_grad))
    terms = terms + arrived
    terms = pick(core, terms[:2], terms[2:]) + swap(pick(core, terms[2:], terms[:2]), "section")
    return (
        layer_outputs[None, :, None],
        input_grads[None, :, None],
        (terms[0] / attn_scale[:, 0])[None],
        (terms[1] / mlp_scale[:, 0])[None],
        query_grad[None],
        key_grad[None],
        value_grad[None],
        out_weight_grad.T[None],
        gate_grad[None],
        up_grad[None],
        down_grad.T[None],
    )


def solution(mesh):
    split = Mesh(mesh.devices.reshape(2, 4, 2, 4, 2), ("section", "y", "zl", "x", "tensor"))
    dp = ("y", "zl", "x")
    rows = P("section", dp, "tensor")
    columns = P("section", "tensor", dp)
    return jax.shard_map(
        per_device,
        mesh=split,
        in_specs=(
            P(None, dp, "tensor", None),
            P(None, dp, "tensor", None),
            P(),
            P("section", dp),
            P("section", dp),
            rows,
            rows,
            rows,
            columns,
            rows,
            rows,
            columns,
        ),
        out_specs=(
            P("section", None, dp, "tensor", None),
            P("section", None, dp, "tensor", None),
            P("section", dp),
            P("section", dp),
            rows,
            rows,
            rows,
            columns,
            rows,
            rows,
            columns,
        ),
        check_vma=False,
    )
```

```python
import functools

import jax
import jax.numpy as jnp
from jax import lax
from jax.experimental import pallas as pl
from jax.experimental.pallas import tpu as pltpu
from jax.sharding import Mesh, PartitionSpec as P

HEAD_WIDTH = 96
EPSILON = 1e-05
BLOCKED = -1e30
SCORE_SCALE = HEAD_WIDTH ** (-0.5)
BF16 = jnp.bfloat16
F32 = jnp.float32

QUERY_COLS, KV_COLS = 384, 192
QKV_COLS = QUERY_COLS + 2 * KV_COLS
OUT_COLS = 384
HIDDEN_COLS = 1024
ATTN_COLS = QKV_COLS + OUT_COLS
MLP_COLS = 3 * HIDDEN_COLS
LAYER_COLS = MLP_COLS + ATTN_COLS
REST_COLS = LAYER_COLS + ATTN_COLS
HIDDEN_TILE = 512
AHEAD = 3
WIDTH = 1536
HALF = WIDTH // 2
PARTS = 2
MIB = 1024 * 1024


def swap(value, axis):
    return lax.ppermute(value, axis, [(0, 1), (1, 0)])


def pick(index, first, second):
    return jnp.where(index == 0, first, second)


def norm_back(weighted, residual, inverse):
    scaled = residual * inverse
    return inverse * (weighted - scaled * jnp.mean(weighted * scaled, axis=-1, keepdims=True))


def vmem_whole():
    return pl.BlockSpec(memory_space=pltpu.VMEM)


def smem_whole():
    return pl.BlockSpec(memory_space=pltpu.SMEM)


def shape(rows, columns, dtype):
    return jax.ShapeDtypeStruct((rows, columns), dtype)


def half_of(core_ref, which):
    position = core_ref[0] if which == 0 else 1 - core_ref[0]
    return pl.ds(pl.multiple_of(position * HALF, HALF), HALF)


def nt_dot(left_side, right_side):
    return lax.dot_general(
        left_side, right_side, (((1,), (1,)), ((), ())), preferred_element_type=F32
    )


def tn_dot(left_side, right_side):
    return lax.dot_general(
        left_side, right_side, (((0,), (0,)), ((), ())), preferred_element_type=F32
    )


def nn_dot(left_side, right_side):
    return jnp.dot(left_side, right_side, preferred_element_type=F32)


def row_parts(rows):
    return [slice(rows // PARTS * part, rows // PARTS * (part + 1)) for part in range(PARTS)]


def part_shapes(rows):
    return [shape(rows // PARTS, HALF, BF16)] * (2 * PARTS)


class Outward:
    def __init__(self, sems):
        self.sems, self.copies = sems, []

    def send(self, source, target):
        self.copies.append(pltpu.make_async_copy(source, target, self.sems.at[len(self.copies)]))
        self.copies[-1].start()

    def wait(self):
        for copy in self.copies:
            copy.wait()


def far(array):
    return pltpu.HBM(array.shape, array.dtype)


def each_sum(core_ref, sum_refs):
    rows = sum_refs[0].shape[0] * PARTS
    for which in range(2):
        for part, at in enumerate(row_parts(rows)):
            yield at, half_of(core_ref, which), sum_refs[PARTS * which + part]


def write_half(core_ref, which, left_ref, w_ref, columns, outs):
    product = nt_dot(left_ref[...], w_ref[half_of(core_ref, which), columns]).astype(BF16)
    refs = outs[PARTS * which : PARTS * (which + 1)]
    for at, ref in zip(row_parts(left_ref.shape[0]), refs):
        ref[...] = product[at]


def write_partial(core_ref, left_ref, w_ref, columns, outs):
    for which in (1, 0):
        write_half(core_ref, which, left_ref, w_ref, columns, outs)


def params(mib):
    return pltpu.CompilerParams(vmem_limit_bytes=mib * MIB)


def inverse_norm(rows):
    return lax.rsqrt(jnp.mean(rows * rows, axis=-1, keepdims=True) + EPSILON)


def causal_mask():
    row = lax.broadcasted_iota(jnp.int32, (128, 128), 0)
    return row >= lax.broadcasted_iota(jnp.int32, (128, 128), 1)


def two_heads(ref, rows, start):
    return jnp.concatenate(
        [
            ref[rows, start : start + HEAD_WIDTH],
            ref[rows, start + HEAD_WIDTH : start + 2 * HEAD_WIDTH],
        ],
        axis=0,
    )


def ahead_copy(w_any, w_ref, sem, column):
    return pltpu.make_async_copy(w_any.at[:, pl.ds(column, w_ref.shape[1])], w_ref, sem)


def attention_forward_body(sequences, core_ref, outward, first_ref, w_ref, qkv_any, prob_any, mix_ref, *rest):
    parts, (qkv_ref, prob_ref) = rest[:-2], rest[-2:]
    qkv_ref[...] = nn_dot(first_ref[...], w_ref[:, :QKV_COLS]).astype(BF16)
    outward.send(qkv_ref, qkv_any)
    mask = causal_mask()
    mask = jnp.concatenate([mask, mask], axis=0)
    for sequence in range(sequences):
        rows = slice(128 * sequence, 128 * (sequence + 1))
        for group in range(2):
            queries = two_heads(qkv_ref, rows, 2 * HEAD_WIDTH * group)
            key_at = QUERY_COLS + HEAD_WIDTH * group
            value_at = key_at + KV_COLS
            scores = nt_dot(queries, qkv_ref[rows, key_at : key_at + HEAD_WIDTH]) * SCORE_SCALE
            scores = jnp.where(mask, scores, BLOCKED)
            expanded = jnp.exp(scores - jnp.max(scores, axis=-1, keepdims=True))
            probability = expanded / jnp.sum(expanded, axis=-1, keepdims=True)
            prob_ref[2 * sequence + group] = probability
            mixed = nn_dot(
                probability.astype(BF16), qkv_ref[rows, value_at : value_at + HEAD_WIDTH]
            ).astype(BF16)
            at = 2 * HEAD_WIDTH * group
            mix_ref[rows, at : at + HEAD_WIDTH] = mixed[:128]
            mix_ref[rows, at + HEAD_WIDTH : at + 2 * HEAD_WIDTH] = mixed[128:]
        both = pl.ds(2 * sequence, 2)
        outward.send(prob_ref.at[both], prob_any.at[both])
    write_partial(core_ref, mix_ref, w_ref, slice(QKV_COLS, ATTN_COLS), parts)
    outward.wait()


def attention_first_kernel(sequences, column, core_ref, x_ref, w_any, first_any, *rest):
    outs, (first_ref, w_ref, sem, sems) = rest[:-4], rest[-4:]
    copy = ahead_copy(w_any, w_ref, sem, column)
    copy.start()
    rows = x_ref[...].astype(F32)
    first_ref[...] = (rows * inverse_norm(rows)).astype(BF16)
    copy.wait()
    outward = Outward(sems)
    outward.send(first_ref, first_any)
    attention_forward_body(sequences, core_ref, outward, first_ref, w_ref, *outs)


def attention_next_kernel(sequences, core_ref, middle_ref, *rest):
    sums, (w_ref, _, x_any, first_any) = rest[: 2 * PARTS], rest[2 * PARTS : 2 * PARTS + 4]
    outs, (x_ref, first_ref, sems) = rest[2 * PARTS + 4 : -3], rest[-3:]
    outward = Outward(sems)
    for at, columns, part in each_sum(core_ref, sums):
        x_ref[at, columns] = (middle_ref[at, columns] + part[...].astype(F32)).astype(BF16)
    outward.send(x_ref, x_any)
    rows = x_ref[...].astype(F32)
    first_ref[...] = (rows * inverse_norm(rows)).astype(BF16)
    outward.send(first_ref, first_any)
    attention_forward_body(sequences, core_ref, outward, first_ref, w_ref, *outs)


def in_hbm(value):
    return pltpu.with_memory_space_constraint(value, pltpu.HBM)


def hbm_whole():
    return pl.BlockSpec(memory_space=pltpu.HBM)


def attention_scratch():
    return [pltpu.VMEM((WIDTH, ATTN_COLS), BF16), pltpu.SemaphoreType.DMA(())]


def attention_outs(rows):
    outs = [
        shape(rows, WIDTH, BF16),
        far(shape(rows, QKV_COLS, BF16)),
        pltpu.HBM((rows // 64, 256, 128), F32),
        shape(rows, OUT_COLS, BF16),
    ]
    return outs + part_shapes(rows), [vmem_whole(), hbm_whole(), hbm_whole()] + [vmem_whole()] * (1 + 2 * PARTS)


def attention_cost(rows):
    return pl.CostEstimate(
        flops=2 * rows * WIDTH * ATTN_COLS, bytes_accessed=8_000_000, transcendentals=0
    )


def fetch_kernel(column, w_any, *rest):
    out_ref, token_ref, sem = rest[-3:]
    copy = ahead_copy(w_any, out_ref, sem, column)
    copy.start()
    token_ref[...] = jnp.zeros_like(token_ref)
    copy.wait()


TOKEN = jax.ShapeDtypeStruct((8, 128), F32)


def fetch(weights, column, columns, *after):
    return pl.pallas_call(
        functools.partial(fetch_kernel, column),
        in_specs=[hbm_whole()] * (1 + len(after)),
        out_specs=[vmem_whole()] * 2,
        out_shape=[shape(WIDTH, columns, BF16), TOKEN],
        scratch_shapes=[pltpu.SemaphoreType.DMA(())],
        compiler_params=params(12),
        cost_estimate=pl.CostEstimate(
            flops=0, bytes_accessed=2 * WIDTH * columns * 2, transcendentals=0
        ),
        name="fetch",
    )(in_hbm(weights), *[in_hbm(value) for value in after])


def attention_first(core, x, weights, column):
    rows = x.shape[0]
    outs, specs = attention_outs(rows)
    return pl.pallas_call(
        functools.partial(attention_first_kernel, rows // 128, column),
        in_specs=[smem_whole(), vmem_whole(), hbm_whole()],
        out_specs=[hbm_whole()] + specs[1:],
        out_shape=[far(outs[0])] + outs[1:],
        scratch_shapes=[
            pltpu.VMEM((rows, QKV_COLS), BF16),
            pltpu.VMEM((rows // 64, 256, 128), F32),
            pltpu.VMEM((rows, WIDTH), BF16),
        ]
        + attention_scratch()
        + [pltpu.SemaphoreType.DMA((2 + rows // 128,))],
        compiler_params=params(20),
        cost_estimate=attention_cost(rows),
        name="attention_first",
    )(core, x, in_hbm(weights))


def attention_next(core, middle, sums, weights, token):
    rows = middle.shape[0]
    outs, specs = attention_outs(rows)
    whole = shape(rows, WIDTH, BF16)
    return pl.pallas_call(
        functools.partial(attention_next_kernel, rows // 128),
        in_specs=[smem_whole()] + [vmem_whole()] * (2 + 2 * PARTS) + [hbm_whole()],
        out_specs=[hbm_whole()] * 2 + specs[1:],
        out_shape=[far(whole)] * 2 + outs[1:],
        scratch_shapes=[
            pltpu.VMEM((rows, QKV_COLS), BF16),
            pltpu.VMEM((rows // 64, 256, 128), F32),
            pltpu.VMEM(whole.shape, BF16),
            pltpu.VMEM(whole.shape, BF16),
            pltpu.SemaphoreType.DMA((3 + rows // 128,)),
        ],
        compiler_params=params(16),
        cost_estimate=attention_cost(rows),
        name="attention_next",
    )(core, middle, *sums, weights, token)


def column_tiles(first):
    return [pl.ds(first + HIDDEN_TILE * step, HIDDEN_TILE) for step in range(HIDDEN_STEPS)]


def sigmoid(values):
    return 0.5 * jnp.tanh(0.5 * values) + 0.5


def arrivals(copies):
    for copy in copies[:AHEAD]:
        copy.start()
    place = iter(range(len(copies)))

    def arrive():
        number = next(place)
        copies[number].wait()
        if number + AHEAD < len(copies):
            copies[number + AHEAD].start()

    return arrive


def mlp_forward_kernel(core_ref, x_ref, *rest):
    sums, rest = rest[: 2 * PARTS], rest[2 * PARTS :]
    (w_ref, _, middle_any, second_any, gate_any, up_any, hidden_any), rest = rest[:7], rest[7:]
    outs, (middle_ref, second_ref, gate_ref, up_ref, hidden_ref, out_sems) = rest[:-6], rest[-6:]
    tiles = [(gate, up) for gate, up in zip(column_tiles(0), column_tiles(HIDDEN_COLS))]
    down = pl.ds(2 * HIDDEN_COLS, HIDDEN_COLS)
    for at, columns, part in each_sum(core_ref, sums):
        middle_ref[at, columns] = x_ref[at, columns].astype(F32) + part[...].astype(F32)
    rows = middle_ref[...]
    second_ref[...] = (rows * inverse_norm(rows)).astype(BF16)
    outward = Outward(out_sems)
    outward.send(middle_ref, middle_any)
    outward.send(second_ref, second_any)
    for step, (gate, up) in enumerate(tiles):
        at = slice(HIDDEN_TILE * step, HIDDEN_TILE * (step + 1))
        gate_out = nn_dot(second_ref[...], w_ref[:, gate])
        up_out = nn_dot(second_ref[...], w_ref[:, up])
        gate_ref[:, at] = gate_out
        up_ref[:, at] = up_out
        hidden_ref[:, at] = (gate_out * sigmoid(gate_out) * up_out).astype(BF16)
        for ref, target in ((gate_ref, gate_any), (up_ref, up_any), (hidden_ref, hidden_any)):
            outward.send(ref.at[:, at], target.at[:, at])
    write_partial(core_ref, hidden_ref, w_ref, down, outs)
    outward.wait()


HIDDEN_STEPS = HIDDEN_COLS // HIDDEN_TILE


def mlp_cost(rows):
    return pl.CostEstimate(
        flops=2 * rows * WIDTH * MLP_COLS, bytes_accessed=15_000_000, transcendentals=0
    )


def mlp_forward(core, x, sums, weights, token):
    rows = x.shape[0]
    saved = [
        shape(rows, WIDTH, F32),
        shape(rows, WIDTH, BF16),
        shape(rows, HIDDEN_COLS, F32),
        shape(rows, HIDDEN_COLS, F32),
        shape(rows, HIDDEN_COLS, BF16),
    ]
    return pl.pallas_call(
        mlp_forward_kernel,
        in_specs=[smem_whole()] + [vmem_whole()] * (2 + 2 * PARTS) + [hbm_whole()],
        out_specs=[hbm_whole()] * 5 + [vmem_whole()] * (2 * PARTS),
        out_shape=[far(array) for array in saved] + part_shapes(rows),
        scratch_shapes=[pltpu.VMEM(out.shape, out.dtype) for out in saved]
        + [pltpu.SemaphoreType.DMA((2 + 3 * HIDDEN_STEPS,))],
        compiler_params=params(24),
        cost_estimate=mlp_cost(rows),
        name="mlp_forward",
    )(core, x, *sums, weights, token)


def mlp_grads(hidden_grad, gate_out, up_out):
    sigmoid_gate = sigmoid(gate_out)
    gate_grad = hidden_grad * up_out * (sigmoid_gate * (1.0 + gate_out * (1.0 - sigmoid_gate)))
    return gate_grad.astype(BF16), (hidden_grad * (gate_out * sigmoid_gate)).astype(BF16)


def mlp_backward_kernel(core_ref, x_ref, middle_grad_ref, *rest):
    sums, rest = rest[: 2 * PARTS], rest[2 * PARTS :]
    (gate_ref, up_ref, w_ref, _, g_ref, pair_grad_ref), rest = rest[:6], rest[6:]
    outs, weighted = rest[:-1], rest[-1]
    for at, columns, part in each_sum(core_ref, sums):
        weighted[at, columns] = part[...].astype(F32)
    rows = x_ref[...].astype(F32)
    g_ref[...] = (
        middle_grad_ref[...] + norm_back(weighted[...], rows, inverse_norm(rows))
    ).astype(BF16)
    for step, down in enumerate(column_tiles(2 * HIDDEN_COLS)):
        at = slice(HIDDEN_TILE * step, HIDDEN_TILE * (step + 1))
        up_at = slice(HIDDEN_COLS + at.start, HIDDEN_COLS + at.stop)
        hidden_grad = nn_dot(g_ref[...], w_ref[:, down])
        pair_grad_ref[:, at], pair_grad_ref[:, up_at] = mlp_grads(
            hidden_grad, gate_ref[:, at], up_ref[:, at]
        )
    write_partial(core_ref, pair_grad_ref, w_ref, slice(0, 2 * HIDDEN_COLS), outs)


def mlp_backward(core, above, gate_out, up_out, weights, token):
    rows = gate_out.shape[0]
    return pl.pallas_call(
        mlp_backward_kernel,
        in_specs=[smem_whole()] + [vmem_whole()] * (5 + 2 * PARTS) + [hbm_whole()],
        out_specs=[vmem_whole()] * (2 + 2 * PARTS),
        out_shape=[shape(rows, WIDTH, BF16), shape(rows, 2 * HIDDEN_COLS, BF16)]
        + part_shapes(rows),
        scratch_shapes=[pltpu.VMEM((rows, WIDTH), F32)],
        compiler_params=params(26),
        cost_estimate=mlp_cost(rows),
        name="mlp_backward",
    )(core, *above, gate_out, up_out, weights, token)


def mlp_ahead_kernel(g_ref, w_any, hidden_grad_ref, pair_ref, token_ref, down_ref, sems):
    down = ahead_copy(w_any, down_ref, sems.at[0], 2 * HIDDEN_COLS)
    pair = ahead_copy(w_any, pair_ref, sems.at[1], 0)
    down.start()
    pair.start()
    token_ref[...] = jnp.zeros_like(token_ref)
    down.wait()
    hidden_grad_ref[...] = nn_dot(g_ref[...], down_ref[...])
    pair.wait()


def mlp_ahead(g, weights):
    rows = g.shape[0]
    return pl.pallas_call(
        mlp_ahead_kernel,
        in_specs=[vmem_whole(), hbm_whole()],
        out_specs=[vmem_whole()] * 3,
        out_shape=[
            shape(rows, HIDDEN_COLS, F32),
            shape(WIDTH, 2 * HIDDEN_COLS, BF16),
            TOKEN,
        ],
        scratch_shapes=[pltpu.VMEM((WIDTH, HIDDEN_COLS), BF16), pltpu.SemaphoreType.DMA((2,))],
        compiler_params=params(15),
        cost_estimate=pl.CostEstimate(
            flops=2 * rows * WIDTH * HIDDEN_COLS, bytes_accessed=14_000_000, transcendentals=0
        ),
        name="mlp_ahead",
    )(g, in_hbm(weights))


def mlp_last_kernel(core_ref, x_ref, *rest):
    sums, rest = rest[: 2 * PARTS], rest[2 * PARTS :]
    (hidden_grad_ref, w_ref, _, middle_any, hidden_any, second_ref, hidden_ref, pair_grad_ref), rest = rest[:8], rest[8:]
    middle_ref, out_sems = rest
    for at, columns, part in each_sum(core_ref, sums):
        middle_ref[at, columns] = x_ref[at, columns].astype(F32) + part[...].astype(F32)
    rows = middle_ref[...]
    second_ref[...] = (rows * inverse_norm(rows)).astype(BF16)
    outward = Outward(out_sems)
    outward.send(middle_ref, middle_any)
    for step, (gate, up) in enumerate(zip(column_tiles(0), column_tiles(HIDDEN_COLS))):
        at = slice(HIDDEN_TILE * step, HIDDEN_TILE * (step + 1))
        up_at = slice(HIDDEN_COLS + at.start, HIDDEN_COLS + at.stop)
        gate_out = nn_dot(second_ref[...], w_ref[:, gate])
        up_out = nn_dot(second_ref[...], w_ref[:, up])
        hidden_ref[:, at] = (gate_out * sigmoid(gate_out) * up_out).astype(BF16)
        pair_grad_ref[:, at], pair_grad_ref[:, up_at] = mlp_grads(
            hidden_grad_ref[:, at], gate_out, up_out
        )
    outward.send(hidden_ref, hidden_any)
    outward.wait()


def mlp_last(core, x, sums, hidden_grad, pair_weights, token):
    rows = x.shape[0]
    return pl.pallas_call(
        mlp_last_kernel,
        in_specs=[smem_whole()] + [vmem_whole()] * (3 + 2 * PARTS) + [hbm_whole()],
        out_specs=[hbm_whole()] * 2 + [vmem_whole()] * 3,
        out_shape=[
            pltpu.HBM((rows, WIDTH), F32),
            pltpu.HBM((rows, HIDDEN_COLS), BF16),
            shape(rows, WIDTH, BF16),
            shape(rows, HIDDEN_COLS, BF16),
            shape(rows, 2 * HIDDEN_COLS, BF16),
        ],
        scratch_shapes=[pltpu.VMEM((rows, WIDTH), F32), pltpu.SemaphoreType.DMA((2,))],
        compiler_params=params(28),
        cost_estimate=mlp_cost(rows),
        name="mlp_last",
    )(core, x, *sums, hidden_grad, pair_weights, token)


def mlp_in_kernel(core_ref, pair_grad_any, w_any, _, *rest):
    outs, (pair_grad_ref, w_ref, sems) = rest[:-3], rest[-3:]
    fetched = pltpu.make_async_copy(pair_grad_any, pair_grad_ref, sems.at[4])
    fetched.start()
    quarter = HALF // 2
    pieces = []
    for number, (which, part) in enumerate(((1, 0), (1, 1), (0, 0), (0, 1))):
        position = core_ref[0] if which == 0 else 1 - core_ref[0]
        features = pl.ds(pl.multiple_of(position * HALF + part * quarter, quarter), quarter)
        source = w_any.at[features, pl.ds(0, 2 * HIDDEN_COLS)]
        copy = pltpu.make_async_copy(source, w_ref.at[number], sems.at[number])
        copy.start()
        pieces.append((copy, which, slice(part * quarter, (part + 1) * quarter)))
    fetched.wait()
    for number, (copy, which, columns) in enumerate(pieces):
        copy.wait()
        product = nt_dot(pair_grad_ref[...], w_ref[number]).astype(BF16)
        refs = outs[PARTS * which : PARTS * (which + 1)]
        for at, ref in zip(row_parts(product.shape[0]), refs):
            ref[:, columns] = product[at]


def mlp_in(core, pair_grad, weights, token):
    rows = pair_grad.shape[0]
    return pl.pallas_call(
        mlp_in_kernel,
        in_specs=[smem_whole()] + [hbm_whole()] * 3,
        out_specs=[vmem_whole()] * (2 * PARTS),
        out_shape=part_shapes(rows),
        scratch_shapes=[
            pltpu.VMEM(pair_grad.shape, BF16),
            pltpu.VMEM((4, HALF // 2, 2 * HIDDEN_COLS), BF16),
            pltpu.SemaphoreType.DMA((5,)),
        ],
        compiler_params=params(18),
        cost_estimate=pl.CostEstimate(
            flops=4 * rows * WIDTH * HIDDEN_COLS, bytes_accessed=9_000_000, transcendentals=0
        ),
        name="mlp_in",
    )(core, in_hbm(pair_grad), in_hbm(weights), token)


def mlp_down_kernel(core_ref, hidden_ref, w_any, *rest):
    outs, w_ref, sem = rest[:-2], rest[-2], rest[-1]
    copy = pltpu.make_async_copy(w_any.at[:, pl.ds(2 * HIDDEN_COLS, HIDDEN_COLS)], w_ref, sem)
    copy.start()
    copy.wait()
    write_partial(core_ref, hidden_ref, w_ref, slice(0, HIDDEN_COLS), outs)


def mlp_down(core, hidden, weights):
    rows = hidden.shape[0]
    return pl.pallas_call(
        mlp_down_kernel,
        in_specs=[smem_whole(), vmem_whole(), hbm_whole()],
        out_specs=[vmem_whole()] * (2 * PARTS),
        out_shape=part_shapes(rows),
        scratch_shapes=[pltpu.VMEM((WIDTH, HIDDEN_COLS), BF16), pltpu.SemaphoreType.DMA(())],
        compiler_params=params(14),
        cost_estimate=pl.CostEstimate(
            flops=2 * rows * WIDTH * HIDDEN_COLS, bytes_accessed=5_000_000, transcendentals=0
        ),
        name="mlp_down",
    )(core, hidden, in_hbm(weights))


def attention_backward_kernel(sequences, near, core_ref, g_ref, middle_ref, *rest):
    sums, rest = rest[: 2 * PARTS], rest[2 * PARTS :]
    (w_ref, qkv_any, prob_any, _, middle_grad_out, attn_in_ref, qkv_grad_ref), rest = rest[:7], rest[7:]
    outs, (middle_grad_ref, qkv_ref, prob_ref, mix_grad, sems) = rest[:-5], rest[-5:]
    copies = [
        pltpu.make_async_copy(qkv_any, qkv_ref, sems.at[0]),
        pltpu.make_async_copy(prob_any, prob_ref, sems.at[1]),
    ]
    for copy in copies:
        copy.start()
    for at, columns, part in each_sum(core_ref, sums):
        middle_grad_ref[at, columns] = part[...].astype(F32)
    middle = middle_ref[...]
    middle_grad = g_ref[...].astype(F32) + norm_back(
        middle_grad_ref[...], middle, inverse_norm(middle)
    )
    if near:
        middle_grad_out[...] = middle_grad
    else:
        middle_grad_ref[...] = middle_grad
        outward = pltpu.make_async_copy(middle_grad_ref, middle_grad_out, sems.at[2])
        outward.start()
    attn_in_ref[...] = middle_grad.astype(BF16)
    mix_grad[...] = nn_dot(attn_in_ref[...], w_ref[:, QKV_COLS:]).astype(BF16)
    for copy in copies:
        copy.wait()
    for sequence in range(sequences):
        rows = slice(128 * sequence, 128 * (sequence + 1))
        for group in range(2):
            at = 2 * HEAD_WIDTH * group
            key_at = QUERY_COLS + HEAD_WIDTH * group
            value_at = key_at + KV_COLS
            grads = two_heads(mix_grad, rows, at)
            queries = two_heads(qkv_ref, rows, at)
            keys = qkv_ref[rows, key_at : key_at + HEAD_WIDTH]
            probability = prob_ref[2 * sequence + group]
            prob_grad = nt_dot(grads, qkv_ref[rows, value_at : value_at + HEAD_WIDTH])
            centred = jnp.sum(probability * prob_grad, axis=-1, keepdims=True)
            score_grad = (probability * (prob_grad - centred)).astype(BF16)
            query_grad = (nn_dot(score_grad, keys) * SCORE_SCALE).astype(BF16)
            qkv_grad_ref[rows, at : at + HEAD_WIDTH] = query_grad[:128]
            qkv_grad_ref[rows, at + HEAD_WIDTH : at + 2 * HEAD_WIDTH] = query_grad[128:]
            qkv_grad_ref[rows, key_at : key_at + HEAD_WIDTH] = (
                tn_dot(score_grad, queries) * SCORE_SCALE
            ).astype(BF16)
            qkv_grad_ref[rows, value_at : value_at + HEAD_WIDTH] = tn_dot(
                probability.astype(BF16), grads
            ).astype(BF16)
    if near:
        write_partial(core_ref, qkv_grad_ref, w_ref, slice(0, QKV_COLS), outs)
    else:
        outward.wait()


def attention_in_kernel(core_ref, qkv_grad_ref, w_ref, _, *outs):
    write_partial(core_ref, qkv_grad_ref, w_ref, slice(0, QKV_COLS), outs)


def attention_in(core, qkv_grad, weights, token):
    rows = qkv_grad.shape[0]
    return pl.pallas_call(
        attention_in_kernel,
        in_specs=[smem_whole()] + [vmem_whole()] * 2 + [hbm_whole()],
        out_specs=[vmem_whole()] * (2 * PARTS),
        out_shape=part_shapes(rows),
        compiler_params=params(14),
        cost_estimate=pl.CostEstimate(
            flops=2 * rows * WIDTH * QKV_COLS, bytes_accessed=5_000_000, transcendentals=0
        ),
        name="attention_in",
    )(core, qkv_grad, weights, token)


def attention_backward(core, g, middle, sums, qkv, probability, weights, token, near):
    rows = g.shape[0]
    residual, parts = shape(rows, WIDTH, F32), part_shapes(rows) if near else []
    return pl.pallas_call(
        functools.partial(attention_backward_kernel, rows // 128, near),
        in_specs=[smem_whole()] + [vmem_whole()] * (3 + 2 * PARTS) + [hbm_whole()] * 3,
        out_specs=[vmem_whole() if near else hbm_whole()] + [vmem_whole()] * (2 + len(parts)),
        out_shape=[
            residual if near else far(residual),
            shape(rows, WIDTH, BF16),
            shape(rows, QKV_COLS, BF16),
        ]
        + parts,
        scratch_shapes=[
            pltpu.VMEM((rows, WIDTH), F32),
            pltpu.VMEM(qkv.shape, BF16),
            pltpu.VMEM(probability.shape, F32),
            pltpu.VMEM((rows, OUT_COLS), BF16),
            pltpu.SemaphoreType.DMA((3,)),
        ],
        compiler_params=params(24),
        cost_estimate=attention_cost(rows),
        name="attention_backward",
    )(core, g, middle, *sums, weights, in_hbm(qkv), in_hbm(probability), token)


def write_products(start, pairs, out_any, slots, sems):
    _, height, width = slots.shape
    copies = []
    for number in range(WIDTH // height):
        features = pl.ds(height * number, height)
        if number >= 2:
            copies[number - 2].wait()
        slot = slots.at[number % 2]
        at = 0
        for left, right in pairs:
            columns = right.shape[1]
            slot[:, at : at + columns] = tn_dot(left[:, features], right[...]).astype(BF16)
            at += columns
        target = out_any.at[features, pl.ds(start, width)]
        copies.append(pltpu.make_async_copy(slot, target, sems.at[number % 2]))
        copies[-1].start()
    for copy in copies[-2:]:
        copy.wait()


def mlp_weights_kernel(second_ref, g_ref, pair_grad_ref, hidden_ref, *rest):
    out_any, token_ref, slots, sems = rest[-4:]
    token_ref[...] = jnp.zeros_like(token_ref)
    write_products(0, [(second_ref, pair_grad_ref), (g_ref, hidden_ref)], out_any, slots, sems)


def into_buffer(kernel, buffer, columns, slot, operands, flops, name, mib):
    aliases, specs = {}, [vmem_whole()] * len(operands)
    if buffer is not None:
        aliases = {len(operands): 0}
        specs, operands = specs + [hbm_whole()], operands + (in_hbm(buffer),)
    return pl.pallas_call(
        kernel,
        in_specs=specs,
        out_specs=[hbm_whole(), vmem_whole()],
        out_shape=[pltpu.HBM((WIDTH, columns), BF16), TOKEN],
        input_output_aliases=aliases,
        scratch_shapes=[pltpu.VMEM((2, *slot), BF16), pltpu.SemaphoreType.DMA((2,))],
        compiler_params=params(mib),
        cost_estimate=pl.CostEstimate(flops=flops, bytes_accessed=flops // 250, transcendentals=0),
        name=name,
    )(*operands)


def mlp_weights(buffer, columns, second, g, pair_grad, hidden):
    return into_buffer(
        mlp_weights_kernel,
        buffer,
        columns,
        (512, MLP_COLS),
        (second, g, pair_grad, hidden),
        2 * second.shape[0] * WIDTH * MLP_COLS,
        "mlp_weights",
        18,
    )


def attention_weights_kernel(start, first_ref, attn_in_ref, qkv_grad_ref, mix_ref, *rest):
    out_any, token_ref, slots, sems = rest[-4:]
    token_ref[...] = jnp.zeros_like(token_ref)
    pairs = [(first_ref, qkv_grad_ref), (attn_in_ref, mix_ref)]
    write_products(start, pairs, out_any, slots, sems)


def attention_weights(buffer, columns, start, first, attn_in, qkv_grad, mixture):
    return into_buffer(
        functools.partial(attention_weights_kernel, start),
        buffer,
        columns,
        (768, ATTN_COLS),
        (first, attn_in, qkv_grad, mixture),
        2 * first.shape[0] * WIDTH * ATTN_COLS,
        "attention_weights",
        14,
    )


def sum_four(partial, beside=None, within=None):
    keeps, gives = list(partial[:PARTS]), list(partial[PARTS:])
    chips = [
        (keep.astype(F32) + swap(give, "section").astype(F32)).astype(BF16)
        for keep, give in zip(keeps, gives)
    ]
    arrived = [swap(chip, "tensor") for chip in chips]
    if beside is not None:
        arrived[-1], beside = lax.optimization_barrier((arrived[-1], beside))
    totals = [
        (chip.astype(F32) + other.astype(F32)).astype(BF16)
        for chip, other in zip(chips, arrived)
    ]
    if within is not None:

        def tie(value):
            totals[0], value = lax.optimization_barrier((totals[0], value))
            return value

        beside = within(tie)
    return totals + [swap(total, "section") for total in totals], beside


def row_scales(gain_ref):
    row = lax.broadcasted_iota(jnp.int32, (48, 48), 0)
    column = lax.broadcasted_iota(jnp.int32, (48, 48), 1)
    return jnp.where(row == column, gain_ref[...].astype(F32), 0.0).astype(BF16)


def pack_kernel(core_ref, *rest):
    sources, (mine_ref, give_ref), shards, sems = rest[:9], rest[9:11], rest[11:20], rest[20]
    copies = [
        pltpu.make_async_copy(source, shard, sems.at[number])
        for number, (source, shard) in enumerate(zip(sources, shards))
    ]
    for copy in copies:
        copy.start()
    is_first = core_ref[0] == 0
    (attn_gain_ref, mlp_gain_ref), shards = shards[:2], shards[2:]
    for copy in copies[:2]:
        copy.wait()
    attn_scale, mlp_scale = row_scales(attn_gain_ref), row_scales(mlp_gain_ref)
    start = 0
    for copy, shard, scale in zip(
        copies[2:],
        shards,
        (mlp_scale, mlp_scale, None, attn_scale, attn_scale, attn_scale, None),
    ):
        copy.wait()
        weight = shard[...]
        if scale is not None:
            weight = nn_dot(scale, weight).astype(BF16)
        width = weight.shape[1] // 2
        low, high = weight[:, :width], weight[:, width:]
        mine_ref[:, start : start + width] = jnp.where(is_first, low, high)
        give_ref[:, start : start + width] = jnp.where(is_first, high, low)
        start += width


def pack_shards(core, *shards):
    return pl.pallas_call(
        pack_kernel,
        in_specs=[smem_whole()] + [hbm_whole()] * len(shards),
        out_specs=[vmem_whole()] * 2,
        out_shape=[shape(48, LAYER_COLS, BF16)] * 2,
        scratch_shapes=[pltpu.VMEM(shard.shape, shard.dtype) for shard in shards]
        + [pltpu.SemaphoreType.DMA((len(shards),))],
        compiler_params=params(16),
        name="pack_shards",
    )(core, *[in_hbm(shard) for shard in shards])


def combine_kernel(core_ref, keep_ref, arrived_ref, last_ref, zero_w_ref, one_w_ref, mine_ref, give_ref, terms_ref, zero, one):
    rest = (keep_ref[...].astype(F32) + arrived_ref[...].astype(F32)).astype(BF16)
    zero[:, :MLP_COLS] = rest[:, :MLP_COLS]
    zero[:, MLP_COLS:] = rest[:, LAYER_COLS:]
    one[:, :MLP_COLS] = last_ref[...]
    one[:, MLP_COLS:] = rest[:, MLP_COLS:LAYER_COLS]
    is_first = core_ref[0] == 0
    mine_ref[...] = jnp.where(is_first, zero[...], one[...])
    give_ref[...] = jnp.where(is_first, one[...], zero[...])
    row = 0
    for grad, weights in ((zero, zero_w_ref), (one, one_w_ref)):
        products = weights[...].astype(F32) * grad[...].astype(F32)
        for columns in (slice(MLP_COLS, MLP_COLS + QKV_COLS), slice(0, 2 * HIDDEN_COLS)):
            terms_ref[row, :] = jnp.sum(products[:, columns], axis=1)
            row += 1


def combine_grads(core, *operands):
    return pl.pallas_call(
        combine_kernel,
        in_specs=[smem_whole()] + [vmem_whole()] * len(operands),
        out_specs=[vmem_whole()] * 3,
        out_shape=[shape(48, LAYER_COLS, BF16)] * 2 + [shape(4, 48, F32)],
        scratch_shapes=[pltpu.VMEM((48, LAYER_COLS), BF16)] * 2,
        compiler_params=params(16),
        name="combine_grads",
    )(core, *operands)


def unpack_kernel(core_ref, attn_scale_ref, mlp_scale_ref, mine_ref, got_ref, gate_ref, up_ref, down_ref, query_ref, key_ref, value_ref, out_ref):
    is_first = core_ref[0] == 0

    def place(out, start, scale_ref):
        width = out.shape[1] // 2
        mine = mine_ref[:, start : start + width].astype(F32)
        got = got_ref[:, start : start + width].astype(F32)
        if scale_ref is not None:
            mine, got = mine * scale_ref[...], got * scale_ref[...]
        out[:, :width] = jnp.where(is_first, mine, got)
        out[:, width:] = jnp.where(is_first, got, mine)

    place(gate_ref, 0, mlp_scale_ref)
    place(up_ref, HIDDEN_COLS, mlp_scale_ref)
    place(down_ref, 2 * HIDDEN_COLS, None)
    place(query_ref, MLP_COLS, attn_scale_ref)
    place(key_ref, MLP_COLS + QUERY_COLS, attn_scale_ref)
    place(value_ref, MLP_COLS + QUERY_COLS + KV_COLS, attn_scale_ref)
    place(out_ref, MLP_COLS + QKV_COLS, None)


def unpack_grads(core, *operands):
    widths = [HIDDEN_COLS] * 3 + [QUERY_COLS, KV_COLS, KV_COLS, OUT_COLS]
    return pl.pallas_call(
        unpack_kernel,
        in_specs=[smem_whole()] + [vmem_whole()] * len(operands),
        out_specs=[vmem_whole()] * len(widths),
        out_shape=[shape(48, 2 * width, F32) for width in widths],
        compiler_params=params(16),
        name="unpack_grads",
    )(core, *operands)


def gather_rows(z_low, share):
    other = swap(share, "zl")
    pair = jnp.concatenate([pick(z_low, share, other), pick(z_low, other, share)], axis=0)
    return lax.all_gather(pair, ("y", "x"), axis=0, tiled=True)


def scatter_pair(grad):
    return lax.psum_scatter(grad, ("y", "x"), scatter_dimension=0, tiled=True)


def scatter_low(z_low, pair):
    keep = pick(z_low, pair[:48], pair[48:])
    give = pick(z_low, pair[48:], pair[:48])
    return (keep.astype(F32) + swap(give, "zl").astype(F32)).astype(BF16)


def to_ring_order(rows):
    lead = rows.shape[:-1]
    return jnp.swapaxes(rows.reshape(lead + (4, 2, 4, 48)), -3, -2).reshape(rows.shape)


def from_ring_order(rows):
    lead = rows.shape[:-1]
    return jnp.swapaxes(rows.reshape(lead + (4, 4, 2, 48)), -3, -2).reshape(rows.shape)


def join_positions(tensor, own):
    other = swap(own, "tensor")
    return jnp.concatenate(
        [pick(tensor, own, other), pick(tensor, other, own)], axis=1
    ).reshape(384, WIDTH)


def own_positions(tensor, rows):
    rows = rows.reshape(3, 128, 1536)
    return pick(tensor, rows[:, :64], rows[:, 64:])


def per_device(
    inputs, cotangent, plan, attn_gain, mlp_gain, w_query, key_weight, value_weight,
    w_out, w_gate, w_up, w_down,
):
    core = lax.axis_index("section")
    z_low = lax.axis_index("zl")
    tensor = lax.axis_index("tensor")

    attn_scale = attn_gain[0].astype(F32)[:, None]
    mlp_scale = mlp_gain[0].astype(F32)[:, None]

    core_ref = core.astype(jnp.int32).reshape(1)
    mine, give = pack_shards(
        core_ref, attn_gain, mlp_gain,
        w_gate[0], w_up[0], w_down[0].T, w_query[0], key_weight[0], value_weight[0], w_out[0].T,
    )
    got = swap(give, "section")
    layer_zero, layer_one = pick(core, mine, got), pick(core, got, mine)
    first_weights = gather_rows(
        z_low, jnp.concatenate([layer_zero, layer_one[:, MLP_COLS:]], axis=1)
    )
    last_weights = gather_rows(z_low, layer_one[:, :MLP_COLS])

    stream = join_positions(tensor, to_ring_order(inputs[:, 0][plan]))
    stream, late = lax.optimization_barrier((stream, cotangent))
    out_grad = join_positions(tensor, to_ring_order(late[:, 0][plan]))
    stream, out_grad = lax.optimization_barrier((stream, out_grad))

    def whole_rows(sums):
        own, other = jnp.concatenate(sums[:PARTS]), jnp.concatenate(sums[PARTS:])
        return jnp.concatenate([pick(core, own, other), pick(core, other, own)], axis=1).astype(F32)

    x_zero = stream
    first_zero, qkv_zero, prob_zero, mix_zero, *partial = attention_first(
        core_ref, x_zero, first_weights, MLP_COLS
    )
    near, token = fetch(first_weights, 0, MLP_COLS)
    sums, token = sum_four(partial, beside=token)
    middle_zero, second_zero, gate_zero, up_zero, hidden_zero, *partial = mlp_forward(
        core_ref, x_zero, sums, near, token
    )
    near, token = fetch(first_weights, LAYER_COLS, ATTN_COLS)
    sums, token = sum_four(partial, beside=token)
    x_one, first_one, qkv_one, prob_one, mix_one, *partial = attention_next(
        core_ref, middle_zero, sums, near, token
    )
    sums, ahead = sum_four(partial, within=lambda tie: mlp_ahead(out_grad, tie(last_weights)))
    hidden_grad, near, token = ahead

    middle_one, hidden_far, second_one, hidden_one, pair_grad = mlp_last(
        core_ref, x_one, sums, hidden_grad, near, token
    )
    one_mlp, done = mlp_weights(None, MLP_COLS, second_one, out_grad, pair_grad, hidden_one)
    last_pair = scatter_pair(one_mlp)
    partial = mlp_in(core_ref, pair_grad, last_weights, done)
    near, token = fetch(first_weights, LAYER_COLS, ATTN_COLS, one_mlp)
    sums, token = sum_four(partial, beside=token)
    middle_grad, attn_in, qkv_grad, *partial = attention_backward(
        core_ref, out_grad, middle_one, sums, qkv_one, prob_one, near, token, True
    )
    buffer, _ = attention_weights(None, REST_COLS, MLP_COLS, first_one, attn_in, qkv_grad, mix_one)
    near, token = fetch(first_weights, 0, MLP_COLS, buffer)
    sums, (buffer, token) = sum_four(partial, beside=(buffer, token))

    grad_one, pair_grad, *partial = mlp_backward(
        core_ref, (x_one, middle_grad, *sums), gate_zero, up_zero, near, token
    )
    buffer, _ = mlp_weights(buffer, REST_COLS, second_zero, grad_one, pair_grad, hidden_zero)
    near, token = fetch(first_weights, MLP_COLS, ATTN_COLS, buffer)
    sums, (buffer, token) = sum_four(partial, beside=(buffer, token))
    hidden_far, sums[0] = lax.optimization_barrier((hidden_far, sums[0]))
    down_partial = mlp_down(core_ref, hidden_far, last_weights)
    middle_grad, attn_in, qkv_grad = attention_backward(
        core_ref, grad_one, middle_zero, sums, qkv_zero, prob_zero, near, token, False
    )
    buffer, done = attention_weights(
        buffer, REST_COLS, LAYER_COLS, first_zero, attn_in, qkv_grad, mix_zero
    )
    rest_pair = scatter_pair(buffer)
    sums, _ = sum_four(attention_in(core_ref, qkv_grad, near, done))
    rows = x_zero.astype(F32)
    grad_zero = middle_grad + norm_back(whole_rows(sums), rows, inverse_norm(rows))
    down_sums, _ = sum_four(down_partial)
    result_one = (middle_one + whole_rows(down_sums)).astype(BF16)
    outputs = [own_positions(tensor, x_one), own_positions(tensor, result_one)]
    grads = [own_positions(tensor, grad_zero.astype(BF16)), own_positions(tensor, grad_one)]

    layer_outputs = from_ring_order(pick(core, outputs[0], outputs[1]))
    input_grads = from_ring_order(pick(core, grads[0], grads[1]))
    last_grad = scatter_low(z_low, last_pair)
    rest_pair, layer_outputs, input_grads, last_grad = lax.optimization_barrier(
        (rest_pair, layer_outputs, input_grads, last_grad)
    )
    keep = pick(z_low, rest_pair[:48], rest_pair[48:])
    arrived = swap(pick(z_low, rest_pair[48:], rest_pair[:48]), "zl")
    mine, give, terms = combine_grads(
        core_ref, keep, arrived, last_grad, layer_zero, layer_one
    )
    got = swap(give, "section")
    arrived = swap(terms, "tensor")
    gate_grad, up_grad, down_grad, query_grad, key_grad, value_grad, out_weight_grad = unpack_grads(
        core_ref, attn_scale, mlp_scale, mine, got
    )
    arrived, key_grad = lax.optimization_barrier((arrived, key_grad))
    terms = terms + arrived
    terms = pick(core, terms[:2], terms[2:]) + swap(pick(core, terms[2:], terms[:2]), "section")
    return (
        layer_outputs[None, :, None],
        input_grads[None, :, None],
        (terms[0] / attn_scale[:, 0])[None],
        (terms[1] / mlp_scale[:, 0])[None],
        query_grad[None],
        key_grad[None],
        value_grad[None],
        out_weight_grad.T[None],
        gate_grad[None],
        up_grad[None],
        down_grad.T[None],
    )


def solution(mesh):
    split = Mesh(mesh.devices.reshape(2, 4, 2, 4, 2), ("section", "y", "zl", "x", "tensor"))
    dp = ("y", "zl", "x")
    rows = P("section", dp, "tensor")
    columns = P("section", "tensor", dp)
    return jax.shard_map(
        per_device,
        mesh=split,
        in_specs=(
            P(None, dp, "tensor", None),
            P(None, dp, "tensor", None),
            P(),
            P("section", dp),
            P("section", dp),
            rows,
            rows,
            rows,
            columns,
            rows,
            rows,
            columns,
        ),
        out_specs=(
            P("section", None, dp, "tensor", None),
            P("section", None, dp, "tensor", None),
            P("section", dp),
            P("section", dp),
            rows,
            rows,
            rows,
            columns,
            rows,
            rows,
            columns,
        ),
        check_vma=False,
    )
```

```python
import functools

import jax
import jax.numpy as jnp
from jax import lax
from jax.experimental import pallas as pl
from jax.experimental.pallas import tpu as pltpu
from jax.sharding import Mesh, PartitionSpec as P

HEAD_WIDTH = 96
EPSILON = 1e-05
BLOCKED = -1e30
SCORE_SCALE = HEAD_WIDTH ** (-0.5)
BF16 = jnp.bfloat16
F32 = jnp.float32

QUERY_COLS, KV_COLS = 384, 192
QKV_COLS = QUERY_COLS + 2 * KV_COLS
OUT_COLS = 384
HIDDEN_COLS = 1024
ATTN_COLS = QKV_COLS + OUT_COLS
MLP_COLS = 3 * HIDDEN_COLS
LAYER_COLS = MLP_COLS + ATTN_COLS
REST_COLS = LAYER_COLS + ATTN_COLS
HIDDEN_TILE = 1024
AHEAD = 3
WIDTH = 1536
HALF = WIDTH // 2
PARTS = 2
MIB = 1024 * 1024


def swap(value, axis):
    return lax.ppermute(value, axis, [(0, 1), (1, 0)])


def pick(index, first, second):
    return jnp.where(index == 0, first, second)


def norm_back(weighted, residual, inverse):
    scaled = residual * inverse
    return inverse * (weighted - scaled * jnp.mean(weighted * scaled, axis=-1, keepdims=True))


def vmem_whole():
    return pl.BlockSpec(memory_space=pltpu.VMEM)


def smem_whole():
    return pl.BlockSpec(memory_space=pltpu.SMEM)


def shape(rows, columns, dtype):
    return jax.ShapeDtypeStruct((rows, columns), dtype)


def half_of(core_ref, which):
    position = core_ref[0] if which == 0 else 1 - core_ref[0]
    return pl.ds(pl.multiple_of(position * HALF, HALF), HALF)


def nt_dot(left_side, right_side):
    return lax.dot_general(
        left_side, right_side, (((1,), (1,)), ((), ())), preferred_element_type=F32
    )


def tn_dot(left_side, right_side):
    return lax.dot_general(
        left_side, right_side, (((0,), (0,)), ((), ())), preferred_element_type=F32
    )


def nn_dot(left_side, right_side):
    return jnp.dot(left_side, right_side, preferred_element_type=F32)


def row_parts(rows):
    return [slice(rows // PARTS * part, rows // PARTS * (part + 1)) for part in range(PARTS)]


def part_shapes(rows):
    return [shape(rows // PARTS, HALF, BF16)] * (2 * PARTS)


class Outward:
    def __init__(self, sems):
        self.sems, self.copies = sems, []

    def send(self, source, target):
        self.copies.append(pltpu.make_async_copy(source, target, self.sems.at[len(self.copies)]))
        self.copies[-1].start()

    def wait(self):
        for copy in self.copies:
            copy.wait()


def far(array):
    return pltpu.HBM(array.shape, array.dtype)


def each_sum(core_ref, sum_refs):
    rows = sum_refs[0].shape[0] * PARTS
    for which in range(2):
        for part, at in enumerate(row_parts(rows)):
            yield at, half_of(core_ref, which), sum_refs[PARTS * which + part]


def write_half(core_ref, which, left_ref, w_ref, columns, outs):
    product = nt_dot(left_ref[...], w_ref[half_of(core_ref, which), columns]).astype(BF16)
    refs = outs[PARTS * which : PARTS * (which + 1)]
    for at, ref in zip(row_parts(left_ref.shape[0]), refs):
        ref[...] = product[at]


def write_partial(core_ref, left_ref, w_ref, columns, outs):
    for which in (1, 0):
        write_half(core_ref, which, left_ref, w_ref, columns, outs)


def params(mib):
    return pltpu.CompilerParams(vmem_limit_bytes=mib * MIB)


def inverse_norm(rows):
    return lax.rsqrt(jnp.mean(rows * rows, axis=-1, keepdims=True) + EPSILON)


def causal_mask():
    row = lax.broadcasted_iota(jnp.int32, (128, 128), 0)
    return row >= lax.broadcasted_iota(jnp.int32, (128, 128), 1)


def two_heads(ref, rows, start):
    return jnp.concatenate(
        [
            ref[rows, start : start + HEAD_WIDTH],
            ref[rows, start + HEAD_WIDTH : start + 2 * HEAD_WIDTH],
        ],
        axis=0,
    )


def ahead_copy(w_any, w_ref, sem, column):
    return pltpu.make_async_copy(w_any.at[:, pl.ds(column, w_ref.shape[1])], w_ref, sem)


def attention_forward_body(sequences, core_ref, outward, first_ref, w_ref, qkv_any, prob_any, mix_ref, *rest):
    parts, (qkv_ref, prob_ref) = rest[:-2], rest[-2:]
    qkv_ref[...] = nn_dot(first_ref[...], w_ref[:, :QKV_COLS]).astype(BF16)
    outward.send(qkv_ref, qkv_any)
    mask = causal_mask()
    mask = jnp.concatenate([mask, mask], axis=0)
    for sequence in range(sequences):
        rows = slice(128 * sequence, 128 * (sequence + 1))
        for group in range(2):
            queries = two_heads(qkv_ref, rows, 2 * HEAD_WIDTH * group)
            key_at = QUERY_COLS + HEAD_WIDTH * group
            value_at = key_at + KV_COLS
            scores = nt_dot(queries, qkv_ref[rows, key_at : key_at + HEAD_WIDTH]) * SCORE_SCALE
            scores = jnp.where(mask, scores, BLOCKED)
            expanded = jnp.exp(scores - jnp.max(scores, axis=-1, keepdims=True))
            probability = expanded / jnp.sum(expanded, axis=-1, keepdims=True)
            prob_ref[2 * sequence + group] = probability
            mixed = nn_dot(
                probability.astype(BF16), qkv_ref[rows, value_at : value_at + HEAD_WIDTH]
            ).astype(BF16)
            at = 2 * HEAD_WIDTH * group
            mix_ref[rows, at : at + HEAD_WIDTH] = mixed[:128]
            mix_ref[rows, at + HEAD_WIDTH : at + 2 * HEAD_WIDTH] = mixed[128:]
        both = pl.ds(2 * sequence, 2)
        outward.send(prob_ref.at[both], prob_any.at[both])
    write_partial(core_ref, mix_ref, w_ref, slice(QKV_COLS, ATTN_COLS), parts)
    outward.wait()


def attention_first_kernel(sequences, column, core_ref, x_ref, w_any, first_any, *rest):
    outs, (first_ref, w_ref, sem, sems) = rest[:-4], rest[-4:]
    copy = ahead_copy(w_any, w_ref, sem, column)
    copy.start()
    rows = x_ref[...].astype(F32)
    first_ref[...] = (rows * inverse_norm(rows)).astype(BF16)
    copy.wait()
    outward = Outward(sems)
    outward.send(first_ref, first_any)
    attention_forward_body(sequences, core_ref, outward, first_ref, w_ref, *outs)


def attention_next_kernel(sequences, core_ref, middle_ref, *rest):
    sums, (w_ref, _, x_any, first_any) = rest[: 2 * PARTS], rest[2 * PARTS : 2 * PARTS + 4]
    outs, (x_ref, first_ref, sems) = rest[2 * PARTS + 4 : -3], rest[-3:]
    outward = Outward(sems)
    for at, columns, part in each_sum(core_ref, sums):
        x_ref[at, columns] = (middle_ref[at, columns] + part[...].astype(F32)).astype(BF16)
    outward.send(x_ref, x_any)
    rows = x_ref[...].astype(F32)
    first_ref[...] = (rows * inverse_norm(rows)).astype(BF16)
    outward.send(first_ref, first_any)
    attention_forward_body(sequences, core_ref, outward, first_ref, w_ref, *outs)


def in_hbm(value):
    return pltpu.with_memory_space_constraint(value, pltpu.HBM)


def hbm_whole():
    return pl.BlockSpec(memory_space=pltpu.HBM)


def attention_scratch():
    return [pltpu.VMEM((WIDTH, ATTN_COLS), BF16), pltpu.SemaphoreType.DMA(())]


def attention_outs(rows):
    outs = [
        shape(rows, WIDTH, BF16),
        far(shape(rows, QKV_COLS, BF16)),
        pltpu.HBM((rows // 64, 256, 128), F32),
        shape(rows, OUT_COLS, BF16),
    ]
    return outs + part_shapes(rows), [vmem_whole(), hbm_whole(), hbm_whole()] + [vmem_whole()] * (1 + 2 * PARTS)


def attention_cost(rows):
    return pl.CostEstimate(
        flops=2 * rows * WIDTH * ATTN_COLS, bytes_accessed=8_000_000, transcendentals=0
    )


def fetch_kernel(column, w_any, *rest):
    out_ref, token_ref, sem = rest[-3:]
    copy = ahead_copy(w_any, out_ref, sem, column)
    copy.start()
    token_ref[...] = jnp.zeros_like(token_ref)
    copy.wait()


TOKEN = jax.ShapeDtypeStruct((8, 128), F32)


def fetch(weights, column, columns, *after):
    return pl.pallas_call(
        functools.partial(fetch_kernel, column),
        in_specs=[hbm_whole()] * (1 + len(after)),
        out_specs=[vmem_whole()] * 2,
        out_shape=[shape(WIDTH, columns, BF16), TOKEN],
        scratch_shapes=[pltpu.SemaphoreType.DMA(())],
        compiler_params=params(12),
        cost_estimate=pl.CostEstimate(
            flops=0, bytes_accessed=2 * WIDTH * columns * 2, transcendentals=0
        ),
        name="fetch",
    )(in_hbm(weights), *[in_hbm(value) for value in after])


def attention_first(core, x, weights, column):
    rows = x.shape[0]
    outs, specs = attention_outs(rows)
    return pl.pallas_call(
        functools.partial(attention_first_kernel, rows // 128, column),
        in_specs=[smem_whole(), vmem_whole(), hbm_whole()],
        out_specs=[hbm_whole()] + specs[1:],
        out_shape=[far(outs[0])] + outs[1:],
        scratch_shapes=[
            pltpu.VMEM((rows, QKV_COLS), BF16),
            pltpu.VMEM((rows // 64, 256, 128), F32),
            pltpu.VMEM((rows, WIDTH), BF16),
        ]
        + attention_scratch()
        + [pltpu.SemaphoreType.DMA((2 + rows // 128,))],
        compiler_params=params(20),
        cost_estimate=attention_cost(rows),
        name="attention_first",
    )(core, x, in_hbm(weights))


def attention_next(core, middle, sums, weights, token):
    rows = middle.shape[0]
    outs, specs = attention_outs(rows)
    whole = shape(rows, WIDTH, BF16)
    return pl.pallas_call(
        functools.partial(attention_next_kernel, rows // 128),
        in_specs=[smem_whole()] + [vmem_whole()] * (2 + 2 * PARTS) + [hbm_whole()],
        out_specs=[hbm_whole()] * 2 + specs[1:],
        out_shape=[far(whole)] * 2 + outs[1:],
        scratch_shapes=[
            pltpu.VMEM((rows, QKV_COLS), BF16),
            pltpu.VMEM((rows // 64, 256, 128), F32),
            pltpu.VMEM(whole.shape, BF16),
            pltpu.VMEM(whole.shape, BF16),
            pltpu.SemaphoreType.DMA((3 + rows // 128,)),
        ],
        compiler_params=params(16),
        cost_estimate=attention_cost(rows),
        name="attention_next",
    )(core, middle, *sums, weights, token)


def column_tiles(first):
    return [pl.ds(first + HIDDEN_TILE * step, HIDDEN_TILE) for step in range(HIDDEN_STEPS)]


def sigmoid(values):
    return 0.5 * jnp.tanh(0.5 * values) + 0.5


def arrivals(copies):
    for copy in copies[:AHEAD]:
        copy.start()
    place = iter(range(len(copies)))

    def arrive():
        number = next(place)
        copies[number].wait()
        if number + AHEAD < len(copies):
            copies[number + AHEAD].start()

    return arrive


def mlp_forward_kernel(core_ref, x_ref, *rest):
    sums, rest = rest[: 2 * PARTS], rest[2 * PARTS :]
    (w_ref, _, middle_any, second_any, gate_any, up_any, hidden_any), rest = rest[:7], rest[7:]
    outs, (middle_ref, second_ref, gate_ref, up_ref, hidden_ref, out_sems) = rest[:-6], rest[-6:]
    tiles = [(gate, up) for gate, up in zip(column_tiles(0), column_tiles(HIDDEN_COLS))]
    down = pl.ds(2 * HIDDEN_COLS, HIDDEN_COLS)
    for at, columns, part in each_sum(core_ref, sums):
        middle_ref[at, columns] = x_ref[at, columns].astype(F32) + part[...].astype(F32)
    rows = middle_ref[...]
    second_ref[...] = (rows * inverse_norm(rows)).astype(BF16)
    outward = Outward(out_sems)
    outward.send(middle_ref, middle_any)
    outward.send(second_ref, second_any)
    for step, (gate, up) in enumerate(tiles):
        at = slice(HIDDEN_TILE * step, HIDDEN_TILE * (step + 1))
        gate_out = nn_dot(second_ref[...], w_ref[:, gate])
        up_out = nn_dot(second_ref[...], w_ref[:, up])
        gate_ref[:, at] = gate_out
        up_ref[:, at] = up_out
        hidden_ref[:, at] = (gate_out * sigmoid(gate_out) * up_out).astype(BF16)
        for ref, target in ((gate_ref, gate_any), (up_ref, up_any), (hidden_ref, hidden_any)):
            outward.send(ref.at[:, at], target.at[:, at])
    write_partial(core_ref, hidden_ref, w_ref, down, outs)
    outward.wait()


HIDDEN_STEPS = HIDDEN_COLS // HIDDEN_TILE


def mlp_cost(rows):
    return pl.CostEstimate(
        flops=2 * rows * WIDTH * MLP_COLS, bytes_accessed=15_000_000, transcendentals=0
    )


def mlp_forward(core, x, sums, weights, token):
    rows = x.shape[0]
    saved = [
        shape(rows, WIDTH, F32),
        shape(rows, WIDTH, BF16),
        shape(rows, HIDDEN_COLS, F32),
        shape(rows, HIDDEN_COLS, F32),
        shape(rows, HIDDEN_COLS, BF16),
    ]
    return pl.pallas_call(
        mlp_forward_kernel,
        in_specs=[smem_whole()] + [vmem_whole()] * (2 + 2 * PARTS) + [hbm_whole()],
        out_specs=[hbm_whole()] * 5 + [vmem_whole()] * (2 * PARTS),
        out_shape=[far(array) for array in saved] + part_shapes(rows),
        scratch_shapes=[pltpu.VMEM(out.shape, out.dtype) for out in saved]
        + [pltpu.SemaphoreType.DMA((2 + 3 * HIDDEN_STEPS,))],
        compiler_params=params(24),
        cost_estimate=mlp_cost(rows),
        name="mlp_forward",
    )(core, x, *sums, weights, token)


def mlp_grads(hidden_grad, gate_out, up_out):
    sigmoid_gate = sigmoid(gate_out)
    gate_grad = hidden_grad * up_out * (sigmoid_gate * (1.0 + gate_out * (1.0 - sigmoid_gate)))
    return gate_grad.astype(BF16), (hidden_grad * (gate_out * sigmoid_gate)).astype(BF16)


def mlp_backward_kernel(core_ref, x_ref, middle_grad_ref, *rest):
    sums, rest = rest[: 2 * PARTS], rest[2 * PARTS :]
    (gate_ref, up_ref, w_ref, _, g_ref, pair_grad_ref), rest = rest[:6], rest[6:]
    outs, weighted = rest[:-1], rest[-1]
    for at, columns, part in each_sum(core_ref, sums):
        weighted[at, columns] = part[...].astype(F32)
    rows = x_ref[...].astype(F32)
    g_ref[...] = (
        middle_grad_ref[...] + norm_back(weighted[...], rows, inverse_norm(rows))
    ).astype(BF16)
    for step, down in enumerate(column_tiles(2 * HIDDEN_COLS)):
        at = slice(HIDDEN_TILE * step, HIDDEN_TILE * (step + 1))
        up_at = slice(HIDDEN_COLS + at.start, HIDDEN_COLS + at.stop)
        hidden_grad = nn_dot(g_ref[...], w_ref[:, down])
        pair_grad_ref[:, at], pair_grad_ref[:, up_at] = mlp_grads(
            hidden_grad, gate_ref[:, at], up_ref[:, at]
        )
    write_partial(core_ref, pair_grad_ref, w_ref, slice(0, 2 * HIDDEN_COLS), outs)


def mlp_backward(core, above, gate_out, up_out, weights, token):
    rows = gate_out.shape[0]
    return pl.pallas_call(
        mlp_backward_kernel,
        in_specs=[smem_whole()] + [vmem_whole()] * (5 + 2 * PARTS) + [hbm_whole()],
        out_specs=[vmem_whole()] * (2 + 2 * PARTS),
        out_shape=[shape(rows, WIDTH, BF16), shape(rows, 2 * HIDDEN_COLS, BF16)]
        + part_shapes(rows),
        scratch_shapes=[pltpu.VMEM((rows, WIDTH), F32)],
        compiler_params=params(26),
        cost_estimate=mlp_cost(rows),
        name="mlp_backward",
    )(core, *above, gate_out, up_out, weights, token)


def mlp_ahead_kernel(g_ref, w_any, hidden_grad_ref, pair_ref, token_ref, down_ref, sems):
    down = ahead_copy(w_any, down_ref, sems.at[0], 2 * HIDDEN_COLS)
    pair = ahead_copy(w_any, pair_ref, sems.at[1], 0)
    down.start()
    pair.start()
    token_ref[...] = jnp.zeros_like(token_ref)
    down.wait()
    hidden_grad_ref[...] = nn_dot(g_ref[...], down_ref[...])
    pair.wait()


def mlp_ahead(g, weights):
    rows = g.shape[0]
    return pl.pallas_call(
        mlp_ahead_kernel,
        in_specs=[vmem_whole(), hbm_whole()],
        out_specs=[vmem_whole()] * 3,
        out_shape=[
            shape(rows, HIDDEN_COLS, F32),
            shape(WIDTH, 2 * HIDDEN_COLS, BF16),
            TOKEN,
        ],
        scratch_shapes=[pltpu.VMEM((WIDTH, HIDDEN_COLS), BF16), pltpu.SemaphoreType.DMA((2,))],
        compiler_params=params(15),
        cost_estimate=pl.CostEstimate(
            flops=2 * rows * WIDTH * HIDDEN_COLS, bytes_accessed=14_000_000, transcendentals=0
        ),
        name="mlp_ahead",
    )(g, in_hbm(weights))


def mlp_last_kernel(core_ref, x_ref, *rest):
    sums, rest = rest[: 2 * PARTS], rest[2 * PARTS :]
    (hidden_grad_ref, w_ref, _, middle_any, hidden_any, second_ref, hidden_ref, pair_grad_ref), rest = rest[:8], rest[8:]
    middle_ref, out_sems = rest
    for at, columns, part in each_sum(core_ref, sums):
        middle_ref[at, columns] = x_ref[at, columns].astype(F32) + part[...].astype(F32)
    rows = middle_ref[...]
    second_ref[...] = (rows * inverse_norm(rows)).astype(BF16)
    outward = Outward(out_sems)
    outward.send(middle_ref, middle_any)
    for step, (gate, up) in enumerate(zip(column_tiles(0), column_tiles(HIDDEN_COLS))):
        at = slice(HIDDEN_TILE * step, HIDDEN_TILE * (step + 1))
        up_at = slice(HIDDEN_COLS + at.start, HIDDEN_COLS + at.stop)
        gate_out = nn_dot(second_ref[...], w_ref[:, gate])
        up_out = nn_dot(second_ref[...], w_ref[:, up])
        hidden_ref[:, at] = (gate_out * sigmoid(gate_out) * up_out).astype(BF16)
        pair_grad_ref[:, at], pair_grad_ref[:, up_at] = mlp_grads(
            hidden_grad_ref[:, at], gate_out, up_out
        )
    outward.send(hidden_ref, hidden_any)
    outward.wait()


def mlp_last(core, x, sums, hidden_grad, pair_weights, token):
    rows = x.shape[0]
    return pl.pallas_call(
        mlp_last_kernel,
        in_specs=[smem_whole()] + [vmem_whole()] * (3 + 2 * PARTS) + [hbm_whole()],
        out_specs=[hbm_whole()] * 2 + [vmem_whole()] * 3,
        out_shape=[
            pltpu.HBM((rows, WIDTH), F32),
            pltpu.HBM((rows, HIDDEN_COLS), BF16),
            shape(rows, WIDTH, BF16),
            shape(rows, HIDDEN_COLS, BF16),
            shape(rows, 2 * HIDDEN_COLS, BF16),
        ],
        scratch_shapes=[pltpu.VMEM((rows, WIDTH), F32), pltpu.SemaphoreType.DMA((2,))],
        compiler_params=params(28),
        cost_estimate=mlp_cost(rows),
        name="mlp_last",
    )(core, x, *sums, hidden_grad, pair_weights, token)


def mlp_in_kernel(core_ref, pair_grad_ref, w_any, _, *rest):
    outs, w_ref, sems = rest[:-2], rest[-2], rest[-1]
    copies = []
    for which in (1, 0):
        half = half_of(core_ref, which)
        source = w_any.at[half, pl.ds(0, 2 * HIDDEN_COLS)]
        copies.append(pltpu.make_async_copy(source, w_ref.at[half, :], sems.at[which]))
        copies[-1].start()
    for copy, which in zip(copies, (1, 0)):
        copy.wait()
        write_half(core_ref, which, pair_grad_ref, w_ref, slice(0, 2 * HIDDEN_COLS), outs)


def mlp_in(core, pair_grad, weights, token):
    rows = pair_grad.shape[0]
    return pl.pallas_call(
        mlp_in_kernel,
        in_specs=[smem_whole(), vmem_whole()] + [hbm_whole()] * 2,
        out_specs=[vmem_whole()] * (2 * PARTS),
        out_shape=part_shapes(rows),
        scratch_shapes=[
            pltpu.VMEM((WIDTH, 2 * HIDDEN_COLS), BF16),
            pltpu.SemaphoreType.DMA((2,)),
        ],
        compiler_params=params(18),
        cost_estimate=pl.CostEstimate(
            flops=4 * rows * WIDTH * HIDDEN_COLS, bytes_accessed=9_000_000, transcendentals=0
        ),
        name="mlp_in",
    )(core, pair_grad, in_hbm(weights), token)


def mlp_down_kernel(core_ref, hidden_ref, w_any, *rest):
    outs, w_ref, sem = rest[:-2], rest[-2], rest[-1]
    copy = pltpu.make_async_copy(w_any.at[:, pl.ds(2 * HIDDEN_COLS, HIDDEN_COLS)], w_ref, sem)
    copy.start()
    copy.wait()
    write_partial(core_ref, hidden_ref, w_ref, slice(0, HIDDEN_COLS), outs)


def mlp_down(core, hidden, weights):
    rows = hidden.shape[0]
    return pl.pallas_call(
        mlp_down_kernel,
        in_specs=[smem_whole(), vmem_whole(), hbm_whole()],
        out_specs=[vmem_whole()] * (2 * PARTS),
        out_shape=part_shapes(rows),
        scratch_shapes=[pltpu.VMEM((WIDTH, HIDDEN_COLS), BF16), pltpu.SemaphoreType.DMA(())],
        compiler_params=params(14),
        cost_estimate=pl.CostEstimate(
            flops=2 * rows * WIDTH * HIDDEN_COLS, bytes_accessed=5_000_000, transcendentals=0
        ),
        name="mlp_down",
    )(core, hidden, in_hbm(weights))


def attention_backward_kernel(sequences, near, core_ref, g_ref, middle_ref, *rest):
    sums, rest = rest[: 2 * PARTS], rest[2 * PARTS :]
    (w_ref, qkv_any, prob_any, _, middle_grad_out, attn_in_ref, qkv_grad_ref), rest = rest[:7], rest[7:]
    outs, (middle_grad_ref, qkv_ref, prob_ref, mix_grad, sems) = rest[:-5], rest[-5:]
    copies = [
        pltpu.make_async_copy(qkv_any, qkv_ref, sems.at[0]),
        pltpu.make_async_copy(prob_any, prob_ref, sems.at[1]),
    ]
    for copy in copies:
        copy.start()
    for at, columns, part in each_sum(core_ref, sums):
        middle_grad_ref[at, columns] = part[...].astype(F32)
    middle = middle_ref[...]
    middle_grad = g_ref[...].astype(F32) + norm_back(
        middle_grad_ref[...], middle, inverse_norm(middle)
    )
    if near:
        middle_grad_out[...] = middle_grad
    else:
        middle_grad_ref[...] = middle_grad
        outward = pltpu.make_async_copy(middle_grad_ref, middle_grad_out, sems.at[2])
        outward.start()
    attn_in_ref[...] = middle_grad.astype(BF16)
    mix_grad[...] = nn_dot(attn_in_ref[...], w_ref[:, QKV_COLS:]).astype(BF16)
    for copy in copies:
        copy.wait()
    for sequence in range(sequences):
        rows = slice(128 * sequence, 128 * (sequence + 1))
        for group in range(2):
            at = 2 * HEAD_WIDTH * group
            key_at = QUERY_COLS + HEAD_WIDTH * group
            value_at = key_at + KV_COLS
            grads = two_heads(mix_grad, rows, at)
            queries = two_heads(qkv_ref, rows, at)
            keys = qkv_ref[rows, key_at : key_at + HEAD_WIDTH]
            probability = prob_ref[2 * sequence + group]
            prob_grad = nt_dot(grads, qkv_ref[rows, value_at : value_at + HEAD_WIDTH])
            centred = jnp.sum(probability * prob_grad, axis=-1, keepdims=True)
            score_grad = (probability * (prob_grad - centred)).astype(BF16)
            query_grad = (nn_dot(score_grad, keys) * SCORE_SCALE).astype(BF16)
            qkv_grad_ref[rows, at : at + HEAD_WIDTH] = query_grad[:128]
            qkv_grad_ref[rows, at + HEAD_WIDTH : at + 2 * HEAD_WIDTH] = query_grad[128:]
            qkv_grad_ref[rows, key_at : key_at + HEAD_WIDTH] = (
                tn_dot(score_grad, queries) * SCORE_SCALE
            ).astype(BF16)
            qkv_grad_ref[rows, value_at : value_at + HEAD_WIDTH] = tn_dot(
                probability.astype(BF16), grads
            ).astype(BF16)
    if near:
        write_partial(core_ref, qkv_grad_ref, w_ref, slice(0, QKV_COLS), outs)
    else:
        outward.wait()


def attention_in_kernel(core_ref, qkv_grad_ref, w_ref, _, *outs):
    write_partial(core_ref, qkv_grad_ref, w_ref, slice(0, QKV_COLS), outs)


def attention_in(core, qkv_grad, weights, token):
    rows = qkv_grad.shape[0]
    return pl.pallas_call(
        attention_in_kernel,
        in_specs=[smem_whole()] + [vmem_whole()] * 2 + [hbm_whole()],
        out_specs=[vmem_whole()] * (2 * PARTS),
        out_shape=part_shapes(rows),
        compiler_params=params(14),
        cost_estimate=pl.CostEstimate(
            flops=2 * rows * WIDTH * QKV_COLS, bytes_accessed=5_000_000, transcendentals=0
        ),
        name="attention_in",
    )(core, qkv_grad, weights, token)


def attention_backward(core, g, middle, sums, qkv, probability, weights, token, near):
    rows = g.shape[0]
    residual, parts = shape(rows, WIDTH, F32), part_shapes(rows) if near else []
    return pl.pallas_call(
        functools.partial(attention_backward_kernel, rows // 128, near),
        in_specs=[smem_whole()] + [vmem_whole()] * (3 + 2 * PARTS) + [hbm_whole()] * 3,
        out_specs=[vmem_whole() if near else hbm_whole()] + [vmem_whole()] * (2 + len(parts)),
        out_shape=[
            residual if near else far(residual),
            shape(rows, WIDTH, BF16),
            shape(rows, QKV_COLS, BF16),
        ]
        + parts,
        scratch_shapes=[
            pltpu.VMEM((rows, WIDTH), F32),
            pltpu.VMEM(qkv.shape, BF16),
            pltpu.VMEM(probability.shape, F32),
            pltpu.VMEM((rows, OUT_COLS), BF16),
            pltpu.SemaphoreType.DMA((3,)),
        ],
        compiler_params=params(24),
        cost_estimate=attention_cost(rows),
        name="attention_backward",
    )(core, g, middle, *sums, weights, in_hbm(qkv), in_hbm(probability), token)


def write_products(start, pairs, out_any, slots, sems):
    _, height, width = slots.shape
    copies = []
    for number in range(WIDTH // height):
        features = pl.ds(height * number, height)
        if number >= 2:
            copies[number - 2].wait()
        slot = slots.at[number % 2]
        at = 0
        for left, right in pairs:
            columns = right.shape[1]
            slot[:, at : at + columns] = tn_dot(left[:, features], right[...]).astype(BF16)
            at += columns
        target = out_any.at[features, pl.ds(start, width)]
        copies.append(pltpu.make_async_copy(slot, target, sems.at[number % 2]))
        copies[-1].start()
    for copy in copies[-2:]:
        copy.wait()


def mlp_weights_kernel(second_ref, g_ref, pair_grad_ref, hidden_ref, *rest):
    out_any, token_ref, slots, sems = rest[-4:]
    token_ref[...] = jnp.zeros_like(token_ref)
    write_products(0, [(second_ref, pair_grad_ref), (g_ref, hidden_ref)], out_any, slots, sems)


def into_buffer(kernel, buffer, columns, slot, operands, flops, name, mib):
    aliases, specs = {}, [vmem_whole()] * len(operands)
    if buffer is not None:
        aliases = {len(operands): 0}
        specs, operands = specs + [hbm_whole()], operands + (in_hbm(buffer),)
    return pl.pallas_call(
        kernel,
        in_specs=specs,
        out_specs=[hbm_whole(), vmem_whole()],
        out_shape=[pltpu.HBM((WIDTH, columns), BF16), TOKEN],
        input_output_aliases=aliases,
        scratch_shapes=[pltpu.VMEM((2, *slot), BF16), pltpu.SemaphoreType.DMA((2,))],
        compiler_params=params(mib),
        cost_estimate=pl.CostEstimate(flops=flops, bytes_accessed=flops // 250, transcendentals=0),
        name=name,
    )(*operands)


def mlp_weights(buffer, columns, second, g, pair_grad, hidden):
    return into_buffer(
        mlp_weights_kernel,
        buffer,
        columns,
        (512, MLP_COLS),
        (second, g, pair_grad, hidden),
        2 * second.shape[0] * WIDTH * MLP_COLS,
        "mlp_weights",
        18,
    )


def attention_weights_kernel(start, first_ref, attn_in_ref, qkv_grad_ref, mix_ref, *rest):
    out_any, token_ref, slots, sems = rest[-4:]
    token_ref[...] = jnp.zeros_like(token_ref)
    pairs = [(first_ref, qkv_grad_ref), (attn_in_ref, mix_ref)]
    write_products(start, pairs, out_any, slots, sems)


def attention_weights(buffer, columns, start, first, attn_in, qkv_grad, mixture):
    return into_buffer(
        functools.partial(attention_weights_kernel, start),
        buffer,
        columns,
        (768, ATTN_COLS),
        (first, attn_in, qkv_grad, mixture),
        2 * first.shape[0] * WIDTH * ATTN_COLS,
        "attention_weights",
        14,
    )


def sum_four(partial, beside=None, within=None):
    keeps, gives = list(partial[:PARTS]), list(partial[PARTS:])
    chips = [
        (keep.astype(F32) + swap(give, "section").astype(F32)).astype(BF16)
        for keep, give in zip(keeps, gives)
    ]
    arrived = [swap(chip, "tensor") for chip in chips]
    if beside is not None:
        arrived[-1], beside = lax.optimization_barrier((arrived[-1], beside))
    totals = [
        (chip.astype(F32) + other.astype(F32)).astype(BF16)
        for chip, other in zip(chips, arrived)
    ]
    if within is not None:

        def tie(value):
            totals[0], value = lax.optimization_barrier((totals[0], value))
            return value

        beside = within(tie)
    return totals + [swap(total, "section") for total in totals], beside


def row_scales(gain_ref):
    row = lax.broadcasted_iota(jnp.int32, (48, 48), 0)
    column = lax.broadcasted_iota(jnp.int32, (48, 48), 1)
    return jnp.where(row == column, gain_ref[...].astype(F32), 0.0).astype(BF16)


def pack_kernel(core_ref, *rest):
    sources, (mine_ref, give_ref), shards, sems = rest[:9], rest[9:11], rest[11:20], rest[20]
    copies = [
        pltpu.make_async_copy(source, shard, sems.at[number])
        for number, (source, shard) in enumerate(zip(sources, shards))
    ]
    for copy in copies:
        copy.start()
    is_first = core_ref[0] == 0
    (attn_gain_ref, mlp_gain_ref), shards = shards[:2], shards[2:]
    for copy in copies[:2]:
        copy.wait()
    attn_scale, mlp_scale = row_scales(attn_gain_ref), row_scales(mlp_gain_ref)
    start = 0
    for copy, shard, scale in zip(
        copies[2:],
        shards,
        (mlp_scale, mlp_scale, None, attn_scale, attn_scale, attn_scale, None),
    ):
        copy.wait()
        weight = shard[...]
        if scale is not None:
            weight = nn_dot(scale, weight).astype(BF16)
        width = weight.shape[1] // 2
        low, high = weight[:, :width], weight[:, width:]
        mine_ref[:, start : start + width] = jnp.where(is_first, low, high)
        give_ref[:, start : start + width] = jnp.where(is_first, high, low)
        start += width


def pack_shards(core, *shards):
    return pl.pallas_call(
        pack_kernel,
        in_specs=[smem_whole()] + [hbm_whole()] * len(shards),
        out_specs=[vmem_whole()] * 2,
        out_shape=[shape(48, LAYER_COLS, BF16)] * 2,
        scratch_shapes=[pltpu.VMEM(shard.shape, shard.dtype) for shard in shards]
        + [pltpu.SemaphoreType.DMA((len(shards),))],
        compiler_params=params(16),
        name="pack_shards",
    )(core, *[in_hbm(shard) for shard in shards])


def combine_kernel(core_ref, keep_ref, arrived_ref, last_ref, zero_w_ref, one_w_ref, mine_ref, give_ref, terms_ref, zero, one):
    rest = (keep_ref[...].astype(F32) + arrived_ref[...].astype(F32)).astype(BF16)
    zero[:, :MLP_COLS] = rest[:, :MLP_COLS]
    zero[:, MLP_COLS:] = rest[:, LAYER_COLS:]
    one[:, :MLP_COLS] = last_ref[...]
    one[:, MLP_COLS:] = rest[:, MLP_COLS:LAYER_COLS]
    is_first = core_ref[0] == 0
    mine_ref[...] = jnp.where(is_first, zero[...], one[...])
    give_ref[...] = jnp.where(is_first, one[...], zero[...])
    row = 0
    for grad, weights in ((zero, zero_w_ref), (one, one_w_ref)):
        products = weights[...].astype(F32) * grad[...].astype(F32)
        for columns in (slice(MLP_COLS, MLP_COLS + QKV_COLS), slice(0, 2 * HIDDEN_COLS)):
            terms_ref[row, :] = jnp.sum(products[:, columns], axis=1)
            row += 1


def combine_grads(core, *operands):
    return pl.pallas_call(
        combine_kernel,
        in_specs=[smem_whole()] + [vmem_whole()] * len(operands),
        out_specs=[vmem_whole()] * 3,
        out_shape=[shape(48, LAYER_COLS, BF16)] * 2 + [shape(4, 48, F32)],
        scratch_shapes=[pltpu.VMEM((48, LAYER_COLS), BF16)] * 2,
        compiler_params=params(16),
        name="combine_grads",
    )(core, *operands)


def unpack_kernel(core_ref, attn_scale_ref, mlp_scale_ref, mine_ref, got_ref, gate_ref, up_ref, down_ref, query_ref, key_ref, value_ref, out_ref):
    is_first = core_ref[0] == 0

    def place(out, start, scale_ref):
        width = out.shape[1] // 2
        mine = mine_ref[:, start : start + width].astype(F32)
        got = got_ref[:, start : start + width].astype(F32)
        if scale_ref is not None:
            mine, got = mine * scale_ref[...], got * scale_ref[...]
        out[:, :width] = jnp.where(is_first, mine, got)
        out[:, width:] = jnp.where(is_first, got, mine)

    place(gate_ref, 0, mlp_scale_ref)
    place(up_ref, HIDDEN_COLS, mlp_scale_ref)
    place(down_ref, 2 * HIDDEN_COLS, None)
    place(query_ref, MLP_COLS, attn_scale_ref)
    place(key_ref, MLP_COLS + QUERY_COLS, attn_scale_ref)
    place(value_ref, MLP_COLS + QUERY_COLS + KV_COLS, attn_scale_ref)
    place(out_ref, MLP_COLS + QKV_COLS, None)


def unpack_grads(core, *operands):
    widths = [HIDDEN_COLS] * 3 + [QUERY_COLS, KV_COLS, KV_COLS, OUT_COLS]
    return pl.pallas_call(
        unpack_kernel,
        in_specs=[smem_whole()] + [vmem_whole()] * len(operands),
        out_specs=[vmem_whole()] * len(widths),
        out_shape=[shape(48, 2 * width, F32) for width in widths],
        compiler_params=params(16),
        name="unpack_grads",
    )(core, *operands)


def gather_rows(z_low, share):
    other = swap(share, "zl")
    pair = jnp.concatenate([pick(z_low, share, other), pick(z_low, other, share)], axis=0)
    return lax.all_gather(pair, ("y", "x"), axis=0, tiled=True)


def scatter_pair(grad):
    return lax.psum_scatter(grad, ("y", "x"), scatter_dimension=0, tiled=True)


def scatter_low(z_low, pair):
    keep = pick(z_low, pair[:48], pair[48:])
    give = pick(z_low, pair[48:], pair[:48])
    return (keep.astype(F32) + swap(give, "zl").astype(F32)).astype(BF16)


def to_ring_order(rows):
    lead = rows.shape[:-1]
    return jnp.swapaxes(rows.reshape(lead + (4, 2, 4, 48)), -3, -2).reshape(rows.shape)


def from_ring_order(rows):
    lead = rows.shape[:-1]
    return jnp.swapaxes(rows.reshape(lead + (4, 4, 2, 48)), -3, -2).reshape(rows.shape)


def join_positions(tensor, own):
    other = swap(own, "tensor")
    return jnp.concatenate(
        [pick(tensor, own, other), pick(tensor, other, own)], axis=1
    ).reshape(384, WIDTH)


def own_positions(tensor, rows):
    rows = rows.reshape(3, 128, 1536)
    return pick(tensor, rows[:, :64], rows[:, 64:])


def per_device(
    inputs, cotangent, plan, attn_gain, mlp_gain, w_query, key_weight, value_weight,
    w_out, w_gate, w_up, w_down,
):
    core = lax.axis_index("section")
    z_low = lax.axis_index("zl")
    tensor = lax.axis_index("tensor")

    attn_scale = attn_gain[0].astype(F32)[:, None]
    mlp_scale = mlp_gain[0].astype(F32)[:, None]

    core_ref = core.astype(jnp.int32).reshape(1)
    mine, give = pack_shards(
        core_ref, attn_gain, mlp_gain,
        w_gate[0], w_up[0], w_down[0].T, w_query[0], key_weight[0], value_weight[0], w_out[0].T,
    )
    got = swap(give, "section")
    layer_zero, layer_one = pick(core, mine, got), pick(core, got, mine)
    first_weights = gather_rows(
        z_low, jnp.concatenate([layer_zero, layer_one[:, MLP_COLS:]], axis=1)
    )
    last_weights = gather_rows(z_low, layer_one[:, :MLP_COLS])

    stream = join_positions(tensor, to_ring_order(inputs[:, 0][plan]))
    stream, late = lax.optimization_barrier((stream, cotangent))
    out_grad = join_positions(tensor, to_ring_order(late[:, 0][plan]))
    stream, out_grad = lax.optimization_barrier((stream, out_grad))

    def whole_rows(sums):
        own, other = jnp.concatenate(sums[:PARTS]), jnp.concatenate(sums[PARTS:])
        return jnp.concatenate([pick(core, own, other), pick(core, other, own)], axis=1).astype(F32)

    x_zero = stream
    first_zero, qkv_zero, prob_zero, mix_zero, *partial = attention_first(
        core_ref, x_zero, first_weights, MLP_COLS
    )
    near, token = fetch(first_weights, 0, MLP_COLS)
    sums, token = sum_four(partial, beside=token)
    middle_zero, second_zero, gate_zero, up_zero, hidden_zero, *partial = mlp_forward(
        core_ref, x_zero, sums, near, token
    )
    near, token = fetch(first_weights, LAYER_COLS, ATTN_COLS)
    sums, token = sum_four(partial, beside=token)
    x_one, first_one, qkv_one, prob_one, mix_one, *partial = attention_next(
        core_ref, middle_zero, sums, near, token
    )
    sums, ahead = sum_four(partial, within=lambda tie: mlp_ahead(out_grad, tie(last_weights)))
    hidden_grad, near, token = ahead

    middle_one, hidden_far, second_one, hidden_one, pair_grad = mlp_last(
        core_ref, x_one, sums, hidden_grad, near, token
    )
    one_mlp, done = mlp_weights(None, MLP_COLS, second_one, out_grad, pair_grad, hidden_one)
    last_pair = scatter_pair(one_mlp)
    partial = mlp_in(core_ref, pair_grad, last_weights, done)
    near, token = fetch(first_weights, LAYER_COLS, ATTN_COLS, one_mlp)
    sums, token = sum_four(partial, beside=token)
    middle_grad, attn_in, qkv_grad, *partial = attention_backward(
        core_ref, out_grad, middle_one, sums, qkv_one, prob_one, near, token, True
    )
    buffer, _ = attention_weights(None, REST_COLS, MLP_COLS, first_one, attn_in, qkv_grad, mix_one)
    near, token = fetch(first_weights, 0, MLP_COLS, buffer)
    sums, (buffer, token) = sum_four(partial, beside=(buffer, token))

    grad_one, pair_grad, *partial = mlp_backward(
        core_ref, (x_one, middle_grad, *sums), gate_zero, up_zero, near, token
    )
    buffer, _ = mlp_weights(buffer, REST_COLS, second_zero, grad_one, pair_grad, hidden_zero)
    near, token = fetch(first_weights, MLP_COLS, ATTN_COLS, buffer)
    sums, (buffer, token) = sum_four(partial, beside=(buffer, token))
    hidden_far, sums[0] = lax.optimization_barrier((hidden_far, sums[0]))
    down_partial = mlp_down(core_ref, hidden_far, last_weights)
    middle_grad, attn_in, qkv_grad = attention_backward(
        core_ref, grad_one, middle_zero, sums, qkv_zero, prob_zero, near, token, False
    )
    buffer, done = attention_weights(
        buffer, REST_COLS, LAYER_COLS, first_zero, attn_in, qkv_grad, mix_zero
    )
    rest_pair = scatter_pair(buffer)
    sums, _ = sum_four(attention_in(core_ref, qkv_grad, near, done))
    rows = x_zero.astype(F32)
    grad_zero = middle_grad + norm_back(whole_rows(sums), rows, inverse_norm(rows))
    down_sums, _ = sum_four(down_partial)
    result_one = (middle_one + whole_rows(down_sums)).astype(BF16)
    outputs = [own_positions(tensor, x_one), own_positions(tensor, result_one)]
    grads = [own_positions(tensor, grad_zero.astype(BF16)), own_positions(tensor, grad_one)]

    layer_outputs = from_ring_order(pick(core, outputs[0], outputs[1]))
    input_grads = from_ring_order(pick(core, grads[0], grads[1]))
    last_grad = scatter_low(z_low, last_pair)
    rest_pair, layer_outputs, input_grads, last_grad = lax.optimization_barrier(
        (rest_pair, layer_outputs, input_grads, last_grad)
    )
    keep = pick(z_low, rest_pair[:48], rest_pair[48:])
    arrived = swap(pick(z_low, rest_pair[48:], rest_pair[:48]), "zl")
    mine, give, terms = combine_grads(
        core_ref, keep, arrived, last_grad, layer_zero, layer_one
    )
    got = swap(give, "section")
    arrived = swap(terms, "tensor")
    gate_grad, up_grad, down_grad, query_grad, key_grad, value_grad, out_weight_grad = unpack_grads(
        core_ref, attn_scale, mlp_scale, mine, got
    )
    arrived, key_grad = lax.optimization_barrier((arrived, key_grad))
    terms = terms + arrived
    terms = pick(core, terms[:2], terms[2:]) + swap(pick(core, terms[2:], terms[:2]), "section")
    return (
        layer_outputs[None, :, None],
        input_grads[None, :, None],
        (terms[0] / attn_scale[:, 0])[None],
        (terms[1] / mlp_scale[:, 0])[None],
        query_grad[None],
        key_grad[None],
        value_grad[None],
        out_weight_grad.T[None],
        gate_grad[None],
        up_grad[None],
        down_grad.T[None],
    )


def solution(mesh):
    split = Mesh(mesh.devices.reshape(2, 4, 2, 4, 2), ("section", "y", "zl", "x", "tensor"))
    dp = ("y", "zl", "x")
    rows = P("section", dp, "tensor")
    columns = P("section", "tensor", dp)
    return jax.shard_map(
        per_device,
        mesh=split,
        in_specs=(
            P(None, dp, "tensor", None),
            P(None, dp, "tensor", None),
            P(),
            P("section", dp),
            P("section", dp),
            rows,
            rows,
            rows,
            columns,
            rows,
            rows,
            columns,
        ),
        out_specs=(
            P("section", None, dp, "tensor", None),
            P("section", None, dp, "tensor", None),
            P("section", dp),
            P("section", dp),
            rows,
            rows,
            rows,
            columns,
            rows,
            rows,
            columns,
        ),
        check_vma=False,
    )
```
